32 devices in a mesh: tok: 8 (over z, core), hid: 4 (over y, x).
Axes of the slice: x: 2, y: 2, z: 4, core: 2. Of those that a mesh axis runs over, the one named last changes fastest.
Arguments:
- tokens: bfloat16 [32768, 1024], P('tok', 'hid'), may hold values from -6 to 6
- middle_cond: bfloat16 [8192, 1024], P('tok', 'hid'), may hold values from -6 to 6
- coarse_cond: bfloat16 [2048, 1024], P('tok', 'hid'), may hold values from -6 to 6
- first_gain: float32 [1024], P('hid'), may hold values from 0.1 to 1.9
- first_shift: float32 [1024], P('hid'), may hold values from -3 to 3
- attend_weight: bfloat16 [1024, 3, 1024], P('tok', None, 'hid'), may hold values from -0.1875 to 0.1875
- query_bias: float32 [1024], P('hid'), may hold values from -3 to 3
- value_bias: float32 [1024], P('hid'), may hold values from -3 to 3
- output_weight: bfloat16 [1024, 1024], P('hid', 'tok'), may hold values from -0.75 to 0.75
- mixer_bias: float32 [1024], P('hid'), may hold values from -3 to 3
- second_gain: float32 [1024], P('hid'), may hold values from 0.1 to 1.9
- second_shift: float32 [1024], P('hid'), may hold values from -3 to 3
- up_weight: bfloat16 [1024, 4096], P('tok', 'hid'), may hold values from -1 to 1
- hidden_bias: float32 [4096], P('hid'), may hold values from -3 to 3
- down_weight: bfloat16 [4096, 1024], P('hid', 'tok'), may hold values from -0.09375 to 0.09375
- down_bias: float32 [1024], P('hid'), may hold values from -3 to 3
- cotangent: bfloat16 [32768, 1024], P('tok', 'hid'), may hold values from -6 to 6
Outputs:
- layer_out: bfloat16 [32768, 1024], P('tok', 'hid')
- grad_tokens: float32 [32768, 1024], P('tok', 'hid')
- grad_middle: float32 [8192, 1024], P('tok', 'hid')
- grad_coarse: float32 [2048, 1024], P('tok', 'hid')
- grad_first_gain: float32 [1024], P(('hid', 'tok'))
- grad_first_shift: float32 [1024], P(('hid', 'tok'))
- grad_attend: float32 [1024, 3, 1024], P('tok', None, 'hid')
- grad_query_bias: float32 [1024], P(('hid', 'tok'))
- grad_value_bias: float32 [1024], P(('hid', 'tok'))
- grad_output: float32 [1024, 1024], P('hid', 'tok')
- grad_mixer_bias: float32 [1024], P(('hid', 'tok'))
- grad_second_gain: float32 [1024], P(('hid', 'tok'))
- grad_second_shift: float32 [1024], P(('hid', 'tok'))
- grad_up: float32 [1024, 4096], P('tok', 'hid')
- grad_hidden_bias: float32 [4096], P(('hid', 'tok'))
- grad_down: float32 [4096, 1024], P('hid', 'tok')
- grad_down_bias: float32 [1024], P(('hid', 'tok'))
The draws below stay inside these ranges and needn't reach their ends.
All inputs are finite; a program needn't handle non-finite values.
Results may differ from the reference program's by a relative error of at most 0.017.
Values may be sent and summed in bfloat16 or wider, within the bound.
A program may use at most 256 MiB of HBM per device.

```python
import math
import jax
import jax.numpy as jnp
from jax import lax

D = 1024
HEADS = 16
HEAD = 64
FF = 4096
BLOCK = 128
TOKENS = 32768


def draw_up_weight(key, part):
    key = jax.random.fold_in(key, 11)
    entry_key, column_key = jax.random.split(key)
    entries = jax.random.truncated_normal(entry_key, -6.0, 6.0, (D, FF), jnp.float32)
    columns = jax.random.truncated_normal(column_key, -6.0, 6.0, (FF,), jnp.float32)
    return ((entries + 0.4 * columns[None, :]) * D ** (-0.5)).astype(jnp.bfloat16)


def levels(rng, shape, shards, least, top_value):
    factor_of = 1.0
    for dim, blocks in shards:
        steps = jax.random.uniform(jax.random.fold_in(jax.random.fold_in(rng, 6), dim), (blocks,), jnp.float32, least / len(shards), top_value / len(shards))
        factor_of = factor_of * jnp.repeat(jnp.exp(steps), shape[dim] // blocks).reshape((-1,) + (1,) * (len(shape) - 1 - dim))
    return factor_of


def normal_values(stream_key, shape, spread, most, pieces=(), held_as=jnp.bfloat16):
    array = spread * jax.random.normal(stream_key, shape, jnp.float32)
    if pieces:
        array = array * levels(stream_key, shape, pieces, -0.22, 0.18)
    return jnp.clip(array, -most, most).astype(held_as)


def setup_inputs(seed: int = 0) -> dict:
    key_list = jax.random.split(jax.random.key(seed), 18)
    tokens = normal_values(key_list[0], (TOKENS, D), 1.0, 6.0, ((0, 8), (1, 4)))
    middle_cond = normal_values(key_list[1], (TOKENS // 4, D), 1.0, 6.0, ((0, 8), (1, 4)))
    coarse_cond = normal_values(key_list[2], (TOKENS // 16, D), 1.0, 6.0, ((0, 8), (1, 4)))
    first_gain = jnp.clip(1.0 + 0.18 * jax.random.normal(key_list[3], (D,), jnp.float32), 0.1, 1.9)
    first_shift = normal_values(key_list[4], (D,), 0.5, 3.0, ((0, 4),), jnp.float32)
    attend_weight = normal_values(key_list[5], (D, 3, D), D ** -0.5, 0.1875, ((0, 8), (2, 4)))
    query_bias = normal_values(key_list[6], (D,), 0.5, 3.0, ((0, 4),), jnp.float32)
    value_bias = normal_values(key_list[7], (D,), 0.5, 3.0, ((0, 4),), jnp.float32)
    output_weight = normal_values(key_list[8], (D, D), (D // 16) ** -0.5, 0.75, ((0, 4), (1, 8)))
    mixer_bias = normal_values(key_list[9], (D,), 0.5, 3.0, ((0, 4),), jnp.float32)
    second_gain = jnp.clip(1.0 + 0.18 * jax.random.normal(key_list[10], (D,), jnp.float32), 0.1, 1.9)
    second_shift = normal_values(key_list[11], (D,), 0.5, 3.0, ((0, 4),), jnp.float32)
    up_weight = draw_up_weight(jax.random.fold_in(key_list[17], 71), 0)
    hidden_bias = normal_values(key_list[13], (FF,), 0.5, 3.0, ((0, 4),), jnp.float32)
    down_weight = normal_values(key_list[14], (FF, D), FF ** -0.5, 0.09375, ((0, 4), (1, 8)))
    down_bias = normal_values(key_list[15], (D,), 0.5, 3.0, ((0, 4),), jnp.float32)
    cotangent = normal_values(key_list[16], (TOKENS, D), 1.0, 6.0, ((0, 8), (1, 4)))
    return {"tokens": tokens, "middle_cond": middle_cond, "coarse_cond": coarse_cond, "first_gain": first_gain, "first_shift": first_shift, "attend_weight": attend_weight, "query_bias": query_bias, "value_bias": value_bias, "output_weight": output_weight, "mixer_bias": mixer_bias, "second_gain": second_gain, "second_shift": second_shift, "up_weight": up_weight, "hidden_bias": hidden_bias, "down_weight": down_weight, "down_bias": down_bias, "cotangent": cotangent}


@jax.custom_vjp
def low(v):
    return lax.optimization_barrier(v.astype(jnp.bfloat16)).astype(jnp.float32)

@jax.custom_vjp
def low_back(v):
    return v

def low_keep(v):
    return (low(v), None)

def low_pass(kept, grad):
    return (grad,)

def back_keep(v):
    return (v, None)

def back_low(kept, grad):
    return (low(grad),)
low.defvjp(low_keep, low_pass)
low_back.defvjp(back_keep, back_low)
highest = lax.Precision.HIGHEST

def product(left, right):
    return jnp.dot(left, right, precision=highest)

def norm_rows(values, gain_row, shift_row):
    average = lax.optimization_barrier(jnp.mean(values, axis=1, keepdims=True))
    variance = lax.optimization_barrier(jnp.mean(values * values, axis=1, keepdims=True)) - average * average
    return (values - average) * lax.rsqrt(variance + 1e-05) * gain_row + shift_row

def attend_group(stacked):
    length = stacked.shape[1]
    queries = stacked[0].reshape(length // BLOCK, BLOCK, HEADS, HEAD)
    key_rows = stacked[1].reshape(length // BLOCK, BLOCK, HEADS, HEAD)
    value_rows = stacked[2].reshape(length // BLOCK, BLOCK, HEADS, HEAD)
    scores = low_back(jnp.einsum('bqhd,bkhd->bhqk', queries, key_rows, precision=highest))
    logits = scores * HEAD ** (-0.5)
    places = jnp.arange(BLOCK)
    allowed = places[:, None] >= places[None, :]
    logits = jnp.where(allowed, logits, -1e+30)
    totals = jax.nn.logsumexp(logits, axis=-1, keepdims=True)
    attention = low(jnp.exp(logits - totals))
    attended = jnp.einsum('bhqk,bkhd->bqhd', attention, value_rows, precision=highest)
    return attended.reshape(length, HEADS * HEAD)

def forward(tokens, middle_cond, coarse_cond, first_gain, first_shift, attend_weight, query_bias, value_bias, output_weight, mixer_bias, second_gain, second_shift, up_weight, hidden_bias, down_weight, down_bias):
    summed = tokens + jnp.repeat(middle_cond, 4, axis=0) + jnp.repeat(coarse_cond, 16, axis=0)
    normed = low(norm_rows(summed, first_gain, first_shift))
    no_bias = jnp.zeros_like(query_bias)
    biases = jnp.stack([query_bias, no_bias, value_bias])
    projected = jnp.einsum('td,dck->tck', normed, attend_weight, precision=highest) + biases[None]
    projected = low_back(low(projected))
    group_rows = math.gcd(TOKENS, 4096)
    stacked = projected.reshape(TOKENS // group_rows, group_rows, 3, D).transpose(0, 2, 1, 3)
    attended = lax.map(jax.checkpoint(attend_group), stacked).reshape(TOKENS, D)
    attended = low_back(low(attended))
    branch_out = low_back(product(attended, output_weight) + mixer_bias)
    residual = summed + branch_out
    normed_two = low(norm_rows(residual, second_gain, second_shift))
    before = low_back(product(normed_two, up_weight) + hidden_bias)
    hidden = low(jax.nn.gelu(before))
    feed_out = low_back(product(hidden, down_weight) + down_bias)
    return residual + feed_out

def reference(tokens, middle_cond, coarse_cond, first_gain, first_shift, attend_weight, query_bias, value_bias, output_weight, mixer_bias, second_gain, second_shift, up_weight, hidden_bias, down_weight, down_bias, cotangent):
    inputs = [member.astype(jnp.float32) for member in (tokens, middle_cond, coarse_cond, first_gain, first_shift, attend_weight, query_bias, value_bias, output_weight, mixer_bias, second_gain, second_shift, up_weight, hidden_bias, down_weight, down_bias)]
    result, pullback = jax.vjp(forward, *inputs)
    gradients = pullback(cotangent.astype(jnp.float32))
    return (result.astype(jnp.bfloat16), gradients[0], gradients[1], gradients[2], gradients[3], gradients[4], gradients[5], gradients[6], gradients[7], gradients[8], gradients[9], gradients[10], gradients[11], gradients[12], gradients[13], gradients[14], gradients[15])
```

```python
import jax
import jax.numpy as jnp
from jax import lax
from jax.sharding import PartitionSpec as P

D = 1024
HEAD = 64
BLOCK = 128


epsilon = 1e-05


def split_heads(values):
    positions, features = values.shape
    return values.reshape(positions // BLOCK, BLOCK, features // HEAD, HEAD)


def block_logits(queries, key_rows):
    scores = jnp.einsum("bqhd,bkhd->bhqk", queries, key_rows, preferred_element_type=jnp.float32)
    logits = scores * HEAD ** (-0.5)
    places = jnp.arange(BLOCK)
    allowed = places[:, None] >= places[None, :]
    return jnp.where(allowed, logits, -1e30)


def project_heads(normed, attend_full, biases):
    return (
        jnp.einsum("td,dck->tck", normed, attend_full, preferred_element_type=jnp.float32) + biases
    ).astype(jnp.bfloat16)


def attend_forward(projected):
    queries = split_heads(projected[:, 0])
    key_rows = split_heads(projected[:, 1])
    value_rows = split_heads(projected[:, 2])
    logits = block_logits(queries, key_rows)
    totals = jax.nn.logsumexp(logits, axis=-1, keepdims=True)
    attention = jnp.exp(logits - totals).astype(jnp.bfloat16)
    attended = jnp.einsum(
        "bhqk,bkhd->bqhd", attention, value_rows, preferred_element_type=jnp.float32
    )
    return (attended.reshape(projected.shape[0], projected.shape[2]).astype(jnp.bfloat16), totals)


def attend_backward(projected, totals, grad_attended):
    positions, features = grad_attended.shape
    queries = split_heads(projected[:, 0])
    key_rows = split_heads(projected[:, 1])
    value_rows = split_heads(projected[:, 2])
    grad_heads = split_heads(grad_attended)
    logits = block_logits(queries, key_rows)
    attention_f = jnp.exp(logits - totals)
    attention_b = attention_f.astype(jnp.bfloat16)
    grad_attention = jnp.einsum(
        "bqhd,bkhd->bhqk", grad_heads, value_rows, preferred_element_type=jnp.float32
    )
    grad_values = jnp.einsum(
        "bhqk,bqhd->bkhd", attention_b, grad_heads, preferred_element_type=jnp.float32
    )
    centre = jnp.sum(attention_f * grad_attention, axis=-1, keepdims=True)
    grad_scores = (attention_f * (grad_attention - centre) * HEAD ** (-0.5)).astype(jnp.bfloat16)
    grad_queries = jnp.einsum(
        "bhqk,bkhd->bqhd", grad_scores, key_rows, preferred_element_type=jnp.float32
    )
    grad_keys = jnp.einsum(
        "bhqk,bqhd->bkhd", grad_scores, queries, preferred_element_type=jnp.float32
    )
    pieces = [
        member.reshape(positions, features) for member in (grad_queries, grad_keys, grad_values)
    ]
    return jnp.stack(pieces, axis=1).astype(jnp.bfloat16)


def spread(values):
    return lax.all_to_all(values, "hid", split_axis=0, concat_axis=1, tiled=True)


def unspread(values):
    return lax.all_to_all(values, "hid", split_axis=1, concat_axis=0, tiled=True)


def gather_all(part):
    return lax.all_gather(part, ("hid", "tok"), axis=0)


def scatter_all(partial_value):
    return lax.psum_scatter(
        partial_value.astype(jnp.bfloat16), ("hid", "tok"), scatter_dimension=0
    ).astype(jnp.float32)


def whole(vector):
    return lax.all_gather(vector, "hid", axis=0, tiled=True)


def norm_stats(values):
    average = jnp.mean(values, axis=1, keepdims=True)
    inverse = lax.rsqrt(
        jnp.mean(values * values, axis=1, keepdims=True) - average * average + epsilon
    )
    return (values - average) * inverse, inverse


def norm_backward(upstream, scaled, inverse, gain_row):
    weighted = upstream * gain_row
    mean_weighted = jnp.mean(weighted, axis=1, keepdims=True)
    mean_dot = jnp.mean(weighted * scaled, axis=1, keepdims=True)
    grad_input = inverse * (weighted - mean_weighted - scaled * mean_dot)
    return (grad_input, jnp.sum(upstream * scaled, axis=0), jnp.sum(upstream, axis=0))


def shards(
    tokens,
    middle_cond,
    coarse_cond,
    first_gain,
    first_shift,
    attend_weight,
    query_bias,
    value_bias,
    output_weight,
    mixer_bias,
    second_gain,
    second_shift,
    up_weight,
    hidden_bias,
    down_weight,
    down_bias,
    cotangent,
):
    positions, features = tokens.shape
    n_hid = lax.axis_size("hid")
    n_tok = lax.axis_size("tok")
    summed_part = (
        tokens.astype(jnp.float32).reshape(positions // 16, 4, 4, features)
        + middle_cond.astype(jnp.float32).reshape(positions // 16, 4, 1, features)
        + coarse_cond.astype(jnp.float32)[:, None, None, :]
    ).reshape(positions, features)
    summed = spread(summed_part.astype(jnp.bfloat16)).astype(jnp.float32)
    first_gain, first_shift, query_bias, value_bias = map(
        whole, (first_gain, first_shift, query_bias, value_bias)
    )
    mixer_bias, second_gain, second_shift, down_bias, hidden_bias = map(
        whole, (mixer_bias, second_gain, second_shift, down_bias, hidden_bias)
    )
    attend_full = (
        gather_all(attend_weight)
        .reshape(n_hid, D, 3, features)
        .transpose(1, 2, 0, 3)
        .reshape(D, 3, D)
    )
    output_full = (
        gather_all(output_weight)
        .reshape(n_hid, n_tok, features, D // n_tok)
        .transpose(0, 2, 1, 3)
        .reshape(D, D)
    )
    up_full = gather_all(up_weight).reshape(n_hid, D, up_weight.shape[1])
    down_full = (
        gather_all(down_weight)
        .reshape(n_hid, n_tok, down_weight.shape[0], D // n_tok)
        .transpose(0, 2, 1, 3)
        .reshape(n_hid, down_weight.shape[0], D)
    )
    scaled, inverse = norm_stats(summed)
    normed = (scaled * first_gain + first_shift).astype(jnp.bfloat16)
    biases = jnp.stack([query_bias, jnp.zeros_like(query_bias), value_bias])
    projected = project_heads(normed, attend_full, biases)
    attended, totals = attend_forward(projected)
    branch_out = jnp.dot(attended, output_full, preferred_element_type=jnp.float32)
    residual = summed + (branch_out + mixer_bias)
    scaled_two, inverse_two = norm_stats(residual)
    normed_two = (scaled_two * second_gain + second_shift).astype(jnp.bfloat16)
    upstream_low = spread(cotangent)
    upstream = upstream_low.astype(jnp.float32)
    hidden_chunk = up_weight.shape[1]
    feed_out = 0.0
    grad_normed_two = 0.0
    grad_ups, grad_downs, grad_hidden_biases = [], [], []
    for chunk in range(n_hid):
        bias = hidden_bias[chunk * hidden_chunk : (chunk + 1) * hidden_chunk]
        before = jnp.dot(normed_two, up_full[chunk], preferred_element_type=jnp.float32) + bias
        activated, gelu_pull = jax.vjp(jax.nn.gelu, before)
        hidden = activated.astype(jnp.bfloat16)
        feed_out = feed_out + jnp.dot(hidden, down_full[chunk], preferred_element_type=jnp.float32)
        grad_downs.append(
            jnp.einsum("tf,td->fd", hidden, upstream_low, preferred_element_type=jnp.float32)
        )
        grad_hidden = jnp.einsum(
            "td,fd->tf", upstream_low, down_full[chunk], preferred_element_type=jnp.float32
        )
        grad_before = gelu_pull(grad_hidden)[0].astype(jnp.bfloat16)
        grad_hidden_biases.append(jnp.sum(grad_before.astype(jnp.float32), axis=0))
        grad_ups.append(
            jnp.einsum("td,tf->df", normed_two, grad_before, preferred_element_type=jnp.float32)
        )
        grad_normed_two = grad_normed_two + jnp.einsum(
            "tf,df->td", grad_before, up_full[chunk], preferred_element_type=jnp.float32
        )
    layer_out = unspread((residual + (feed_out + down_bias)).astype(jnp.bfloat16))
    grad_up = scatter_all(
        jnp.stack(grad_ups).astype(jnp.bfloat16).reshape(n_hid * n_tok, D // n_tok, hidden_chunk)
    )
    grad_down = scatter_all(
        jnp.stack(grad_downs)
        .astype(jnp.bfloat16)
        .reshape(n_hid, hidden_chunk, n_tok, D // n_tok)
        .transpose(0, 2, 1, 3)
        .reshape(n_hid * n_tok, hidden_chunk, D // n_tok)
    )
    grad_down_bias = jnp.sum(upstream, axis=0)
    grad_back_two, grad_second_gain, grad_second_shift = norm_backward(
        grad_normed_two, scaled_two, inverse_two, second_gain
    )
    grad_residual = upstream + grad_back_two
    grad_mixed = grad_residual.astype(jnp.bfloat16)
    grad_mixer_bias = jnp.sum(grad_mixed.astype(jnp.float32), axis=0)
    grad_output = scatter_all(
        jnp.einsum("tk,td->kd", attended, grad_mixed, preferred_element_type=jnp.float32)
        .astype(jnp.bfloat16)
        .reshape(n_hid, features, n_tok, D // n_tok)
        .transpose(0, 2, 1, 3)
        .reshape(n_hid * n_tok, features, D // n_tok)
    )
    grad_attended = jnp.einsum(
        "td,kd->tk", grad_mixed, output_full, preferred_element_type=jnp.float32
    ).astype(jnp.bfloat16)
    grad_projected = attend_backward(projected, totals, grad_attended)
    grad_query_bias = jnp.sum(grad_projected[:, 0].astype(jnp.float32), axis=0)
    grad_value_bias = jnp.sum(grad_projected[:, 2].astype(jnp.float32), axis=0)
    grad_attend = scatter_all(
        jnp.einsum("td,tck->dck", normed, grad_projected, preferred_element_type=jnp.float32)
        .astype(jnp.bfloat16)
        .reshape(n_tok, D // n_tok, 3, n_hid, features)
        .transpose(3, 0, 1, 2, 4)
        .reshape(n_hid * n_tok, D // n_tok, 3, features)
    )
    grad_normed = jnp.einsum(
        "tck,dck->td", grad_projected, attend_full, preferred_element_type=jnp.float32
    )
    grad_back, grad_first_gain, grad_first_shift = norm_backward(
        grad_normed, scaled, inverse, first_gain
    )
    grad_tokens = unspread((grad_residual + grad_back).astype(jnp.bfloat16)).astype(jnp.float32)
    grad_middle = jnp.sum(grad_tokens.reshape(positions // 4, 4, features), axis=1)
    grad_coarse = jnp.sum(grad_tokens.reshape(positions // 16, 16, features), axis=1)
    small_grads = jnp.stack(
        [
            grad_first_gain,
            grad_first_shift,
            grad_second_gain,
            grad_second_shift,
            grad_query_bias,
            grad_value_bias,
            grad_mixer_bias,
            grad_down_bias,
        ]
    )
    share = D // (n_hid * n_tok)
    wide = hidden_chunk // n_tok
    packed = jnp.concatenate(
        [
            small_grads.reshape(8, n_hid * n_tok, share)
            .transpose(1, 0, 2)
            .reshape(n_hid * n_tok, 8 * share),
            jnp.concatenate(grad_hidden_biases).reshape(n_hid * n_tok, wide),
        ],
        axis=1,
    )
    packed = lax.psum_scatter(packed, ("hid", "tok"), scatter_dimension=0)
    small = packed[: 8 * share].reshape(8, share)
    return (
        layer_out,
        grad_tokens,
        grad_middle,
        grad_coarse,
        small[0],
        small[1],
        grad_attend,
        small[4],
        small[5],
        grad_output,
        small[6],
        small[2],
        small[3],
        grad_up,
        packed[8 * share :],
        grad_down,
        small[7],
    )


def solution(mesh):
    return jax.shard_map(
        shards,
        mesh=mesh,
        in_specs=(
            P("tok", "hid"),
            P("tok", "hid"),
            P("tok", "hid"),
            P("hid"),
            P("hid"),
            P("tok", None, "hid"),
            P("hid"),
            P("hid"),
            P("hid", "tok"),
            P("hid"),
            P("hid"),
            P("hid"),
            P("tok", "hid"),
            P("hid"),
            P("hid", "tok"),
            P("hid"),
            P("tok", "hid"),
        ),
        out_specs=(
            P("tok", "hid"),
            P("tok", "hid"),
            P("tok", "hid"),
            P("tok", "hid"),
            P(("hid", "tok")),
            P(("hid", "tok")),
            P("tok", None, "hid"),
            P(("hid", "tok")),
            P(("hid", "tok")),
            P("hid", "tok"),
            P(("hid", "tok")),
            P(("hid", "tok")),
            P(("hid", "tok")),
            P("tok", "hid"),
            P(("hid", "tok")),
            P("hid", "tok"),
            P(("hid", "tok")),
        ),
        check_vma=False,
    )
```

```python
import functools

import jax
import jax.numpy as jnp
from jax import lax
from jax.experimental import pallas as pl
from jax.experimental.pallas import tpu as pltpu
from jax.sharding import PartitionSpec as P

HEAD = 64
BLOCK = 128
PAIR = 2 * HEAD
EPSILON = 1e-05
MESH = pl.DeviceIdType.MESH
BF16 = jnp.bfloat16
F32 = jnp.float32
SMALL_ROWS = 16


class Tree:
    def __init__(self, n_hid):
        self.n = n_hid
        self.bits = n_hid.bit_length() - 1
        units = [(r, f) for r in range(n_hid) for f in (0, 1)]
        self.units = sorted(units, key=lambda u: (u[0].bit_count(), len(self.children(*u)), u))
        self.pos = {u: k for k, u in enumerate(self.units)}

    def children(self, r, f):
        held = [b for b in range(self.bits) if r >> b & 1]
        free = [b for b in range(self.bits) if not r >> b & 1]
        if held:
            free = [b for b in free if (b < held[0] if f == 0 else b > held[-1])]
        return [(r | 1 << b, b) for b in free]

    def parent(self, r, f):
        held = [b for b in range(self.bits) if r >> b & 1]
        return held[0] if f == 0 else held[-1]


class Schedule:
    def __init__(self, tree, done, weights_lag, last_point):
        self.at = {}
        self.turn = {}
        self.before = {}
        self.first = set()
        sent = {}
        holders = [None, None]
        waiting = sorted(done, key=lambda u: done[u])
        held = None
        point = 0
        while waiting or held is not None:
            actions = []
            if held is not None:
                actions.append(("finish", held))
                sent[held] = point
                held = None
            for unit in waiting:
                kind, r, f = unit
                kids = [(kind, k, f) for k, _ in tree.children(r, f)]
                if point <= done[unit] or any(k not in sent for k in kids):
                    continue
                if point < last_point and any(point < sent[k] + weights_lag[kind] for k in kids):
                    continue
                actions.append(("fetch", unit))
                held = unit
                self.turn[unit] = k = len(self.turn) % 2
                self.before[unit] = holders[k]
                if (kind, r) not in {(other[0], other[1]) for other in self.turn if other != unit}:
                    self.first.add(unit)
                holders[k] = unit
                waiting.remove(unit)
                break
            if actions:
                self.at[point] = actions
            point += 1
        self.end = point
        self.holders = holders


def dot(a, b):
    return jnp.dot(a, b, preferred_element_type=F32)


def dot_t(a, b):
    return lax.dot_general(a, b, (((1,), (1,)), ((), ())), preferred_element_type=F32)


def dot_l(a, b):
    return lax.dot_general(a, b, (((0,), (0,)), ((), ())), preferred_element_type=F32)


def repeat_matrix(rows, times):
    row = lax.broadcasted_iota(jnp.int32, (rows, rows // times), 0)
    column = lax.broadcasted_iota(jnp.int32, (rows, rows // times), 1) * times
    return ((row >= column) & (row < column + times)).astype(BF16)


def group_matrix(rows, times):
    row = lax.broadcasted_iota(jnp.int32, (rows // times, rows), 0) * times
    column = lax.broadcasted_iota(jnp.int32, (rows // times, rows), 1)
    return ((column >= row) & (column < row + times)).astype(BF16)


def scaled_rows(values):
    width = values.shape[1]
    average = jnp.sum(values, axis=1, keepdims=True) / width
    square = jnp.sum(values * values, axis=1, keepdims=True) / width
    inverse = lax.rsqrt(square - average * average + EPSILON)
    return (values - average) * inverse, inverse


def norm_pull(grad, gain, scaled, inverse):
    width = grad.shape[1]
    weighted = grad * gain
    mean = jnp.sum(weighted, axis=1, keepdims=True) / width
    along = jnp.sum(weighted * scaled, axis=1, keepdims=True) / width
    return inverse * (weighted - mean - scaled * along)


def row_sum(values):
    return jnp.sum(values, axis=0, keepdims=True)


def two_heads(values):
    low = lax.broadcasted_iota(jnp.int32, values.shape, 1) < HEAD
    zero = jnp.zeros_like(values)
    return jnp.concatenate([jnp.where(low, values, zero), jnp.where(low, zero, values)], axis=0)


def pick_heads(both):
    low = lax.broadcasted_iota(jnp.int32, (BLOCK, PAIR), 1) < HEAD
    return jnp.where(low, both[:BLOCK], both[BLOCK:])


INPUTS = ("tokens", "middle", "coarse", "cotangent", "a_own", "m_own", "params")
OUTPUTS = (
    "layer_out",
    "grad_rows",
    "grad_a",
    "grad_m",
    "small",
    "all_a",
    "all_m",
    "own_ga",
    "sib_ga",
    "got_ga",
    "own_gm",
    "sib_gm",
    "got_gm",
    "z_ga",
    "z_gm",
)


class Sizes:
    def __init__(self, positions, features, d, ff, n_tok, n_hid):
        self.d, self.n_hid, self.n_tok = d, n_hid, n_tok
        self.z = n_tok // 2
        self.n = positions // n_hid
        self.kh = features
        self.fs = ff // n_hid // 2
        self.tb = d // n_tok
        self.half = self.tb // 2
        self.wide = 4 * features
        self.pairs = features // PAIR
        self.tile = min(256, self.n)
        self.tiles = self.n // self.tile
        self.blocks = self.n // BLOCK
        self.positions = positions


def layer_kernel(size, tree, *refs):
    names = list(INPUTS) + list(OUTPUTS) + list(scratch(size, tree))
    ref = dict(zip(names, refs, strict=True))
    s_ = size
    n_units = len(tree.units)
    tok, h = lax.axis_index("tok"), lax.axis_index("hid")
    z, c = tok // 2, lax.rem(tok, 2)

    def block_of(r):
        total = 0
        for b in range(tree.bits):
            total = total + lax.rem(h // (1 << b) + r // (1 << b), 2) * (1 << b)
        return total

    def peer(r):
        return (tok, block_of(r))

    sibling = (tok + 1 - 2 * c, h)

    def z_peer(step):
        return (lax.rem(z + step, s_.z) * 2 + c, h)

    def columns(j, width):
        return pl.ds(pl.multiple_of(j * width, width), width)

    def remote(name, index, src, dst, device):
        return pltpu.make_async_remote_copy(
            src_ref=src,
            dst_ref=dst,
            send_sem=ref[name + "_s"].at[index],
            recv_sem=ref[name + "_r"].at[index],
            device_id=device,
            device_id_type=MESH,
        )

    def send(name, index, src, dst, device):
        remote(name, index, src, dst, device).start()

    def arrived(name, index, dst):
        remote(name, index, dst, dst, sibling).wait_recv()

    def left(name, index, src):
        remote(name, index, src, src, sibling).wait_send()

    def local(index, src, dst):
        return pltpu.make_async_copy(src, dst, ref["local"].at[index])

    barrier = pltpu.get_barrier_semaphore()
    everyone = [peer(r) for r in range(1, s_.n_hid)] + [sibling]
    everyone += [z_peer(k) for k in range(1, s_.z)]
    for device in everyone:
        pl.semaphore_signal(barrier, inc=1, device_id=device, device_id_type=MESH)
    pl.semaphore_wait(barrier, len(everyone))

    def z_send(name, index, src, dst):
        for step in range(1, s_.z):
            send(name, index * s_.z + step, src, dst, z_peer(step))

    def z_arrived(name, index, dst):
        for step in range(1, s_.z):
            arrived(name, index * s_.z + step, dst)

    def z_left(name, index, src):
        for step in range(1, s_.z):
            left(name, index * s_.z + step, src)

    def a_part(r, f, core):
        return ref["all_a"].at[r, :, core, pl.ds(f * s_.half, s_.half)]

    def m_part(r, f, core):
        return ref["all_m"].at[tree.pos[r, f], :, core]

    part = {"a": a_part, "m": m_part}

    for r in range(1, s_.n_hid):
        here = ref["params_all"].at[:, columns(h, s_.kh)]
        send("params", r, ref["params"], here, peer(r))
    own_params = local(0, ref["params"], ref["params_all"].at[:, columns(h, s_.kh)])
    own_params.start()
    z_send("za", 0, ref["a_own"], ref["all_a"].at[0, z, c])
    own_a = local(1, ref["a_own"], ref["all_a"].at[0, z, c])
    own_a.start()
    own_m = []
    for f in (0, 1):
        own_m.append(local(2 + f, ref["m_own"].at[f], ref["all_m"].at[tree.pos[0, f], z, c]))
        own_m[f].start()

    kh, n, tile = s_.kh, s_.n, s_.tile
    rows_m, rows_c = n // 4, n // 16
    loads = {}
    order = list(range(1, s_.n_hid)) + [0]
    for r in order:
        j = block_of(r)
        sources = (
            (ref["tokens"].at[columns(j, n)], ref["pj"].at[r, :, pl.ds(0, kh)]),
            (ref["middle"].at[columns(j, rows_m)], ref["pj"].at[r, pl.ds(0, rows_m), pl.ds(2 * kh, kh)]),
            (ref["coarse"].at[columns(j, rows_c)], ref["pj"].at[r, pl.ds(rows_m, rows_c), pl.ds(2 * kh, kh)]),
        )
        loads[r] = [local(4 + 3 * r + k, *pair) for k, pair in enumerate(sources)]
        for copy in loads[r]:
            copy.start()
    repeat_4, repeat_16 = repeat_matrix(tile, 4), repeat_matrix(tile, 16)

    def xs_rows(i, j):
        return ref["xs"].at[pl.ds(i * tile, tile), columns(j, kh)]

    own_xs = []
    for i in range(s_.tiles):
        for r in order:
            if i == 0:
                for copy in loads[r]:
                    copy.wait()
            rows = pl.ds(i * tile, tile)
            middle = ref["pj"][r, pl.ds(i * (tile // 4), tile // 4), pl.ds(2 * kh, kh)]
            coarse = ref["pj"][r, pl.ds(rows_m + i * (tile // 16), tile // 16), pl.ds(2 * kh, kh)]
            total = ref["pj"][r, rows, pl.ds(0, kh)].astype(F32)
            total = total + dot(repeat_4, middle) + dot(repeat_16, coarse)
            ref["pj"][r, rows, pl.ds(kh, kh)] = total.astype(BF16)
            source = ref["pj"].at[r, rows, pl.ds(kh, kh)]
            if r:
                send("xs", i * s_.n_hid + r, source, xs_rows(i, h), peer(r))
            else:
                copy = local(4 + 3 * s_.n_hid + i, source, xs_rows(i, h))
                copy.start()
                own_xs.append(copy)

    for f in (0, 1):
        z_send("zm", f, ref["m_own"].at[f], ref["all_m"].at[tree.pos[0, f], z, c])

    def pass_on(kind, r, f):
        k = tree.pos[r, f]
        for child, b in tree.children(r, f):
            send(kind + "x", tree.pos[child, f], part[kind](r, f, c), part[kind](child, f, c), peer(1 << b))
        send(kind + "c", k, part[kind](r, f, c), part[kind](r, f, c), sibling)

    def take(kind, r, f):
        arrived(kind + "x", tree.pos[r, f], part[kind](r, f, c))
        pass_on(kind, r, f)

    def take_sibling(kind, r, f):
        arrived(kind + "c", tree.pos[r, f], part[kind](r, f, 1 - c))

    own_a.wait()
    z_arrived("za", 0, ref["all_a"].at[0, z, c])
    for f in (0, 1):
        pass_on("a", 0, f)

    own_params.wait()
    for r in range(1, s_.n_hid):
        arrived("params", r, ref["params_all"].at[:, columns(h, kh)])

    def gain_row(k):
        return ref["params_all"][pl.ds(k, 1), :]

    for k, (r, f) in enumerate(tree.units):
        parts = [
            ref["params_all"][pl.ds(8 + 2 * f + i, 1), columns(block_of(r), kh)] for i in range(s_.fs // kh)
        ]
        ref["hidden_bias"][k] = jnp.concatenate(parts, axis=1)
        ref["hidden_sum"][k] = jnp.zeros((1, s_.fs), F32)
    ref["sums"][...] = jnp.zeros_like(ref["sums"])

    def add_sum(k, values):
        ref["sums"][pl.ds(k, 1), :] = ref["sums"][pl.ds(k, 1), :] + row_sum(values)

    for i in range(s_.tiles):
        own_xs[i].wait()
        for r in range(1, s_.n_hid):
            arrived("xs", i * s_.n_hid + r, xs_rows(i, h))
        rows = pl.ds(i * tile, tile)
        scaled, _ = scaled_rows(ref["xs"][rows, :].astype(F32))
        normed = (scaled * gain_row(0) + gain_row(1)).astype(BF16)
        ref["nrm"][rows, :] = normed
        ref["nrm_t"][:, rows] = normed.T

    for i in range(s_.tiles):
        for r in range(1, s_.n_hid):
            left("xs", i * s_.n_hid + r, xs_rows(i, h))

    def weight_load(slot, source):
        return pltpu.make_async_copy(source, ref["wa"].at[slot], ref["wload"].at[slot])

    def matrix(slot, first, width):
        return ref["wa"][slot, :, :, :, pl.ds(first, width)].reshape(s_.d, width)

    def put_rows(slot, zz, first, values):
        width = values.shape[1]
        ref["wa"][slot, zz, :, :, pl.ds(first, width)] = values.reshape(2, s_.tb, width)

    def cot_rows(j):
        return ref["ct"].at[:, columns(j, kh)]

    own_ct = local(0, ref["cotangent"].at[columns(h, n)], cot_rows(h))

    def before_chunk(r):
        if r == 0:
            pass
        elif r.bit_count() == 1:
            if r == 1:
                for u, f in tree.units:
                    if u.bit_count() == 1:
                        take("a", u, f)
                own_ct.start()
                for k in range(1, s_.n_hid):
                    send("ct", k, ref["cotangent"].at[columns(block_of(k), n)], cot_rows(h), peer(k))
        else:
            for f in (0, 1):
                take("a", r, f)
        if r == s_.n_hid - 1:
            for f in (0, 1):
                own_m[f].wait()
                z_arrived("zm", f, ref["all_m"].at[tree.pos[0, f], z, c])
            for f in (0, 1):
                pass_on("m", 0, f)
        for f in (0, 1):
            take_sibling("a", r, f)
        load = weight_load(r, ref["all_a"].at[r])
        load.start()
        load.wait()

    causal_row = lax.broadcasted_iota(jnp.int32, (BLOCK, 2 * BLOCK), 0)
    causal_col = lax.rem(lax.broadcasted_iota(jnp.int32, (BLOCK, 2 * BLOCK), 1), BLOCK)
    allowed = causal_row >= causal_col

    def halves(values, f):
        return [f(values[:, :BLOCK]), f(values[:, BLOCK:])]

    def spread(pair):
        return jnp.concatenate([jnp.broadcast_to(v, (BLOCK, BLOCK)) for v in pair], axis=1)

    def row_max(v):
        return jnp.max(v, axis=1, keepdims=True)

    def row_add(v):
        return jnp.sum(v, axis=1, keepdims=True)

    def attend_chunk(r):
        for k in range(s_.n_hid):
            pl.when(r == k)(functools.partial(before_chunk, k))
        cols = columns(block_of(r), kh)
        bias = jnp.concatenate(
            [ref["params_all"][4:5, cols], jnp.zeros((1, kh), F32), ref["params_all"][5:6, cols]], axis=1
        )

        def project(i, _):
            rows = pl.ds(pl.multiple_of(i * tile, tile), tile)
            values = dot(ref["nrm"][rows, :], matrix(r, 0, 3 * kh)) + bias
            ref["pj"][r, rows, :] = values.astype(BF16)
            return 0

        lax.fori_loop(0, s_.tiles, project, 0)

        def attend(i, _):
            rows = pl.ds(pl.multiple_of(i * BLOCK, BLOCK), BLOCK)
            for p in range(s_.pairs):
                query, key, value = (ref["pj"][r, rows, pl.ds(k * kh + p * PAIR, PAIR)] for k in range(3))
                logits = jnp.where(allowed, dot_t(query, two_heads(key)) * HEAD ** (-0.5), -1e30)
                powers = jnp.exp(logits - spread(halves(logits, row_max)))
                shares = [1.0 / v for v in halves(powers, row_add)]
                attention = (powers * spread(shares)).astype(BF16)
                ref["probs"][r, p, rows, :] = attention
                out = dot(attention, two_heads(value))
                ref["att"][r, rows, pl.ds(p * PAIR, PAIR)] = out.astype(BF16)
            return 0

        lax.fori_loop(0, s_.blocks, attend, 0)

    lax.fori_loop(0, s_.n_hid, lambda r, _: (attend_chunk(r), 0)[1], 0)

    def mix(i, _):
        rows = pl.ds(pl.multiple_of(i * tile, tile), tile)
        total = ref["xs"][rows, :].astype(F32) + gain_row(6)
        for r in range(s_.n_hid):
            total = total + dot_t(ref["att"][r, rows, :], matrix(r, 3 * kh, kh))
        ref["res"][rows, :] = total
        scaled, _inverse = scaled_rows(total)
        normed = (scaled * gain_row(2) + gain_row(3)).astype(BF16)
        ref["n2"][rows, :] = normed
        return 0

    lax.fori_loop(0, s_.tiles, mix, 0)

    own_ct.wait()
    for k in range(1, s_.n_hid):
        arrived("ct", k, cot_rows(h))
    for i in range(s_.tiles):
        rows = pl.ds(i * tile, tile)
        ref["n2_t"][:, rows] = ref["n2"][rows, :].T
        upstream = ref["ct"][rows, :]
        ref["ct_t"][:, rows] = upstream.T
        add_sum(7, upstream.astype(F32))
        ref["facc"][rows, :] = jnp.zeros((tile, s_.d), F32)
        ref["gacc"][rows, :] = jnp.zeros((tile, s_.d), F32)

    mlp_points = 2 * n_units
    chunk_points = mlp_points + 2
    last_point = chunk_points + 4 * s_.n_hid
    done = {("m", r, f): 2 * k + 1 for k, (r, f) in enumerate(tree.units)}
    for r in range(s_.n_hid):
        for f in (0, 1):
            done["a", r, f] = chunk_points + 4 * (s_.n_hid - 1 - r) + 3
    plan = Schedule(tree, done, {"m": 6, "a": 4}, last_point)

    def own_grad(kind, r, f):
        if kind == "a":
            return ref["own_ga"].at[r, :, pl.ds(f * s_.half, s_.half)]
        return ref["own_gm"].at[tree.pos[r, f]]

    def sib_grad(kind, r, f):
        if kind == "a":
            return ref["sib_ga"].at[r, :, pl.ds(f * s_.half, s_.half)]
        return ref["sib_gm"].at[tree.pos[r, f]]

    def got_grad(kind, r, f):
        if kind == "a":
            return ref["got_ga"].at[tree.pos[r, f]]
        return ref["got_gm"].at[tree.pos[r, f]]

    def buffer(name, kind, k=None):
        whole = ref[name] if k is None else ref[name].at[k]
        return whole.at[:, pl.ds(0, s_.half)] if kind == "a" else whole

    def z_name(kind):
        return ("zga", 0) if kind == "a" else ("zgm", 1)

    def z_slot(kind, f, step):
        if kind == "a":
            return ref["z_ga"].at[f, step]
        return ref["z_gm"].at[f, step]

    def free_buffer(k, holder):
        if holder is None:
            return
        kind, r, f = holder
        source = buffer("acc", kind, k)
        if r:
            left("g" + kind, tree.pos[r, f], source)
        else:
            for step in range(1, s_.z):
                left("zg" + kind, f * s_.z + step, source.at[0])
            local(40 + k, source.at[0], source.at[0]).wait()

    def fetches(unit, k):
        kind, r, f = unit
        kids = tree.children(r, f)
        out = [(30 + 3 * k, own_grad(*unit), buffer("acc", kind, k))]
        out.append((31 + 3 * k, sib_grad(*unit), buffer("tmp", kind, k)))
        if kids:
            out.append((32 + 3 * k, got_grad(kind, kids[0][0], f), buffer("more", kind)))
        return out

    def fetch(unit):
        kind, r, f = unit
        k = plan.turn[unit]
        free_buffer(k, plan.before[unit])
        if kind == "m" or unit in plan.first:
            slot = tree.pos[r, f] if kind == "m" else r
            whole = ref["sib_gm"].at[slot] if kind == "m" else ref["sib_ga"].at[r]
            arrived("s" + kind, slot, whole)
        for kid, _ in tree.children(r, f)[:1]:
            arrived("g" + kind, tree.pos[kid, f], got_grad(kind, kid, f))
        for item in fetches(unit, k):
            local(*item).start()

    def finish(unit):
        kind, r, f = unit
        k = plan.turn[unit]
        kids = tree.children(r, f)
        for item in fetches(unit, k):
            local(*item).wait()
        acc, tmp, more = buffer("acc", kind, k), buffer("tmp", kind, k), buffer("more", kind)
        for zz in range(s_.z):
            total = acc[zz].astype(F32) + tmp[zz].astype(F32)
            if kids:
                total = total + more[zz].astype(F32)
            acc[zz] = total.astype(BF16)
        for kid, _ in kids[1:]:
            source = got_grad(kind, kid, f)
            arrived("g" + kind, tree.pos[kid, f], source)
            copy = local(36, source, more)
            copy.start()
            copy.wait()
            for zz in range(s_.z):
                acc[zz] = (acc[zz].astype(F32) + more[zz].astype(F32)).astype(BF16)
        if r:
            send("g" + kind, tree.pos[r, f], acc, got_grad(kind, r, f), peer(1 << tree.parent(r, f)))
        else:
            for step in range(1, s_.z):
                to = lax.rem(z + step, s_.z)
                send("zg" + kind, f * s_.z + step, acc.at[to], z_slot(kind, f, step), z_peer(step))
            local(40 + k, acc.at[z], z_slot(kind, f, 0)).start()

    def act(point):
        for verb, unit in plan.at.get(point, ()):
            (fetch if verb == "fetch" else finish)(unit)

    def loop_point(step, first, stride, offset, count):
        for k in range(count):
            if first + stride * k + offset in plan.at:
                pl.when(step == k)(functools.partial(act, first + stride * k + offset))

    def stage_copies(kind, index, slot):
        own = ref["own_g" + kind].at[index]
        theirs = ref["sib_g" + kind].at[index]
        keep = pltpu.make_async_copy(ref["wa"].at[slot, :, c], own, ref["keep"].at[slot - 2])
        give = pltpu.make_async_remote_copy(
            src_ref=ref["wa"].at[slot, :, 1 - c],
            dst_ref=theirs,
            send_sem=ref["s" + kind + "_s"].at[index],
            recv_sem=ref["s" + kind + "_r"].at[index],
            device_id=sibling,
            device_id_type=MESH,
        )
        return keep, give

    def stage_out(kind, index, slot):
        for copy in stage_copies(kind, index, slot):
            copy.start()

    def stage_kept(kind, index, slot):
        stage_copies(kind, index, slot)[0].wait()

    def stage_free(kind, index, slot):
        stage_copies(kind, index, slot)[1].wait_send()

    fs = s_.fs
    for k in (0, 1):
        take_sibling("m", *tree.units[k])
    weight_load(0, ref["all_m"].at[0]).start()
    gelu_scale = (2.0 / jnp.pi) ** 0.5

    def feed(step, _):
        slot = lax.rem(step, 2)
        weight_load(slot, ref["all_m"].at[step]).wait()

        def rows_of(i, _):
            rows = pl.ds(pl.multiple_of(i * tile, tile), tile)
            up, down = matrix(slot, 0, fs), matrix(slot, fs, fs)
            before = dot(ref["n2"][rows, :], up) + ref["hidden_bias"][step]
            square = before * before
            bent = jnp.tanh(before * (gelu_scale + (gelu_scale * 0.044715) * square))
            share = 0.5 + 0.5 * bent
            hidden = (before * share).astype(BF16)
            slope = share + 0.5 * before * (1.0 - bent * bent) * (
                gelu_scale + (3.0 * gelu_scale * 0.044715) * square
            )
            grad_before = (dot(ref["ct"][rows, :], down) * slope).astype(BF16)
            ref["hid"][rows, :] = hidden
            ref["gb"][rows, :] = grad_before
            ref["facc"][rows, :] = ref["facc"][rows, :] + dot_t(hidden, down)
            ref["gacc"][rows, :] = ref["gacc"][rows, :] + dot_t(grad_before, up)
            ref["hidden_sum"][step] = ref["hidden_sum"][step] + row_sum(grad_before.astype(F32))
            return 0

        lax.fori_loop(0, s_.tiles, rows_of, 0)
        for k in range(1, n_units - 1):
            pl.when(step == k)(functools.partial(take, "m", *tree.units[k + 1]))

        @pl.when(step >= 1)
        def _():
            stage_kept("m", step - 1, 3 - slot)

        loop_point(step, 0, 2, 0, n_units)
        stage = 2 + slot

        @pl.when(step >= 2)
        def _():
            stage_free("m", step - 2, stage)

        def grads(zz, _):
            rows = pl.ds(pl.multiple_of(zz * (2 * s_.tb), 2 * s_.tb), 2 * s_.tb)
            put_rows(stage, zz, 0, dot(ref["n2_t"][rows, :], ref["gb"][...]).astype(BF16))
            put_rows(stage, zz, fs, dot(ref["ct_t"][rows, :], ref["hid"][...]).astype(BF16))
            return 0

        lax.fori_loop(0, s_.z // 2, grads, 0)
        for k in range(n_units - 1):

            def load_next(k=k):
                if k:
                    take_sibling("m", *tree.units[k + 1])
                weight_load((k + 1) % 2, ref["all_m"].at[k + 1]).start()

            pl.when(step == k)(load_next)
        lax.fori_loop(s_.z // 2, s_.z, grads, 0)
        stage_out("m", step, stage)
        loop_point(step, 0, 2, 1, n_units)
        return 0

    lax.fori_loop(0, n_units, feed, 0)

    stage_kept("m", n_units - 1, 2 + (n_units - 1) % 2)
    act(mlp_points)
    weight_load(0, ref["all_a"].at[s_.n_hid - 1]).start()

    def back_two(i, _):
        rows = pl.ds(pl.multiple_of(i * tile, tile), tile)
        residual = ref["res"][rows, :]
        ref["n2"][rows, :] = (residual + (ref["facc"][rows, :] + gain_row(7))).astype(BF16)
        scaled, inverse = scaled_rows(residual)
        grad = ref["gacc"][rows, :]
        add_sum(2, grad * scaled)
        add_sum(3, grad)
        grad = ref["ct"][rows, :].astype(F32) + norm_pull(grad, gain_row(2), scaled, inverse)
        mixed = grad.astype(BF16)
        add_sum(6, mixed.astype(F32))
        ref["facc"][rows, :] = grad
        ref["gacc"][rows, :] = jnp.zeros((tile, s_.d), F32)
        ref["nrm"][rows, :] = mixed
        return 0

    lax.fori_loop(0, s_.tiles, back_two, 0)

    def out_rows(name, j):
        return ref[name].at[columns(j, n)]

    for r in range(1, s_.n_hid):
        j = block_of(r)
        send("lo", r, ref["n2"].at[:, columns(j, kh)], out_rows("layer_out", h), peer(r))
    own_lo = local(0, ref["n2"].at[:, columns(h, kh)], out_rows("layer_out", h))
    own_lo.start()
    for i in range(s_.tiles):
        rows = pl.ds(i * tile, tile)
        ref["n2_t"][:, rows] = ref["nrm"][rows, :].T
    act(mlp_points + 1)
    for k in range(n_units - 2, n_units):
        stage_free("m", k, 2 + k % 2)

    def back_chunk(step, _):
        r = s_.n_hid - 1 - step
        slot = lax.rem(step, 2)
        stage = 2 + slot
        weight_load(slot, ref["all_a"].at[r]).wait()

        @pl.when(step + 1 < s_.n_hid)
        def _():
            weight_load(1 - slot, ref["all_a"].at[lax.rem(2 * s_.n_hid - 2 - step, s_.n_hid)]).start()

        def pull_out(i, _):
            rows = pl.ds(pl.multiple_of(i * tile, tile), tile)
            ref["hid"][rows, pl.ds(0, kh)] = dot(ref["nrm"][rows, :], matrix(slot, 3 * kh, kh)).astype(BF16)
            return 0

        lax.fori_loop(0, s_.tiles, pull_out, 0)

        @pl.when(step >= 1)
        def _():
            stage_kept("a", r + 1, 3 - slot)

        loop_point(step, chunk_points, 4, 0, s_.n_hid)

        def pull_attention(i, _):
            rows = pl.ds(pl.multiple_of(i * BLOCK, BLOCK), BLOCK)
            for p in range(s_.pairs):
                query, key, value = (ref["pj"][r, rows, pl.ds(k * kh + p * PAIR, PAIR)] for k in range(3))
                grad = ref["hid"][rows, pl.ds(p * PAIR, PAIR)]
                attention = ref["probs"][r, p, rows, :]
                weights = attention.astype(F32)
                grad_attention = dot_t(grad, two_heads(value))
                centre = spread(halves(weights * grad_attention, row_add))
                grad_scores = (weights * (grad_attention - centre) * HEAD ** (-0.5)).astype(BF16)
                grad_query = dot(grad_scores, two_heads(key))
                grad_key = pick_heads(dot_l(grad_scores, query))
                grad_value = pick_heads(dot_l(attention, grad))
                for k, values in enumerate((grad_query, grad_key, grad_value)):
                    ref["pj"][r, rows, pl.ds(k * kh + p * PAIR, PAIR)] = values.astype(BF16)
            return 0

        lax.fori_loop(0, s_.blocks, pull_attention, 0)
        loop_point(step, chunk_points, 4, 1, s_.n_hid)

        @pl.when(step >= 2)
        def _():
            stage_free("a", r + 2, stage)

        cols = columns(block_of(r), kh)

        def grads(zz, _):
            rows = pl.ds(pl.multiple_of(zz * (2 * s_.tb), 2 * s_.tb), 2 * s_.tb)
            put_rows(stage, zz, 0, dot(ref["nrm_t"][rows, :], ref["pj"][r]).astype(BF16))
            put_rows(stage, zz, 3 * kh, dot(ref["n2_t"][rows, :], ref["att"][r]).astype(BF16))
            return 0

        lax.fori_loop(0, s_.z, grads, 0)
        stage_out("a", r, stage)
        loop_point(step, chunk_points, 4, 2, s_.n_hid)

        def pull_rows(i, _):
            rows = pl.ds(pl.multiple_of(i * tile, tile), tile)
            grad = ref["pj"][r, rows, :]
            ref["gacc"][rows, :] = ref["gacc"][rows, :] + dot_t(grad, matrix(slot, 0, 3 * kh))
            for k, first in ((4, 0), (5, 2 * kh)):
                part_sum = row_sum(ref["pj"][r, rows, pl.ds(first, kh)].astype(F32))
                ref["sums"][pl.ds(k, 1), cols] = ref["sums"][pl.ds(k, 1), cols] + part_sum
            return 0

        lax.fori_loop(0, s_.tiles, pull_rows, 0)
        loop_point(step, chunk_points, 4, 3, s_.n_hid)
        return 0

    lax.fori_loop(0, s_.n_hid, back_chunk, 0)
    stage_kept("a", 0, 2 + (s_.n_hid - 1) % 2)

    def back_one(i, _):
        rows = pl.ds(pl.multiple_of(i * tile, tile), tile)
        scaled, inverse = scaled_rows(ref["xs"][rows, :].astype(F32))
        grad = ref["gacc"][rows, :]
        add_sum(0, grad * scaled)
        add_sum(1, grad)
        total = ref["facc"][rows, :] + norm_pull(grad, gain_row(0), scaled, inverse)
        ref["ct"][rows, :] = total.astype(BF16)
        return 0

    lax.fori_loop(0, s_.tiles, back_one, 0)
    for k, (r, f) in enumerate(tree.units):
        for i in range(s_.fs // kh):
            ref["sums"][pl.ds(8 + 2 * f + i, 1), columns(block_of(r), kh)] = ref["hidden_sum"][
                k, :, pl.ds(i * kh, kh)
            ]
    for r in range(1, s_.n_hid):
        send("sum1", r, ref["sums"].at[:, columns(block_of(r), kh)], ref["sum1"].at[r], peer(r))
    for r in range(1, s_.n_hid):
        send("gt", r, ref["ct"].at[:, columns(block_of(r), kh)], out_rows("grad_rows", h), peer(r))
    own_gt = local(1, ref["ct"].at[:, columns(h, kh)], out_rows("grad_rows", h))
    own_gt.start()

    total = ref["sums"][:, columns(h, kh)]
    for r in range(1, s_.n_hid):
        arrived("sum1", r, ref["sum1"].at[r])
        total = total + ref["sum1"][r]
    ref["sum2"][0] = total
    send("sum2", 0, ref["sum2"].at[0], ref["sum2"].at[1], sibling)
    for point in range(last_point, plan.end):
        act(point)
    arrived("sum2", 0, ref["sum2"].at[1])
    ref["sum3"][0] = ref["sum2"][0] + ref["sum2"][1]
    for step in range(1, s_.z):
        send("sum3", step, ref["sum3"].at[0], ref["sum3"].at[step], z_peer(step))
    for k in (0, 1):
        free_buffer(k, plan.holders[k])

    finals = [("m", 0), ("m", 1), ("a", 0), ("a", 1)]

    def final_load(k, kind, f):
        return local(30 + k, ref["z_g" + kind].at[f], buffer("acc", kind, k))

    def final_store(k, kind, f):
        if kind == "a":
            source = ref["final"].at[k, pl.ds(0, s_.half)]
            return local(34 + k, source, ref["grad_a"].at[pl.ds(f * s_.half, s_.half)])
        return local(34 + k, ref["final"].at[k], ref["grad_m"].at[f])

    for number, (kind, f) in enumerate(finals):
        k = number % 2
        for step in range(1, s_.z):
            arrived("zg" + kind, f * s_.z + step, z_slot(kind, f, step))
        load = final_load(k, kind, f)
        load.start()
        load.wait()
        total = ref["acc"][k, 0].astype(F32) if kind == "m" else ref["acc"][k, 0, pl.ds(0, s_.half)].astype(F32)
        for step in range(1, s_.z):
            more = ref["acc"][k, step] if kind == "m" else ref["acc"][k, step, pl.ds(0, s_.half)]
            total = total + more.astype(F32)
        if number >= 2:
            final_store(k, *finals[number - 2]).wait()
        if kind == "a":
            ref["final"][k, pl.ds(0, s_.half)] = total
        else:
            ref["final"][k] = total
        final_store(k, kind, f).start()
    total = ref["sum3"][0]
    for step in range(1, s_.z):
        arrived("sum3", step, ref["sum3"].at[step])
        total = total + ref["sum3"][step]
    ref["sum2"][2] = total
    small = local(2, ref["sum2"].at[2], ref["small"])
    small.start()

    small.wait()
    for number in (2, 3):
        final_store(number % 2, *finals[number]).wait()
    own_lo.wait()
    own_gt.wait()
    for r in range(1, s_.n_hid):
        arrived("lo", r, out_rows("layer_out", h))
        arrived("gt", r, out_rows("grad_rows", h))
        left("params", r, ref["params"])
        left("ct", r, cot_rows(h))
        left("lo", r, cot_rows(h))
        left("gt", r, cot_rows(h))
        left("sum1", r, ref["sum1"].at[r])
    left("sum2", 0, ref["sum2"].at[0])
    for step in range(1, s_.z):
        left("sum3", step, ref["sum3"].at[0])
    z_left("za", 0, ref["a_own"])
    for f in (0, 1):
        z_left("zm", f, ref["m_own"].at[f])
    for kind in ("a", "m"):
        for r, f in tree.units:
            source = part[kind](r, f, c)
            left(kind + "c", tree.pos[r, f], source)
            for child, _ in tree.children(r, f):
                left(kind + "x", tree.pos[child, f], source)
    for k in range(max(0, s_.n_hid - 2), s_.n_hid):
        stage_free("a", s_.n_hid - 1 - k, 2 + k % 2)


def scratch(size, tree):
    s_ = size
    units = len(tree.units)
    vmem = {
        "params_all": ((SMALL_ROWS, s_.d), F32),
        "xs": ((s_.n, s_.d), BF16),
        "ct": ((s_.n, s_.d), BF16),
        "nrm": ((s_.n, s_.d), BF16),
        "nrm_t": ((s_.d, s_.n), BF16),
        "n2": ((s_.n, s_.d), BF16),
        "n2_t": ((s_.d, s_.n), BF16),
        "ct_t": ((s_.d, s_.n), BF16),
        "pj": ((s_.n_hid, s_.n, 3 * s_.kh), BF16),
        "probs": ((s_.n_hid, s_.pairs, s_.n, 2 * BLOCK), BF16),
        "att": ((s_.n_hid, s_.n, s_.kh), BF16),
        "res": ((s_.n, s_.d), F32),
        "facc": ((s_.n, s_.d), F32),
        "gacc": ((s_.n, s_.d), F32),
        "wa": ((s_.n_hid, s_.z, 2, s_.tb, s_.wide), BF16),
        "hid": ((s_.n, s_.fs), BF16),
        "gb": ((s_.n, s_.fs), BF16),
        "acc": ((2, s_.z, s_.tb, s_.wide), BF16),
        "tmp": ((2, s_.z, s_.tb, s_.wide), BF16),
        "more": ((s_.z, s_.tb, s_.wide), BF16),
        "final": ((2, s_.tb, s_.wide), F32),
        "hidden_bias": ((units, 1, s_.fs), F32),
        "hidden_sum": ((units, 1, s_.fs), F32),
        "sums": ((SMALL_ROWS, s_.d), F32),
        "sum1": ((s_.n_hid, SMALL_ROWS, s_.kh), F32),
        "sum2": ((3, SMALL_ROWS, s_.kh), F32),
        "sum3": ((s_.z, SMALL_ROWS, s_.kh), F32),
    }
    pairs = {
        "params": s_.n_hid,
        "za": s_.z,
        "zm": 2 * s_.z,
        "xs": s_.tiles * s_.n_hid,
        "ax": units,
        "ac": units,
        "mx": units,
        "mc": units,
        "ct": s_.n_hid,
        "sa": s_.n_hid,
        "sm": units,
        "ga": units,
        "gm": units,
        "zga": 2 * s_.z,
        "zgm": 2 * s_.z,
        "lo": s_.n_hid,
        "gt": s_.n_hid,
        "sum1": s_.n_hid,
        "sum2": 1,
        "sum3": s_.z,
    }
    out = {name: pltpu.VMEM(shape, kind) for name, (shape, kind) in vmem.items()}
    for name, count in pairs.items():
        out[name + "_s"] = pltpu.SemaphoreType.DMA((count,))
        out[name + "_r"] = pltpu.SemaphoreType.DMA((count,))
    out["local"] = pltpu.SemaphoreType.DMA((48,))
    out["wload"] = pltpu.SemaphoreType.DMA((s_.n_hid,))
    out["keep"] = pltpu.SemaphoreType.DMA((2,))
    return out


def finish_kernel(grad_ref, tokens_ref, middle_ref, coarse_ref):
    grad = grad_ref[...]
    rows = grad.shape[0]
    tokens_ref[...] = grad.astype(F32)
    middle_ref[...] = dot(group_matrix(rows, 4), grad)
    coarse_ref[...] = dot(group_matrix(rows, 16), grad)


def finish(grad):
    positions, features = grad.shape
    rows = 256
    return pl.pallas_call(
        finish_kernel,
        grid=(positions // rows,),
        in_specs=[pl.BlockSpec((rows, features), lambda i: (i, 0))],
        out_specs=[pl.BlockSpec((rows // t, features), lambda i: (i, 0)) for t in (1, 4, 16)],
        out_shape=[jax.ShapeDtypeStruct((positions // t, features), F32) for t in (1, 4, 16)],
        name="token_gradients",
    )(grad)


def shards(
    tokens,
    middle_cond,
    coarse_cond,
    first_gain,
    first_shift,
    attend_weight,
    query_bias,
    value_bias,
    output_weight,
    mixer_bias,
    second_gain,
    second_shift,
    up_weight,
    hidden_bias,
    down_weight,
    down_bias,
    cotangent,
):
    positions, features = tokens.shape
    n_hid, n_tok = lax.axis_size("hid"), lax.axis_size("tok")
    d = features * n_hid
    ff = up_weight.shape[1] * n_hid
    size = Sizes(positions, features, d, ff, n_tok, n_hid)
    tree = Tree(n_hid)
    tb, fs, wide, z = size.tb, size.fs, size.wide, size.z
    a_own = jnp.concatenate([attend_weight.reshape(tb, 3 * features), output_weight.T], axis=1)
    m_own = jnp.stack(
        [
            jnp.concatenate([up_weight[:, f * fs : f * fs + fs], down_weight[f * fs : f * fs + fs].T], axis=1)
            for f in (0, 1)
        ]
    )
    vectors = (first_gain, first_shift, second_gain, second_shift, query_bias, value_bias, mixer_bias, down_bias)
    params = jnp.concatenate(
        [
            jnp.stack(vectors),
            hidden_bias.reshape(ff // d, features),
            jnp.zeros((SMALL_ROWS - 8 - ff // d, features), F32),
        ]
    )
    units = len(tree.units)
    outputs = {
        "layer_out": ((positions, features), BF16),
        "grad_rows": ((positions, features), BF16),
        "grad_a": ((tb, wide), F32),
        "grad_m": ((2, tb, wide), F32),
        "small": ((SMALL_ROWS, features), F32),
        "all_a": ((n_hid, z, 2, tb, wide), BF16),
        "all_m": ((units, z, 2, tb, wide), BF16),
        "own_ga": ((n_hid, z, tb, wide), BF16),
        "sib_ga": ((n_hid, z, tb, wide), BF16),
        "got_ga": ((units, z, size.half, wide), BF16),
        "own_gm": ((units, z, tb, wide), BF16),
        "sib_gm": ((units, z, tb, wide), BF16),
        "got_gm": ((units, z, tb, wide), BF16),
        "z_ga": ((2, z, size.half, wide), BF16),
        "z_gm": ((2, z, tb, wide), BF16),
    }
    hbm = pl.BlockSpec(memory_space=pltpu.HBM)
    results = pl.pallas_call(
        functools.partial(layer_kernel, size, tree),
        out_shape=[jax.ShapeDtypeStruct(*outputs[name]) for name in OUTPUTS],
        in_specs=[hbm] * len(INPUTS),
        out_specs=[hbm] * len(OUTPUTS),
        scratch_shapes=list(scratch(size, tree).values()),
        compiler_params=pltpu.CompilerParams(
            collective_id=0, has_side_effects=True, vmem_limit_bytes=62 * 2**20
        ),
        cost_estimate=pl.CostEstimate(flops=80 * 10**9, bytes_accessed=2 * 10**8, transcendentals=10**7),
        name="layer",
    )(tokens, middle_cond, coarse_cond, cotangent, a_own, m_own, params)
    layer_out, grad_rows, grad_a, grad_m, small = results[:5]
    grad_tokens, grad_middle, grad_coarse = finish(grad_rows)
    tok = lax.axis_index("tok")
    share = features // n_tok
    mine = lax.dynamic_slice_in_dim(small[:8], tok * share, share, 1)
    hidden_share = fs * 2 // n_tok
    grad_hidden_bias = lax.dynamic_slice_in_dim(
        small[8 : 8 + ff // d].reshape(-1), tok * hidden_share, hidden_share, 0
    )
    grad_up = jnp.concatenate([grad_m[0, :, :fs], grad_m[1, :, :fs]], axis=1)
    grad_down = jnp.concatenate([grad_m[0, :, fs:].T, grad_m[1, :, fs:].T], axis=0)
    return (
        layer_out,
        grad_tokens,
        grad_middle,
        grad_coarse,
        mine[0],
        mine[1],
        grad_a[:, : 3 * features].reshape(tb, 3, features),
        mine[4],
        mine[5],
        grad_a[:, 3 * features :].T,
        mine[6],
        mine[2],
        mine[3],
        grad_up,
        grad_hidden_bias,
        grad_down,
        mine[7],
    )


def solution(mesh):
    return jax.shard_map(
        shards,
        mesh=mesh,
        in_specs=(
            P("tok", "hid"),
            P("tok", "hid"),
            P("tok", "hid"),
            P("hid"),
            P("hid"),
            P("tok", None, "hid"),
            P("hid"),
            P("hid"),
            P("hid", "tok"),
            P("hid"),
            P("hid"),
            P("hid"),
            P("tok", "hid"),
            P("hid"),
            P("hid", "tok"),
            P("hid"),
            P("tok", "hid"),
        ),
        out_specs=(
            P("tok", "hid"),
            P("tok", "hid"),
            P("tok", "hid"),
            P("tok", "hid"),
            P(("hid", "tok")),
            P(("hid", "tok")),
            P("tok", None, "hid"),
            P(("hid", "tok")),
            P(("hid", "tok")),
            P("hid", "tok"),
            P(("hid", "tok")),
            P(("hid", "tok")),
            P(("hid", "tok")),
            P("tok", "hid"),
            P(("hid", "tok")),
            P("hid", "tok"),
            P(("hid", "tok")),
        ),
        check_vma=False,
    )
```

```python
import functools

import jax
import jax.numpy as jnp
from jax import lax
from jax.experimental import pallas as pl
from jax.experimental.pallas import tpu as pltpu
from jax.sharding import PartitionSpec as P

HEAD = 64
BLOCK = 128
PAIR = 2 * HEAD
EPSILON = 1e-05
MESH = pl.DeviceIdType.MESH
BF16 = jnp.bfloat16
F32 = jnp.float32
SMALL_ROWS = 16


class Tree:
    def __init__(self, n_hid):
        self.n = n_hid
        self.bits = n_hid.bit_length() - 1
        units = [(r, f) for r in range(n_hid) for f in (0, 1)]
        self.units = sorted(units, key=lambda u: (u[0].bit_count(), len(self.children(*u)), u))
        self.pos = {u: k for k, u in enumerate(self.units)}
        self.near = [1 << b for b in range(self.bits)]
        self.far = [r for r in range(n_hid) if r.bit_count() > 1]
        first = [(1 << b, b % 2) for b in range(self.bits)]
        second = [(1 << b, 1 - b % 2) for b in range(self.bits)]
        self.m_near = first + second
        self.m_units = [(0, 0), (0, 1)] + first + [(r, f) for r in self.far for f in (0, 1)] + second
        self.m_pos = {u: k for k, u in enumerate(self.m_units)}

    def children(self, r, f):
        held = [b for b in range(self.bits) if r >> b & 1]
        free = [b for b in range(self.bits) if not r >> b & 1]
        if held:
            free = [b for b in free if (b < held[0] if f == 0 else b > held[-1])]
        return [(r | 1 << b, b) for b in free]

    def parent(self, r, f):
        held = [b for b in range(self.bits) if r >> b & 1]
        return held[0] if f == 0 else held[-1]


class Schedule:
    def __init__(self, done, kids, lag, last_point):
        self.at = {}
        self.turn = {}
        self.before = {}
        self.first = set()
        sent = {}
        seen = set()
        holders = [None, None]
        waiting = sorted(done, key=lambda u: done[u])
        held = None
        point = 0
        while waiting or held is not None:
            actions = []
            if held is not None:
                actions.append(("finish", held))
                sent[held] = point
                held = None
            for unit in waiting:
                if point <= done[unit] or any(k not in sent for k in kids[unit]):
                    continue
                if point < last_point and any(point < sent[k] + lag[unit[0]] for k in kids[unit]):
                    continue
                actions.append(("fetch", unit))
                held = unit
                self.turn[unit] = k = len(self.turn) % 2
                self.before[unit] = holders[k]
                holders[k] = unit
                if unit[:2] not in seen:
                    self.first.add(unit)
                seen.add(unit[:2])
                waiting.remove(unit)
                break
            if actions:
                self.at[point] = actions
            point += 1
        self.end = point
        self.holders = holders


def dot(a, b):
    return jnp.dot(a, b, preferred_element_type=F32)


def dot_t(a, b):
    return lax.dot_general(a, b, (((1,), (1,)), ((), ())), preferred_element_type=F32)


def dot_l(a, b):
    return lax.dot_general(a, b, (((0,), (0,)), ((), ())), preferred_element_type=F32)


def repeat_matrix(rows, times):
    row = lax.broadcasted_iota(jnp.int32, (rows, rows // times), 0)
    column = lax.broadcasted_iota(jnp.int32, (rows, rows // times), 1) * times
    return ((row >= column) & (row < column + times)).astype(BF16)


def group_matrix(rows, times):
    row = lax.broadcasted_iota(jnp.int32, (rows // times, rows), 0) * times
    column = lax.broadcasted_iota(jnp.int32, (rows // times, rows), 1)
    return ((column >= row) & (column < row + times)).astype(BF16)


def scaled_rows(values):
    width = values.shape[1]
    average = jnp.sum(values, axis=1, keepdims=True) / width
    square = jnp.sum(values * values, axis=1, keepdims=True) / width
    inverse = lax.rsqrt(square - average * average + EPSILON)
    return (values - average) * inverse, inverse


def norm_pull(grad, gain, scaled, inverse):
    width = grad.shape[1]
    weighted = grad * gain
    mean = jnp.sum(weighted, axis=1, keepdims=True) / width
    along = jnp.sum(weighted * scaled, axis=1, keepdims=True) / width
    return inverse * (weighted - mean - scaled * along)


def row_sum(values):
    return jnp.sum(values, axis=0, keepdims=True)


def two_heads(values):
    low = lax.broadcasted_iota(jnp.int32, values.shape, 1) < HEAD
    zero = jnp.zeros_like(values)
    return jnp.concatenate([jnp.where(low, values, zero), jnp.where(low, zero, values)], axis=0)


def pick_heads(both):
    low = lax.broadcasted_iota(jnp.int32, (BLOCK, PAIR), 1) < HEAD
    return jnp.where(low, both[:BLOCK], both[BLOCK:])


INPUTS = ("tokens", "middle", "coarse", "cotangent", "a_own", "m_own", "params")
OUTPUTS = (
    "layer_out",
    "grad_rows",
    "grad_a",
    "grad_m",
    "small",
    "all_a",
    "all_m",
    "own_ga",
    "sib_ga",
    "got_ga",
    "own_gm",
    "sib_gm",
    "got_gm",
    "z_ga",
    "z_gm",
    "z_far",
)


class Sizes:
    def __init__(self, positions, features, d, ff, n_tok, n_hid):
        self.d, self.n_hid, self.n_tok = d, n_hid, n_tok
        self.z = n_tok // 2
        self.n = positions // n_hid
        self.kh = features
        self.fs = ff // n_hid // 2
        self.tb = d // n_tok
        self.half = self.tb // 2
        self.wide = 4 * features
        self.pairs = features // PAIR
        self.tile = min(256, self.n)
        self.tiles = self.n // self.tile
        self.blocks = self.n // BLOCK
        self.positions = positions


def layer_kernel(size, tree, *refs):
    names = list(INPUTS) + list(OUTPUTS) + list(scratch(size, tree))
    ref = dict(zip(names, refs, strict=True))
    s_ = size
    n_units = len(tree.units)
    tok, h = lax.axis_index("tok"), lax.axis_index("hid")
    z, c = tok // 2, lax.rem(tok, 2)

    def block_of(r):
        total = 0
        for b in range(tree.bits):
            total = total + lax.rem(h // (1 << b) + r // (1 << b), 2) * (1 << b)
        return total

    def peer(r):
        return (tok, block_of(r))

    sibling = (tok + 1 - 2 * c, h)

    def z_peer(step):
        return (lax.rem(z + step, s_.z) * 2 + c, h)

    def columns(j, width):
        return pl.ds(pl.multiple_of(j * width, width), width)

    def remote(name, index, src, dst, device):
        return pltpu.make_async_remote_copy(
            src_ref=src,
            dst_ref=dst,
            send_sem=ref[name + "_s"].at[index],
            recv_sem=ref[name + "_r"].at[index],
            device_id=device,
            device_id_type=MESH,
        )

    def send(name, index, src, dst, device):
        remote(name, index, src, dst, device).start()

    def arrived(name, index, dst):
        remote(name, index, dst, dst, sibling).wait_recv()

    def left(name, index, src):
        remote(name, index, src, src, sibling).wait_send()

    def local(index, src, dst):
        return pltpu.make_async_copy(src, dst, ref["local"].at[index])

    barrier = pltpu.get_barrier_semaphore()
    everyone = [peer(r) for r in range(1, s_.n_hid)] + [sibling]
    everyone += [z_peer(k) for k in range(1, s_.z)]
    for device in everyone:
        pl.semaphore_signal(barrier, inc=1, device_id=device, device_id_type=MESH)
    pl.semaphore_wait(barrier, len(everyone))

    def z_send(name, index, src, dst):
        for step in range(1, s_.z):
            send(name, index * s_.z + step, src, dst, z_peer(step))

    def z_arrived(name, index, dst):
        for step in range(1, s_.z):
            arrived(name, index * s_.z + step, dst)

    def z_left(name, index, src):
        for step in range(1, s_.z):
            left(name, index * s_.z + step, src)

    def a_part(r, f, core):
        return ref["all_a"].at[r, :, core, pl.ds(f * s_.half, s_.half)]

    def m_part(r, f, core):
        return ref["all_m"].at[tree.m_pos[r, f], :, core]

    part = {"a": a_part, "m": m_part}

    for r in range(1, s_.n_hid):
        here = ref["params_all"].at[:, columns(h, s_.kh)]
        send("params", r, ref["params"], here, peer(r))
    own_params = local(0, ref["params"], ref["params_all"].at[:, columns(h, s_.kh)])
    own_params.start()
    z_send("za", 0, ref["a_own"], ref["all_a"].at[0, z, c])
    own_a = local(1, ref["a_own"], ref["all_a"].at[0, z, c])
    own_a.start()
    own_m = []
    for f in (0, 1):
        own_m.append(local(2 + f, ref["m_own"].at[f], ref["all_m"].at[tree.m_pos[0, f], z, c]))
        own_m[f].start()

    def m_block(r, f):
        return ref["all_m"].at[tree.m_pos[r, f], z, c]

    far_units = [(r, f) for r in tree.far for f in (0, 1)]
    for r, f in far_units:
        send("fs", tree.m_pos[r, f], ref["m_own"].at[f], m_block(r, f), peer(r))

    kh, n, tile = s_.kh, s_.n, s_.tile
    rows_m, rows_c = n // 4, n // 16
    loads = {}
    order = list(range(1, s_.n_hid)) + [0]
    for r in order:
        j = block_of(r)
        sources = (
            (ref["tokens"].at[columns(j, n)], ref["pj"].at[r, :, pl.ds(0, kh)]),
            (ref["middle"].at[columns(j, rows_m)], ref["pj"].at[r, pl.ds(0, rows_m), pl.ds(2 * kh, kh)]),
            (ref["coarse"].at[columns(j, rows_c)], ref["pj"].at[r, pl.ds(rows_m, rows_c), pl.ds(2 * kh, kh)]),
        )
        loads[r] = [local(4 + 3 * r + k, *pair) for k, pair in enumerate(sources)]
        for copy in loads[r]:
            copy.start()
    repeat_4, repeat_16 = repeat_matrix(tile, 4), repeat_matrix(tile, 16)

    def xs_rows(i, j):
        return ref["xs"].at[pl.ds(i * tile, tile), columns(j, kh)]

    own_xs = []
    for i in range(s_.tiles):
        for r in order:
            if i == 0:
                for copy in loads[r]:
                    copy.wait()
            rows = pl.ds(i * tile, tile)
            middle = ref["pj"][r, pl.ds(i * (tile // 4), tile // 4), pl.ds(2 * kh, kh)]
            coarse = ref["pj"][r, pl.ds(rows_m + i * (tile // 16), tile // 16), pl.ds(2 * kh, kh)]
            total = ref["pj"][r, rows, pl.ds(0, kh)].astype(F32)
            total = total + dot(repeat_4, middle) + dot(repeat_16, coarse)
            ref["pj"][r, rows, pl.ds(kh, kh)] = total.astype(BF16)
            source = ref["pj"].at[r, rows, pl.ds(kh, kh)]
            if r:
                send("xs", i * s_.n_hid + r, source, xs_rows(i, h), peer(r))
            else:
                copy = local(4 + 3 * s_.n_hid + i, source, xs_rows(i, h))
                copy.start()
                own_xs.append(copy)

    for f in (0, 1):
        z_send("zm", f, ref["m_own"].at[f], m_block(0, f))
    for r, f in far_units:
        arrived("fs", tree.m_pos[r, f], m_block(r, f))
        z_send("zf", tree.m_pos[r, f], m_block(r, f), m_block(r, f))

    def to_sibling(kind, r, f):
        k = tree.pos[r, f] if kind == "a" else tree.m_pos[r, f]
        send(kind + "c", k, part[kind](r, f, c), part[kind](r, f, c), sibling)

    def take_a(r, f):
        arrived("ax", tree.pos[r, f], a_part(r, f, c))
        for child, b in tree.children(r, f):
            send("ax", tree.pos[child, f], a_part(r, f, c), a_part(child, f, c), peer(1 << b))
        to_sibling("a", r, f)

    def take_m(r, f):
        if r in tree.far:
            z_arrived("zf", tree.m_pos[r, f], m_block(r, f))
        else:
            arrived("mx", tree.m_pos[r, f], m_part(r, f, c))
        to_sibling("m", r, f)

    def take_sibling(kind, r, f):
        k = tree.pos[r, f] if kind == "a" else tree.m_pos[r, f]
        arrived(kind + "c", k, part[kind](r, f, 1 - c))

    a_near = sorted([u for u in tree.units if u[0] in tree.near], key=lambda u: -len(tree.children(*u)))
    own_a.wait()
    z_arrived("za", 0, ref["all_a"].at[0, z, c])
    for r, f in a_near:
        send("ax", tree.pos[r, f], a_part(0, f, c), a_part(r, f, c), peer(r))
    for f in (0, 1):
        to_sibling("a", 0, f)

    own_params.wait()
    for r in range(1, s_.n_hid):
        arrived("params", r, ref["params_all"].at[:, columns(h, kh)])

    def gain_row(k):
        return ref["params_all"][pl.ds(k, 1), :]

    for k, (r, f) in enumerate(tree.m_units):
        parts = [
            ref["params_all"][pl.ds(8 + 2 * f + i, 1), columns(block_of(r), kh)] for i in range(s_.fs // kh)
        ]
        ref["hidden_bias"][k] = jnp.concatenate(parts, axis=1)
        ref["hidden_sum"][k] = jnp.zeros((1, s_.fs), F32)
    ref["sums"][...] = jnp.zeros_like(ref["sums"])

    def add_sum(k, values):
        ref["sums"][pl.ds(k, 1), :] = ref["sums"][pl.ds(k, 1), :] + row_sum(values)

    for i in range(s_.tiles):
        own_xs[i].wait()
        for r in range(1, s_.n_hid):
            arrived("xs", i * s_.n_hid + r, xs_rows(i, h))
        rows = pl.ds(i * tile, tile)
        scaled, _ = scaled_rows(ref["xs"][rows, :].astype(F32))
        normed = (scaled * gain_row(0) + gain_row(1)).astype(BF16)
        ref["nrm"][rows, :] = normed
        ref["nrm_t"][:, rows] = normed.T

    for i in range(s_.tiles):
        for r in range(1, s_.n_hid):
            left("xs", i * s_.n_hid + r, xs_rows(i, h))

    def weight_load(slot, source):
        return pltpu.make_async_copy(source, ref["wa"].at[slot], ref["wload"].at[slot])

    def matrix(slot, first, width):
        return ref["wa"][slot, :, :, :, pl.ds(first, width)].reshape(s_.d, width)

    def put_rows(slot, zz, first, values):
        width = values.shape[1]
        ref["wa"][slot, zz, :, :, pl.ds(first, width)] = values.reshape(2, s_.tb, width)

    def cot_rows(j):
        return ref["ct"].at[:, columns(j, kh)]

    own_ct = local(0, ref["cotangent"].at[columns(h, n)], cot_rows(h))

    def before_chunk(r):
        if r == 0:
            pass
        elif r.bit_count() == 1:
            if r == 1:
                for u, f in a_near:
                    take_a(u, f)
                own_ct.start()
                for k in range(1, s_.n_hid):
                    send("ct", k, ref["cotangent"].at[columns(block_of(k), n)], cot_rows(h), peer(k))
        else:
            for f in (0, 1):
                take_a(r, f)
        if r == s_.n_hid - 1:
            for f in (0, 1):
                own_m[f].wait()
                z_arrived("zm", f, m_block(0, f))
            for u, f in tree.m_near:
                send("mx", tree.m_pos[u, f], m_part(0, f, c), m_part(u, f, c), peer(u))
            for f in (0, 1):
                to_sibling("m", 0, f)
        for f in (0, 1):
            take_sibling("a", r, f)
        load = weight_load(r, ref["all_a"].at[r])
        load.start()
        load.wait()

    causal_row = lax.broadcasted_iota(jnp.int32, (BLOCK, 2 * BLOCK), 0)
    causal_col = lax.rem(lax.broadcasted_iota(jnp.int32, (BLOCK, 2 * BLOCK), 1), BLOCK)
    allowed = causal_row >= causal_col

    def halves(values, f):
        return [f(values[:, :BLOCK]), f(values[:, BLOCK:])]

    def spread(pair):
        return jnp.concatenate([jnp.broadcast_to(v, (BLOCK, BLOCK)) for v in pair], axis=1)

    def row_max(v):
        return jnp.max(v, axis=1, keepdims=True)

    def row_add(v):
        return jnp.sum(v, axis=1, keepdims=True)

    def attend_chunk(r):
        for k in range(s_.n_hid):
            pl.when(r == k)(functools.partial(before_chunk, k))
        cols = columns(block_of(r), kh)
        bias = jnp.concatenate(
            [ref["params_all"][4:5, cols], jnp.zeros((1, kh), F32), ref["params_all"][5:6, cols]], axis=1
        )

        def project(i, _):
            rows = pl.ds(pl.multiple_of(i * tile, tile), tile)
            values = dot(ref["nrm"][rows, :], matrix(r, 0, 3 * kh)) + bias
            ref["pj"][r, rows, :] = values.astype(BF16)
            return 0

        lax.fori_loop(0, s_.tiles, project, 0)

        def attend(i, _):
            rows = pl.ds(pl.multiple_of(i * BLOCK, BLOCK), BLOCK)
            for p in range(s_.pairs):
                query, key, value = (ref["pj"][r, rows, pl.ds(k * kh + p * PAIR, PAIR)] for k in range(3))
                logits = jnp.where(allowed, dot_t(query, two_heads(key)) * HEAD ** (-0.5), -1e30)
                powers = jnp.exp(logits - spread(halves(logits, row_max)))
                shares = [1.0 / v for v in halves(powers, row_add)]
                attention = (powers * spread(shares)).astype(BF16)
                ref["probs"][r, p, rows, :] = attention
                out = dot(attention, two_heads(value))
                ref["att"][r, rows, pl.ds(p * PAIR, PAIR)] = out.astype(BF16)
            return 0

        lax.fori_loop(0, s_.blocks, attend, 0)

    lax.fori_loop(0, s_.n_hid, lambda r, _: (attend_chunk(r), 0)[1], 0)

    def mix(i, _):
        rows = pl.ds(pl.multiple_of(i * tile, tile), tile)
        total = ref["xs"][rows, :].astype(F32) + gain_row(6)
        for r in range(s_.n_hid):
            total = total + dot_t(ref["att"][r, rows, :], matrix(r, 3 * kh, kh))
        ref["res"][rows, :] = total
        scaled, _inverse = scaled_rows(total)
        normed = (scaled * gain_row(2) + gain_row(3)).astype(BF16)
        ref["n2"][rows, :] = normed
        return 0

    lax.fori_loop(0, s_.tiles, mix, 0)

    own_ct.wait()
    for k in range(1, s_.n_hid):
        arrived("ct", k, cot_rows(h))
    for i in range(s_.tiles):
        rows = pl.ds(i * tile, tile)
        ref["n2_t"][:, rows] = ref["n2"][rows, :].T
        upstream = ref["ct"][rows, :]
        ref["ct_t"][:, rows] = upstream.T
        add_sum(7, upstream.astype(F32))
        ref["facc"][rows, :] = jnp.zeros((tile, s_.d), F32)
        ref["gacc"][rows, :] = jnp.zeros((tile, s_.d), F32)

    mlp_points = 2 * n_units
    chunk_points = mlp_points + 2
    last_point = chunk_points + 4 * s_.n_hid
    done, kids = {}, {}
    for k, (r, f) in enumerate(tree.m_units):
        done["m", r, f] = 2 * k + 1
        kids["m", r, f] = [("m", u, f) for u in tree.near] if r == 0 else []
    for r, f in far_units:
        done["fold", r, f] = 0
        kids["fold", r, f] = [("m", r, f)]
    for r in range(s_.n_hid):
        for f in (0, 1):
            done["a", r, f] = chunk_points + 4 * (s_.n_hid - 1 - r) + 3
            kids["a", r, f] = [("a", child, f) for child, _ in tree.children(r, f)]
    plan = Schedule(done, kids, {"m": 6, "a": 4, "fold": 9}, last_point)

    def place(kind, r, f):
        return tree.pos[r, f] if kind == "a" else tree.m_pos[r, f]

    def own_grad(kind, r, f):
        if kind == "a":
            return ref["own_ga"].at[r, :, pl.ds(f * s_.half, s_.half)]
        return ref["own_gm"].at[tree.m_pos[r, f]]

    def sib_grad(kind, r, f):
        if kind == "a":
            return ref["sib_ga"].at[r, :, pl.ds(f * s_.half, s_.half)]
        return ref["sib_gm"].at[tree.m_pos[r, f]]

    def got_grad(kind, r, f):
        return ref["got_g" + kind].at[place(kind, r, f)]

    def buffer(name, kind, k=None):
        whole = ref[name] if k is None else ref[name].at[k]
        return whole.at[pl.ds(0, s_.z), pl.ds(0, s_.half if kind == "a" else s_.tb)]

    def z_slot(kind, f, step):
        return ref["z_g" + kind].at[f, step]

    def scattered(kind, r, f):
        if r == 0:
            return "zg" + kind, f * s_.z, ref["z_g" + kind].at[f]
        return "zfar", tree.m_pos[r, f] * s_.z, ref["z_far"].at[tree.m_pos[r, f]]

    def scatters(kind, r):
        return r == 0 or (kind == "m" and r in tree.far)

    def free_buffer(k, holder):
        if holder is None:
            return
        kind, r, f = holder
        source = buffer("acc", kind, k)
        if kind == "fold":
            left("fold", tree.m_pos[r, f], source.at[0])
        elif scatters(kind, r):
            name, first, _ = scattered(kind, r, f)
            for step in range(1, s_.z):
                left(name, first + step, source.at[0])
        else:
            left("g" + kind, place(kind, r, f), source)

    def fetches(unit, k):
        kind, r, f = unit
        if kind == "fold":
            return [(30 + 3 * k, ref["z_far"].at[tree.m_pos[r, f]], buffer("acc", kind, k))]
        out = [(30 + 3 * k, own_grad(*unit), buffer("acc", kind, k))]
        out.append((31 + 3 * k, sib_grad(*unit), buffer("tmp", kind, k)))
        if kids[unit]:
            out.append((32 + 3 * k, got_grad(*kids[unit][0]), buffer("more", kind)))
        return out

    def fetch(unit):
        kind, r, f = unit
        k = plan.turn[unit]
        free_buffer(k, plan.before[unit])
        if kind == "fold":
            for step in range(1, s_.z):
                name, first, slots = scattered("m", r, f)
                arrived(name, first + step, slots.at[step])
        elif kind == "m" or unit in plan.first:
            slot = tree.m_pos[r, f] if kind == "m" else r
            arrived("s" + kind, slot, ref["sib_g" + kind].at[slot])
        if kind != "fold":
            for kid in kids[unit][:1]:
                arrived("g" + kind, place(*kid), got_grad(*kid))
        for item in fetches(unit, k):
            local(*item).start()

    def finish(unit):
        kind, r, f = unit
        k = plan.turn[unit]
        for item in fetches(unit, k):
            local(*item).wait()
        acc, tmp, more = buffer("acc", kind, k), buffer("tmp", kind, k), buffer("more", kind)
        if kind == "fold":
            total = acc[0].astype(F32)
            for zz in range(1, s_.z):
                total = total + acc[zz].astype(F32)
            acc[0] = total.astype(BF16)
            slot = ref["z_gm"].at[f, s_.z + tree.far.index(r)]
            send("fold", tree.m_pos[r, f], acc.at[0], slot, peer(r))
            return
        for zz in range(s_.z):
            total = acc[zz].astype(F32) + tmp[zz].astype(F32)
            if kids[unit]:
                total = total + more[zz].astype(F32)
            acc[zz] = total.astype(BF16)
        for kid in kids[unit][1:]:
            source = got_grad(*kid)
            arrived("g" + kind, place(*kid), source)
            copy = local(36, source, more)
            copy.start()
            copy.wait()
            for zz in range(s_.z):
                acc[zz] = (acc[zz].astype(F32) + more[zz].astype(F32)).astype(BF16)
        if scatters(kind, r):
            name, first, slots = scattered(kind, r, f)
            keep = local(40, acc.at[z], slots.at[0])
            keep.start()
            for step in range(1, s_.z):
                to = lax.rem(z + step, s_.z)
                send(name, first + step, acc.at[to], slots.at[step], z_peer(step))
            keep.wait()
        else:
            to = r if kind == "m" else 1 << tree.parent(r, f)
            send("g" + kind, place(kind, r, f), acc, got_grad(kind, r, f), peer(to))

    def act(point):
        for verb, unit in plan.at.get(point, ()):
            (fetch if verb == "fetch" else finish)(unit)

    def loop_point(step, first, stride, offset, count):
        for k in range(count):
            if first + stride * k + offset in plan.at:
                pl.when(step == k)(functools.partial(act, first + stride * k + offset))

    def stage_copies(kind, index, slot):
        own = ref["own_g" + kind].at[index]
        theirs = ref["sib_g" + kind].at[index]
        keep = pltpu.make_async_copy(ref["wa"].at[slot, :, c], own, ref["keep"].at[slot - 2])
        give = pltpu.make_async_remote_copy(
            src_ref=ref["wa"].at[slot, :, 1 - c],
            dst_ref=theirs,
            send_sem=ref["s" + kind + "_s"].at[index],
            recv_sem=ref["s" + kind + "_r"].at[index],
            device_id=sibling,
            device_id_type=MESH,
        )
        return keep, give

    def stage_out(kind, index, slot):
        for copy in stage_copies(kind, index, slot):
            copy.start()

    def stage_kept(kind, index, slot):
        stage_copies(kind, index, slot)[0].wait()

    def stage_free(kind, index, slot):
        stage_copies(kind, index, slot)[1].wait_send()

    fs = s_.fs
    for k in (0, 1):
        take_sibling("m", *tree.m_units[k])
    weight_load(0, ref["all_m"].at[0]).start()
    gelu_scale = (2.0 / jnp.pi) ** 0.5

    def feed(step, _):
        slot = lax.rem(step, 2)
        weight_load(slot, ref["all_m"].at[step]).wait()

        def rows_of(i, _):
            rows = pl.ds(pl.multiple_of(i * tile, tile), tile)
            up, down = matrix(slot, 0, fs), matrix(slot, fs, fs)
            before = dot(ref["n2"][rows, :], up) + ref["hidden_bias"][step]
            square = before * before
            bent = jnp.tanh(before * (gelu_scale + (gelu_scale * 0.044715) * square))
            share = 0.5 + 0.5 * bent
            hidden = (before * share).astype(BF16)
            slope = share + 0.5 * before * (1.0 - bent * bent) * (
                gelu_scale + (3.0 * gelu_scale * 0.044715) * square
            )
            grad_before = (dot(ref["ct"][rows, :], down) * slope).astype(BF16)
            ref["hid"][rows, :] = hidden
            ref["gb"][rows, :] = grad_before
            ref["facc"][rows, :] = ref["facc"][rows, :] + dot_t(hidden, down)
            ref["gacc"][rows, :] = ref["gacc"][rows, :] + dot_t(grad_before, up)
            ref["hidden_sum"][step] = ref["hidden_sum"][step] + row_sum(grad_before.astype(F32))
            return 0

        lax.fori_loop(0, s_.tiles, rows_of, 0)
        for k in range(1, n_units - 1):
            pl.when(step == k)(functools.partial(take_m, *tree.m_units[k + 1]))

        @pl.when(step >= 1)
        def _():
            stage_kept("m", step - 1, 3 - slot)

        loop_point(step, 0, 2, 0, n_units)
        stage = 2 + slot

        @pl.when(step >= 2)
        def _():
            stage_free("m", step - 2, stage)

        def grads(zz, _):
            rows = pl.ds(pl.multiple_of(zz * (2 * s_.tb), 2 * s_.tb), 2 * s_.tb)
            put_rows(stage, zz, 0, dot(ref["n2_t"][rows, :], ref["gb"][...]).astype(BF16))
            put_rows(stage, zz, fs, dot(ref["ct_t"][rows, :], ref["hid"][...]).astype(BF16))
            return 0

        lax.fori_loop(0, s_.z // 2, grads, 0)
        for k in range(n_units - 1):

            def load_next(k=k):
                if k:
                    take_sibling("m", *tree.m_units[k + 1])
                weight_load((k + 1) % 2, ref["all_m"].at[k + 1]).start()

            pl.when(step == k)(load_next)
        lax.fori_loop(s_.z // 2, s_.z, grads, 0)
        stage_out("m", step, stage)
        loop_point(step, 0, 2, 1, n_units)
        return 0

    lax.fori_loop(0, n_units, feed, 0)

    stage_kept("m", n_units - 1, 2 + (n_units - 1) % 2)
    act(mlp_points)
    weight_load(0, ref["all_a"].at[s_.n_hid - 1]).start()

    def back_two(i, _):
        rows = pl.ds(pl.multiple_of(i * tile, tile), tile)
        residual = ref["res"][rows, :]
        ref["n2"][rows, :] = (residual + (ref["facc"][rows, :] + gain_row(7))).astype(BF16)
        scaled, inverse = scaled_rows(residual)
        grad = ref["gacc"][rows, :]
        add_sum(2, grad * scaled)
        add_sum(3, grad)
        grad = ref["ct"][rows, :].astype(F32) + norm_pull(grad, gain_row(2), scaled, inverse)
        mixed = grad.astype(BF16)
        add_sum(6, mixed.astype(F32))
        ref["facc"][rows, :] = grad
        ref["gacc"][rows, :] = jnp.zeros((tile, s_.d), F32)
        ref["nrm"][rows, :] = mixed
        return 0

    lax.fori_loop(0, s_.tiles, back_two, 0)

    def out_rows(name, j):
        return ref[name].at[columns(j, n)]

    for i in range(s_.tiles):
        rows = pl.ds(i * tile, tile)
        ref["n2_t"][:, rows] = ref["nrm"][rows, :].T
    act(mlp_points + 1)
    for r in range(1, s_.n_hid):
        j = block_of(r)
        send("lo", r, ref["n2"].at[:, columns(j, kh)], out_rows("layer_out", h), peer(r))
    own_lo = local(0, ref["n2"].at[:, columns(h, kh)], out_rows("layer_out", h))
    own_lo.start()
    for k in range(n_units - 2, n_units):
        stage_free("m", k, 2 + k % 2)

    def back_chunk(step, _):
        r = s_.n_hid - 1 - step
        slot = lax.rem(step, 2)
        stage = 2 + slot
        weight_load(slot, ref["all_a"].at[r]).wait()

        @pl.when(step + 1 < s_.n_hid)
        def _():
            weight_load(1 - slot, ref["all_a"].at[lax.rem(2 * s_.n_hid - 2 - step, s_.n_hid)]).start()

        def pull_out(i, _):
            rows = pl.ds(pl.multiple_of(i * tile, tile), tile)
            ref["hid"][rows, pl.ds(0, kh)] = dot(ref["nrm"][rows, :], matrix(slot, 3 * kh, kh)).astype(BF16)
            return 0

        lax.fori_loop(0, s_.tiles, pull_out, 0)

        @pl.when(step >= 1)
        def _():
            stage_kept("a", r + 1, 3 - slot)

        loop_point(step, chunk_points, 4, 0, s_.n_hid)

        def pull_attention(i, _):
            rows = pl.ds(pl.multiple_of(i * BLOCK, BLOCK), BLOCK)
            for p in range(s_.pairs):
                query, key, value = (ref["pj"][r, rows, pl.ds(k * kh + p * PAIR, PAIR)] for k in range(3))
                grad = ref["hid"][rows, pl.ds(p * PAIR, PAIR)]
                attention = ref["probs"][r, p, rows, :]
                weights = attention.astype(F32)
                grad_attention = dot_t(grad, two_heads(value))
                centre = spread(halves(weights * grad_attention, row_add))
                grad_scores = (weights * (grad_attention - centre) * HEAD ** (-0.5)).astype(BF16)
                grad_query = dot(grad_scores, two_heads(key))
                grad_key = pick_heads(dot_l(grad_scores, query))
                grad_value = pick_heads(dot_l(attention, grad))
                for k, values in enumerate((grad_query, grad_key, grad_value)):
                    ref["pj"][r, rows, pl.ds(k * kh + p * PAIR, PAIR)] = values.astype(BF16)
            return 0

        lax.fori_loop(0, s_.blocks, pull_attention, 0)
        loop_point(step, chunk_points, 4, 1, s_.n_hid)

        @pl.when(step >= 2)
        def _():
            stage_free("a", r + 2, stage)

        cols = columns(block_of(r), kh)

        def grads(zz, _):
            rows = pl.ds(pl.multiple_of(zz * (2 * s_.tb), 2 * s_.tb), 2 * s_.tb)
            put_rows(stage, zz, 0, dot(ref["nrm_t"][rows, :], ref["pj"][r]).astype(BF16))
            put_rows(stage, zz, 3 * kh, dot(ref["n2_t"][rows, :], ref["att"][r]).astype(BF16))
            return 0

        lax.fori_loop(0, s_.z, grads, 0)
        stage_out("a", r, stage)
        loop_point(step, chunk_points, 4, 2, s_.n_hid)

        def pull_rows(i, _):
            rows = pl.ds(pl.multiple_of(i * tile, tile), tile)
            grad = ref["pj"][r, rows, :]
            ref["gacc"][rows, :] = ref["gacc"][rows, :] + dot_t(grad, matrix(slot, 0, 3 * kh))
            for k, first in ((4, 0), (5, 2 * kh)):
                part_sum = row_sum(ref["pj"][r, rows, pl.ds(first, kh)].astype(F32))
                ref["sums"][pl.ds(k, 1), cols] = ref["sums"][pl.ds(k, 1), cols] + part_sum
            return 0

        lax.fori_loop(0, s_.tiles, pull_rows, 0)
        loop_point(step, chunk_points, 4, 3, s_.n_hid)
        return 0

    lax.fori_loop(0, s_.n_hid, back_chunk, 0)
    stage_kept("a", 0, 2 + (s_.n_hid - 1) % 2)

    def back_one(i, _):
        rows = pl.ds(pl.multiple_of(i * tile, tile), tile)
        scaled, inverse = scaled_rows(ref["xs"][rows, :].astype(F32))
        grad = ref["gacc"][rows, :]
        add_sum(0, grad * scaled)
        add_sum(1, grad)
        total = ref["facc"][rows, :] + norm_pull(grad, gain_row(0), scaled, inverse)
        ref["ct"][rows, :] = total.astype(BF16)
        return 0

    lax.fori_loop(0, s_.tiles, back_one, 0)
    for k, (r, f) in enumerate(tree.m_units):
        for i in range(s_.fs // kh):
            ref["sums"][pl.ds(8 + 2 * f + i, 1), columns(block_of(r), kh)] = ref["hidden_sum"][
                k, :, pl.ds(i * kh, kh)
            ]
    for r in range(1, s_.n_hid):
        send("sum1", r, ref["sums"].at[:, columns(block_of(r), kh)], ref["sum1"].at[r], peer(r))
    own_gt = local(1, ref["ct"].at[:, columns(h, kh)], out_rows("grad_rows", h))
    own_gt.start()

    def send_rows():
        for r in range(1, s_.n_hid):
            send("gt", r, ref["ct"].at[:, columns(block_of(r), kh)], out_rows("grad_rows", h), peer(r))

    total = ref["sums"][:, columns(h, kh)]
    for r in range(1, s_.n_hid):
        arrived("sum1", r, ref["sum1"].at[r])
        total = total + ref["sum1"][r]
    ref["sum2"][0] = total
    send("sum2", 0, ref["sum2"].at[0], ref["sum2"].at[1], sibling)
    rows_sent = False
    for point in range(last_point, plan.end):
        if not rows_sent and any(verb == "fetch" and unit[:2] == ("a", 0) for verb, unit in plan.at.get(point, ())):
            send_rows()
            rows_sent = True
        act(point)
    if not rows_sent:
        send_rows()
    arrived("sum2", 0, ref["sum2"].at[1])
    ref["sum3"][0] = ref["sum2"][0] + ref["sum2"][1]
    for step in range(1, s_.z):
        send("sum3", step, ref["sum3"].at[0], ref["sum3"].at[step], z_peer(step))
    for k in (0, 1):
        free_buffer(k, plan.holders[k])

    finals = [("m", 0), ("m", 1), ("a", 0), ("a", 1)]

    def final_load(k, kind, f):
        slots = ref["z_g" + kind].at[f]
        if kind == "a":
            return local(30 + k, slots, ref["acc"].at[k, pl.ds(0, s_.z), pl.ds(0, s_.half)])
        return local(30 + k, slots, ref["acc"].at[k])

    def final_store(k, kind, f):
        if kind == "a":
            source = ref["final"].at[k, pl.ds(0, s_.half)]
            return local(34 + k, source, ref["grad_a"].at[pl.ds(f * s_.half, s_.half)])
        return local(34 + k, ref["final"].at[k], ref["grad_m"].at[f])

    for number, (kind, f) in enumerate(finals):
        k = number % 2
        for step in range(1, s_.z):
            arrived("zg" + kind, f * s_.z + step, z_slot(kind, f, step))
        if kind == "m":
            for i, r in enumerate(tree.far):
                arrived("fold", tree.m_pos[r, f], z_slot(kind, f, s_.z + i))
        load = final_load(k, kind, f)
        load.start()
        load.wait()
        total = ref["acc"][k, 0].astype(F32) if kind == "m" else ref["acc"][k, 0, pl.ds(0, s_.half)].astype(F32)
        for step in range(1, s_.z + (len(tree.far) if kind == "m" else 0)):
            more = ref["acc"][k, step] if kind == "m" else ref["acc"][k, step, pl.ds(0, s_.half)]
            total = total + more.astype(F32)
        if number >= 2:
            final_store(k, *finals[number - 2]).wait()
        if kind == "a":
            ref["final"][k, pl.ds(0, s_.half)] = total
        else:
            ref["final"][k] = total
        final_store(k, kind, f).start()
    total = ref["sum3"][0]
    for step in range(1, s_.z):
        arrived("sum3", step, ref["sum3"].at[step])
        total = total + ref["sum3"][step]
    ref["sum2"][2] = total
    small = local(2, ref["sum2"].at[2], ref["small"])
    small.start()

    small.wait()
    for number in (2, 3):
        final_store(number % 2, *finals[number]).wait()
    own_lo.wait()
    own_gt.wait()
    for r in range(1, s_.n_hid):
        arrived("lo", r, out_rows("layer_out", h))
        arrived("gt", r, out_rows("grad_rows", h))
        left("params", r, ref["params"])
        left("ct", r, cot_rows(h))
        left("lo", r, cot_rows(h))
        left("gt", r, cot_rows(h))
        left("sum1", r, ref["sum1"].at[r])
    left("sum2", 0, ref["sum2"].at[0])
    for step in range(1, s_.z):
        left("sum3", step, ref["sum3"].at[0])
    z_left("za", 0, ref["a_own"])
    for f in (0, 1):
        z_left("zm", f, ref["m_own"].at[f])
    for r, f in tree.units:
        left("ac", tree.pos[r, f], a_part(r, f, c))
        if r:
            left("ax", tree.pos[r, f], a_part(r, f, c))
    for r, f in tree.m_units:
        left("mc", tree.m_pos[r, f], m_part(r, f, c))
    for r, f in tree.m_near:
        left("mx", tree.m_pos[r, f], m_part(r, f, c))
    for r, f in far_units:
        left("fs", tree.m_pos[r, f], m_block(r, f))
        z_left("zf", tree.m_pos[r, f], m_block(r, f))
    for k in range(max(0, s_.n_hid - 2), s_.n_hid):
        stage_free("a", s_.n_hid - 1 - k, 2 + k % 2)


def scratch(size, tree):
    s_ = size
    units = len(tree.units)
    vmem = {
        "params_all": ((SMALL_ROWS, s_.d), F32),
        "xs": ((s_.n, s_.d), BF16),
        "ct": ((s_.n, s_.d), BF16),
        "nrm": ((s_.n, s_.d), BF16),
        "nrm_t": ((s_.d, s_.n), BF16),
        "n2": ((s_.n, s_.d), BF16),
        "n2_t": ((s_.d, s_.n), BF16),
        "ct_t": ((s_.d, s_.n), BF16),
        "pj": ((s_.n_hid, s_.n, 3 * s_.kh), BF16),
        "probs": ((s_.n_hid, s_.pairs, s_.n, 2 * BLOCK), BF16),
        "att": ((s_.n_hid, s_.n, s_.kh), BF16),
        "res": ((s_.n, s_.d), F32),
        "facc": ((s_.n, s_.d), F32),
        "gacc": ((s_.n, s_.d), F32),
        "wa": ((s_.n_hid, s_.z, 2, s_.tb, s_.wide), BF16),
        "hid": ((s_.n, s_.fs), BF16),
        "gb": ((s_.n, s_.fs), BF16),
        "acc": ((2, s_.z + len(tree.far), s_.tb, s_.wide), BF16),
        "tmp": ((2, s_.z, s_.tb, s_.wide), BF16),
        "more": ((s_.z, s_.tb, s_.wide), BF16),
        "final": ((2, s_.tb, s_.wide), F32),
        "hidden_bias": ((units, 1, s_.fs), F32),
        "hidden_sum": ((units, 1, s_.fs), F32),
        "sums": ((SMALL_ROWS, s_.d), F32),
        "sum1": ((s_.n_hid, SMALL_ROWS, s_.kh), F32),
        "sum2": ((3, SMALL_ROWS, s_.kh), F32),
        "sum3": ((s_.z, SMALL_ROWS, s_.kh), F32),
    }
    pairs = {
        "params": s_.n_hid,
        "za": s_.z,
        "zm": 2 * s_.z,
        "xs": s_.tiles * s_.n_hid,
        "ax": units,
        "ac": units,
        "mx": units,
        "mc": units,
        "ct": s_.n_hid,
        "sa": s_.n_hid,
        "sm": units,
        "ga": units,
        "gm": units,
        "fs": units,
        "zf": units * s_.z,
        "zfar": units * s_.z,
        "fold": units,
        "zga": 2 * s_.z,
        "zgm": 2 * s_.z,
        "lo": s_.n_hid,
        "gt": s_.n_hid,
        "sum1": s_.n_hid,
        "sum2": 1,
        "sum3": s_.z,
    }
    out = {name: pltpu.VMEM(shape, kind) for name, (shape, kind) in vmem.items()}
    for name, count in pairs.items():
        out[name + "_s"] = pltpu.SemaphoreType.DMA((count,))
        out[name + "_r"] = pltpu.SemaphoreType.DMA((count,))
    out["local"] = pltpu.SemaphoreType.DMA((48,))
    out["wload"] = pltpu.SemaphoreType.DMA((s_.n_hid,))
    out["keep"] = pltpu.SemaphoreType.DMA((2,))
    return out


def finish_kernel(kh, fs, grad_ref, a_ref, m_ref, tokens_ref, middle_ref, coarse_ref, output_ref, up_ref, down_ref):
    grad = grad_ref[...]
    rows = grad.shape[0]
    part = min(512, rows)
    by_4, by_16 = group_matrix(part, 4), group_matrix(part, 16)
    tokens_ref[...] = grad.astype(F32)
    for i in range(rows // part):
        piece = grad[i * part : i * part + part]
        middle_ref[pl.ds(i * part // 4, part // 4), :] = dot(by_4, piece)
        coarse_ref[pl.ds(i * part // 16, part // 16), :] = dot(by_16, piece)

    @pl.when(pl.program_id(0) == 0)
    def _():
        output_ref[...] = a_ref[:, pl.ds(3 * kh, kh)].T
        for f in (0, 1):
            up_ref[:, pl.ds(f * fs, fs)] = m_ref[f, :, pl.ds(0, fs)]
            down_ref[pl.ds(f * fs, fs), :] = m_ref[f, :, pl.ds(fs, fs)].T


def finish(size, grad, grad_a, grad_m):
    positions, features = grad.shape
    rows = min(1024, positions)
    tb, fs = size.tb, size.fs
    whole = [((features, tb), F32), ((tb, 2 * fs), F32), ((2 * fs, tb), F32)]
    return pl.pallas_call(
        functools.partial(finish_kernel, features, fs),
        grid=(positions // rows,),
        in_specs=[
            pl.BlockSpec((rows, features), lambda i: (i, 0)),
            pl.BlockSpec(grad_a.shape, lambda i: (0, 0)),
            pl.BlockSpec(grad_m.shape, lambda i: (0, 0, 0)),
        ],
        out_specs=[pl.BlockSpec((rows // t, features), lambda i: (i, 0)) for t in (1, 4, 16)]
        + [pl.BlockSpec(shape, lambda i: (0, 0)) for shape, _ in whole],
        out_shape=[jax.ShapeDtypeStruct((positions // t, features), F32) for t in (1, 4, 16)]
        + [jax.ShapeDtypeStruct(*x) for x in whole],
        compiler_params=pltpu.CompilerParams(vmem_limit_bytes=32 * 2**20),
        name="token_gradients",
    )(grad, grad_a, grad_m)


def shards(
    tokens,
    middle_cond,
    coarse_cond,
    first_gain,
    first_shift,
    attend_weight,
    query_bias,
    value_bias,
    output_weight,
    mixer_bias,
    second_gain,
    second_shift,
    up_weight,
    hidden_bias,
    down_weight,
    down_bias,
    cotangent,
):
    positions, features = tokens.shape
    n_hid, n_tok = lax.axis_size("hid"), lax.axis_size("tok")
    d = features * n_hid
    ff = up_weight.shape[1] * n_hid
    size = Sizes(positions, features, d, ff, n_tok, n_hid)
    tree = Tree(n_hid)
    tb, fs, wide, z = size.tb, size.fs, size.wide, size.z
    a_own = jnp.concatenate([attend_weight.reshape(tb, 3 * features), output_weight.T], axis=1)
    m_own = jnp.stack(
        [
            jnp.concatenate([up_weight[:, f * fs : f * fs + fs], down_weight[f * fs : f * fs + fs].T], axis=1)
            for f in (0, 1)
        ]
    )
    vectors = (first_gain, first_shift, second_gain, second_shift, query_bias, value_bias, mixer_bias, down_bias)
    params = jnp.concatenate(
        [
            jnp.stack(vectors),
            hidden_bias.reshape(ff // d, features),
            jnp.zeros((SMALL_ROWS - 8 - ff // d, features), F32),
        ]
    )
    units = len(tree.units)
    outputs = {
        "layer_out": ((positions, features), BF16),
        "grad_rows": ((positions, features), BF16),
        "grad_a": ((tb, wide), F32),
        "grad_m": ((2, tb, wide), F32),
        "small": ((SMALL_ROWS, features), F32),
        "all_a": ((n_hid, z, 2, tb, wide), BF16),
        "all_m": ((units, z, 2, tb, wide), BF16),
        "own_ga": ((n_hid, z, tb, wide), BF16),
        "sib_ga": ((n_hid, z, tb, wide), BF16),
        "got_ga": ((units, z, size.half, wide), BF16),
        "own_gm": ((units, z, tb, wide), BF16),
        "sib_gm": ((units, z, tb, wide), BF16),
        "got_gm": ((units, z, tb, wide), BF16),
        "z_ga": ((2, z, size.half, wide), BF16),
        "z_gm": ((2, z + len(tree.far), tb, wide), BF16),
        "z_far": ((units, z, tb, wide), BF16),
    }
    hbm = pl.BlockSpec(memory_space=pltpu.HBM)
    results = pl.pallas_call(
        functools.partial(layer_kernel, size, tree),
        out_shape=[jax.ShapeDtypeStruct(*outputs[name]) for name in OUTPUTS],
        in_specs=[hbm] * len(INPUTS),
        out_specs=[hbm] * len(OUTPUTS),
        scratch_shapes=list(scratch(size, tree).values()),
        compiler_params=pltpu.CompilerParams(
            collective_id=0, has_side_effects=True, vmem_limit_bytes=62 * 2**20
        ),
        cost_estimate=pl.CostEstimate(flops=80 * 10**9, bytes_accessed=2 * 10**8, transcendentals=10**7),
        name="layer",
    )(tokens, middle_cond, coarse_cond, cotangent, a_own, m_own, params)
    layer_out, grad_rows, grad_a, grad_m, small = results[:5]
    grad_tokens, grad_middle, grad_coarse, grad_output, grad_up, grad_down = finish(
        size, grad_rows, grad_a, grad_m
    )
    tok = lax.axis_index("tok")
    share = features // n_tok
    mine = lax.dynamic_slice_in_dim(small[:8], tok * share, share, 1)
    hidden_share = fs * 2 // n_tok
    grad_hidden_bias = lax.dynamic_slice_in_dim(
        small[8 : 8 + ff // d].reshape(-1), tok * hidden_share, hidden_share, 0
    )
    return (
        layer_out,
        grad_tokens,
        grad_middle,
        grad_coarse,
        mine[0],
        mine[1],
        grad_a[:, : 3 * features].reshape(tb, 3, features),
        mine[4],
        mine[5],
        grad_output,
        mine[6],
        mine[2],
        mine[3],
        grad_up,
        grad_hidden_bias,
        grad_down,
        mine[7],
    )


def solution(mesh):
    return jax.shard_map(
        shards,
        mesh=mesh,
        in_specs=(
            P("tok", "hid"),
            P("tok", "hid"),
            P("tok", "hid"),
            P("hid"),
            P("hid"),
            P("tok", None, "hid"),
            P("hid"),
            P("hid"),
            P("hid", "tok"),
            P("hid"),
            P("hid"),
            P("hid"),
            P("tok", "hid"),
            P("hid"),
            P("hid", "tok"),
            P("hid"),
            P("tok", "hid"),
        ),
        out_specs=(
            P("tok", "hid"),
            P("tok", "hid"),
            P("tok", "hid"),
            P("tok", "hid"),
            P(("hid", "tok")),
            P(("hid", "tok")),
            P("tok", None, "hid"),
            P(("hid", "tok")),
            P(("hid", "tok")),
            P("hid", "tok"),
            P(("hid", "tok")),
            P(("hid", "tok")),
            P(("hid", "tok")),
            P("tok", "hid"),
            P(("hid", "tok")),
            P("hid", "tok"),
            P(("hid", "tok")),
        ),
        check_vma=False,
    )
```

```python
import functools

import jax
import jax.numpy as jnp
from jax import lax
from jax.experimental import pallas as pl
from jax.experimental.pallas import tpu as pltpu
from jax.sharding import PartitionSpec as P

HEAD = 64
BLOCK = 128
PAIR = 2 * HEAD
EPSILON = 1e-05
MESH = pl.DeviceIdType.MESH
BF16 = jnp.bfloat16
F32 = jnp.float32
SMALL_ROWS = 16
SUM_BUFFERS = 6


class Tree:
    def __init__(self, n_hid):
        self.n = n_hid
        self.bits = n_hid.bit_length() - 1
        units = [(r, f) for r in range(n_hid) for f in (0, 1)]
        self.units = sorted(units, key=lambda u: (u[0].bit_count(), len(self.children(*u)), u))
        self.pos = {u: k for k, u in enumerate(self.units)}
        self.near = [1 << b for b in range(self.bits)]
        self.far = [r for r in range(n_hid) if r.bit_count() > 1]
        first = [(1 << b, b % 2) for b in range(self.bits)]
        second = [(1 << b, 1 - b % 2) for b in range(self.bits)]
        self.m_near = first + second
        self.m_units = [(0, 0), (0, 1)] + first + [(r, f) for r in self.far for f in (0, 1)] + second
        self.m_pos = {u: k for k, u in enumerate(self.m_units)}

    def children(self, r, f):
        held = [b for b in range(self.bits) if r >> b & 1]
        free = [b for b in range(self.bits) if not r >> b & 1]
        if held:
            free = [b for b in free if (b < held[0] if f == 0 else b > held[-1])]
        return [(r | 1 << b, b) for b in free]

    def parent(self, r, f):
        held = [b for b in range(self.bits) if r >> b & 1]
        return held[0] if f == 0 else held[-1]


class Schedule:
    def __init__(self, done, kids, lag, last_point):
        self.at = {}
        self.turn = {}
        self.before = {}
        self.first = set()
        sent = {}
        seen = set()
        holders = [None] * SUM_BUFFERS
        waiting = sorted(done, key=lambda u: done[u])
        held = None
        point = 0
        while waiting or held is not None:
            actions = []
            if held is not None:
                actions.append(("finish", held))
                sent[held] = point
                held = None
            for unit in waiting:
                if point <= done[unit] or any(k not in sent for k in kids[unit]):
                    continue
                if point < last_point and any(point < sent[k] + lag[unit[0]] for k in kids[unit]):
                    continue
                actions.append(("fetch", unit))
                held = unit
                self.turn[unit] = k = len(self.turn) % SUM_BUFFERS
                self.before[unit] = holders[k]
                holders[k] = unit
                if unit[:2] not in seen:
                    self.first.add(unit)
                seen.add(unit[:2])
                waiting.remove(unit)
                break
            if actions:
                self.at[point] = actions
            point += 1
        self.end = point
        self.holders = holders


def dot(a, b):
    return jnp.dot(a, b, preferred_element_type=F32)


def dot_t(a, b):
    return lax.dot_general(a, b, (((1,), (1,)), ((), ())), preferred_element_type=F32)


def dot_l(a, b):
    return lax.dot_general(a, b, (((0,), (0,)), ((), ())), preferred_element_type=F32)


def repeat_matrix(rows, times):
    row = lax.broadcasted_iota(jnp.int32, (rows, rows // times), 0)
    column = lax.broadcasted_iota(jnp.int32, (rows, rows // times), 1) * times
    return ((row >= column) & (row < column + times)).astype(BF16)


def group_matrix(rows, times):
    row = lax.broadcasted_iota(jnp.int32, (rows // times, rows), 0) * times
    column = lax.broadcasted_iota(jnp.int32, (rows // times, rows), 1)
    return ((column >= row) & (column < row + times)).astype(BF16)


def scaled_rows(values):
    width = values.shape[1]
    average = jnp.sum(values, axis=1, keepdims=True) / width
    square = jnp.sum(values * values, axis=1, keepdims=True) / width
    inverse = lax.rsqrt(square - average * average + EPSILON)
    return (values - average) * inverse, inverse


def norm_pull(grad, gain, scaled, inverse):
    width = grad.shape[1]
    weighted = grad * gain
    mean = jnp.sum(weighted, axis=1, keepdims=True) / width
    along = jnp.sum(weighted * scaled, axis=1, keepdims=True) / width
    return inverse * (weighted - mean - scaled * along)


def row_sum(values):
    return jnp.sum(values, axis=0, keepdims=True)


def two_heads(values):
    low = lax.broadcasted_iota(jnp.int32, values.shape, 1) < HEAD
    zero = jnp.zeros_like(values)
    return jnp.concatenate([jnp.where(low, values, zero), jnp.where(low, zero, values)], axis=0)


def pick_heads(both):
    low = lax.broadcasted_iota(jnp.int32, (BLOCK, PAIR), 1) < HEAD
    return jnp.where(low, both[:BLOCK], both[BLOCK:])


INPUTS = ("tokens", "middle", "coarse", "cotangent", "a_own", "m_own", "params")
OUTPUTS = (
    "layer_out",
    "grad_rows",
    "grad_a",
    "grad_m",
    "small",
    "all_a",
    "all_m",
    "own_ga",
    "sib_ga",
    "got_ga",
    "own_gm",
    "sib_gm",
    "got_gm",
    "z_ga",
    "z_gm",
    "z_far",
)


class Sizes:
    def __init__(self, positions, features, d, ff, n_tok, n_hid):
        self.d, self.n_hid, self.n_tok = d, n_hid, n_tok
        self.z = n_tok // 2
        self.n = positions // n_hid
        self.kh = features
        self.fs = ff // n_hid // 2
        self.tb = d // n_tok
        self.half = self.tb // 2
        self.wide = 4 * features
        self.pairs = features // PAIR
        self.tile = min(256, self.n)
        self.tiles = self.n // self.tile
        self.blocks = self.n // BLOCK
        self.positions = positions


def layer_kernel(size, tree, *refs):
    names = list(INPUTS) + list(OUTPUTS) + list(scratch(size, tree))
    ref = dict(zip(names, refs, strict=True))
    s_ = size
    n_units = len(tree.units)
    tok, h = lax.axis_index("tok"), lax.axis_index("hid")
    z, c = tok // 2, lax.rem(tok, 2)

    def block_of(r):
        total = 0
        for b in range(tree.bits):
            total = total + lax.rem(h // (1 << b) + r // (1 << b), 2) * (1 << b)
        return total

    def peer(r):
        return (tok, block_of(r))

    sibling = (tok + 1 - 2 * c, h)

    def z_peer(step):
        return (lax.rem(z + step, s_.z) * 2 + c, h)

    def columns(j, width):
        return pl.ds(pl.multiple_of(j * width, width), width)

    def remote(name, index, src, dst, device):
        return pltpu.make_async_remote_copy(
            src_ref=src,
            dst_ref=dst,
            send_sem=ref[name + "_s"].at[index],
            recv_sem=ref[name + "_r"].at[index],
            device_id=device,
            device_id_type=MESH,
        )

    def send(name, index, src, dst, device):
        remote(name, index, src, dst, device).start()

    def arrived(name, index, dst):
        remote(name, index, dst, dst, sibling).wait_recv()

    def left(name, index, src):
        remote(name, index, src, src, sibling).wait_send()

    def local(index, src, dst):
        return pltpu.make_async_copy(src, dst, ref["local"].at[index])

    barrier = pltpu.get_barrier_semaphore()
    everyone = [peer(r) for r in range(1, s_.n_hid)] + [sibling]
    everyone += [z_peer(k) for k in range(1, s_.z)]
    for device in everyone:
        pl.semaphore_signal(barrier, inc=1, device_id=device, device_id_type=MESH)
    pl.semaphore_wait(barrier, len(everyone))

    def z_send(name, index, src, dst):
        for step in range(1, s_.z):
            send(name, index * s_.z + step, src, dst, z_peer(step))

    def z_arrived(name, index, dst):
        for step in range(1, s_.z):
            arrived(name, index * s_.z + step, dst)

    def z_left(name, index, src):
        for step in range(1, s_.z):
            left(name, index * s_.z + step, src)

    def a_part(r, f, core):
        return ref["all_a"].at[r, :, core, pl.ds(f * s_.half, s_.half)]

    def m_part(r, f, core):
        return ref["all_m"].at[tree.m_pos[r, f], :, core]

    part = {"a": a_part, "m": m_part}

    for r in range(1, s_.n_hid):
        here = ref["params_all"].at[:, columns(h, s_.kh)]
        send("params", r, ref["params"], here, peer(r))
    own_params = local(0, ref["params"], ref["params_all"].at[:, columns(h, s_.kh)])
    own_params.start()
    z_send("za", 0, ref["a_own"], ref["all_a"].at[0, z, c])
    own_a = local(1, ref["a_own"], ref["all_a"].at[0, z, c])
    own_a.start()
    own_m = []
    for f in (0, 1):
        own_m.append(local(2 + f, ref["m_own"].at[f], ref["all_m"].at[tree.m_pos[0, f], z, c]))
        own_m[f].start()

    def m_block(r, f):
        return ref["all_m"].at[tree.m_pos[r, f], z, c]

    far_units = [(r, f) for r in tree.far for f in (0, 1)]

    kh, n, tile = s_.kh, s_.n, s_.tile
    rows_m, rows_c = n // 4, n // 16
    loads = {}
    order = list(range(1, s_.n_hid)) + [0]
    for r in order:
        j = block_of(r)
        sources = (
            (ref["tokens"].at[columns(j, n)], ref["pj"].at[r, :, pl.ds(0, kh)]),
            (ref["middle"].at[columns(j, rows_m)], ref["pj"].at[r, pl.ds(0, rows_m), pl.ds(2 * kh, kh)]),
            (ref["coarse"].at[columns(j, rows_c)], ref["pj"].at[r, pl.ds(rows_m, rows_c), pl.ds(2 * kh, kh)]),
        )
        loads[r] = [local(4 + 3 * r + k, *pair) for k, pair in enumerate(sources)]
        for copy in loads[r]:
            copy.start()
    repeat_4, repeat_16 = repeat_matrix(tile, 4), repeat_matrix(tile, 16)

    def xs_rows(i, j):
        return ref["xs"].at[pl.ds(i * tile, tile), columns(j, kh)]

    own_xs = []
    for i in range(s_.tiles):
        for r in order:
            if i == 0:
                for copy in loads[r]:
                    copy.wait()
            rows = pl.ds(i * tile, tile)
            middle = ref["pj"][r, pl.ds(i * (tile // 4), tile // 4), pl.ds(2 * kh, kh)]
            coarse = ref["pj"][r, pl.ds(rows_m + i * (tile // 16), tile // 16), pl.ds(2 * kh, kh)]
            total = ref["pj"][r, rows, pl.ds(0, kh)].astype(F32)
            total = total + dot(repeat_4, middle) + dot(repeat_16, coarse)
            ref["pj"][r, rows, pl.ds(kh, kh)] = total.astype(BF16)
            source = ref["pj"].at[r, rows, pl.ds(kh, kh)]
            if r:
                send("xs", i * s_.n_hid + r, source, xs_rows(i, h), peer(r))
            else:
                copy = local(4 + 3 * s_.n_hid + i, source, xs_rows(i, h))
                copy.start()
                own_xs.append(copy)

    for f in (0, 1):
        z_send("zm", f, ref["m_own"].at[f], m_block(0, f))

    def to_sibling(kind, r, f):
        k = tree.pos[r, f] if kind == "a" else tree.m_pos[r, f]
        send(kind + "c", k, part[kind](r, f, c), part[kind](r, f, c), sibling)

    def take_a(r, f):
        arrived("ax", tree.pos[r, f], a_part(r, f, c))
        for child, b in tree.children(r, f):
            send("ax", tree.pos[child, f], a_part(r, f, c), a_part(child, f, c), peer(1 << b))
        to_sibling("a", r, f)

    def take_m(r, f):
        if r in tree.far:
            z_arrived("zf", tree.m_pos[r, f], m_block(r, f))
        else:
            arrived("mx", tree.m_pos[r, f], m_part(r, f, c))
        to_sibling("m", r, f)

    def take_sibling(kind, r, f):
        k = tree.pos[r, f] if kind == "a" else tree.m_pos[r, f]
        arrived(kind + "c", k, part[kind](r, f, 1 - c))

    a_near = sorted([u for u in tree.units if u[0] in tree.near], key=lambda u: -len(tree.children(*u)))
    own_a.wait()
    z_arrived("za", 0, ref["all_a"].at[0, z, c])
    for r, f in a_near:
        send("ax", tree.pos[r, f], a_part(0, f, c), a_part(r, f, c), peer(r))
    for f in (0, 1):
        to_sibling("a", 0, f)
    for r, f in far_units:
        send("fs", tree.m_pos[r, f], ref["m_own"].at[f], m_block(r, f), peer(r))

    own_params.wait()
    for r in range(1, s_.n_hid):
        arrived("params", r, ref["params_all"].at[:, columns(h, kh)])

    def gain_row(k):
        return ref["params_all"][pl.ds(k, 1), :]

    for k, (r, f) in enumerate(tree.m_units):
        parts = [
            ref["params_all"][pl.ds(8 + 2 * f + i, 1), columns(block_of(r), kh)] for i in range(s_.fs // kh)
        ]
        ref["hidden_bias"][k] = jnp.concatenate(parts, axis=1)
        ref["hidden_sum"][k] = jnp.zeros((1, s_.fs), F32)
    ref["sums"][...] = jnp.zeros_like(ref["sums"])

    def add_sum(k, values):
        ref["sums"][pl.ds(k, 1), :] = ref["sums"][pl.ds(k, 1), :] + row_sum(values)

    for i in range(s_.tiles):
        own_xs[i].wait()
        for r in range(1, s_.n_hid):
            arrived("xs", i * s_.n_hid + r, xs_rows(i, h))
        rows = pl.ds(i * tile, tile)
        scaled, _ = scaled_rows(ref["xs"][rows, :].astype(F32))
        normed = (scaled * gain_row(0) + gain_row(1)).astype(BF16)
        ref["nrm"][rows, :] = normed
        ref["nrm_t"][:, rows] = normed.T

    for i in range(s_.tiles):
        for r in range(1, s_.n_hid):
            left("xs", i * s_.n_hid + r, xs_rows(i, h))

    def weight_load(slot, source):
        return pltpu.make_async_copy(source, ref["wa"].at[slot], ref["wload"].at[slot])

    def matrix(slot, first, width):
        return ref["wa"][slot, :, :, :, pl.ds(first, width)].reshape(s_.d, width)

    def put_rows(slot, zz, first, values):
        width = values.shape[1]
        ref["wa"][slot, zz, :, :, pl.ds(first, width)] = values.reshape(2, s_.tb, width)

    def cot_rows(j):
        return ref["ct"].at[:, columns(j, kh)]

    own_ct = local(0, ref["cotangent"].at[columns(h, n)], cot_rows(h))

    def before_chunk(r):
        if r == 0:
            pass
        elif r.bit_count() == 1:
            if r == 1:
                for u, f in a_near:
                    take_a(u, f)
                for u, f in far_units:
                    arrived("fs", tree.m_pos[u, f], m_block(u, f))
                    z_send("zf", tree.m_pos[u, f], m_block(u, f), m_block(u, f))
                own_ct.start()
                for k in range(1, s_.n_hid):
                    send("ct", k, ref["cotangent"].at[columns(block_of(k), n)], cot_rows(h), peer(k))
        else:
            for f in (0, 1):
                take_a(r, f)
        if r == s_.n_hid - 1:
            for f in (0, 1):
                own_m[f].wait()
                z_arrived("zm", f, m_block(0, f))
            for u, f in tree.m_near:
                send("mx", tree.m_pos[u, f], m_part(0, f, c), m_part(u, f, c), peer(u))
            for f in (0, 1):
                to_sibling("m", 0, f)
        for f in (0, 1):
            take_sibling("a", r, f)
        load = weight_load(r, ref["all_a"].at[r])
        load.start()
        load.wait()

    causal_row = lax.broadcasted_iota(jnp.int32, (BLOCK, 2 * BLOCK), 0)
    causal_col = lax.rem(lax.broadcasted_iota(jnp.int32, (BLOCK, 2 * BLOCK), 1), BLOCK)
    allowed = causal_row >= causal_col

    def halves(values, f):
        return [f(values[:, :BLOCK]), f(values[:, BLOCK:])]

    def spread(pair):
        return jnp.concatenate([jnp.broadcast_to(v, (BLOCK, BLOCK)) for v in pair], axis=1)

    def row_max(v):
        return jnp.max(v, axis=1, keepdims=True)

    def row_add(v):
        return jnp.sum(v, axis=1, keepdims=True)

    def attend_chunk(r):
        for k in range(s_.n_hid):
            pl.when(r == k)(functools.partial(before_chunk, k))
        cols = columns(block_of(r), kh)
        bias = jnp.concatenate(
            [ref["params_all"][4:5, cols], jnp.zeros((1, kh), F32), ref["params_all"][5:6, cols]], axis=1
        )

        def project(i, _):
            rows = pl.ds(pl.multiple_of(i * tile, tile), tile)
            values = dot(ref["nrm"][rows, :], matrix(r, 0, 3 * kh)) + bias
            ref["pj"][r, rows, :] = values.astype(BF16)
            return 0

        lax.fori_loop(0, s_.tiles, project, 0)

        def attend(i, _):
            rows = pl.ds(pl.multiple_of(i * BLOCK, BLOCK), BLOCK)
            for p in range(s_.pairs):
                query, key, value = (ref["pj"][r, rows, pl.ds(k * kh + p * PAIR, PAIR)] for k in range(3))
                logits = jnp.where(allowed, dot_t(query, two_heads(key)) * HEAD ** (-0.5), -1e30)
                powers = jnp.exp(logits - spread(halves(logits, row_max)))
                shares = [1.0 / v for v in halves(powers, row_add)]
                attention = (powers * spread(shares)).astype(BF16)
                ref["probs"][r, p, rows, :] = attention
                out = dot(attention, two_heads(value))
                ref["att"][r, rows, pl.ds(p * PAIR, PAIR)] = out.astype(BF16)
            return 0

        lax.fori_loop(0, s_.blocks, attend, 0)

    lax.fori_loop(0, s_.n_hid, lambda r, _: (attend_chunk(r), 0)[1], 0)

    def mix(i, _):
        rows = pl.ds(pl.multiple_of(i * tile, tile), tile)
        total = ref["xs"][rows, :].astype(F32) + gain_row(6)
        for r in range(s_.n_hid):
            total = total + dot_t(ref["att"][r, rows, :], matrix(r, 3 * kh, kh))
        ref["res"][rows, :] = total
        scaled, _inverse = scaled_rows(total)
        normed = (scaled * gain_row(2) + gain_row(3)).astype(BF16)
        ref["n2"][rows, :] = normed
        return 0

    lax.fori_loop(0, s_.tiles, mix, 0)

    own_ct.wait()
    for k in range(1, s_.n_hid):
        arrived("ct", k, cot_rows(h))
    for i in range(s_.tiles):
        rows = pl.ds(i * tile, tile)
        ref["n2_t"][:, rows] = ref["n2"][rows, :].T
        upstream = ref["ct"][rows, :]
        ref["ct_t"][:, rows] = upstream.T
        add_sum(7, upstream.astype(F32))
        ref["facc"][rows, :] = jnp.zeros((tile, s_.d), F32)
        ref["gacc"][rows, :] = jnp.zeros((tile, s_.d), F32)

    mlp_points = 2 * n_units
    chunk_points = mlp_points + 2
    last_point = chunk_points + 4 * s_.n_hid
    done, kids = {}, {}
    for k, (r, f) in enumerate(tree.m_units):
        done["m", r, f] = 2 * k + 1
        kids["m", r, f] = [("m", u, f) for u in tree.near] if r == 0 else []
    for r, f in far_units:
        done["fold", r, f] = 0
        kids["fold", r, f] = [("m", r, f)]
    for r in range(s_.n_hid):
        for f in (0, 1):
            done["a", r, f] = chunk_points + 4 * (s_.n_hid - 1 - r) + 3
            kids["a", r, f] = [("a", child, f) for child, _ in tree.children(r, f)]
    plan = Schedule(done, kids, {"m": 6, "a": 4, "fold": 9}, last_point)

    def place(kind, r, f):
        return tree.pos[r, f] if kind == "a" else tree.m_pos[r, f]

    def own_grad(kind, r, f):
        if kind == "a":
            return ref["own_ga"].at[r, :, pl.ds(f * s_.half, s_.half)]
        return ref["own_gm"].at[tree.m_pos[r, f]]

    def sib_grad(kind, r, f):
        if kind == "a":
            return ref["sib_ga"].at[r, :, pl.ds(f * s_.half, s_.half)]
        return ref["sib_gm"].at[tree.m_pos[r, f]]

    def got_grad(kind, r, f):
        return ref["got_g" + kind].at[place(kind, r, f)]

    def buffer(name, kind, k=None):
        whole = ref[name] if k is None else ref[name].at[k]
        return whole.at[pl.ds(0, s_.z), pl.ds(0, s_.half if kind == "a" else s_.tb)]

    def z_slot(kind, f, step):
        return ref["z_g" + kind].at[f, step]

    def scattered(kind, r, f):
        if r == 0:
            return "zg" + kind, f * s_.z, ref["z_g" + kind].at[f]
        return "zfar", tree.m_pos[r, f] * s_.z, ref["z_far"].at[tree.m_pos[r, f]]

    def scatters(kind, r):
        return r == 0 or (kind == "m" and r in tree.far)

    def free_buffer(k, holder):
        if holder is None:
            return
        kind, r, f = holder
        source = buffer("acc", kind, k)
        if kind == "fold":
            left("fold", tree.m_pos[r, f], source.at[0])
        elif scatters(kind, r):
            name, first, _ = scattered(kind, r, f)
            for step in range(1, s_.z):
                left(name, first + step, source.at[0])
        else:
            left("g" + kind, place(kind, r, f), source)

    def fetches(unit, k):
        kind, r, f = unit
        if kind == "fold":
            return [(30, ref["z_far"].at[tree.m_pos[r, f]], buffer("acc", kind, k))]
        out = [(30, own_grad(*unit), buffer("acc", kind, k))]
        out.append((31, sib_grad(*unit), buffer("tmp", kind)))
        if kids[unit]:
            out.append((32, got_grad(*kids[unit][0]), buffer("more", kind)))
        return out

    def fetch(unit):
        kind, r, f = unit
        k = plan.turn[unit]
        free_buffer(k, plan.before[unit])
        if kind == "fold":
            for step in range(1, s_.z):
                name, first, slots = scattered("m", r, f)
                arrived(name, first + step, slots.at[step])
        elif kind == "m" or unit in plan.first:
            slot = tree.m_pos[r, f] if kind == "m" else r
            arrived("s" + kind, slot, ref["sib_g" + kind].at[slot])
        if kind != "fold":
            for kid in kids[unit][:1]:
                arrived("g" + kind, place(*kid), got_grad(*kid))
        for item in fetches(unit, k):
            local(*item).start()

    def finish(unit):
        kind, r, f = unit
        k = plan.turn[unit]
        for item in fetches(unit, k):
            local(*item).wait()
        acc, tmp, more = buffer("acc", kind, k), buffer("tmp", kind), buffer("more", kind)
        if kind == "fold":
            total = acc[0].astype(F32)
            for zz in range(1, s_.z):
                total = total + acc[zz].astype(F32)
            acc[0] = total.astype(BF16)
            slot = ref["z_gm"].at[f, s_.z + tree.far.index(r)]
            send("fold", tree.m_pos[r, f], acc.at[0], slot, peer(r))
            return
        for zz in range(s_.z):
            total = acc[zz].astype(F32) + tmp[zz].astype(F32)
            if kids[unit]:
                total = total + more[zz].astype(F32)
            acc[zz] = total.astype(BF16)
        for kid in kids[unit][1:]:
            source = got_grad(*kid)
            arrived("g" + kind, place(*kid), source)
            copy = local(36, source, more)
            copy.start()
            copy.wait()
            for zz in range(s_.z):
                acc[zz] = (acc[zz].astype(F32) + more[zz].astype(F32)).astype(BF16)
        if scatters(kind, r):
            name, first, slots = scattered(kind, r, f)
            keep = local(40, acc.at[z], slots.at[0])
            keep.start()
            for step in range(1, s_.z):
                to = lax.rem(z + step, s_.z)
                send(name, first + step, acc.at[to], slots.at[step], z_peer(step))
            keep.wait()
        else:
            to = r if kind == "m" else 1 << tree.parent(r, f)
            send("g" + kind, place(kind, r, f), acc, got_grad(kind, r, f), peer(to))

    def act(point):
        for verb, unit in plan.at.get(point, ()):
            (fetch if verb == "fetch" else finish)(unit)

    def loop_point(step, first, stride, offset, count):
        for k in range(count):
            if first + stride * k + offset in plan.at:
                pl.when(step == k)(functools.partial(act, first + stride * k + offset))

    def stage_copies(kind, index, slot):
        own = ref["own_g" + kind].at[index]
        theirs = ref["sib_g" + kind].at[index]
        keep = pltpu.make_async_copy(ref["wa"].at[slot, :, c], own, ref["keep"].at[slot - 2])
        give = pltpu.make_async_remote_copy(
            src_ref=ref["wa"].at[slot, :, 1 - c],
            dst_ref=theirs,
            send_sem=ref["s" + kind + "_s"].at[index],
            recv_sem=ref["s" + kind + "_r"].at[index],
            device_id=sibling,
            device_id_type=MESH,
        )
        return keep, give

    def stage_out(kind, index, slot):
        for copy in stage_copies(kind, index, slot):
            copy.start()

    def stage_kept(kind, index, slot):
        stage_copies(kind, index, slot)[0].wait()

    def stage_free(kind, index, slot):
        stage_copies(kind, index, slot)[1].wait_send()

    fs = s_.fs
    for k in (0, 1):
        take_sibling("m", *tree.m_units[k])
    weight_load(0, ref["all_m"].at[0]).start()
    gelu_scale = (2.0 / jnp.pi) ** 0.5

    def feed(step, _):
        slot = lax.rem(step, 2)
        weight_load(slot, ref["all_m"].at[step]).wait()

        def rows_of(i, _):
            rows = pl.ds(pl.multiple_of(i * tile, tile), tile)
            up, down = matrix(slot, 0, fs), matrix(slot, fs, fs)
            before = dot(ref["n2"][rows, :], up) + ref["hidden_bias"][step]
            square = before * before
            bent = jnp.tanh(before * (gelu_scale + (gelu_scale * 0.044715) * square))
            share = 0.5 + 0.5 * bent
            hidden = (before * share).astype(BF16)
            slope = share + 0.5 * before * (1.0 - bent * bent) * (
                gelu_scale + (3.0 * gelu_scale * 0.044715) * square
            )
            grad_before = (dot(ref["ct"][rows, :], down) * slope).astype(BF16)
            ref["hid"][rows, :] = hidden
            ref["gb"][rows, :] = grad_before
            ref["facc"][rows, :] = ref["facc"][rows, :] + dot_t(hidden, down)
            ref["gacc"][rows, :] = ref["gacc"][rows, :] + dot_t(grad_before, up)
            ref["hidden_sum"][step] = ref["hidden_sum"][step] + row_sum(grad_before.astype(F32))
            return 0

        lax.fori_loop(0, s_.tiles, rows_of, 0)
        for k in range(1, n_units - 1):
            pl.when(step == k)(functools.partial(take_m, *tree.m_units[k + 1]))

        @pl.when(step >= 1)
        def _():
            stage_kept("m", step - 1, 3 - slot)

        loop_point(step, 0, 2, 0, n_units)
        stage = 2 + slot

        @pl.when(step >= 2)
        def _():
            stage_free("m", step - 2, stage)

        def grads(zz, _):
            rows = pl.ds(pl.multiple_of(zz * (2 * s_.tb), 2 * s_.tb), 2 * s_.tb)
            put_rows(stage, zz, 0, dot(ref["n2_t"][rows, :], ref["gb"][...]).astype(BF16))
            put_rows(stage, zz, fs, dot(ref["ct_t"][rows, :], ref["hid"][...]).astype(BF16))
            return 0

        lax.fori_loop(0, s_.z // 2, grads, 0)
        for k in range(n_units - 1):

            def load_next(k=k):
                if k:
                    take_sibling("m", *tree.m_units[k + 1])
                weight_load((k + 1) % 2, ref["all_m"].at[k + 1]).start()

            pl.when(step == k)(load_next)
        lax.fori_loop(s_.z // 2, s_.z, grads, 0)
        stage_out("m", step, stage)
        loop_point(step, 0, 2, 1, n_units)
        return 0

    lax.fori_loop(0, n_units, feed, 0)

    stage_kept("m", n_units - 1, 2 + (n_units - 1) % 2)
    act(mlp_points)
    weight_load(0, ref["all_a"].at[s_.n_hid - 1]).start()

    def back_two(i, _):
        rows = pl.ds(pl.multiple_of(i * tile, tile), tile)
        residual = ref["res"][rows, :]
        ref["n2"][rows, :] = (residual + (ref["facc"][rows, :] + gain_row(7))).astype(BF16)
        scaled, inverse = scaled_rows(residual)
        grad = ref["gacc"][rows, :]
        add_sum(2, grad * scaled)
        add_sum(3, grad)
        grad = ref["ct"][rows, :].astype(F32) + norm_pull(grad, gain_row(2), scaled, inverse)
        mixed = grad.astype(BF16)
        add_sum(6, mixed.astype(F32))
        ref["facc"][rows, :] = grad
        ref["gacc"][rows, :] = jnp.zeros((tile, s_.d), F32)
        ref["nrm"][rows, :] = mixed
        return 0

    lax.fori_loop(0, s_.tiles, back_two, 0)

    def out_rows(name, j):
        return ref[name].at[columns(j, n)]

    for i in range(s_.tiles):
        rows = pl.ds(i * tile, tile)
        ref["n2_t"][:, rows] = ref["nrm"][rows, :].T
    act(mlp_points + 1)
    for r in range(1, s_.n_hid):
        j = block_of(r)
        send("lo", r, ref["n2"].at[:, columns(j, kh)], out_rows("layer_out", h), peer(r))
    own_lo = local(0, ref["n2"].at[:, columns(h, kh)], out_rows("layer_out", h))
    own_lo.start()
    for k in range(n_units - 2, n_units):
        stage_free("m", k, 2 + k % 2)

    def back_chunk(step, _):
        r = s_.n_hid - 1 - step
        slot = lax.rem(step, 2)
        stage = 2 + slot
        weight_load(slot, ref["all_a"].at[r]).wait()

        @pl.when(step + 1 < s_.n_hid)
        def _():
            weight_load(1 - slot, ref["all_a"].at[lax.rem(2 * s_.n_hid - 2 - step, s_.n_hid)]).start()

        def pull_out(i, _):
            rows = pl.ds(pl.multiple_of(i * tile, tile), tile)
            ref["hid"][rows, pl.ds(0, kh)] = dot(ref["nrm"][rows, :], matrix(slot, 3 * kh, kh)).astype(BF16)
            return 0

        lax.fori_loop(0, s_.tiles, pull_out, 0)

        @pl.when(step >= 1)
        def _():
            stage_kept("a", r + 1, 3 - slot)

        loop_point(step, chunk_points, 4, 0, s_.n_hid)

        def pull_attention(i, _):
            rows = pl.ds(pl.multiple_of(i * BLOCK, BLOCK), BLOCK)
            for p in range(s_.pairs):
                query, key, value = (ref["pj"][r, rows, pl.ds(k * kh + p * PAIR, PAIR)] for k in range(3))
                grad = ref["hid"][rows, pl.ds(p * PAIR, PAIR)]
                attention = ref["probs"][r, p, rows, :]
                weights = attention.astype(F32)
                grad_attention = dot_t(grad, two_heads(value))
                centre = spread(halves(weights * grad_attention, row_add))
                grad_scores = (weights * (grad_attention - centre) * HEAD ** (-0.5)).astype(BF16)
                grad_query = dot(grad_scores, two_heads(key))
                grad_key = pick_heads(dot_l(grad_scores, query))
                grad_value = pick_heads(dot_l(attention, grad))
                for k, values in enumerate((grad_query, grad_key, grad_value)):
                    ref["pj"][r, rows, pl.ds(k * kh + p * PAIR, PAIR)] = values.astype(BF16)
            return 0

        lax.fori_loop(0, s_.blocks, pull_attention, 0)
        loop_point(step, chunk_points, 4, 1, s_.n_hid)

        @pl.when(step >= 2)
        def _():
            stage_free("a", r + 2, stage)

        cols = columns(block_of(r), kh)

        def grads(zz, _):
            rows = pl.ds(pl.multiple_of(zz * (2 * s_.tb), 2 * s_.tb), 2 * s_.tb)
            put_rows(stage, zz, 0, dot(ref["nrm_t"][rows, :], ref["pj"][r]).astype(BF16))
            put_rows(stage, zz, 3 * kh, dot(ref["n2_t"][rows, :], ref["att"][r]).astype(BF16))
            return 0

        lax.fori_loop(0, s_.z, grads, 0)
        stage_out("a", r, stage)
        loop_point(step, chunk_points, 4, 2, s_.n_hid)

        def pull_rows(i, _):
            rows = pl.ds(pl.multiple_of(i * tile, tile), tile)
            grad = ref["pj"][r, rows, :]
            ref["gacc"][rows, :] = ref["gacc"][rows, :] + dot_t(grad, matrix(slot, 0, 3 * kh))
            for k, first in ((4, 0), (5, 2 * kh)):
                part_sum = row_sum(ref["pj"][r, rows, pl.ds(first, kh)].astype(F32))
                ref["sums"][pl.ds(k, 1), cols] = ref["sums"][pl.ds(k, 1), cols] + part_sum
            return 0

        lax.fori_loop(0, s_.tiles, pull_rows, 0)
        loop_point(step, chunk_points, 4, 3, s_.n_hid)
        return 0

    lax.fori_loop(0, s_.n_hid, back_chunk, 0)
    stage_kept("a", 0, 2 + (s_.n_hid - 1) % 2)

    def back_one(i, _):
        rows = pl.ds(pl.multiple_of(i * tile, tile), tile)
        scaled, inverse = scaled_rows(ref["xs"][rows, :].astype(F32))
        grad = ref["gacc"][rows, :]
        add_sum(0, grad * scaled)
        add_sum(1, grad)
        total = ref["facc"][rows, :] + norm_pull(grad, gain_row(0), scaled, inverse)
        ref["ct"][rows, :] = total.astype(BF16)
        return 0

    lax.fori_loop(0, s_.tiles, back_one, 0)
    for k, (r, f) in enumerate(tree.m_units):
        for i in range(s_.fs // kh):
            ref["sums"][pl.ds(8 + 2 * f + i, 1), columns(block_of(r), kh)] = ref["hidden_sum"][
                k, :, pl.ds(i * kh, kh)
            ]
    for r in range(1, s_.n_hid):
        send("sum1", r, ref["sums"].at[:, columns(block_of(r), kh)], ref["sum1"].at[r], peer(r))
    own_gt = local(1, ref["ct"].at[:, columns(h, kh)], out_rows("grad_rows", h))
    own_gt.start()

    def send_rows():
        for r in range(1, s_.n_hid):
            send("gt", r, ref["ct"].at[:, columns(block_of(r), kh)], out_rows("grad_rows", h), peer(r))

    total = ref["sums"][:, columns(h, kh)]
    for r in range(1, s_.n_hid):
        arrived("sum1", r, ref["sum1"].at[r])
        total = total + ref["sum1"][r]
    ref["sum2"][0] = total
    send("sum2", 0, ref["sum2"].at[0], ref["sum2"].at[1], sibling)
    rows_sent = False
    for point in range(last_point, plan.end):
        if not rows_sent and any(verb == "fetch" and unit[:2] == ("a", 0) for verb, unit in plan.at.get(point, ())):
            send_rows()
            rows_sent = True
        act(point)
    if not rows_sent:
        send_rows()
    arrived("sum2", 0, ref["sum2"].at[1])
    ref["sum3"][0] = ref["sum2"][0] + ref["sum2"][1]
    for step in range(1, s_.z):
        send("sum3", step, ref["sum3"].at[0], ref["sum3"].at[step], z_peer(step))
    for k in range(SUM_BUFFERS):
        free_buffer(k, plan.holders[k])

    finals = [("m", 0), ("m", 1), ("a", 0), ("a", 1)]

    def final_loads(k, kind, f):
        slots = ref["z_g" + kind].at[f]
        if kind == "a":
            return [local(30 + k, slots, buffer("acc", kind, k))]
        rest = ref["tmp" if f == 0 else "more"].at[pl.ds(0, len(tree.far))]
        out = [local(30 + k, slots.at[pl.ds(0, s_.z)], buffer("acc", kind, k))]
        if tree.far:
            out.append(local(41 + k, slots.at[pl.ds(s_.z, len(tree.far))], rest))
        return out

    def final_store(k, kind, f):
        if kind == "a":
            source = ref["facc"].at[pl.ds(k * s_.tb, s_.half), pl.ds(0, s_.wide)]
            return local(34 + k, source, ref["grad_a"].at[pl.ds(f * s_.half, s_.half)])
        return local(34 + k, ref["facc"].at[pl.ds(k * s_.tb, s_.tb), pl.ds(0, s_.wide)], ref["grad_m"].at[f])

    for k, (kind, f) in enumerate(finals):
        for step in range(1, s_.z):
            arrived("zg" + kind, f * s_.z + step, z_slot(kind, f, step))
        if kind == "m":
            for i, r in enumerate(tree.far):
                arrived("fold", tree.m_pos[r, f], z_slot(kind, f, s_.z + i))
        for load in final_loads(k, kind, f):
            load.start()
        for load in final_loads(k, kind, f):
            load.wait()
        rows = pl.ds(0, s_.half if kind == "a" else s_.tb)
        total = ref["acc"][k, 0, rows].astype(F32)
        for step in range(1, s_.z):
            total = total + ref["acc"][k, step, rows].astype(F32)
        if kind == "m":
            for i in range(len(tree.far)):
                total = total + ref["tmp" if f == 0 else "more"][i].astype(F32)
        ref["facc"][pl.ds(k * s_.tb, rows.size), pl.ds(0, s_.wide)] = total
        final_store(k, kind, f).start()
    total = ref["sum3"][0]
    for step in range(1, s_.z):
        arrived("sum3", step, ref["sum3"].at[step])
        total = total + ref["sum3"][step]
    ref["sum2"][2] = total
    small = local(2, ref["sum2"].at[2], ref["small"])
    small.start()

    small.wait()
    for k, (kind, f) in enumerate(finals):
        final_store(k, kind, f).wait()
    own_lo.wait()
    own_gt.wait()
    for r in range(1, s_.n_hid):
        arrived("lo", r, out_rows("layer_out", h))
        arrived("gt", r, out_rows("grad_rows", h))
        left("params", r, ref["params"])
        left("ct", r, cot_rows(h))
        left("lo", r, cot_rows(h))
        left("gt", r, cot_rows(h))
        left("sum1", r, ref["sum1"].at[r])
    left("sum2", 0, ref["sum2"].at[0])
    for step in range(1, s_.z):
        left("sum3", step, ref["sum3"].at[0])
    z_left("za", 0, ref["a_own"])
    for f in (0, 1):
        z_left("zm", f, ref["m_own"].at[f])
    for r, f in tree.units:
        left("ac", tree.pos[r, f], a_part(r, f, c))
        if r:
            left("ax", tree.pos[r, f], a_part(r, f, c))
    for r, f in tree.m_units:
        left("mc", tree.m_pos[r, f], m_part(r, f, c))
    for r, f in tree.m_near:
        left("mx", tree.m_pos[r, f], m_part(r, f, c))
    for r, f in far_units:
        left("fs", tree.m_pos[r, f], m_block(r, f))
        z_left("zf", tree.m_pos[r, f], m_block(r, f))
    for k in range(max(0, s_.n_hid - 2), s_.n_hid):
        stage_free("a", s_.n_hid - 1 - k, 2 + k % 2)


def scratch(size, tree):
    s_ = size
    units = len(tree.units)
    vmem = {
        "params_all": ((SMALL_ROWS, s_.d), F32),
        "xs": ((s_.n, s_.d), BF16),
        "ct": ((s_.n, s_.d), BF16),
        "nrm": ((s_.n, s_.d), BF16),
        "nrm_t": ((s_.d, s_.n), BF16),
        "n2": ((s_.n, s_.d), BF16),
        "n2_t": ((s_.d, s_.n), BF16),
        "ct_t": ((s_.d, s_.n), BF16),
        "pj": ((s_.n_hid, s_.n, 3 * s_.kh), BF16),
        "probs": ((s_.n_hid, s_.pairs, s_.n, 2 * BLOCK), BF16),
        "att": ((s_.n_hid, s_.n, s_.kh), BF16),
        "res": ((s_.n, s_.d), F32),
        "facc": ((s_.n, s_.d), F32),
        "gacc": ((s_.n, s_.d), F32),
        "wa": ((s_.n_hid, s_.z, 2, s_.tb, s_.wide), BF16),
        "hid": ((s_.n, s_.fs), BF16),
        "gb": ((s_.n, s_.fs), BF16),
        "acc": ((SUM_BUFFERS, s_.z, s_.tb, s_.wide), BF16),
        "tmp": ((s_.z, s_.tb, s_.wide), BF16),
        "more": ((s_.z, s_.tb, s_.wide), BF16),
        "hidden_bias": ((units, 1, s_.fs), F32),
        "hidden_sum": ((units, 1, s_.fs), F32),
        "sums": ((SMALL_ROWS, s_.d), F32),
        "sum1": ((s_.n_hid, SMALL_ROWS, s_.kh), F32),
        "sum2": ((3, SMALL_ROWS, s_.kh), F32),
        "sum3": ((s_.z, SMALL_ROWS, s_.kh), F32),
    }
    pairs = {
        "params": s_.n_hid,
        "za": s_.z,
        "zm": 2 * s_.z,
        "xs": s_.tiles * s_.n_hid,
        "ax": units,
        "ac": units,
        "mx": units,
        "mc": units,
        "ct": s_.n_hid,
        "sa": s_.n_hid,
        "sm": units,
        "ga": units,
        "gm": units,
        "fs": units,
        "zf": units * s_.z,
        "zfar": units * s_.z,
        "fold": units,
        "zga": 2 * s_.z,
        "zgm": 2 * s_.z,
        "lo": s_.n_hid,
        "gt": s_.n_hid,
        "sum1": s_.n_hid,
        "sum2": 1,
        "sum3": s_.z,
    }
    out = {name: pltpu.VMEM(shape, kind) for name, (shape, kind) in vmem.items()}
    for name, count in pairs.items():
        out[name + "_s"] = pltpu.SemaphoreType.DMA((count,))
        out[name + "_r"] = pltpu.SemaphoreType.DMA((count,))
    out["local"] = pltpu.SemaphoreType.DMA((48,))
    out["wload"] = pltpu.SemaphoreType.DMA((s_.n_hid,))
    out["keep"] = pltpu.SemaphoreType.DMA((2,))
    return out


def finish_kernel(kh, fs, grad_ref, a_ref, m_ref, tokens_ref, middle_ref, coarse_ref, output_ref, up_ref, down_ref):
    grad = grad_ref[...]
    rows = grad.shape[0]
    part = min(512, rows)
    by_4, by_16 = group_matrix(part, 4), group_matrix(part, 16)
    tokens_ref[...] = grad.astype(F32)
    for i in range(rows // part):
        piece = grad[i * part : i * part + part]
        middle_ref[pl.ds(i * part // 4, part // 4), :] = dot(by_4, piece)
        coarse_ref[pl.ds(i * part // 16, part // 16), :] = dot(by_16, piece)

    @pl.when(pl.program_id(0) == 0)
    def _():
        output_ref[...] = a_ref[:, pl.ds(3 * kh, kh)].T
        for f in (0, 1):
            up_ref[:, pl.ds(f * fs, fs)] = m_ref[f, :, pl.ds(0, fs)]
            down_ref[pl.ds(f * fs, fs), :] = m_ref[f, :, pl.ds(fs, fs)].T


def finish(size, grad, grad_a, grad_m):
    positions, features = grad.shape
    rows = min(1024, positions)
    tb, fs = size.tb, size.fs
    whole = [((features, tb), F32), ((tb, 2 * fs), F32), ((2 * fs, tb), F32)]
    return pl.pallas_call(
        functools.partial(finish_kernel, features, fs),
        grid=(positions // rows,),
        in_specs=[
            pl.BlockSpec((rows, features), lambda i: (i, 0)),
            pl.BlockSpec(grad_a.shape, lambda i: (0, 0)),
            pl.BlockSpec(grad_m.shape, lambda i: (0, 0, 0)),
        ],
        out_specs=[pl.BlockSpec((rows // t, features), lambda i: (i, 0)) for t in (1, 4, 16)]
        + [pl.BlockSpec(shape, lambda i: (0, 0)) for shape, _ in whole],
        out_shape=[jax.ShapeDtypeStruct((positions // t, features), F32) for t in (1, 4, 16)]
        + [jax.ShapeDtypeStruct(*x) for x in whole],
        compiler_params=pltpu.CompilerParams(vmem_limit_bytes=32 * 2**20),
        name="token_gradients",
    )(grad, grad_a, grad_m)


def shards(
    tokens,
    middle_cond,
    coarse_cond,
    first_gain,
    first_shift,
    attend_weight,
    query_bias,
    value_bias,
    output_weight,
    mixer_bias,
    second_gain,
    second_shift,
    up_weight,
    hidden_bias,
    down_weight,
    down_bias,
    cotangent,
):
    positions, features = tokens.shape
    n_hid, n_tok = lax.axis_size("hid"), lax.axis_size("tok")
    d = features * n_hid
    ff = up_weight.shape[1] * n_hid
    size = Sizes(positions, features, d, ff, n_tok, n_hid)
    tree = Tree(n_hid)
    tb, fs, wide, z = size.tb, size.fs, size.wide, size.z
    a_own = jnp.concatenate([attend_weight.reshape(tb, 3 * features), output_weight.T], axis=1)
    m_own = jnp.stack(
        [
            jnp.concatenate([up_weight[:, f * fs : f * fs + fs], down_weight[f * fs : f * fs + fs].T], axis=1)
            for f in (0, 1)
        ]
    )
    vectors = (first_gain, first_shift, second_gain, second_shift, query_bias, value_bias, mixer_bias, down_bias)
    params = jnp.concatenate(
        [
            jnp.stack(vectors),
            hidden_bias.reshape(ff // d, features),
            jnp.zeros((SMALL_ROWS - 8 - ff // d, features), F32),
        ]
    )
    units = len(tree.units)
    outputs = {
        "layer_out": ((positions, features), BF16),
        "grad_rows": ((positions, features), BF16),
        "grad_a": ((tb, wide), F32),
        "grad_m": ((2, tb, wide), F32),
        "small": ((SMALL_ROWS, features), F32),
        "all_a": ((n_hid, z, 2, tb, wide), BF16),
        "all_m": ((units, z, 2, tb, wide), BF16),
        "own_ga": ((n_hid, z, tb, wide), BF16),
        "sib_ga": ((n_hid, z, tb, wide), BF16),
        "got_ga": ((units, z, size.half, wide), BF16),
        "own_gm": ((units, z, tb, wide), BF16),
        "sib_gm": ((units, z, tb, wide), BF16),
        "got_gm": ((units, z, tb, wide), BF16),
        "z_ga": ((2, z, size.half, wide), BF16),
        "z_gm": ((2, z + len(tree.far), tb, wide), BF16),
        "z_far": ((units, z, tb, wide), BF16),
    }
    hbm = pl.BlockSpec(memory_space=pltpu.HBM)
    results = pl.pallas_call(
        functools.partial(layer_kernel, size, tree),
        out_shape=[jax.ShapeDtypeStruct(*outputs[name]) for name in OUTPUTS],
        in_specs=[hbm] * len(INPUTS),
        out_specs=[hbm] * len(OUTPUTS),
        scratch_shapes=list(scratch(size, tree).values()),
        compiler_params=pltpu.CompilerParams(
            collective_id=0, has_side_effects=True, vmem_limit_bytes=62 * 2**20
        ),
        cost_estimate=pl.CostEstimate(flops=80 * 10**9, bytes_accessed=2 * 10**8, transcendentals=10**7),
        name="layer",
    )(tokens, middle_cond, coarse_cond, cotangent, a_own, m_own, params)
    layer_out, grad_rows, grad_a, grad_m, small = results[:5]
    grad_tokens, grad_middle, grad_coarse, grad_output, grad_up, grad_down = finish(
        size, grad_rows, grad_a, grad_m
    )
    tok = lax.axis_index("tok")
    share = features // n_tok
    mine = lax.dynamic_slice_in_dim(small[:8], tok * share, share, 1)
    hidden_share = fs * 2 // n_tok
    grad_hidden_bias = lax.dynamic_slice_in_dim(
        small[8 : 8 + ff // d].reshape(-1), tok * hidden_share, hidden_share, 0
    )
    return (
        layer_out,
        grad_tokens,
        grad_middle,
        grad_coarse,
        mine[0],
        mine[1],
        grad_a[:, : 3 * features].reshape(tb, 3, features),
        mine[4],
        mine[5],
        grad_output,
        mine[6],
        mine[2],
        mine[3],
        grad_up,
        grad_hidden_bias,
        grad_down,
        mine[7],
    )


def solution(mesh):
    return jax.shard_map(
        shards,
        mesh=mesh,
        in_specs=(
            P("tok", "hid"),
            P("tok", "hid"),
            P("tok", "hid"),
            P("hid"),
            P("hid"),
            P("tok", None, "hid"),
            P("hid"),
            P("hid"),
            P("hid", "tok"),
            P("hid"),
            P("hid"),
            P("hid"),
            P("tok", "hid"),
            P("hid"),
            P("hid", "tok"),
            P("hid"),
            P("tok", "hid"),
        ),
        out_specs=(
            P("tok", "hid"),
            P("tok", "hid"),
            P("tok", "hid"),
            P("tok", "hid"),
            P(("hid", "tok")),
            P(("hid", "tok")),
            P("tok", None, "hid"),
            P(("hid", "tok")),
            P(("hid", "tok")),
            P("hid", "tok"),
            P(("hid", "tok")),
            P(("hid", "tok")),
            P(("hid", "tok")),
            P("tok", "hid"),
            P(("hid", "tok")),
            P("hid", "tok"),
            P(("hid", "tok")),
        ),
        check_vma=False,
    )
```

```python
import functools

import jax
import jax.numpy as jnp
from jax import lax
from jax.experimental import pallas as pl
from jax.experimental.pallas import tpu as pltpu
from jax.sharding import PartitionSpec as P

HEAD = 64
BLOCK = 128
PAIR = 2 * HEAD
EPSILON = 1e-05
MESH = pl.DeviceIdType.MESH
BF16 = jnp.bfloat16
F32 = jnp.float32
SMALL_ROWS = 16
SUM_BUFFERS = 4


class Tree:
    def __init__(self, n_hid):
        self.n = n_hid
        self.bits = n_hid.bit_length() - 1
        units = [(r, f) for r in range(n_hid) for f in (0, 1)]
        self.units = sorted(units, key=lambda u: (u[0].bit_count(), len(self.children(*u)), u))
        self.pos = {u: k for k, u in enumerate(self.units)}
        self.near = [1 << b for b in range(self.bits)]
        self.far = [r for r in range(n_hid) if r.bit_count() > 1]
        first = [(1 << b, b % 2) for b in range(self.bits)]
        second = [(1 << b, 1 - b % 2) for b in range(self.bits)]
        self.m_near = first + second
        rest = [(r, f) for r in self.far for f in (0, 1)]
        mixed = [u for k in range(max(len(second), len(rest))) for u in second[k : k + 1] + rest[k : k + 1]]
        self.m_units = [(0, 0), (0, 1)] + first + mixed
        self.m_pos = {u: k for k, u in enumerate(self.m_units)}

    def children(self, r, f):
        held = [b for b in range(self.bits) if r >> b & 1]
        free = [b for b in range(self.bits) if not r >> b & 1]
        if held:
            free = [b for b in free if (b < held[0] if f == 0 else b > held[-1])]
        return [(r | 1 << b, b) for b in free]

    def parent(self, r, f):
        held = [b for b in range(self.bits) if r >> b & 1]
        return held[0] if f == 0 else held[-1]


class Schedule:
    def __init__(self, done, kids, lag, last_point):
        self.at = {}
        self.turn = {}
        self.before = {}
        self.first = set()
        sent = {}
        seen = set()
        holders = {True: [None] * SUM_BUFFERS, False: [None] * SUM_BUFFERS}
        turns = {True: 0, False: 0}
        waiting = sorted(done, key=lambda u: done[u])
        held = None
        point = 0
        while waiting or held is not None:
            actions = []
            if held is not None:
                actions.append(("finish", held))
                sent[held] = point
                held = None
            for unit in waiting:
                if point <= done[unit] or any(k not in sent for k in kids[unit]):
                    continue
                if point < last_point and any(point < sent[k] + lag[unit[0]] for k in kids[unit]):
                    continue
                actions.append(("fetch", unit))
                held = unit
                pool = unit[0] == "a"
                self.turn[unit] = k = turns[pool] % SUM_BUFFERS
                turns[pool] += 1
                self.before[unit] = holders[pool][k]
                holders[pool][k] = unit
                if unit[:2] not in seen:
                    self.first.add(unit)
                seen.add(unit[:2])
                waiting.remove(unit)
                break
            if actions:
                self.at[point] = actions
            point += 1
        self.end = point
        self.holders = holders[True] + holders[False]


def dot(a, b):
    return jnp.dot(a, b, preferred_element_type=F32)


def dot_t(a, b):
    return lax.dot_general(a, b, (((1,), (1,)), ((), ())), preferred_element_type=F32)


def dot_l(a, b):
    return lax.dot_general(a, b, (((0,), (0,)), ((), ())), preferred_element_type=F32)


def repeat_matrix(rows, times):
    row = lax.broadcasted_iota(jnp.int32, (rows, rows // times), 0)
    column = lax.broadcasted_iota(jnp.int32, (rows, rows // times), 1) * times
    return ((row >= column) & (row < column + times)).astype(BF16)


def group_matrix(rows, times):
    row = lax.broadcasted_iota(jnp.int32, (rows // times, rows), 0) * times
    column = lax.broadcasted_iota(jnp.int32, (rows // times, rows), 1)
    return ((column >= row) & (column < row + times)).astype(BF16)


def scaled_rows(values):
    width = values.shape[1]
    average = jnp.sum(values, axis=1, keepdims=True) / width
    square = jnp.sum(values * values, axis=1, keepdims=True) / width
    inverse = lax.rsqrt(square - average * average + EPSILON)
    return (values - average) * inverse, inverse


def norm_pull(grad, gain, scaled, inverse):
    width = grad.shape[1]
    weighted = grad * gain
    mean = jnp.sum(weighted, axis=1, keepdims=True) / width
    along = jnp.sum(weighted * scaled, axis=1, keepdims=True) / width
    return inverse * (weighted - mean - scaled * along)


def row_sum(values):
    return jnp.sum(values, axis=0, keepdims=True)


def two_heads(values):
    low = lax.broadcasted_iota(jnp.int32, values.shape, 1) < HEAD
    zero = jnp.zeros_like(values)
    return jnp.concatenate([jnp.where(low, values, zero), jnp.where(low, zero, values)], axis=0)


def pick_heads(both):
    low = lax.broadcasted_iota(jnp.int32, (BLOCK, PAIR), 1) < HEAD
    return jnp.where(low, both[:BLOCK], both[BLOCK:])


INPUTS = ("tokens", "middle", "coarse", "cotangent", "a_own", "m_own", "params")
OUTPUTS = (
    "layer_out",
    "grad_rows",
    "grad_a",
    "grad_m",
    "small",
    "all_a",
    "all_m",
    "own_ga",
    "sib_ga",
    "got_ga",
    "own_gm",
    "sib_gm",
    "got_gm",
    "z_ga",
    "z_gm",
    "z_far",
)


class Sizes:
    def __init__(self, positions, features, d, ff, n_tok, n_hid):
        self.d, self.n_hid, self.n_tok = d, n_hid, n_tok
        self.z = n_tok // 2
        self.n = positions // n_hid
        self.kh = features
        self.fs = ff // n_hid // 2
        self.tb = d // n_tok
        self.half = self.tb // 2
        self.wide = 4 * features
        self.pairs = features // PAIR
        self.tile = min(256, self.n)
        self.tiles = self.n // self.tile
        self.blocks = self.n // BLOCK
        self.positions = positions


def layer_kernel(size, tree, *refs):
    names = list(INPUTS) + list(OUTPUTS) + list(scratch(size, tree))
    ref = dict(zip(names, refs, strict=True))
    s_ = size
    n_units = len(tree.units)
    tok, h = lax.axis_index("tok"), lax.axis_index("hid")
    z, c = tok // 2, lax.rem(tok, 2)

    def block_of(r):
        total = 0
        for b in range(tree.bits):
            total = total + lax.rem(h // (1 << b) + r // (1 << b), 2) * (1 << b)
        return total

    def peer(r):
        return (tok, block_of(r))

    sibling = (tok + 1 - 2 * c, h)

    def z_peer(step):
        return (lax.rem(z + step, s_.z) * 2 + c, h)

    def columns(j, width):
        return pl.ds(pl.multiple_of(j * width, width), width)

    def remote(name, index, src, dst, device):
        return pltpu.make_async_remote_copy(
            src_ref=src,
            dst_ref=dst,
            send_sem=ref[name + "_s"].at[index],
            recv_sem=ref[name + "_r"].at[index],
            device_id=device,
            device_id_type=MESH,
        )

    def send(name, index, src, dst, device):
        remote(name, index, src, dst, device).start()

    def arrived(name, index, dst):
        remote(name, index, dst, dst, sibling).wait_recv()

    def left(name, index, src):
        remote(name, index, src, src, sibling).wait_send()

    def local(index, src, dst):
        return pltpu.make_async_copy(src, dst, ref["local"].at[index])

    barrier = pltpu.get_barrier_semaphore()
    everyone = [peer(r) for r in range(1, s_.n_hid)] + [sibling]
    everyone += [z_peer(k) for k in range(1, s_.z)]
    for device in everyone:
        pl.semaphore_signal(barrier, inc=1, device_id=device, device_id_type=MESH)
    pl.semaphore_wait(barrier, len(everyone))

    def z_send(name, index, src, dst):
        for step in range(1, s_.z):
            send(name, index * s_.z + step, src, dst, z_peer(step))

    def z_arrived(name, index, dst):
        for step in range(1, s_.z):
            arrived(name, index * s_.z + step, dst)

    def z_left(name, index, src):
        for step in range(1, s_.z):
            left(name, index * s_.z + step, src)

    def a_part(r, f, core):
        return ref["all_a"].at[r, :, core, pl.ds(f * s_.half, s_.half)]

    def m_part(r, f, core):
        return ref["all_m"].at[tree.m_pos[r, f], :, core]

    part = {"a": a_part, "m": m_part}

    for r in range(1, s_.n_hid):
        here = ref["params_all"].at[:, columns(h, s_.kh)]
        send("params", r, ref["params"], here, peer(r))
    own_params = local(0, ref["params"], ref["params_all"].at[:, columns(h, s_.kh)])
    own_params.start()
    z_send("za", 0, ref["a_own"], ref["all_a"].at[0, z, c])
    own_blocks = [(ref["a_own"], ref["all_a"].at[0, z, c])]
    own_blocks += [(ref["m_own"].at[f], ref["all_m"].at[tree.m_pos[0, f], z, c]) for f in (0, 1)]
    own_in = [local(1 + k, source, ref["acc"].at[k, 0]) for k, (source, _) in enumerate(own_blocks)]
    own_out = [local(1 + k, ref["acc"].at[k, 0], to) for k, (_, to) in enumerate(own_blocks)]
    for copy in own_in:
        copy.start()

    def m_block(r, f):
        return ref["all_m"].at[tree.m_pos[r, f], z, c]

    far_units = [(r, f) for r in tree.far for f in (0, 1)]

    kh, n, tile = s_.kh, s_.n, s_.tile
    rows_m, rows_c = n // 4, n // 16
    loads = {}
    order = list(range(1, s_.n_hid)) + [0]
    for r in order:
        j = block_of(r)
        sources = (
            (ref["tokens"].at[columns(j, n)], ref["pj"].at[r, :, pl.ds(0, kh)]),
            (ref["middle"].at[columns(j, rows_m)], ref["pj"].at[r, pl.ds(0, rows_m), pl.ds(2 * kh, kh)]),
            (ref["coarse"].at[columns(j, rows_c)], ref["pj"].at[r, pl.ds(rows_m, rows_c), pl.ds(2 * kh, kh)]),
        )
        loads[r] = [local(4 + 3 * r + k, *pair) for k, pair in enumerate(sources)]
        for copy in loads[r]:
            copy.start()
    repeat_4, repeat_16 = repeat_matrix(tile, 4), repeat_matrix(tile, 16)

    def xs_rows(i, j):
        return ref["xs"].at[pl.ds(i * tile, tile), columns(j, kh)]

    own_xs = []
    for i in range(s_.tiles):
        for r in order:
            if i == 0:
                for copy in loads[r]:
                    copy.wait()
            rows = pl.ds(i * tile, tile)
            middle = ref["pj"][r, pl.ds(i * (tile // 4), tile // 4), pl.ds(2 * kh, kh)]
            coarse = ref["pj"][r, pl.ds(rows_m + i * (tile // 16), tile // 16), pl.ds(2 * kh, kh)]
            total = ref["pj"][r, rows, pl.ds(0, kh)].astype(F32)
            total = total + dot(repeat_4, middle) + dot(repeat_16, coarse)
            ref["pj"][r, rows, pl.ds(kh, kh)] = total.astype(BF16)
            source = ref["pj"].at[r, rows, pl.ds(kh, kh)]
            if r:
                send("xs", i * s_.n_hid + r, source, xs_rows(i, h), peer(r))
            else:
                copy = local(4 + 3 * s_.n_hid + i, source, xs_rows(i, h))
                copy.start()
                own_xs.append(copy)

    for load, store in zip(own_in, own_out, strict=True):
        load.wait()
        store.start()

    def to_sibling(kind, r, f):
        k = tree.pos[r, f] if kind == "a" else tree.m_pos[r, f]
        send(kind + "c", k, part[kind](r, f, c), part[kind](r, f, c), sibling)

    def take_a(r, f):
        arrived("ax", tree.pos[r, f], a_part(r, f, c))
        for child, b in tree.children(r, f):
            send("ax", tree.pos[child, f], a_part(r, f, c), a_part(child, f, c), peer(1 << b))
        to_sibling("a", r, f)

    def take_m(r, f):
        if r in tree.far:
            z_arrived("zf", tree.m_pos[r, f], m_block(r, f))
        else:
            arrived("mx", tree.m_pos[r, f], m_part(r, f, c))
        to_sibling("m", r, f)

    def take_sibling(kind, r, f):
        k = tree.pos[r, f] if kind == "a" else tree.m_pos[r, f]
        arrived(kind + "c", k, part[kind](r, f, 1 - c))

    a_near = sorted([u for u in tree.units if u[0] in tree.near], key=lambda u: -len(tree.children(*u)))
    for store in own_out:
        store.wait()
    z_arrived("za", 0, ref["all_a"].at[0, z, c])
    for f in (0, 1):
        z_send("zm", f, ref["m_own"].at[f], m_block(0, f))
    for r, f in a_near:
        send("ax", tree.pos[r, f], a_part(0, f, c), a_part(r, f, c), peer(r))
    for f in (0, 1):
        to_sibling("a", 0, f)

    own_params.wait()
    for r in range(1, s_.n_hid):
        arrived("params", r, ref["params_all"].at[:, columns(h, kh)])

    def gain_row(k):
        return ref["params_all"][pl.ds(k, 1), :]

    for k, (r, f) in enumerate(tree.m_units):
        parts = [
            ref["params_all"][pl.ds(8 + 2 * f + i, 1), columns(block_of(r), kh)] for i in range(s_.fs // kh)
        ]
        ref["hidden_bias"][k] = jnp.concatenate(parts, axis=1)
        ref["hidden_sum"][k] = jnp.zeros((1, s_.fs), F32)
    ref["sums"][...] = jnp.zeros_like(ref["sums"])

    def add_sum(k, values):
        ref["sums"][pl.ds(k, 1), :] = ref["sums"][pl.ds(k, 1), :] + row_sum(values)

    for i in range(s_.tiles):
        own_xs[i].wait()
        for r in range(1, s_.n_hid):
            arrived("xs", i * s_.n_hid + r, xs_rows(i, h))
        rows = pl.ds(i * tile, tile)
        scaled, _ = scaled_rows(ref["xs"][rows, :].astype(F32))
        normed = (scaled * gain_row(0) + gain_row(1)).astype(BF16)
        ref["nrm"][rows, :] = normed
        ref["nrm_t"][:, rows] = normed.T

    for i in range(s_.tiles):
        for r in range(1, s_.n_hid):
            left("xs", i * s_.n_hid + r, xs_rows(i, h))

    def weight_load(slot, source):
        return pltpu.make_async_copy(source, ref["wa"].at[slot], ref["wload"].at[slot])

    def matrix(slot, first, width):
        return ref["wa"][slot, :, :, :, pl.ds(first, width)].reshape(s_.d, width)

    def put_rows(slot, zz, first, values):
        width = values.shape[1]
        ref["wa"][slot, zz, :, :, pl.ds(first, width)] = values.reshape(2, s_.tb, width)

    def cot_rows(j):
        return ref["ct"].at[:, columns(j, kh)]

    own_ct = local(0, ref["cotangent"].at[columns(h, n)], cot_rows(h))

    def before_chunk(r):
        if r == 0:
            pass
        elif r.bit_count() == 1:
            if r == 1:
                for u, f in a_near:
                    take_a(u, f)
                own_ct.start()
                for k in range(1, s_.n_hid):
                    send("ct", k, ref["cotangent"].at[columns(block_of(k), n)], cot_rows(h), peer(k))
        else:
            for f in (0, 1):
                take_a(r, f)
        for f in (0, 1):
            take_sibling("a", r, f)
        load = weight_load(r, ref["all_a"].at[r])
        load.start()
        load.wait()

    causal_row = lax.broadcasted_iota(jnp.int32, (BLOCK, 2 * BLOCK), 0)
    causal_col = lax.rem(lax.broadcasted_iota(jnp.int32, (BLOCK, 2 * BLOCK), 1), BLOCK)
    allowed = causal_row >= causal_col

    def halves(values, f):
        return [f(values[:, :BLOCK]), f(values[:, BLOCK:])]

    def spread(pair):
        return jnp.concatenate([jnp.broadcast_to(v, (BLOCK, BLOCK)) for v in pair], axis=1)

    def row_max(v):
        return jnp.max(v, axis=1, keepdims=True)

    def row_add(v):
        return jnp.sum(v, axis=1, keepdims=True)

    def attend_chunk(r):
        for k in range(s_.n_hid):
            pl.when(r == k)(functools.partial(before_chunk, k))
        cols = columns(block_of(r), kh)
        bias = jnp.concatenate(
            [ref["params_all"][4:5, cols], jnp.zeros((1, kh), F32), ref["params_all"][5:6, cols]], axis=1
        )

        def project(i, _):
            rows = pl.ds(pl.multiple_of(i * tile, tile), tile)
            values = dot(ref["nrm"][rows, :], matrix(r, 0, 3 * kh)) + bias
            ref["pj"][r, rows, :] = values.astype(BF16)
            return 0

        lax.fori_loop(0, s_.tiles, project, 0)

        def attend(i, _):
            rows = pl.ds(pl.multiple_of(i * BLOCK, BLOCK), BLOCK)
            for p in range(s_.pairs):
                query, key, value = (ref["pj"][r, rows, pl.ds(k * kh + p * PAIR, PAIR)] for k in range(3))
                logits = jnp.where(allowed, dot_t(query, two_heads(key)) * HEAD ** (-0.5), -1e30)
                powers = jnp.exp(logits - spread(halves(logits, row_max)))
                shares = [1.0 / v for v in halves(powers, row_add)]
                attention = (powers * spread(shares)).astype(BF16)
                ref["probs"][r, p, rows, :] = attention
                out = dot(attention, two_heads(value))
                ref["att"][r, rows, pl.ds(p * PAIR, PAIR)] = out.astype(BF16)
            return 0

        def attend_two(i, _):
            attend(2 * i, 0)
            return attend(2 * i + 1, 0)

        lax.fori_loop(0, s_.blocks // 2, attend_two, 0)

    lax.fori_loop(0, s_.n_hid, lambda r, _: (attend_chunk(r), 0)[1], 0)

    for f in (0, 1):
        z_arrived("zm", f, m_block(0, f))
    for f in (0, 1):
        to_sibling("m", 0, f)

    def mix(i, _):
        rows = pl.ds(pl.multiple_of(i * tile, tile), tile)
        total = ref["xs"][rows, :].astype(F32) + gain_row(6)
        for r in range(s_.n_hid):
            total = total + dot_t(ref["att"][r, rows, :], matrix(r, 3 * kh, kh))
        ref["facc"][rows, :] = total + gain_row(7)
        scaled, inverse = scaled_rows(total)
        ref["scaled_two"][rows, :] = scaled.astype(BF16)
        ref["inverse_two"][rows, :] = inverse
        normed = (scaled * gain_row(2) + gain_row(3)).astype(BF16)
        ref["n2"][rows, :] = normed
        return 0

    lax.fori_loop(0, s_.tiles, mix, 0)

    own_ct.wait()
    for k in range(1, s_.n_hid):
        arrived("ct", k, cot_rows(h))
    for r, f in far_units:
        send("fs", tree.m_pos[r, f], ref["m_own"].at[f], m_block(r, f), peer(r))
    for i in range(s_.tiles):
        rows = pl.ds(i * tile, tile)
        ref["n2_t"][:, rows] = ref["n2"][rows, :].T
        upstream = ref["ct"][rows, :]
        ref["ct_t"][:, :, :, rows] = upstream.T.reshape(s_.z, 2, s_.tb, tile)
        add_sum(7, upstream.astype(F32))
        ref["gacc"][rows, :] = jnp.zeros((tile, s_.d), F32)

    mlp_points = 2 * n_units
    chunk_points = mlp_points + 2
    last_point = chunk_points + 4 * s_.n_hid
    done, kids = {}, {}
    for k, (r, f) in enumerate(tree.m_units):
        done["m", r, f] = 2 * k + 1
        kids["m", r, f] = [("m", u, f) for u in tree.near] if r == 0 else []
        if r == 0:
            done["m", r, f] = mlp_points - 1
    for r, f in far_units:
        done["fold", r, f] = 0
        kids["fold", r, f] = [("m", r, f)]
    for r in range(s_.n_hid):
        for f in (0, 1):
            done["a", r, f] = chunk_points + 4 * (s_.n_hid - 1 - r) + 3
            kids["a", r, f] = [("a", child, f) for child, _ in tree.children(r, f)]
    plan = Schedule(done, kids, {"m": 11, "a": 4, "fold": 9}, last_point)

    def place(kind, r, f):
        return tree.pos[r, f] if kind == "a" else tree.m_pos[r, f]

    def own_grad(kind, r, f):
        if kind == "a":
            return ref["own_ga"].at[r, :, pl.ds(f * s_.half, s_.half)]
        return ref["own_gm"].at[tree.m_pos[r, f]]

    def sib_grad(kind, r, f):
        if kind == "a":
            return ref["sib_ga"].at[r, :, pl.ds(f * s_.half, s_.half)]
        return ref["sib_gm"].at[tree.m_pos[r, f]]

    def got_grad(kind, r, f):
        return ref["got_g" + kind].at[place(kind, r, f)]

    def part_of(whole, kind):
        return whole.at[:, pl.ds(0, s_.half if kind == "a" else s_.tb)]

    def spare(first, rows):
        return ref["ct_t"].at[:, first, rows, pl.ds(0, s_.wide)]

    def sum_buffer(unit):
        k = plan.turn[unit]
        if unit[0] != "a":
            return ref["acc"].at[k]
        rows = pl.ds(k % 2 * s_.half, s_.half)
        return ref["acc"].at[SUM_BUFFERS, :, rows] if k < 2 else spare(1, rows)

    def z_slot(kind, f, step):
        return ref["z_g" + kind].at[f, step]

    def scattered(kind, r, f):
        if r == 0:
            return "zg" + kind, f * s_.z, ref["z_g" + kind].at[f]
        return "zfar", tree.m_pos[r, f] * s_.z, ref["z_far"].at[tree.m_pos[r, f]]

    def scatters(kind, r):
        return r == 0 or (kind == "m" and r in tree.far)

    def free_buffer(holder):
        if holder is None:
            return
        kind, r, f = holder
        source = sum_buffer(holder)
        if kind == "fold":
            left("fold", tree.m_pos[r, f], source.at[0])
        elif scatters(kind, r):
            name, first, _ = scattered(kind, r, f)
            for step in range(1, s_.z):
                left(name, first + step, source.at[0])
        else:
            left("g" + kind, place(kind, r, f), source)

    def fetches(unit):
        kind, r, f = unit
        if kind == "fold":
            return [(30, ref["z_far"].at[tree.m_pos[r, f]], sum_buffer(unit))]
        out = [(30, own_grad(*unit), sum_buffer(unit))]
        out.append((31, sib_grad(*unit), part_of(ref["tmp"], kind)))
        if kids[unit]:
            out.append((32, got_grad(*kids[unit][0]), part_of(spare(0, pl.ds(0, s_.tb)), kind)))
        return out

    def fetch(unit):
        kind, r, f = unit
        free_buffer(plan.before[unit])
        if kind == "fold":
            for step in range(1, s_.z):
                name, first, slots = scattered("m", r, f)
                arrived(name, first + step, slots.at[step])
        elif kind == "m" or unit in plan.first:
            slot = tree.m_pos[r, f] if kind == "m" else r
            arrived("s" + kind, slot, ref["sib_g" + kind].at[slot])
        if kind != "fold":
            for kid in kids[unit][:1]:
                arrived("g" + kind, place(*kid), got_grad(*kid))
        for item in fetches(unit):
            local(*item).start()

    def finish(unit):
        kind, r, f = unit
        for item in fetches(unit):
            local(*item).wait()
        acc, tmp, more = sum_buffer(unit), part_of(ref["tmp"], kind), part_of(spare(0, pl.ds(0, s_.tb)), kind)
        if kind == "fold":
            total = acc[0].astype(F32)
            for zz in range(1, s_.z):
                total = total + acc[zz].astype(F32)
            acc[0] = total.astype(BF16)
            slot = ref["z_gm"].at[f, s_.z + tree.far.index(r)]
            send("fold", tree.m_pos[r, f], acc.at[0], slot, peer(r))
            return
        for zz in range(s_.z):
            total = acc[zz].astype(F32) + tmp[zz].astype(F32)
            if kids[unit]:
                total = total + more[zz].astype(F32)
            acc[zz] = total.astype(BF16)
        for kid in kids[unit][1:]:
            source = got_grad(*kid)
            arrived("g" + kind, place(*kid), source)
            copy = local(36, source, more)
            copy.start()
            copy.wait()
            for zz in range(s_.z):
                acc[zz] = (acc[zz].astype(F32) + more[zz].astype(F32)).astype(BF16)
        if scatters(kind, r):
            name, first, slots = scattered(kind, r, f)
            keep = local(40, acc.at[z], slots.at[0])
            keep.start()
            for step in range(1, s_.z):
                to = lax.rem(z + step, s_.z)
                send(name, first + step, acc.at[to], slots.at[step], z_peer(step))
            keep.wait()
        else:
            to = r if kind == "m" else 1 << tree.parent(r, f)
            send("g" + kind, place(kind, r, f), acc, got_grad(kind, r, f), peer(to))

    def act(point):
        for verb, unit in plan.at.get(point, ()):
            (fetch if verb == "fetch" else finish)(unit)

    def loop_point(step, first, stride, offset, count):
        for k in range(count):
            if first + stride * k + offset in plan.at:
                pl.when(step == k)(functools.partial(act, first + stride * k + offset))

    def stage_copies(kind, index, slot):
        own = ref["own_g" + kind].at[index]
        theirs = ref["sib_g" + kind].at[index]
        keep = pltpu.make_async_copy(ref["wa"].at[slot, :, c], own, ref["keep"].at[slot - 2])
        give = pltpu.make_async_remote_copy(
            src_ref=ref["wa"].at[slot, :, 1 - c],
            dst_ref=theirs,
            send_sem=ref["s" + kind + "_s"].at[index],
            recv_sem=ref["s" + kind + "_r"].at[index],
            device_id=sibling,
            device_id_type=MESH,
        )
        return keep, give

    def stage_out(kind, index, slot):
        for copy in stage_copies(kind, index, slot):
            copy.start()

    def stage_kept(kind, index, slot):
        stage_copies(kind, index, slot)[0].wait()

    def stage_free(kind, index, slot):
        stage_copies(kind, index, slot)[1].wait_send()

    fs = s_.fs
    for k in (0, 1):
        take_sibling("m", *tree.m_units[k])
    weight_load(0, ref["all_m"].at[0]).start()
    big = min(256, n)
    gelu_scale = (2.0 / jnp.pi) ** 0.5

    def feed(step, _):
        slot = lax.rem(step, 2)
        weight_load(slot, ref["all_m"].at[step]).wait()

        def rows_of(i, _):
            rows = pl.ds(pl.multiple_of(i * big, big), big)
            up, down = matrix(slot, 0, fs), matrix(slot, fs, fs)
            before = dot(ref["n2"][rows, :], up) + ref["hidden_bias"][step]
            square = before * before
            bent = jnp.tanh(before * (gelu_scale + (gelu_scale * 0.044715) * square))
            share = 0.5 + 0.5 * bent
            hidden = (before * share).astype(BF16)
            slope = share + 0.5 * before * (1.0 - bent * bent) * (
                gelu_scale + (3.0 * gelu_scale * 0.044715) * square
            )
            grad_before = (dot(ref["ct"][rows, :], down) * slope).astype(BF16)
            ref["hid"][rows, :] = hidden
            ref["gb"][rows, :] = grad_before
            ref["facc"][rows, :] = ref["facc"][rows, :] + dot_t(hidden, down)
            ref["gacc"][rows, :] = ref["gacc"][rows, :] + dot_t(grad_before, up)
            ref["hidden_sum"][step] = ref["hidden_sum"][step] + row_sum(grad_before.astype(F32))
            return 0

        lax.fori_loop(0, n // big, rows_of, 0)

        @pl.when(step == 0)
        def _():
            for r, f in far_units:
                arrived("fs", tree.m_pos[r, f], m_block(r, f))
                z_send("zf", tree.m_pos[r, f], m_block(r, f), m_block(r, f))
            for r, f in tree.m_near:
                send("mx", tree.m_pos[r, f], m_part(0, f, c), m_part(r, f, c), peer(r))

        for k in range(1, n_units - 1):
            pl.when(step == k)(functools.partial(take_m, *tree.m_units[k + 1]))

        @pl.when(step >= 1)
        def _():
            stage_kept("m", step - 1, 3 - slot)

        loop_point(step, 0, 2, 0, n_units)
        stage = 2 + slot

        @pl.when(step >= 2)
        def _():
            stage_free("m", step - 2, stage)

        def grads(zz, _):
            rows = pl.ds(pl.multiple_of(zz * (2 * s_.tb), 2 * s_.tb), 2 * s_.tb)
            put_rows(stage, zz, 0, dot(ref["n2_t"][rows, :], ref["gb"][...]).astype(BF16))
            put_rows(stage, zz, fs, dot(ref["ct_t"][zz].reshape(2 * s_.tb, n), ref["hid"][...]).astype(BF16))
            return 0

        lax.fori_loop(0, s_.z // 2, grads, 0)
        for k in range(n_units - 1):

            def load_next(k=k):
                if k:
                    take_sibling("m", *tree.m_units[k + 1])
                weight_load((k + 1) % 2, ref["all_m"].at[k + 1]).start()

            pl.when(step == k)(load_next)
        lax.fori_loop(s_.z // 2, s_.z, grads, 0)
        stage_out("m", step, stage)
        loop_point(step, 0, 2, 1, n_units)
        return 0

    lax.fori_loop(0, n_units, feed, 0)

    stage_kept("m", n_units - 1, 2 + (n_units - 1) % 2)
    act(mlp_points)
    weight_load(0, ref["all_a"].at[s_.n_hid - 1]).start()

    def back_two(i, _):
        rows = pl.ds(pl.multiple_of(i * tile, tile), tile)
        ref["n2"][rows, :] = ref["facc"][rows, :].astype(BF16)
        scaled, inverse = ref["scaled_two"][rows, :].astype(F32), ref["inverse_two"][rows, :]
        grad = ref["gacc"][rows, :]
        add_sum(2, grad * scaled)
        add_sum(3, grad)
        grad = ref["ct"][rows, :].astype(F32) + norm_pull(grad, gain_row(2), scaled, inverse)
        mixed = grad.astype(BF16)
        add_sum(6, mixed.astype(F32))
        ref["facc"][rows, :] = grad
        ref["gacc"][rows, :] = jnp.zeros((tile, s_.d), F32)
        ref["nrm"][rows, :] = mixed
        return 0

    lax.fori_loop(0, s_.tiles, back_two, 0)

    def out_rows(name, j):
        return ref[name].at[columns(j, n)]

    for i in range(s_.tiles):
        rows = pl.ds(i * tile, tile)
        ref["n2_t"][:, rows] = ref["nrm"][rows, :].T
    act(mlp_points + 1)
    for r in range(1, s_.n_hid):
        j = block_of(r)
        send("lo", r, ref["n2"].at[:, columns(j, kh)], out_rows("layer_out", h), peer(r))
    own_lo = local(0, ref["n2"].at[:, columns(h, kh)], out_rows("layer_out", h))
    own_lo.start()
    for k in range(n_units - 2, n_units):
        stage_free("m", k, 2 + k % 2)

    def back_chunk(step, _):
        r = s_.n_hid - 1 - step
        slot = lax.rem(step, 2)
        stage = 2 + slot
        weight_load(slot, ref["all_a"].at[r]).wait()

        @pl.when(step + 1 < s_.n_hid)
        def _():
            weight_load(1 - slot, ref["all_a"].at[lax.rem(2 * s_.n_hid - 2 - step, s_.n_hid)]).start()

        def pull_out(i, _):
            rows = pl.ds(pl.multiple_of(i * tile, tile), tile)
            ref["hid"][rows, pl.ds(0, kh)] = dot(ref["nrm"][rows, :], matrix(slot, 3 * kh, kh)).astype(BF16)
            return 0

        lax.fori_loop(0, s_.tiles, pull_out, 0)

        @pl.when(step >= 1)
        def _():
            stage_kept("a", r + 1, 3 - slot)

        loop_point(step, chunk_points, 4, 0, s_.n_hid)

        def pull_attention(i, _):
            rows = pl.ds(pl.multiple_of(i * BLOCK, BLOCK), BLOCK)
            for p in range(s_.pairs):
                query, key, value = (ref["pj"][r, rows, pl.ds(k * kh + p * PAIR, PAIR)] for k in range(3))
                grad = ref["hid"][rows, pl.ds(p * PAIR, PAIR)]
                attention = ref["probs"][r, p, rows, :]
                weights = attention.astype(F32)
                grad_attention = dot_t(grad, two_heads(value))
                centre = spread(halves(weights * grad_attention, row_add))
                grad_scores = (weights * (grad_attention - centre) * HEAD ** (-0.5)).astype(BF16)
                grad_query = dot(grad_scores, two_heads(key))
                grad_key = pick_heads(dot_l(grad_scores, query))
                grad_value = pick_heads(dot_l(attention, grad))
                for k, values in enumerate((grad_query, grad_key, grad_value)):
                    ref["pj"][r, rows, pl.ds(k * kh + p * PAIR, PAIR)] = values.astype(BF16)
            return 0

        def pull_two(i, _):
            pull_attention(2 * i, 0)
            return pull_attention(2 * i + 1, 0)

        lax.fori_loop(0, s_.blocks // 2, pull_two, 0)
        loop_point(step, chunk_points, 4, 1, s_.n_hid)

        @pl.when(step >= 2)
        def _():
            stage_free("a", r + 2, stage)

        cols = columns(block_of(r), kh)

        def grads(zz, _):
            rows = pl.ds(pl.multiple_of(zz * (2 * s_.tb), 2 * s_.tb), 2 * s_.tb)
            put_rows(stage, zz, 0, dot(ref["nrm_t"][rows, :], ref["pj"][r]).astype(BF16))
            put_rows(stage, zz, 3 * kh, dot(ref["n2_t"][rows, :], ref["att"][r]).astype(BF16))
            return 0

        lax.fori_loop(0, s_.z, grads, 0)
        stage_out("a", r, stage)
        loop_point(step, chunk_points, 4, 2, s_.n_hid)

        def pull_rows(i, _):
            rows = pl.ds(pl.multiple_of(i * tile, tile), tile)
            grad = ref["pj"][r, rows, :]
            ref["gacc"][rows, :] = ref["gacc"][rows, :] + dot_t(grad, matrix(slot, 0, 3 * kh))
            for k, first in ((4, 0), (5, 2 * kh)):
                part_sum = row_sum(ref["pj"][r, rows, pl.ds(first, kh)].astype(F32))
                ref["sums"][pl.ds(k, 1), cols] = ref["sums"][pl.ds(k, 1), cols] + part_sum
            return 0

        @pl.when(step + 2 < s_.n_hid)
        def _():
            lax.fori_loop(0, s_.tiles, pull_rows, 0)

        loop_point(step, chunk_points, 4, 3, s_.n_hid)
        return 0

    lax.fori_loop(0, s_.n_hid, back_chunk, 0)
    stage_kept("a", 0, 2 + (s_.n_hid - 1) % 2)
    last_two = [(r, (s_.n_hid - 1 - r) % 2) for r in (1, 0)]

    def back_one(i):
        rows = pl.ds(i * tile, tile)
        scaled, inverse = scaled_rows(ref["xs"][rows, :].astype(F32))
        grad = ref["gacc"][rows, :]
        for r, slot in last_two:
            grad = grad + dot_t(ref["pj"][r, rows, :], matrix(slot, 0, 3 * kh))
            for k, first in ((4, 0), (5, 2 * kh)):
                cols = columns(block_of(r), kh)
                part_sum = row_sum(ref["pj"][r, rows, pl.ds(first, kh)].astype(F32))
                ref["sums"][pl.ds(k, 1), cols] = ref["sums"][pl.ds(k, 1), cols] + part_sum
        add_sum(0, grad * scaled)
        add_sum(1, grad)
        total = ref["facc"][rows, :] + norm_pull(grad, gain_row(0), scaled, inverse)
        ref["ct"][rows, :] = total.astype(BF16)

    def row_copy(i, r):
        source = ref["ct"].at[pl.ds(i * tile, tile), columns(block_of(r), kh)]
        return source, ref["grad_rows"].at[pl.ds(pl.multiple_of(h * n + i * tile, tile), tile)]

    def send_rows(i):
        for r in range(1, s_.n_hid):
            send("gt", i * s_.n_hid + r, *row_copy(i, r), peer(r))
        local(41 + i, *row_copy(i, 0)).start()

    for i in range(s_.tiles):
        back_one(i)
    for k, (r, f) in enumerate(tree.m_units):
        for i in range(s_.fs // kh):
            ref["sums"][pl.ds(8 + 2 * f + i, 1), columns(block_of(r), kh)] = ref["hidden_sum"][
                k, :, pl.ds(i * kh, kh)
            ]
    for r in range(1, s_.n_hid):
        send("sum1", r, ref["sums"].at[:, columns(block_of(r), kh)], ref["sum1"].at[r], peer(r))
    for i in range(s_.tiles):
        send_rows(i)

    finals = [("m", 0), ("m", 1), ("a", 0), ("a", 1)]

    def final_loads(k, kind, f):
        slots = ref["z_g" + kind].at[f]
        room = ref["wa"].at[k % 2]
        if kind == "a":
            return [local(30, slots, room.at[:, 0, pl.ds(0, s_.half)])]
        out = [local(30, slots.at[pl.ds(0, s_.z)], room.at[:, 0])]
        if tree.far:
            out.append(local(31, slots.at[pl.ds(s_.z, len(tree.far))], room.at[pl.ds(0, len(tree.far)), 1]))
        return out

    def final_store(k, kind, f):
        if kind == "a":
            source = ref["facc"].at[pl.ds(k * s_.tb, s_.half), pl.ds(0, s_.wide)]
            return local(34 + k, source, ref["grad_a"].at[pl.ds(f * s_.half, s_.half)])
        return local(34 + k, ref["facc"].at[pl.ds(k * s_.tb, s_.tb), pl.ds(0, s_.wide)], ref["grad_m"].at[f])

    def final(k):
        kind, f = finals[k]
        for step in range(1, s_.z):
            arrived("zg" + kind, f * s_.z + step, z_slot(kind, f, step))
        if kind == "m":
            for i, r in enumerate(tree.far):
                arrived("fold", tree.m_pos[r, f], z_slot(kind, f, s_.z + i))
        for load in final_loads(k, kind, f):
            load.start()
        for load in final_loads(k, kind, f):
            load.wait()
        rows = pl.ds(0, s_.half if kind == "a" else s_.tb)
        total = ref["wa"][k % 2, 0, 0, rows].astype(F32)
        for step in range(1, s_.z):
            total = total + ref["wa"][k % 2, step, 0, rows].astype(F32)
        if kind == "m":
            for i in range(len(tree.far)):
                total = total + ref["wa"][k % 2, i, 1].astype(F32)
        ref["facc"][pl.ds(k * s_.tb, rows.size), pl.ds(0, s_.wide)] = total
        final_store(k, kind, f).start()

    def first_finals():
        final(0)
        final(1)

    def first_sums():
        total = ref["sums"][:, columns(h, kh)]
        for r in range(1, s_.n_hid):
            arrived("sum1", r, ref["sum1"].at[r])
            total = total + ref["sum1"][r]
        ref["sum2"][0] = total
        send("sum2", 0, ref["sum2"].at[0], ref["sum2"].at[1], sibling)

    feed_done = False
    for point in range(last_point, plan.end):
        units = [unit for verb, unit in plan.at.get(point, ()) if verb == "fetch"]
        if not feed_done and units and units[0][:2] == ("a", 0):
            first_finals()
            feed_done = True
        act(point)
    if not feed_done:
        first_finals()

    first_sums()
    arrived("sum2", 0, ref["sum2"].at[1])
    ref["sum3"][0] = ref["sum2"][0] + ref["sum2"][1]
    for step in range(1, s_.z):
        send("sum3", step, ref["sum3"].at[0], ref["sum3"].at[step], z_peer(step))
    final(2)
    final(3)
    total = ref["sum3"][0]
    for step in range(1, s_.z):
        arrived("sum3", step, ref["sum3"].at[step])
        total = total + ref["sum3"][step]
    ref["sum2"][2] = total
    small = local(2, ref["sum2"].at[2], ref["small"])
    small.start()

    small.wait()
    for k, (kind, f) in enumerate(finals):
        final_store(k, kind, f).wait()
    own_lo.wait()
    for holder in plan.holders:
        free_buffer(holder)
    for i in range(s_.tiles):
        local(41 + i, *row_copy(i, 0)).wait()
        for r in range(1, s_.n_hid):
            source, to = row_copy(i, r)
            arrived("gt", i * s_.n_hid + r, to)
            left("gt", i * s_.n_hid + r, source)
    for r in range(1, s_.n_hid):
        arrived("lo", r, out_rows("layer_out", h))
        left("params", r, ref["params"])
        left("ct", r, cot_rows(h))
        left("lo", r, cot_rows(h))
        left("sum1", r, ref["sum1"].at[r])
    left("sum2", 0, ref["sum2"].at[0])
    for step in range(1, s_.z):
        left("sum3", step, ref["sum3"].at[0])
    z_left("za", 0, ref["a_own"])
    for f in (0, 1):
        z_left("zm", f, ref["m_own"].at[f])
    for r, f in tree.units:
        left("ac", tree.pos[r, f], a_part(r, f, c))
        if r:
            left("ax", tree.pos[r, f], a_part(r, f, c))
    for r, f in tree.m_units:
        left("mc", tree.m_pos[r, f], m_part(r, f, c))
    for r, f in tree.m_near:
        left("mx", tree.m_pos[r, f], m_part(r, f, c))
    for r, f in far_units:
        left("fs", tree.m_pos[r, f], m_block(r, f))
        z_left("zf", tree.m_pos[r, f], m_block(r, f))
    for k in range(max(0, s_.n_hid - 2), s_.n_hid):
        stage_free("a", s_.n_hid - 1 - k, 2 + k % 2)


def scratch(size, tree):
    s_ = size
    units = len(tree.units)
    vmem = {
        "params_all": ((SMALL_ROWS, s_.d), F32),
        "xs": ((s_.n, s_.d), BF16),
        "ct": ((s_.n, s_.d), BF16),
        "nrm": ((s_.n, s_.d), BF16),
        "nrm_t": ((s_.d, s_.n), BF16),
        "n2": ((s_.n, s_.d), BF16),
        "n2_t": ((s_.d, s_.n), BF16),
        "ct_t": ((s_.z, 2, s_.tb, s_.n), BF16),
        "pj": ((s_.n_hid, s_.n, 3 * s_.kh), BF16),
        "probs": ((s_.n_hid, s_.pairs, s_.n, 2 * BLOCK), BF16),
        "att": ((s_.n_hid, s_.n, s_.kh), BF16),
        "scaled_two": ((s_.n, s_.d), BF16),
        "inverse_two": ((s_.n, 1), F32),
        "facc": ((s_.n, s_.d), F32),
        "gacc": ((s_.n, s_.d), F32),
        "wa": ((s_.n_hid, s_.z, 2, s_.tb, s_.wide), BF16),
        "hid": ((s_.n, s_.fs), BF16),
        "gb": ((s_.n, s_.fs), BF16),
        "acc": ((SUM_BUFFERS + 1, s_.z, s_.tb, s_.wide), BF16),
        "tmp": ((s_.z, s_.tb, s_.wide), BF16),
        "hidden_bias": ((units, 1, s_.fs), F32),
        "hidden_sum": ((units, 1, s_.fs), F32),
        "sums": ((SMALL_ROWS, s_.d), F32),
        "sum1": ((s_.n_hid, SMALL_ROWS, s_.kh), F32),
        "sum2": ((3, SMALL_ROWS, s_.kh), F32),
        "sum3": ((s_.z, SMALL_ROWS, s_.kh), F32),
    }
    pairs = {
        "params": s_.n_hid,
        "za": s_.z,
        "zm": 2 * s_.z,
        "xs": s_.tiles * s_.n_hid,
        "ax": units,
        "ac": units,
        "mx": units,
        "mc": units,
        "ct": s_.n_hid,
        "sa": s_.n_hid,
        "sm": units,
        "ga": units,
        "gm": units,
        "fs": units,
        "zf": units * s_.z,
        "zfar": units * s_.z,
        "fold": units,
        "zga": 2 * s_.z,
        "zgm": 2 * s_.z,
        "lo": s_.n_hid,
        "gt": s_.tiles * s_.n_hid,
        "sum1": s_.n_hid,
        "sum2": 1,
        "sum3": s_.z,
    }
    out = {name: pltpu.VMEM(shape, kind) for name, (shape, kind) in vmem.items()}
    for name, count in pairs.items():
        out[name + "_s"] = pltpu.SemaphoreType.DMA((count,))
        out[name + "_r"] = pltpu.SemaphoreType.DMA((count,))
    out["local"] = pltpu.SemaphoreType.DMA((48,))
    out["wload"] = pltpu.SemaphoreType.DMA((s_.n_hid,))
    out["keep"] = pltpu.SemaphoreType.DMA((2,))
    return out


def finish_kernel(kh, fs, grad_ref, a_ref, m_ref, tokens_ref, middle_ref, coarse_ref, output_ref, up_ref, down_ref):
    grad = grad_ref[...]
    rows = grad.shape[0]
    part = min(512, rows)
    by_4, by_16 = group_matrix(part, 4), group_matrix(part, 16)
    tokens_ref[...] = grad.astype(F32)
    for i in range(rows // part):
        piece = grad[i * part : i * part + part]
        middle_ref[pl.ds(i * part // 4, part // 4), :] = dot(by_4, piece)
        coarse_ref[pl.ds(i * part // 16, part // 16), :] = dot(by_16, piece)

    @pl.when(pl.program_id(0) == 0)
    def _():
        output_ref[...] = a_ref[:, pl.ds(3 * kh, kh)].T
        for f in (0, 1):
            up_ref[:, pl.ds(f * fs, fs)] = m_ref[f, :, pl.ds(0, fs)]
            down_ref[pl.ds(f * fs, fs), :] = m_ref[f, :, pl.ds(fs, fs)].T


def finish(size, grad, grad_a, grad_m):
    positions, features = grad.shape
    rows = min(1024, positions)
    tb, fs = size.tb, size.fs
    whole = [((features, tb), F32), ((tb, 2 * fs), F32), ((2 * fs, tb), F32)]
    return pl.pallas_call(
        functools.partial(finish_kernel, features, fs),
        grid=(positions // rows,),
        in_specs=[
            pl.BlockSpec((rows, features), lambda i: (i, 0)),
            pl.BlockSpec(grad_a.shape, lambda i: (0, 0)),
            pl.BlockSpec(grad_m.shape, lambda i: (0, 0, 0)),
        ],
        out_specs=[pl.BlockSpec((rows // t, features), lambda i: (i, 0)) for t in (1, 4, 16)]
        + [pl.BlockSpec(shape, lambda i: (0, 0)) for shape, _ in whole],
        out_shape=[jax.ShapeDtypeStruct((positions // t, features), F32) for t in (1, 4, 16)]
        + [jax.ShapeDtypeStruct(*x) for x in whole],
        compiler_params=pltpu.CompilerParams(vmem_limit_bytes=32 * 2**20),
        name="token_gradients",
    )(grad, grad_a, grad_m)


def shards(
    tokens,
    middle_cond,
    coarse_cond,
    first_gain,
    first_shift,
    attend_weight,
    query_bias,
    value_bias,
    output_weight,
    mixer_bias,
    second_gain,
    second_shift,
    up_weight,
    hidden_bias,
    down_weight,
    down_bias,
    cotangent,
):
    positions, features = tokens.shape
    n_hid, n_tok = lax.axis_size("hid"), lax.axis_size("tok")
    d = features * n_hid
    ff = up_weight.shape[1] * n_hid
    size = Sizes(positions, features, d, ff, n_tok, n_hid)
    tree = Tree(n_hid)
    tb, fs, wide, z = size.tb, size.fs, size.wide, size.z
    a_own = jnp.concatenate([attend_weight.reshape(tb, 3 * features), output_weight.T], axis=1)
    m_own = jnp.stack(
        [
            jnp.concatenate([up_weight[:, f * fs : f * fs + fs], down_weight[f * fs : f * fs + fs].T], axis=1)
            for f in (0, 1)
        ]
    )
    vectors = (first_gain, first_shift, second_gain, second_shift, query_bias, value_bias, mixer_bias, down_bias)
    params = jnp.concatenate(
        [
            jnp.stack(vectors),
            hidden_bias.reshape(ff // d, features),
            jnp.zeros((SMALL_ROWS - 8 - ff // d, features), F32),
        ]
    )
    units = len(tree.units)
    outputs = {
        "layer_out": ((positions, features), BF16),
        "grad_rows": ((positions, features), BF16),
        "grad_a": ((tb, wide), F32),
        "grad_m": ((2, tb, wide), F32),
        "small": ((SMALL_ROWS, features), F32),
        "all_a": ((n_hid, z, 2, tb, wide), BF16),
        "all_m": ((units, z, 2, tb, wide), BF16),
        "own_ga": ((n_hid, z, tb, wide), BF16),
        "sib_ga": ((n_hid, z, tb, wide), BF16),
        "got_ga": ((units, z, size.half, wide), BF16),
        "own_gm": ((units, z, tb, wide), BF16),
        "sib_gm": ((units, z, tb, wide), BF16),
        "got_gm": ((units, z, tb, wide), BF16),
        "z_ga": ((2, z, size.half, wide), BF16),
        "z_gm": ((2, z + len(tree.far), tb, wide), BF16),
        "z_far": ((units, z, tb, wide), BF16),
    }
    hbm = pl.BlockSpec(memory_space=pltpu.HBM)
    results = pl.pallas_call(
        functools.partial(layer_kernel, size, tree),
        out_shape=[jax.ShapeDtypeStruct(*outputs[name]) for name in OUTPUTS],
        in_specs=[hbm] * len(INPUTS),
        out_specs=[hbm] * len(OUTPUTS),
        scratch_shapes=list(scratch(size, tree).values()),
        compiler_params=pltpu.CompilerParams(
            collective_id=0, has_side_effects=True, vmem_limit_bytes=63 * 2**20
        ),
        cost_estimate=pl.CostEstimate(flops=80 * 10**9, bytes_accessed=2 * 10**8, transcendentals=10**7),
        name="layer",
    )(tokens, middle_cond, coarse_cond, cotangent, a_own, m_own, params)
    layer_out, grad_rows, grad_a, grad_m, small = results[:5]
    grad_tokens, grad_middle, grad_coarse, grad_output, grad_up, grad_down = finish(
        size, grad_rows, grad_a, grad_m
    )
    tok = lax.axis_index("tok")
    share = features // n_tok
    mine = lax.dynamic_slice_in_dim(small[:8], tok * share, share, 1)
    hidden_share = fs * 2 // n_tok
    grad_hidden_bias = lax.dynamic_slice_in_dim(
        small[8 : 8 + ff // d].reshape(-1), tok * hidden_share, hidden_share, 0
    )
    return (
        layer_out,
        grad_tokens,
        grad_middle,
        grad_coarse,
        mine[0],
        mine[1],
        grad_a[:, : 3 * features].reshape(tb, 3, features),
        mine[4],
        mine[5],
        grad_output,
        mine[6],
        mine[2],
        mine[3],
        grad_up,
        grad_hidden_bias,
        grad_down,
        mine[7],
    )


def solution(mesh):
    return jax.shard_map(
        shards,
        mesh=mesh,
        in_specs=(
            P("tok", "hid"),
            P("tok", "hid"),
            P("tok", "hid"),
            P("hid"),
            P("hid"),
            P("tok", None, "hid"),
            P("hid"),
            P("hid"),
            P("hid", "tok"),
            P("hid"),
            P("hid"),
            P("hid"),
            P("tok", "hid"),
            P("hid"),
            P("hid", "tok"),
            P("hid"),
            P("tok", "hid"),
        ),
        out_specs=(
            P("tok", "hid"),
            P("tok", "hid"),
            P("tok", "hid"),
            P("tok", "hid"),
            P(("hid", "tok")),
            P(("hid", "tok")),
            P("tok", None, "hid"),
            P(("hid", "tok")),
            P(("hid", "tok")),
            P("hid", "tok"),
            P(("hid", "tok")),
            P(("hid", "tok")),
            P(("hid", "tok")),
            P("tok", "hid"),
            P(("hid", "tok")),
            P("hid", "tok"),
            P(("hid", "tok")),
        ),
        check_vma=False,
    )
```

```python
import functools

import jax
import jax.numpy as jnp
from jax import lax
from jax.experimental import pallas as pl
from jax.experimental.pallas import tpu as pltpu
from jax.sharding import PartitionSpec as P

HEAD = 64
BLOCK = 128
PAIR = 2 * HEAD
EPSILON = 1e-05
MESH = pl.DeviceIdType.MESH
BF16 = jnp.bfloat16
F32 = jnp.float32
SMALL_ROWS = 16
SUM_BUFFERS = 4


class Tree:
    def __init__(self, n_hid):
        self.n = n_hid
        self.bits = n_hid.bit_length() - 1
        units = [(r, f) for r in range(n_hid) for f in (0, 1)]
        self.units = sorted(units, key=lambda u: (u[0].bit_count(), len(self.children(*u)), u))
        self.pos = {u: k for k, u in enumerate(self.units)}
        self.near = [1 << b for b in range(self.bits)]
        self.far = [r for r in range(n_hid) if r.bit_count() > 1]
        first = [(1 << b, b % 2) for b in range(self.bits)]
        second = [(1 << b, 1 - b % 2) for b in range(self.bits)]
        self.m_near = first + second
        rest = [(r, f) for r in self.far for f in (0, 1)]
        self.m_units = [(0, 0), (0, 1)] + first + rest[:1] + second + rest[1:]
        self.m_pos = {u: k for k, u in enumerate(self.m_units)}

    def children(self, r, f):
        held = [b for b in range(self.bits) if r >> b & 1]
        free = [b for b in range(self.bits) if not r >> b & 1]
        if held:
            free = [b for b in free if (b < held[0] if f == 0 else b > held[-1])]
        return [(r | 1 << b, b) for b in free]

    def parent(self, r, f):
        held = [b for b in range(self.bits) if r >> b & 1]
        return held[0] if f == 0 else held[-1]


class Schedule:
    def __init__(self, done, kids, lag, last_point):
        self.at = {}
        self.turn = {}
        self.before = {}
        self.first = set()
        sent = {}
        seen = set()
        holders = {True: [None] * SUM_BUFFERS, False: [None] * SUM_BUFFERS}
        turns = {True: 0, False: 0}
        waiting = sorted(done, key=lambda u: (done[u], len(kids[u])))
        held = None
        point = 0
        while waiting or held is not None:
            actions = []
            if held is not None:
                actions.append(("finish", held))
                sent[held] = point
                held = None
            for unit in waiting:
                if point <= done[unit] or any(k not in sent for k in kids[unit]):
                    continue
                if point < last_point and any(point < sent[k] + lag[unit[0]] for k in kids[unit]):
                    continue
                actions.append(("fetch", unit))
                held = unit
                pool = unit[0] == "a"
                self.turn[unit] = k = turns[pool] % SUM_BUFFERS
                turns[pool] += 1
                self.before[unit] = holders[pool][k]
                holders[pool][k] = unit
                if unit[:2] not in seen:
                    self.first.add(unit)
                seen.add(unit[:2])
                waiting.remove(unit)
                break
            if actions:
                self.at[point] = actions
            point += 1
        self.end = point
        self.holders = holders[True] + holders[False]


def dot(a, b):
    return jnp.dot(a, b, preferred_element_type=F32)


def dot_t(a, b):
    return lax.dot_general(a, b, (((1,), (1,)), ((), ())), preferred_element_type=F32)


def dot_l(a, b):
    return lax.dot_general(a, b, (((0,), (0,)), ((), ())), preferred_element_type=F32)


def repeat_matrix(rows, times):
    row = lax.broadcasted_iota(jnp.int32, (rows, rows // times), 0)
    column = lax.broadcasted_iota(jnp.int32, (rows, rows // times), 1) * times
    return ((row >= column) & (row < column + times)).astype(BF16)


def group_matrix(rows, times):
    row = lax.broadcasted_iota(jnp.int32, (rows // times, rows), 0) * times
    column = lax.broadcasted_iota(jnp.int32, (rows // times, rows), 1)
    return ((column >= row) & (column < row + times)).astype(BF16)


def scaled_rows(values):
    width = values.shape[1]
    average = jnp.sum(values, axis=1, keepdims=True) / width
    square = jnp.sum(values * values, axis=1, keepdims=True) / width
    inverse = lax.rsqrt(square - average * average + EPSILON)
    return (values - average) * inverse, inverse


def norm_pull(grad, gain, scaled, inverse):
    width = grad.shape[1]
    weighted = grad * gain
    mean = jnp.sum(weighted, axis=1, keepdims=True) / width
    along = jnp.sum(weighted * scaled, axis=1, keepdims=True) / width
    return inverse * (weighted - mean - scaled * along)


def row_sum(values):
    return jnp.sum(values, axis=0, keepdims=True)


def two_heads(values):
    low = lax.broadcasted_iota(jnp.int32, values.shape, 1) < HEAD
    zero = jnp.zeros_like(values)
    return jnp.concatenate([jnp.where(low, values, zero), jnp.where(low, zero, values)], axis=0)


def pick_heads(both):
    low = lax.broadcasted_iota(jnp.int32, (BLOCK, PAIR), 1) < HEAD
    return jnp.where(low, both[:BLOCK], both[BLOCK:])


INPUTS = ("tokens", "middle", "coarse", "cotangent", "attend_w", "output_w", "up_w", "down_w", "params")
OUTPUTS = (
    "layer_out",
    "grad_rows",
    "grad_a",
    "grad_m",
    "small",
    "all_a",
    "all_m",
    "own_ga",
    "sib_ga",
    "got_ga",
    "own_gm",
    "sib_gm",
    "got_gm",
    "z_ga",
    "z_gm",
    "z_far",
)


class Sizes:
    def __init__(self, positions, features, d, ff, n_tok, n_hid):
        self.d, self.n_hid, self.n_tok = d, n_hid, n_tok
        self.z = n_tok // 2
        self.n = positions // n_hid
        self.kh = features
        self.fs = ff // n_hid // 2
        self.tb = d // n_tok
        self.half = self.tb // 2
        self.wide = 4 * features
        self.pairs = features // PAIR
        self.tile = min(256, self.n)
        self.tiles = self.n // self.tile
        self.blocks = self.n // BLOCK
        self.positions = positions


def layer_kernel(size, tree, *refs):
    names = list(INPUTS) + list(OUTPUTS) + list(scratch(size, tree))
    ref = dict(zip(names, refs, strict=True))
    s_ = size
    n_units = len(tree.units)
    tok, h = lax.axis_index("tok"), lax.axis_index("hid")
    z, c = tok // 2, lax.rem(tok, 2)

    def block_of(r):
        total = 0
        for b in range(tree.bits):
            total = total + lax.rem(h // (1 << b) + r // (1 << b), 2) * (1 << b)
        return total

    def peer(r):
        return (tok, block_of(r))

    sibling = (tok + 1 - 2 * c, h)

    def z_peer(step):
        return (lax.rem(z + step, s_.z) * 2 + c, h)

    def columns(j, width):
        return pl.ds(pl.multiple_of(j * width, width), width)

    def remote(name, index, src, dst, device):
        return pltpu.make_async_remote_copy(
            src_ref=src,
            dst_ref=dst,
            send_sem=ref[name + "_s"].at[index],
            recv_sem=ref[name + "_r"].at[index],
            device_id=device,
            device_id_type=MESH,
        )

    def send(name, index, src, dst, device):
        remote(name, index, src, dst, device).start()

    def arrived(name, index, dst):
        remote(name, index, dst, dst, sibling).wait_recv()

    def left(name, index, src):
        remote(name, index, src, src, sibling).wait_send()

    def local(index, src, dst):
        return pltpu.make_async_copy(src, dst, ref["local"].at[index])

    barrier = pltpu.get_barrier_semaphore()
    everyone = [peer(r) for r in range(1, s_.n_hid)] + [sibling]
    everyone += [z_peer(k) for k in range(1, s_.z)]
    for device in everyone:
        pl.semaphore_signal(barrier, inc=1, device_id=device, device_id_type=MESH)
    pl.semaphore_wait(barrier, len(everyone))

    def z_send(name, index, src, dst):
        for step in range(1, s_.z):
            send(name, index * s_.z + step, src, dst, z_peer(step))

    def z_arrived(name, index, dst):
        for step in range(1, s_.z):
            arrived(name, index * s_.z + step, dst)

    def z_left(name, index, src):
        for step in range(1, s_.z):
            left(name, index * s_.z + step, src)

    def a_part(r, f, core):
        return ref["all_a"].at[r, :, core, pl.ds(f * s_.half, s_.half)]

    def m_part(r, f, core):
        return ref["all_m"].at[tree.m_pos[r, f], :, core]

    part = {"a": a_part, "m": m_part}

    for r in range(1, s_.n_hid):
        here = ref["params_all"].at[:, columns(h, s_.kh)]
        send("params", r, ref["params"], here, peer(r))
    own_params = local(0, ref["params"], ref["params_all"].at[:, columns(h, s_.kh)])
    own_params.start()
    kh, n, tile, fs = s_.kh, s_.n, s_.tile, s_.fs
    own_block = [ref["acc"].at[k, 0] for k in range(3)]
    own_loads = [local(1 + k, ref["attend_w"].at[k], own_block[0].at[:, pl.ds(k * kh, kh)]) for k in range(3)]
    own_loads.append(local(40, ref["output_w"], ref["out_in"]))
    for f in (0, 1):
        own_loads.append(local(41 + f, ref["up_w"].at[:, pl.ds(f * fs, fs)], own_block[1 + f].at[:, pl.ds(0, fs)]))
    own_loads.append(local(43, ref["down_w"], ref["down_in"]))
    for copy in own_loads:
        copy.start()
    def m_block(r, f):
        return ref["all_m"].at[tree.m_pos[r, f], z, c]

    far_units = [(r, f) for r in tree.far for f in (0, 1)]

    rows_m, rows_c = n // 4, n // 16
    loads = {}
    order = list(range(1, s_.n_hid)) + [0]
    for r in order:
        j = block_of(r)
        sources = (
            (ref["tokens"].at[columns(j, n)], ref["pj"].at[r, :, pl.ds(0, kh)]),
            (ref["middle"].at[columns(j, rows_m)], ref["pj"].at[r, pl.ds(0, rows_m), pl.ds(2 * kh, kh)]),
            (ref["coarse"].at[columns(j, rows_c)], ref["pj"].at[r, pl.ds(rows_m, rows_c), pl.ds(2 * kh, kh)]),
        )
        loads[r] = [local(4 + 3 * r + k, *pair) for k, pair in enumerate(sources)]
        for copy in loads[r]:
            copy.start()
    for copy in own_loads:
        copy.wait()
    ref["acc"][0, 0, :, pl.ds(3 * kh, kh)] = ref["out_in"][...].T
    z_send("za", 0, own_block[0], ref["all_a"].at[0, z, c])
    for f in (0, 1):
        ref["acc"][1 + f, 0, :, pl.ds(fs, fs)] = ref["down_in"][pl.ds(f * fs, fs), :].T
    for r, f in far_units:
        send("fs", tree.m_pos[r, f], own_block[1 + f], m_block(r, f), peer(r))
    own_places = [ref["all_a"].at[0, z, c], m_block(0, 0), m_block(0, 1)]
    own_out = [local(1 + k, own_block[k], place) for k, place in enumerate(own_places)]
    for store in own_out:
        store.start()
    repeat_4, repeat_16 = repeat_matrix(tile, 4), repeat_matrix(tile, 16)

    def xs_rows(i, j):
        return ref["xs"].at[pl.ds(i * tile, tile), columns(j, kh)]

    own_xs = []
    for i in range(s_.tiles):
        for r in order:
            if i == 0:
                for copy in loads[r]:
                    copy.wait()
            rows = pl.ds(i * tile, tile)
            middle = ref["pj"][r, pl.ds(i * (tile // 4), tile // 4), pl.ds(2 * kh, kh)]
            coarse = ref["pj"][r, pl.ds(rows_m + i * (tile // 16), tile // 16), pl.ds(2 * kh, kh)]
            total = ref["pj"][r, rows, pl.ds(0, kh)].astype(F32)
            total = total + dot(repeat_4, middle) + dot(repeat_16, coarse)
            ref["pj"][r, rows, pl.ds(kh, kh)] = total.astype(BF16)
            source = ref["pj"].at[r, rows, pl.ds(kh, kh)]
            if r:
                send("xs", i * s_.n_hid + r, source, xs_rows(i, h), peer(r))
            else:
                copy = local(4 + 3 * s_.n_hid + i, source, xs_rows(i, h))
                copy.start()
                own_xs.append(copy)


    def to_sibling(kind, r, f):
        k = tree.pos[r, f] if kind == "a" else tree.m_pos[r, f]
        send(kind + "c", k, part[kind](r, f, c), part[kind](r, f, c), sibling)

    def take_a(r, f):
        arrived("ax", tree.pos[r, f], a_part(r, f, c))
        for child, b in tree.children(r, f):
            send("ax", tree.pos[child, f], a_part(r, f, c), a_part(child, f, c), peer(1 << b))
        to_sibling("a", r, f)

    def take_m(r, f):
        if r in tree.far:
            z_arrived("zf", tree.m_pos[r, f], m_block(r, f))
        else:
            arrived("mx", tree.m_pos[r, f], m_part(r, f, c))
        to_sibling("m", r, f)

    def take_sibling(kind, r, f):
        k = tree.pos[r, f] if kind == "a" else tree.m_pos[r, f]
        arrived(kind + "c", k, part[kind](r, f, 1 - c))

    a_near = sorted([u for u in tree.units if u[0] in tree.near], key=lambda u: -len(tree.children(*u)))
    for store in own_out:
        store.wait()
    z_arrived("za", 0, ref["all_a"].at[0, z, c])
    for f in (0, 1):
        z_send("zm", f, own_block[1 + f], m_block(0, f))
    for r, f in far_units:
        arrived("fs", tree.m_pos[r, f], m_block(r, f))
        z_send("zf", tree.m_pos[r, f], m_block(r, f), m_block(r, f))
    for r, f in a_near:
        send("ax", tree.pos[r, f], a_part(0, f, c), a_part(r, f, c), peer(r))
    for f in (0, 1):
        to_sibling("a", 0, f)

    own_params.wait()
    for r in range(1, s_.n_hid):
        arrived("params", r, ref["params_all"].at[:, columns(h, kh)])

    def gain_row(k):
        return ref["params_all"][pl.ds(k, 1), :]

    for k, (r, f) in enumerate(tree.m_units):
        parts = [
            ref["params_all"][pl.ds(8 + 2 * f + i, 1), columns(block_of(r), kh)] for i in range(s_.fs // kh)
        ]
        ref["hidden_bias"][k] = jnp.concatenate(parts, axis=1)
        ref["hidden_sum"][k] = jnp.zeros((1, s_.fs), F32)
    ref["sums"][...] = jnp.zeros_like(ref["sums"])

    def add_sum(k, values):
        ref["sums"][pl.ds(k, 1), :] = ref["sums"][pl.ds(k, 1), :] + row_sum(values)

    for i in range(s_.tiles):
        own_xs[i].wait()
        for r in range(1, s_.n_hid):
            arrived("xs", i * s_.n_hid + r, xs_rows(i, h))
        rows = pl.ds(i * tile, tile)
        scaled, _ = scaled_rows(ref["xs"][rows, :].astype(F32))
        normed = (scaled * gain_row(0) + gain_row(1)).astype(BF16)
        ref["nrm"][rows, :] = normed
        ref["nrm_t"][:, rows] = normed.T

    for i in range(s_.tiles):
        for r in range(1, s_.n_hid):
            left("xs", i * s_.n_hid + r, xs_rows(i, h))

    def weight_load(slot, source):
        return pltpu.make_async_copy(source, ref["wa"].at[slot], ref["wload"].at[slot])

    def matrix(slot, first, width):
        return ref["wa"][slot, :, :, :, pl.ds(first, width)].reshape(s_.d, width)

    def put_rows(slot, zz, first, values):
        width = values.shape[1]
        ref["wa"][slot, zz, :, :, pl.ds(first, width)] = values.reshape(2, s_.tb, width)

    def cot_rows(j):
        return ref["ct"].at[:, columns(j, kh)]

    own_ct = local(0, ref["cotangent"].at[columns(h, n)], cot_rows(h))

    def before_chunk(r):
        if r == 0:
            pass
        elif r.bit_count() == 1:
            if r == 1:
                for u, f in a_near:
                    take_a(u, f)
                own_ct.start()
                for k in range(1, s_.n_hid):
                    send("ct", k, ref["cotangent"].at[columns(block_of(k), n)], cot_rows(h), peer(k))
        else:
            for f in (0, 1):
                take_a(r, f)
        for f in (0, 1):
            take_sibling("a", r, f)
        load = weight_load(r, ref["all_a"].at[r])
        load.start()
        load.wait()

    causal_row = lax.broadcasted_iota(jnp.int32, (BLOCK, 2 * BLOCK), 0)
    causal_col = lax.rem(lax.broadcasted_iota(jnp.int32, (BLOCK, 2 * BLOCK), 1), BLOCK)
    allowed = causal_row >= causal_col

    def halves(values, f):
        return [f(values[:, :BLOCK]), f(values[:, BLOCK:])]

    def spread(pair):
        return jnp.concatenate([jnp.broadcast_to(v, (BLOCK, BLOCK)) for v in pair], axis=1)

    def row_max(v):
        return jnp.max(v, axis=1, keepdims=True)

    def row_add(v):
        return jnp.sum(v, axis=1, keepdims=True)

    def attend_chunk(r):
        for k in range(s_.n_hid):
            pl.when(r == k)(functools.partial(before_chunk, k))
        cols = columns(block_of(r), kh)
        bias = jnp.concatenate(
            [ref["params_all"][4:5, cols], jnp.zeros((1, kh), F32), ref["params_all"][5:6, cols]], axis=1
        )

        def project(i, _):
            rows = pl.ds(pl.multiple_of(i * tile, tile), tile)
            values = dot(ref["nrm"][rows, :], matrix(r, 0, 3 * kh)) + bias
            ref["pj"][r, rows, :] = values.astype(BF16)
            return 0

        lax.fori_loop(0, s_.tiles, project, 0)

        def attend(i, _):
            rows = pl.ds(pl.multiple_of(i * BLOCK, BLOCK), BLOCK)
            for p in range(s_.pairs):
                query, key, value = (ref["pj"][r, rows, pl.ds(k * kh + p * PAIR, PAIR)] for k in range(3))
                logits = jnp.where(allowed, dot_t(query, two_heads(key)) * HEAD ** (-0.5), -1e30)
                powers = jnp.exp(logits - spread(halves(logits, row_max)))
                shares = [1.0 / v for v in halves(powers, row_add)]
                attention = (powers * spread(shares)).astype(BF16)
                ref["probs"][r, p, rows, :] = attention
                out = dot(attention, two_heads(value))
                ref["att"][r, rows, pl.ds(p * PAIR, PAIR)] = out.astype(BF16)
            return 0

        def attend_two(i, _):
            attend(2 * i, 0)
            return attend(2 * i + 1, 0)

        lax.fori_loop(0, s_.blocks // 2, attend_two, 0)

    lax.fori_loop(0, s_.n_hid, lambda r, _: (attend_chunk(r), 0)[1], 0)

    for f in (0, 1):
        z_arrived("zm", f, m_block(0, f))
    for f in (0, 1):
        to_sibling("m", 0, f)
    z_left("za", 0, own_block[0])
    for f in (0, 1):
        z_left("zm", f, own_block[1 + f])
    for r, f in far_units:
        left("fs", tree.m_pos[r, f], own_block[1 + f])

    def mix(i, _):
        rows = pl.ds(pl.multiple_of(i * tile, tile), tile)
        total = ref["xs"][rows, :].astype(F32) + gain_row(6)
        for r in range(s_.n_hid):
            total = total + dot_t(ref["att"][r, rows, :], matrix(r, 3 * kh, kh))
        ref["facc"][rows, :] = total + gain_row(7)
        scaled, inverse = scaled_rows(total)
        ref["scaled_two"][rows, :] = scaled.astype(BF16)
        ref["inverse_two"][rows, :] = inverse
        normed = (scaled * gain_row(2) + gain_row(3)).astype(BF16)
        ref["n2"][rows, :] = normed
        return 0

    lax.fori_loop(0, s_.tiles, mix, 0)

    own_ct.wait()
    for k in range(1, s_.n_hid):
        arrived("ct", k, cot_rows(h))
    for r, f in tree.m_near:
        send("mx", tree.m_pos[r, f], m_part(0, f, c), m_part(r, f, c), peer(r))
    for i in range(s_.tiles):
        rows = pl.ds(i * tile, tile)
        ref["n2_t"][:, rows] = ref["n2"][rows, :].T
        upstream = ref["ct"][rows, :]
        ref["ct_t"][:, :, :, rows] = upstream.T.reshape(s_.z, 2, s_.tb, tile)
        add_sum(7, upstream.astype(F32))
        ref["gacc"][rows, :] = jnp.zeros((tile, s_.d), F32)

    mlp_points = 2 * n_units
    chunk_points = mlp_points + 2
    last_point = chunk_points + 4 * s_.n_hid
    done, kids = {}, {}
    for k, (r, f) in enumerate(tree.m_units):
        done["m", r, f] = 2 * k + 1
        kids["m", r, f] = [("m", u, f) for u in tree.near] if r == 0 else []
        if r == 0:
            done["m", r, f] = mlp_points - 1
    for r, f in far_units:
        done["fold", r, f] = 0
        kids["fold", r, f] = [("m", r, f)]
    for r in range(s_.n_hid):
        for f in (0, 1):
            done["a", r, f] = chunk_points + 4 * (s_.n_hid - 1 - r) + 3
            kids["a", r, f] = [("a", child, f) for child, _ in tree.children(r, f)]
    plan = Schedule(done, kids, {"m": 11, "a": 4, "fold": 9}, last_point)

    def place(kind, r, f):
        return tree.pos[r, f] if kind == "a" else tree.m_pos[r, f]

    def own_grad(kind, r, f):
        if kind == "a":
            return ref["own_ga"].at[r, :, pl.ds(f * s_.half, s_.half)]
        return ref["own_gm"].at[tree.m_pos[r, f]]

    def sib_grad(kind, r, f):
        if kind == "a":
            return ref["sib_ga"].at[r, :, pl.ds(f * s_.half, s_.half)]
        return ref["sib_gm"].at[tree.m_pos[r, f]]

    def got_grad(kind, r, f):
        return ref["got_g" + kind].at[place(kind, r, f)]

    def part_of(whole, kind):
        return whole.at[:, pl.ds(0, s_.half if kind == "a" else s_.tb)]

    def spare(first, rows):
        return ref["ct_t"].at[:, first, rows, pl.ds(0, s_.wide)]

    def sum_buffer(unit):
        k = plan.turn[unit]
        if unit[0] != "a":
            return ref["acc"].at[k]
        rows = pl.ds(k % 2 * s_.half, s_.half)
        return ref["acc"].at[SUM_BUFFERS, :, rows] if k < 2 else spare(1, rows)

    def z_slot(kind, f, step):
        return ref["z_g" + kind].at[f, step]

    def scattered(kind, r, f):
        if r == 0:
            return "zg" + kind, f * s_.z, ref["z_g" + kind].at[f]
        return "zfar", tree.m_pos[r, f] * s_.z, ref["z_far"].at[tree.m_pos[r, f]]

    def scatters(kind, r):
        return r == 0 or (kind == "m" and r in tree.far)

    def free_buffer(holder):
        if holder is None:
            return
        kind, r, f = holder
        source = sum_buffer(holder)
        if kind == "fold":
            left("fold", tree.m_pos[r, f], source.at[0])
        elif scatters(kind, r):
            name, first, _ = scattered(kind, r, f)
            for step in range(1, s_.z):
                left(name, first + step, source.at[0])
        else:
            left("g" + kind, place(kind, r, f), source)

    def fetches(unit):
        kind, r, f = unit
        if kind == "fold":
            return [(30, ref["z_far"].at[tree.m_pos[r, f]], sum_buffer(unit))]
        out = [(30, own_grad(*unit), sum_buffer(unit))]
        out.append((31, sib_grad(*unit), part_of(ref["tmp"], kind)))
        if kids[unit]:
            out.append((32, got_grad(*kids[unit][0]), part_of(spare(0, pl.ds(0, s_.tb)), kind)))
        return out

    def fetch(unit):
        kind, r, f = unit
        free_buffer(plan.before[unit])
        if kind == "fold":
            for step in range(1, s_.z):
                name, first, slots = scattered("m", r, f)
                arrived(name, first + step, slots.at[step])
        elif kind == "m" or unit in plan.first:
            slot = tree.m_pos[r, f] if kind == "m" else r
            arrived("s" + kind, slot, ref["sib_g" + kind].at[slot])
        if kind != "fold":
            for kid in kids[unit][:1]:
                arrived("g" + kind, place(*kid), got_grad(*kid))
        for item in fetches(unit):
            local(*item).start()

    def finish(unit):
        kind, r, f = unit
        for item in fetches(unit):
            local(*item).wait()
        acc, tmp, more = sum_buffer(unit), part_of(ref["tmp"], kind), part_of(spare(0, pl.ds(0, s_.tb)), kind)
        if kind == "fold":
            total = acc[0].astype(F32)
            for zz in range(1, s_.z):
                total = total + acc[zz].astype(F32)
            acc[0] = total.astype(BF16)
            slot = ref["z_gm"].at[f, s_.z + tree.far.index(r)]
            send("fold", tree.m_pos[r, f], acc.at[0], slot, peer(r))
            return
        for zz in range(s_.z):
            total = acc[zz].astype(F32) + tmp[zz].astype(F32)
            if kids[unit]:
                total = total + more[zz].astype(F32)
            acc[zz] = total.astype(BF16)
        for kid in kids[unit][1:]:
            source = got_grad(*kid)
            arrived("g" + kind, place(*kid), source)
            copy = local(36, source, more)
            copy.start()
            copy.wait()
            for zz in range(s_.z):
                acc[zz] = (acc[zz].astype(F32) + more[zz].astype(F32)).astype(BF16)
        if scatters(kind, r):
            name, first, slots = scattered(kind, r, f)
            keep = local(40, acc.at[z], slots.at[0])
            keep.start()
            for step in range(1, s_.z):
                to = lax.rem(z + step, s_.z)
                send(name, first + step, acc.at[to], slots.at[step], z_peer(step))
            keep.wait()
        else:
            to = r if kind == "m" else 1 << tree.parent(r, f)
            send("g" + kind, place(kind, r, f), acc, got_grad(kind, r, f), peer(to))

    def act(point):
        for verb, unit in plan.at.get(point, ()):
            (fetch if verb == "fetch" else finish)(unit)

    def loop_point(step, first, stride, offset, count):
        for k in range(count):
            if first + stride * k + offset in plan.at:
                pl.when(step == k)(functools.partial(act, first + stride * k + offset))

    def stage_copies(kind, index, slot):
        own = ref["own_g" + kind].at[index]
        theirs = ref["sib_g" + kind].at[index]
        keep = pltpu.make_async_copy(ref["wa"].at[slot, :, c], own, ref["keep"].at[slot - 2])
        give = pltpu.make_async_remote_copy(
            src_ref=ref["wa"].at[slot, :, 1 - c],
            dst_ref=theirs,
            send_sem=ref["s" + kind + "_s"].at[index],
            recv_sem=ref["s" + kind + "_r"].at[index],
            device_id=sibling,
            device_id_type=MESH,
        )
        return keep, give

    def stage_out(kind, index, slot):
        for copy in stage_copies(kind, index, slot):
            copy.start()

    def stage_kept(kind, index, slot):
        stage_copies(kind, index, slot)[0].wait()

    def stage_free(kind, index, slot):
        stage_copies(kind, index, slot)[1].wait_send()

    for k in (0, 1):
        take_sibling("m", *tree.m_units[k])
    weight_load(0, ref["all_m"].at[0]).start()
    big = min(256, n)
    gelu_scale = (2.0 / jnp.pi) ** 0.5

    def feed(step, _):
        slot = lax.rem(step, 2)
        weight_load(slot, ref["all_m"].at[step]).wait()

        def rows_of(i, _):
            rows = pl.ds(pl.multiple_of(i * big, big), big)
            up, down = matrix(slot, 0, fs), matrix(slot, fs, fs)
            before = dot(ref["n2"][rows, :], up) + ref["hidden_bias"][step]
            square = before * before
            bent = jnp.tanh(before * (gelu_scale + (gelu_scale * 0.044715) * square))
            share = 0.5 + 0.5 * bent
            hidden = (before * share).astype(BF16)
            slope = share + 0.5 * before * (1.0 - bent * bent) * (
                gelu_scale + (3.0 * gelu_scale * 0.044715) * square
            )
            grad_before = (dot(ref["ct"][rows, :], down) * slope).astype(BF16)
            ref["hid"][rows, :] = hidden
            ref["gb"][rows, :] = grad_before
            ref["facc"][rows, :] = ref["facc"][rows, :] + dot_t(hidden, down)
            ref["gacc"][rows, :] = ref["gacc"][rows, :] + dot_t(grad_before, up)
            ref["hidden_sum"][step] = ref["hidden_sum"][step] + row_sum(grad_before.astype(F32))
            return 0

        lax.fori_loop(0, n // big, rows_of, 0)

        for k in range(1, n_units - 1, 2):

            @pl.when(step == k)
            def _(k=k):
                for unit in tree.m_units[k + 1 : k + 3]:
                    take_m(*unit)


        @pl.when(step >= 1)
        def _():
            stage_kept("m", step - 1, 3 - slot)

        loop_point(step, 0, 2, 0, n_units)
        stage = 2 + slot

        @pl.when(step >= 2)
        def _():
            stage_free("m", step - 2, stage)

        def grads(zz, _):
            rows = pl.ds(pl.multiple_of(zz * (2 * s_.tb), 2 * s_.tb), 2 * s_.tb)
            put_rows(stage, zz, 0, dot(ref["n2_t"][rows, :], ref["gb"][...]).astype(BF16))
            put_rows(stage, zz, fs, dot(ref["ct_t"][zz].reshape(2 * s_.tb, n), ref["hid"][...]).astype(BF16))
            return 0

        lax.fori_loop(0, s_.z // 2, grads, 0)
        for k in range(n_units - 1):

            def load_next(k=k):
                if k:
                    take_sibling("m", *tree.m_units[k + 1])
                weight_load((k + 1) % 2, ref["all_m"].at[k + 1]).start()

            pl.when(step == k)(load_next)
        lax.fori_loop(s_.z // 2, s_.z, grads, 0)
        stage_out("m", step, stage)
        loop_point(step, 0, 2, 1, n_units)
        return 0

    lax.fori_loop(0, n_units, feed, 0)

    stage_kept("m", n_units - 1, 2 + (n_units - 1) % 2)
    act(mlp_points)
    weight_load(0, ref["all_a"].at[s_.n_hid - 1]).start()

    def back_two(i, _):
        rows = pl.ds(pl.multiple_of(i * tile, tile), tile)
        ref["n2"][rows, :] = ref["facc"][rows, :].astype(BF16)
        scaled, inverse = ref["scaled_two"][rows, :].astype(F32), ref["inverse_two"][rows, :]
        grad = ref["gacc"][rows, :]
        add_sum(2, grad * scaled)
        add_sum(3, grad)
        grad = ref["ct"][rows, :].astype(F32) + norm_pull(grad, gain_row(2), scaled, inverse)
        mixed = grad.astype(BF16)
        add_sum(6, mixed.astype(F32))
        ref["facc"][rows, :] = grad
        ref["gacc"][rows, :] = jnp.zeros((tile, s_.d), F32)
        ref["nrm"][rows, :] = mixed
        return 0

    lax.fori_loop(0, s_.tiles, back_two, 0)

    def out_rows(name, j):
        return ref[name].at[columns(j, n)]

    for i in range(s_.tiles):
        rows = pl.ds(i * tile, tile)
        ref["n2_t"][:, rows] = ref["nrm"][rows, :].T
    act(mlp_points + 1)
    for r in range(1, s_.n_hid):
        j = block_of(r)
        send("lo", r, ref["n2"].at[:, columns(j, kh)], out_rows("layer_out", h), peer(r))
    own_lo = local(0, ref["n2"].at[:, columns(h, kh)], out_rows("layer_out", h))
    own_lo.start()
    for k in range(n_units - 2, n_units):
        stage_free("m", k, 2 + k % 2)

    def back_chunk(step, _):
        r = s_.n_hid - 1 - step
        slot = lax.rem(step, 2)
        stage = 2 + slot
        weight_load(slot, ref["all_a"].at[r]).wait()

        @pl.when(step + 1 < s_.n_hid)
        def _():
            weight_load(1 - slot, ref["all_a"].at[lax.rem(2 * s_.n_hid - 2 - step, s_.n_hid)]).start()

        def pull_out(i, _):
            rows = pl.ds(pl.multiple_of(i * tile, tile), tile)
            ref["hid"][rows, pl.ds(0, kh)] = dot(ref["nrm"][rows, :], matrix(slot, 3 * kh, kh)).astype(BF16)
            return 0

        lax.fori_loop(0, s_.tiles, pull_out, 0)

        @pl.when(step >= 1)
        def _():
            stage_kept("a", r + 1, 3 - slot)

        loop_point(step, chunk_points, 4, 0, s_.n_hid)

        def pull_attention(i, _):
            rows = pl.ds(pl.multiple_of(i * BLOCK, BLOCK), BLOCK)
            for p in range(s_.pairs):
                query, key, value = (ref["pj"][r, rows, pl.ds(k * kh + p * PAIR, PAIR)] for k in range(3))
                grad = ref["hid"][rows, pl.ds(p * PAIR, PAIR)]
                attention = ref["probs"][r, p, rows, :]
                weights = attention.astype(F32)
                grad_attention = dot_t(grad, two_heads(value))
                centre = spread(halves(weights * grad_attention, row_add))
                grad_scores = (weights * (grad_attention - centre) * HEAD ** (-0.5)).astype(BF16)
                grad_query = dot(grad_scores, two_heads(key))
                grad_key = pick_heads(dot_l(grad_scores, query))
                grad_value = pick_heads(dot_l(attention, grad))
                for k, values in enumerate((grad_query, grad_key, grad_value)):
                    ref["pj"][r, rows, pl.ds(k * kh + p * PAIR, PAIR)] = values.astype(BF16)
            return 0

        def pull_two(i, _):
            pull_attention(2 * i, 0)
            return pull_attention(2 * i + 1, 0)

        lax.fori_loop(0, s_.blocks // 2, pull_two, 0)
        loop_point(step, chunk_points, 4, 1, s_.n_hid)

        @pl.when(step >= 2)
        def _():
            stage_free("a", r + 2, stage)

        cols = columns(block_of(r), kh)

        def grads(zz, _):
            rows = pl.ds(pl.multiple_of(zz * (2 * s_.tb), 2 * s_.tb), 2 * s_.tb)
            put_rows(stage, zz, 0, dot(ref["nrm_t"][rows, :], ref["pj"][r]).astype(BF16))
            put_rows(stage, zz, 3 * kh, dot(ref["n2_t"][rows, :], ref["att"][r]).astype(BF16))
            return 0

        lax.fori_loop(0, s_.z, grads, 0)
        stage_out("a", r, stage)
        loop_point(step, chunk_points, 4, 2, s_.n_hid)

        def pull_rows(i, _):
            rows = pl.ds(pl.multiple_of(i * tile, tile), tile)
            grad = ref["pj"][r, rows, :]
            ref["gacc"][rows, :] = ref["gacc"][rows, :] + dot_t(grad, matrix(slot, 0, 3 * kh))
            for k, first in ((4, 0), (5, 2 * kh)):
                part_sum = row_sum(ref["pj"][r, rows, pl.ds(first, kh)].astype(F32))
                ref["sums"][pl.ds(k, 1), cols] = ref["sums"][pl.ds(k, 1), cols] + part_sum
            return 0

        @pl.when(step + 2 < s_.n_hid)
        def _():
            lax.fori_loop(0, s_.tiles, pull_rows, 0)

        loop_point(step, chunk_points, 4, 3, s_.n_hid)
        return 0

    lax.fori_loop(0, s_.n_hid, back_chunk, 0)
    stage_kept("a", 0, 2 + (s_.n_hid - 1) % 2)
    last_two = [(r, (s_.n_hid - 1 - r) % 2) for r in (1, 0)]

    def back_one(i):
        rows = pl.ds(i * tile, tile)
        scaled, inverse = scaled_rows(ref["xs"][rows, :].astype(F32))
        grad = ref["gacc"][rows, :]
        for r, slot in last_two:
            grad = grad + dot_t(ref["pj"][r, rows, :], matrix(slot, 0, 3 * kh))
            for k, first in ((4, 0), (5, 2 * kh)):
                cols = columns(block_of(r), kh)
                part_sum = row_sum(ref["pj"][r, rows, pl.ds(first, kh)].astype(F32))
                ref["sums"][pl.ds(k, 1), cols] = ref["sums"][pl.ds(k, 1), cols] + part_sum
        add_sum(0, grad * scaled)
        add_sum(1, grad)
        total = ref["facc"][rows, :] + norm_pull(grad, gain_row(0), scaled, inverse)
        ref["ct"][rows, :] = total.astype(BF16)

    def row_copy(i, r):
        source = ref["ct"].at[pl.ds(i * tile, tile), columns(block_of(r), kh)]
        return source, ref["grad_rows"].at[pl.ds(pl.multiple_of(h * n + i * tile, tile), tile)]

    def send_rows(i):
        for r in range(1, s_.n_hid):
            send("gt", i * s_.n_hid + r, *row_copy(i, r), peer(r))
        local(41 + i, *row_copy(i, 0)).start()

    for i in range(s_.tiles):
        back_one(i)
    for k, (r, f) in enumerate(tree.m_units):
        for i in range(s_.fs // kh):
            ref["sums"][pl.ds(8 + 2 * f + i, 1), columns(block_of(r), kh)] = ref["hidden_sum"][
                k, :, pl.ds(i * kh, kh)
            ]
    for r in range(1, s_.n_hid):
        send("sum1", r, ref["sums"].at[:, columns(block_of(r), kh)], ref["sum1"].at[r], peer(r))
    for i in range(s_.tiles):
        send_rows(i)

    finals = [("m", 0), ("m", 1), ("a", 0), ("a", 1)]

    def final_loads(k, kind, f):
        slots = ref["z_g" + kind].at[f]
        room = ref["wa"].at[k % 2]
        if kind == "a":
            return [local(30, slots, room.at[:, 0, pl.ds(0, s_.half)])]
        out = [local(30, slots.at[pl.ds(0, s_.z)], room.at[:, 0])]
        if tree.far:
            out.append(local(31, slots.at[pl.ds(s_.z, len(tree.far))], room.at[pl.ds(0, len(tree.far)), 1]))
        return out

    def final_store(k, kind, f):
        if kind == "a":
            source = ref["facc"].at[pl.ds(k * s_.tb, s_.half), pl.ds(0, s_.wide)]
            return local(34 + k, source, ref["grad_a"].at[pl.ds(f * s_.half, s_.half)])
        return local(34 + k, ref["facc"].at[pl.ds(k * s_.tb, s_.tb), pl.ds(0, s_.wide)], ref["grad_m"].at[f])

    def final(k):
        kind, f = finals[k]
        for step in range(1, s_.z):
            arrived("zg" + kind, f * s_.z + step, z_slot(kind, f, step))
        if kind == "m":
            for i, r in enumerate(tree.far):
                arrived("fold", tree.m_pos[r, f], z_slot(kind, f, s_.z + i))
        for load in final_loads(k, kind, f):
            load.start()
        for load in final_loads(k, kind, f):
            load.wait()
        rows = pl.ds(0, s_.half if kind == "a" else s_.tb)
        total = ref["wa"][k % 2, 0, 0, rows].astype(F32)
        for step in range(1, s_.z):
            total = total + ref["wa"][k % 2, step, 0, rows].astype(F32)
        if kind == "m":
            for i in range(len(tree.far)):
                total = total + ref["wa"][k % 2, i, 1].astype(F32)
        ref["facc"][pl.ds(k * s_.tb, rows.size), pl.ds(0, s_.wide)] = total
        final_store(k, kind, f).start()

    def first_finals():
        final(0)
        final(1)

    def first_sums():
        total = ref["sums"][:, columns(h, kh)]
        for r in range(1, s_.n_hid):
            arrived("sum1", r, ref["sum1"].at[r])
            total = total + ref["sum1"][r]
        ref["sum2"][0] = total
        send("sum2", 0, ref["sum2"].at[0], ref["sum2"].at[1], sibling)
        arrived("sum2", 0, ref["sum2"].at[1])
        ref["sum3"][0] = ref["sum2"][0] + ref["sum2"][1]
        for step in range(1, s_.z):
            send("sum3", step, ref["sum3"].at[0], ref["sum3"].at[step], z_peer(step))

    feed_done = False
    for point in range(last_point, plan.end):
        units = [unit for verb, unit in plan.at.get(point, ()) if verb == "fetch"]
        if not feed_done and units and units[0][:2] == ("a", 0):
            first_finals()
            feed_done = True
        act(point)
        if ("a", 0, 1) in units:
            first_sums()
    if not feed_done:
        first_finals()

    final(2)
    final(3)
    total = ref["sum3"][0]
    for step in range(1, s_.z):
        arrived("sum3", step, ref["sum3"].at[step])
        total = total + ref["sum3"][step]
    ref["sum2"][2] = total
    small = local(2, ref["sum2"].at[2], ref["small"])
    small.start()

    small.wait()
    for k, (kind, f) in enumerate(finals):
        final_store(k, kind, f).wait()
    own_lo.wait()
    for holder in plan.holders:
        free_buffer(holder)
    for i in range(s_.tiles):
        local(41 + i, *row_copy(i, 0)).wait()
        for r in range(1, s_.n_hid):
            source, to = row_copy(i, r)
            arrived("gt", i * s_.n_hid + r, to)
            left("gt", i * s_.n_hid + r, source)
    for r in range(1, s_.n_hid):
        arrived("lo", r, out_rows("layer_out", h))
        left("params", r, ref["params"])
        left("ct", r, cot_rows(h))
        left("lo", r, cot_rows(h))
        left("sum1", r, ref["sum1"].at[r])
    left("sum2", 0, ref["sum2"].at[0])
    for step in range(1, s_.z):
        left("sum3", step, ref["sum3"].at[0])
    for r, f in tree.units:
        left("ac", tree.pos[r, f], a_part(r, f, c))
        if r:
            left("ax", tree.pos[r, f], a_part(r, f, c))
    for r, f in tree.m_units:
        left("mc", tree.m_pos[r, f], m_part(r, f, c))
    for r, f in tree.m_near:
        left("mx", tree.m_pos[r, f], m_part(r, f, c))
    for r, f in far_units:
        z_left("zf", tree.m_pos[r, f], m_block(r, f))
    for k in range(max(0, s_.n_hid - 2), s_.n_hid):
        stage_free("a", s_.n_hid - 1 - k, 2 + k % 2)


def scratch(size, tree):
    s_ = size
    units = len(tree.units)
    vmem = {
        "params_all": ((SMALL_ROWS, s_.d), F32),
        "xs": ((s_.n, s_.d), BF16),
        "ct": ((s_.n, s_.d), BF16),
        "nrm": ((s_.n, s_.d), BF16),
        "nrm_t": ((s_.d, s_.n), BF16),
        "n2": ((s_.n, s_.d), BF16),
        "n2_t": ((s_.d, s_.n), BF16),
        "ct_t": ((s_.z, 2, s_.tb, s_.n), BF16),
        "pj": ((s_.n_hid, s_.n, 3 * s_.kh), BF16),
        "probs": ((s_.n_hid, s_.pairs, s_.n, 2 * BLOCK), BF16),
        "att": ((s_.n_hid, s_.n, s_.kh), BF16),
        "scaled_two": ((s_.n, s_.d), BF16),
        "inverse_two": ((s_.n, 1), F32),
        "facc": ((s_.n, s_.d), F32),
        "gacc": ((s_.n, s_.d), F32),
        "wa": ((s_.n_hid, s_.z, 2, s_.tb, s_.wide), BF16),
        "out_in": ((s_.kh, s_.tb), BF16),
        "down_in": ((2 * s_.fs, s_.tb), BF16),
        "hid": ((s_.n, s_.fs), BF16),
        "gb": ((s_.n, s_.fs), BF16),
        "acc": ((SUM_BUFFERS + 1, s_.z, s_.tb, s_.wide), BF16),
        "tmp": ((s_.z, s_.tb, s_.wide), BF16),
        "hidden_bias": ((units, 1, s_.fs), F32),
        "hidden_sum": ((units, 1, s_.fs), F32),
        "sums": ((SMALL_ROWS, s_.d), F32),
        "sum1": ((s_.n_hid, SMALL_ROWS, s_.kh), F32),
        "sum2": ((3, SMALL_ROWS, s_.kh), F32),
        "sum3": ((s_.z, SMALL_ROWS, s_.kh), F32),
    }
    pairs = {
        "params": s_.n_hid,
        "za": s_.z,
        "zm": 2 * s_.z,
        "xs": s_.tiles * s_.n_hid,
        "ax": units,
        "ac": units,
        "mx": units,
        "mc": units,
        "ct": s_.n_hid,
        "sa": s_.n_hid,
        "sm": units,
        "ga": units,
        "gm": units,
        "fs": units,
        "zf": units * s_.z,
        "zfar": units * s_.z,
        "fold": units,
        "zga": 2 * s_.z,
        "zgm": 2 * s_.z,
        "lo": s_.n_hid,
        "gt": s_.tiles * s_.n_hid,
        "sum1": s_.n_hid,
        "sum2": 1,
        "sum3": s_.z,
    }
    out = {name: pltpu.VMEM(shape, kind) for name, (shape, kind) in vmem.items()}
    for name, count in pairs.items():
        out[name + "_s"] = pltpu.SemaphoreType.DMA((count,))
        out[name + "_r"] = pltpu.SemaphoreType.DMA((count,))
    out["local"] = pltpu.SemaphoreType.DMA((48,))
    out["wload"] = pltpu.SemaphoreType.DMA((s_.n_hid,))
    out["keep"] = pltpu.SemaphoreType.DMA((2,))
    return out


def finish_kernel(
    kh, fs, grad_ref, a_ref, m_ref, tokens_ref, middle_ref, coarse_ref, output_ref, up_ref, down_ref, attend_ref
):
    grad = grad_ref[...]
    rows = grad.shape[0]
    part = min(512, rows)
    by_4, by_16 = group_matrix(part, 4), group_matrix(part, 16)
    tokens_ref[...] = grad.astype(F32)
    for i in range(rows // part):
        piece = grad[i * part : i * part + part]
        middle_ref[pl.ds(i * part // 4, part // 4), :] = dot(by_4, piece)
        coarse_ref[pl.ds(i * part // 16, part // 16), :] = dot(by_16, piece)

    @pl.when(pl.program_id(0) == 0)
    def _():
        output_ref[...] = a_ref[:, pl.ds(3 * kh, kh)].T
        for k in range(3):
            attend_ref[k] = a_ref[:, pl.ds(k * kh, kh)]
        for f in (0, 1):
            up_ref[:, pl.ds(f * fs, fs)] = m_ref[f, :, pl.ds(0, fs)]
            down_ref[pl.ds(f * fs, fs), :] = m_ref[f, :, pl.ds(fs, fs)].T


def finish(size, grad, grad_a, grad_m):
    positions, features = grad.shape
    rows = min(1024, positions)
    tb, fs = size.tb, size.fs
    whole = [((features, tb), F32), ((tb, 2 * fs), F32), ((2 * fs, tb), F32), ((3, tb, features), F32)]
    return pl.pallas_call(
        functools.partial(finish_kernel, features, fs),
        grid=(positions // rows,),
        in_specs=[
            pl.BlockSpec((rows, features), lambda i: (i, 0)),
            pl.BlockSpec(grad_a.shape, lambda i: (0, 0)),
            pl.BlockSpec(grad_m.shape, lambda i: (0, 0, 0)),
        ],
        out_specs=[pl.BlockSpec((rows // t, features), lambda i: (i, 0)) for t in (1, 4, 16)]
        + [pl.BlockSpec(shape, lambda i, n=len(shape): (0,) * n) for shape, _ in whole],
        out_shape=[jax.ShapeDtypeStruct((positions // t, features), F32) for t in (1, 4, 16)]
        + [jax.ShapeDtypeStruct(*x) for x in whole],
        compiler_params=pltpu.CompilerParams(vmem_limit_bytes=60 * 2**20),
        name="token_gradients",
    )(grad, grad_a, grad_m)


def shards(
    tokens,
    middle_cond,
    coarse_cond,
    first_gain,
    first_shift,
    attend_weight,
    query_bias,
    value_bias,
    output_weight,
    mixer_bias,
    second_gain,
    second_shift,
    up_weight,
    hidden_bias,
    down_weight,
    down_bias,
    cotangent,
):
    positions, features = tokens.shape
    n_hid, n_tok = lax.axis_size("hid"), lax.axis_size("tok")
    d = features * n_hid
    ff = up_weight.shape[1] * n_hid
    size = Sizes(positions, features, d, ff, n_tok, n_hid)
    tree = Tree(n_hid)
    tb, fs, wide, z = size.tb, size.fs, size.wide, size.z
    vectors = (first_gain, first_shift, second_gain, second_shift, query_bias, value_bias, mixer_bias, down_bias)
    params = jnp.concatenate(
        [
            jnp.stack(vectors),
            hidden_bias.reshape(ff // d, features),
            jnp.zeros((SMALL_ROWS - 8 - ff // d, features), F32),
        ]
    )
    units = len(tree.units)
    outputs = {
        "layer_out": ((positions, features), BF16),
        "grad_rows": ((positions, features), BF16),
        "grad_a": ((tb, wide), F32),
        "grad_m": ((2, tb, wide), F32),
        "small": ((SMALL_ROWS, features), F32),
        "all_a": ((n_hid, z, 2, tb, wide), BF16),
        "all_m": ((units, z, 2, tb, wide), BF16),
        "own_ga": ((n_hid, z, tb, wide), BF16),
        "sib_ga": ((n_hid, z, tb, wide), BF16),
        "got_ga": ((units, z, size.half, wide), BF16),
        "own_gm": ((units, z, tb, wide), BF16),
        "sib_gm": ((units, z, tb, wide), BF16),
        "got_gm": ((units, z, tb, wide), BF16),
        "z_ga": ((2, z, size.half, wide), BF16),
        "z_gm": ((2, z + len(tree.far), tb, wide), BF16),
        "z_far": ((units, z, tb, wide), BF16),
    }
    hbm = pl.BlockSpec(memory_space=pltpu.HBM)
    results = pl.pallas_call(
        functools.partial(layer_kernel, size, tree),
        out_shape=[jax.ShapeDtypeStruct(*outputs[name]) for name in OUTPUTS],
        in_specs=[hbm] * len(INPUTS),
        out_specs=[hbm] * len(OUTPUTS),
        scratch_shapes=list(scratch(size, tree).values()),
        compiler_params=pltpu.CompilerParams(
            collective_id=0, has_side_effects=True, vmem_limit_bytes=63 * 2**20
        ),
        cost_estimate=pl.CostEstimate(flops=80 * 10**9, bytes_accessed=2 * 10**8, transcendentals=10**7),
        name="layer",
    )(
        tokens,
        middle_cond,
        coarse_cond,
        cotangent,
        attend_weight.transpose(1, 0, 2),
        output_weight,
        up_weight,
        down_weight,
        params,
    )
    layer_out, grad_rows, grad_a, grad_m, small = results[:5]
    grad_tokens, grad_middle, grad_coarse, grad_output, grad_up, grad_down, grad_attend = finish(
        size, grad_rows, grad_a, grad_m
    )
    tok = lax.axis_index("tok")
    share = features // n_tok
    mine = lax.dynamic_slice_in_dim(small[:8], tok * share, share, 1)
    hidden_share = fs * 2 // n_tok
    grad_hidden_bias = lax.dynamic_slice_in_dim(
        small[8 : 8 + ff // d].reshape(-1), tok * hidden_share, hidden_share, 0
    )
    return (
        layer_out,
        grad_tokens,
        grad_middle,
        grad_coarse,
        mine[0],
        mine[1],
        grad_attend.transpose(1, 0, 2),
        mine[4],
        mine[5],
        grad_output,
        mine[6],
        mine[2],
        mine[3],
        grad_up,
        grad_hidden_bias,
        grad_down,
        mine[7],
    )


def solution(mesh):
    return jax.shard_map(
        shards,
        mesh=mesh,
        in_specs=(
            P("tok", "hid"),
            P("tok", "hid"),
            P("tok", "hid"),
            P("hid"),
            P("hid"),
            P("tok", None, "hid"),
            P("hid"),
            P("hid"),
            P("hid", "tok"),
            P("hid"),
            P("hid"),
            P("hid"),
            P("tok", "hid"),
            P("hid"),
            P("hid", "tok"),
            P("hid"),
            P("tok", "hid"),
        ),
        out_specs=(
            P("tok", "hid"),
            P("tok", "hid"),
            P("tok", "hid"),
            P("tok", "hid"),
            P(("hid", "tok")),
            P(("hid", "tok")),
            P("tok", None, "hid"),
            P(("hid", "tok")),
            P(("hid", "tok")),
            P("hid", "tok"),
            P(("hid", "tok")),
            P(("hid", "tok")),
            P(("hid", "tok")),
            P("tok", "hid"),
            P(("hid", "tok")),
            P("hid", "tok"),
            P(("hid", "tok")),
        ),
        check_vma=False,
    )
```

```python
import functools

import jax
import jax.numpy as jnp
from jax import lax
from jax.experimental import pallas as pl
from jax.experimental.pallas import tpu as pltpu
from jax.sharding import PartitionSpec as P

HEAD = 64
BLOCK = 128
PAIR = 2 * HEAD
EPSILON = 1e-05
MESH = pl.DeviceIdType.MESH
BF16 = jnp.bfloat16
F32 = jnp.float32
SMALL_ROWS = 16
WHOLE_BUFFERS = 3
HALF_BUFFERS = 4


class Tree:
    def __init__(self, n_hid):
        self.n = n_hid
        self.bits = n_hid.bit_length() - 1
        units = [(r, f) for r in range(n_hid) for f in (0, 1)]
        self.units = sorted(units, key=lambda u: (u[0].bit_count(), len(self.children(*u)), u))
        self.pos = {u: k for k, u in enumerate(self.units)}
        self.near = [1 << b for b in range(self.bits)]
        self.far = [r for r in range(n_hid) if r.bit_count() > 1]
        first = [(1 << b, b % 2) for b in range(self.bits)]
        second = [(1 << b, 1 - b % 2) for b in range(self.bits)]
        self.m_near = first + second
        rest = [(r, f) for r in self.far for f in (0, 1)]
        self.m_units = [(0, 0), (0, 1)] + first + rest[:1] + second + rest[1:]
        self.m_pos = {u: k for k, u in enumerate(self.m_units)}

    def children(self, r, f):
        held = [b for b in range(self.bits) if r >> b & 1]
        free = [b for b in range(self.bits) if not r >> b & 1]
        if held:
            free = [b for b in free if (b < held[0] if f == 0 else b > held[-1])]
        return [(r | 1 << b, b) for b in free]

    def parent(self, r, f):
        held = [b for b in range(self.bits) if r >> b & 1]
        return held[0] if f == 0 else held[-1]


class Schedule:
    def __init__(self, done, kids, lag, last_point):
        self.at = {}
        self.turn = {}
        self.before = {}
        self.first = set()
        sent = {}
        seen = set()
        holders = {True: [None] * HALF_BUFFERS, False: [None] * WHOLE_BUFFERS}
        turns = {True: 0, False: 0}
        waiting = sorted(done, key=lambda u: (done[u], len(kids[u])))
        held = None
        point = 0
        while waiting or held is not None:
            actions = []
            if held is not None:
                actions.append(("finish", held))
                sent[held] = point
                held = None
            for unit in waiting:
                if point <= done[unit] or any(k not in sent for k in kids[unit]):
                    continue
                if point < last_point and any(point < sent[k] + lag[unit[0]] for k in kids[unit]):
                    continue
                actions.append(("fetch", unit))
                held = unit
                pool = unit[0] == "a"
                self.turn[unit] = k = turns[pool] % len(holders[pool])
                turns[pool] += 1
                self.before[unit] = holders[pool][k]
                holders[pool][k] = unit
                if unit[:2] not in seen:
                    self.first.add(unit)
                seen.add(unit[:2])
                waiting.remove(unit)
                break
            if actions:
                self.at[point] = actions
            point += 1
        self.end = point
        self.holders = holders[True] + holders[False]


def dot(a, b):
    return jnp.dot(a, b, preferred_element_type=F32)


def dot_t(a, b):
    return lax.dot_general(a, b, (((1,), (1,)), ((), ())), preferred_element_type=F32)


def dot_l(a, b):
    return lax.dot_general(a, b, (((0,), (0,)), ((), ())), preferred_element_type=F32)


def repeat_matrix(rows, times):
    row = lax.broadcasted_iota(jnp.int32, (rows, rows // times), 0)
    column = lax.broadcasted_iota(jnp.int32, (rows, rows // times), 1) * times
    return ((row >= column) & (row < column + times)).astype(BF16)


def group_matrix(rows, times):
    row = lax.broadcasted_iota(jnp.int32, (rows // times, rows), 0) * times
    column = lax.broadcasted_iota(jnp.int32, (rows // times, rows), 1)
    return ((column >= row) & (column < row + times)).astype(BF16)


def scaled_rows(values):
    width = values.shape[1]
    average = jnp.sum(values, axis=1, keepdims=True) / width
    square = jnp.sum(values * values, axis=1, keepdims=True) / width
    inverse = lax.rsqrt(square - average * average + EPSILON)
    return (values - average) * inverse, inverse


def norm_pull(grad, gain, scaled, inverse):
    width = grad.shape[1]
    weighted = grad * gain
    mean = jnp.sum(weighted, axis=1, keepdims=True) / width
    along = jnp.sum(weighted * scaled, axis=1, keepdims=True) / width
    return inverse * (weighted - mean - scaled * along)


def row_sum(values):
    return jnp.sum(values, axis=0, keepdims=True)


def two_heads(values):
    low = lax.broadcasted_iota(jnp.int32, values.shape, 1) < HEAD
    zero = jnp.zeros_like(values)
    return jnp.concatenate([jnp.where(low, values, zero), jnp.where(low, zero, values)], axis=0)


def pick_heads(both):
    low = lax.broadcasted_iota(jnp.int32, (BLOCK, PAIR), 1) < HEAD
    return jnp.where(low, both[:BLOCK], both[BLOCK:])


INPUTS = ("tokens", "middle", "coarse", "cotangent", "attend_w", "output_w", "up_w", "down_w", "params")
OUTPUTS = (
    "layer_out",
    "grad_rows",
    "grad_a",
    "grad_m",
    "small",
    "all_a",
    "all_m",
    "own_ga",
    "sib_ga",
    "got_ga",
    "own_gm",
    "sib_gm",
    "got_gm",
    "z_ga",
    "z_gm",
    "z_far",
)


class Sizes:
    def __init__(self, positions, features, d, ff, n_tok, n_hid):
        self.d, self.n_hid, self.n_tok = d, n_hid, n_tok
        self.z = n_tok // 2
        self.n = positions // n_hid
        self.kh = features
        self.fs = ff // n_hid // 2
        self.tb = d // n_tok
        self.half = self.tb // 2
        self.wide = 4 * features
        self.pairs = features // PAIR
        self.tile = min(256, self.n)
        self.tiles = self.n // self.tile
        self.blocks = self.n // BLOCK
        self.positions = positions


def layer_kernel(size, tree, *refs):
    names = list(INPUTS) + list(OUTPUTS) + list(scratch(size, tree))
    ref = dict(zip(names, refs, strict=True))
    s_ = size
    n_units = len(tree.units)
    tok, h = lax.axis_index("tok"), lax.axis_index("hid")
    z, c = tok // 2, lax.rem(tok, 2)

    def block_of(r):
        total = 0
        for b in range(tree.bits):
            total = total + lax.rem(h // (1 << b) + r // (1 << b), 2) * (1 << b)
        return total

    def peer(r):
        return (tok, block_of(r))

    sibling = (tok + 1 - 2 * c, h)

    def z_peer(step):
        return (lax.rem(z + step, s_.z) * 2 + c, h)

    def columns(j, width):
        return pl.ds(pl.multiple_of(j * width, width), width)

    def remote(name, index, src, dst, device):
        return pltpu.make_async_remote_copy(
            src_ref=src,
            dst_ref=dst,
            send_sem=ref[name + "_s"].at[index],
            recv_sem=ref[name + "_r"].at[index],
            device_id=device,
            device_id_type=MESH,
        )

    def send(name, index, src, dst, device):
        remote(name, index, src, dst, device).start()

    def arrived(name, index, dst):
        remote(name, index, dst, dst, sibling).wait_recv()

    def left(name, index, src):
        remote(name, index, src, src, sibling).wait_send()

    def local(index, src, dst):
        return pltpu.make_async_copy(src, dst, ref["local"].at[index])

    barrier = pltpu.get_barrier_semaphore()
    everyone = [peer(r) for r in range(1, s_.n_hid)] + [sibling]
    everyone += [z_peer(k) for k in range(1, s_.z)]
    for device in everyone:
        pl.semaphore_signal(barrier, inc=1, device_id=device, device_id_type=MESH)
    pl.semaphore_wait(barrier, len(everyone))

    def z_send(name, index, src, dst):
        for step in range(1, s_.z):
            send(name, index * s_.z + step, src, dst, z_peer(step))

    def z_arrived(name, index, dst):
        for step in range(1, s_.z):
            arrived(name, index * s_.z + step, dst)

    def z_left(name, index, src):
        for step in range(1, s_.z):
            left(name, index * s_.z + step, src)

    def a_part(r, f, core):
        return ref["all_a"].at[r, :, core, pl.ds(f * s_.half, s_.half)]

    def m_part(r, f, core):
        return ref["all_m"].at[tree.m_pos[r, f], :, core]

    part = {"a": a_part, "m": m_part}

    for r in range(1, s_.n_hid):
        here = ref["params_all"].at[:, columns(h, s_.kh)]
        send("params", r, ref["params"], here, peer(r))
    own_params = local(0, ref["params"], ref["params_all"].at[:, columns(h, s_.kh)])
    own_params.start()
    kh, n, tile, fs = s_.kh, s_.n, s_.tile, s_.fs
    own_block = [ref["acc"].at[k, 0] for k in range(3)]
    own_loads = [local(1 + k, ref["attend_w"].at[k], own_block[0].at[:, pl.ds(k * kh, kh)]) for k in range(3)]
    own_loads.append(local(40, ref["output_w"], ref["out_in"]))
    for f in (0, 1):
        own_loads.append(local(41 + f, ref["up_w"].at[:, pl.ds(f * fs, fs)], own_block[1 + f].at[:, pl.ds(0, fs)]))
    own_loads.append(local(43, ref["down_w"], ref["down_in"]))
    for copy in own_loads:
        copy.start()
    def m_block(r, f):
        return ref["all_m"].at[tree.m_pos[r, f], z, c]

    far_units = [(r, f) for r in tree.far for f in (0, 1)]

    rows_m, rows_c = n // 4, n // 16
    loads = {}
    order = list(range(1, s_.n_hid)) + [0]
    for r in order:
        j = block_of(r)
        sources = (
            (ref["tokens"].at[columns(j, n)], ref["pj"].at[r, :, pl.ds(0, kh)]),
            (ref["middle"].at[columns(j, rows_m)], ref["pj"].at[r, pl.ds(0, rows_m), pl.ds(2 * kh, kh)]),
            (ref["coarse"].at[columns(j, rows_c)], ref["pj"].at[r, pl.ds(rows_m, rows_c), pl.ds(2 * kh, kh)]),
        )
        loads[r] = [local(4 + 3 * r + k, *pair) for k, pair in enumerate(sources)]
        for copy in loads[r]:
            copy.start()
    for copy in own_loads:
        copy.wait()
    ref["acc"][0, 0, :, pl.ds(3 * kh, kh)] = ref["out_in"][...].T
    z_send("za", 0, own_block[0], ref["all_a"].at[0, z, c])
    for f in (0, 1):
        ref["acc"][1 + f, 0, :, pl.ds(fs, fs)] = ref["down_in"][pl.ds(f * fs, fs), :].T
    for r, f in far_units:
        send("fs", tree.m_pos[r, f], own_block[1 + f], m_block(r, f), peer(r))
    own_places = [ref["all_a"].at[0, z, c], m_block(0, 0), m_block(0, 1)]
    own_out = [local(1 + k, own_block[k], place) for k, place in enumerate(own_places)]
    for store in own_out:
        store.start()
    repeat_4, repeat_16 = repeat_matrix(tile, 4), repeat_matrix(tile, 16)

    def xs_rows(i, j):
        return ref["xs"].at[pl.ds(i * tile, tile), columns(j, kh)]

    own_xs = []
    for i in range(s_.tiles):
        for r in order:
            if i == 0:
                for copy in loads[r]:
                    copy.wait()
            rows = pl.ds(i * tile, tile)
            middle = ref["pj"][r, pl.ds(i * (tile // 4), tile // 4), pl.ds(2 * kh, kh)]
            coarse = ref["pj"][r, pl.ds(rows_m + i * (tile // 16), tile // 16), pl.ds(2 * kh, kh)]
            total = ref["pj"][r, rows, pl.ds(0, kh)].astype(F32)
            total = total + dot(repeat_4, middle) + dot(repeat_16, coarse)
            ref["pj"][r, rows, pl.ds(kh, kh)] = total.astype(BF16)
            source = ref["pj"].at[r, rows, pl.ds(kh, kh)]
            if r:
                send("xs", i * s_.n_hid + r, source, xs_rows(i, h), peer(r))
            else:
                copy = local(4 + 3 * s_.n_hid + i, source, xs_rows(i, h))
                copy.start()
                own_xs.append(copy)


    def to_sibling(kind, r, f):
        k = tree.pos[r, f] if kind == "a" else tree.m_pos[r, f]
        send(kind + "c", k, part[kind](r, f, c), part[kind](r, f, c), sibling)

    def take_a(r, f):
        arrived("ax", tree.pos[r, f], a_part(r, f, c))
        for child, b in tree.children(r, f):
            send("ax", tree.pos[child, f], a_part(r, f, c), a_part(child, f, c), peer(1 << b))
        to_sibling("a", r, f)

    def take_m(r, f):
        if r in tree.far:
            z_arrived("zf", tree.m_pos[r, f], m_block(r, f))
        else:
            arrived("mx", tree.m_pos[r, f], m_part(r, f, c))
        to_sibling("m", r, f)

    def take_sibling(kind, r, f):
        k = tree.pos[r, f] if kind == "a" else tree.m_pos[r, f]
        arrived(kind + "c", k, part[kind](r, f, 1 - c))

    a_near = sorted([u for u in tree.units if u[0] in tree.near], key=lambda u: -len(tree.children(*u)))
    for store in own_out:
        store.wait()
    z_arrived("za", 0, ref["all_a"].at[0, z, c])
    for f in (0, 1):
        z_send("zm", f, own_block[1 + f], m_block(0, f))
    for r, f in far_units:
        arrived("fs", tree.m_pos[r, f], m_block(r, f))
        z_send("zf", tree.m_pos[r, f], m_block(r, f), m_block(r, f))
    for r, f in a_near:
        send("ax", tree.pos[r, f], a_part(0, f, c), a_part(r, f, c), peer(r))
    for f in (0, 1):
        to_sibling("a", 0, f)

    own_params.wait()
    for r in range(1, s_.n_hid):
        arrived("params", r, ref["params_all"].at[:, columns(h, kh)])

    def gain_row(k):
        return ref["params_all"][pl.ds(k, 1), :]

    for k, (r, f) in enumerate(tree.m_units):
        parts = [
            ref["params_all"][pl.ds(8 + 2 * f + i, 1), columns(block_of(r), kh)] for i in range(s_.fs // kh)
        ]
        ref["hidden_bias"][k] = jnp.concatenate(parts, axis=1)
        ref["hidden_sum"][k] = jnp.zeros((1, s_.fs), F32)
    ref["sums"][...] = jnp.zeros_like(ref["sums"])

    def add_sum(k, values):
        ref["sums"][pl.ds(k, 1), :] = ref["sums"][pl.ds(k, 1), :] + row_sum(values)

    for i in range(s_.tiles):
        own_xs[i].wait()
        for r in range(1, s_.n_hid):
            arrived("xs", i * s_.n_hid + r, xs_rows(i, h))
        rows = pl.ds(i * tile, tile)
        scaled, _ = scaled_rows(ref["xs"][rows, :].astype(F32))
        normed = (scaled * gain_row(0) + gain_row(1)).astype(BF16)
        ref["nrm"][rows, :] = normed
        ref["nrm_t"][:, rows] = normed.T

    for i in range(s_.tiles):
        for r in range(1, s_.n_hid):
            left("xs", i * s_.n_hid + r, xs_rows(i, h))

    def weight_load(slot, source):
        return pltpu.make_async_copy(source, ref["wa"].at[slot], ref["wload"].at[slot])

    def matrix(slot, first, width):
        return ref["wa"][slot, :, :, :, pl.ds(first, width)].reshape(s_.d, width)

    def put_rows(slot, zz, first, values):
        width = values.shape[1]
        ref["wa"][slot, pl.ds(zz * 2, 2), :, :, pl.ds(first, width)] = values.reshape(2, 2, s_.tb, width)

    def cot_rows(j):
        return ref["ct"].at[:, columns(j, kh)]

    own_ct = local(0, ref["cotangent"].at[columns(h, n)], cot_rows(h))

    def before_chunk(r):
        if r == 0:
            pass
        elif r.bit_count() == 1:
            if r == 1:
                for u, f in a_near:
                    take_a(u, f)
                own_ct.start()
                for k in range(1, s_.n_hid):
                    send("ct", k, ref["cotangent"].at[columns(block_of(k), n)], cot_rows(h), peer(k))
        else:
            for f in (0, 1):
                take_a(r, f)
        for f in (0, 1):
            take_sibling("a", r, f)
        load = weight_load(r, ref["all_a"].at[r])
        load.start()
        load.wait()

    causal_row = lax.broadcasted_iota(jnp.int32, (BLOCK, 2 * BLOCK), 0)
    causal_col = lax.rem(lax.broadcasted_iota(jnp.int32, (BLOCK, 2 * BLOCK), 1), BLOCK)
    allowed = causal_row >= causal_col

    def halves(values, f):
        return [f(values[:, :BLOCK]), f(values[:, BLOCK:])]

    def spread(pair):
        return jnp.concatenate([jnp.broadcast_to(v, (BLOCK, BLOCK)) for v in pair], axis=1)

    def row_max(v):
        return jnp.max(v, axis=1, keepdims=True)

    def row_add(v):
        return jnp.sum(v, axis=1, keepdims=True)

    def attend_chunk(r):
        for k in range(s_.n_hid):
            pl.when(r == k)(functools.partial(before_chunk, k))
        cols = columns(block_of(r), kh)
        bias = jnp.concatenate(
            [ref["params_all"][4:5, cols], jnp.zeros((1, kh), F32), ref["params_all"][5:6, cols]], axis=1
        )

        def project(i, _):
            rows = pl.ds(pl.multiple_of(i * tile, tile), tile)
            values = dot(ref["nrm"][rows, :], matrix(r, 0, 3 * kh)) + bias
            ref["pj"][r, rows, :] = values.astype(BF16)
            return 0

        lax.fori_loop(0, s_.tiles, project, 0)

        def attend(i, _):
            rows = pl.ds(pl.multiple_of(i * BLOCK, BLOCK), BLOCK)
            for p in range(s_.pairs):
                query, key, value = (ref["pj"][r, rows, pl.ds(k * kh + p * PAIR, PAIR)] for k in range(3))
                logits = jnp.where(allowed, dot_t(query, two_heads(key)) * HEAD ** (-0.5), -1e30)
                powers = jnp.exp(logits - spread(halves(logits, row_max)))
                shares = [1.0 / v for v in halves(powers, row_add)]
                attention = (powers * spread(shares)).astype(BF16)
                ref["probs"][r, p, rows, :] = attention
                out = dot(attention, two_heads(value))
                ref["att"][r, rows, pl.ds(p * PAIR, PAIR)] = out.astype(BF16)
            return 0

        def attend_two(i, _):
            attend(2 * i, 0)
            return attend(2 * i + 1, 0)

        lax.fori_loop(0, s_.blocks // 2, attend_two, 0)

    lax.fori_loop(0, s_.n_hid, lambda r, _: (attend_chunk(r), 0)[1], 0)

    for f in (0, 1):
        z_arrived("zm", f, m_block(0, f))
    for f in (0, 1):
        to_sibling("m", 0, f)
    z_left("za", 0, own_block[0])
    for f in (0, 1):
        z_left("zm", f, own_block[1 + f])
    for r, f in far_units:
        left("fs", tree.m_pos[r, f], own_block[1 + f])

    def mix(i, _):
        rows = pl.ds(pl.multiple_of(i * tile, tile), tile)
        total = ref["xs"][rows, :].astype(F32) + gain_row(6)
        for r in range(s_.n_hid):
            total = total + dot_t(ref["att"][r, rows, :], matrix(r, 3 * kh, kh))
        ref["facc"][rows, :] = total + gain_row(7)
        scaled, inverse = scaled_rows(total)
        ref["scaled_two"][rows, :] = scaled.astype(BF16)
        ref["inverse_two"][rows, :] = inverse
        normed = (scaled * gain_row(2) + gain_row(3)).astype(BF16)
        ref["n2"][rows, :] = normed
        return 0

    lax.fori_loop(0, s_.tiles, mix, 0)

    own_ct.wait()
    for k in range(1, s_.n_hid):
        arrived("ct", k, cot_rows(h))
    for r, f in tree.m_near:
        send("mx", tree.m_pos[r, f], m_part(0, f, c), m_part(r, f, c), peer(r))
    for i in range(s_.tiles):
        rows = pl.ds(i * tile, tile)
        ref["n2_t"][:, rows] = ref["n2"][rows, :].T
        upstream = ref["ct"][rows, :]
        ref["ct_t"][:, :, :, rows] = upstream.T.reshape(s_.z, 2, s_.tb, tile)
        add_sum(7, upstream.astype(F32))
        ref["gacc"][rows, :] = jnp.zeros((tile, s_.d), F32)

    mlp_points = 2 * n_units
    chunk_points = mlp_points + 2
    last_point = chunk_points + 4 * s_.n_hid
    done, kids = {}, {}
    for k, (r, f) in enumerate(tree.m_units):
        done["m", r, f] = 2 * k + 1
        kids["m", r, f] = [("m", u, f) for u in tree.near] if r == 0 else []
        if r == 0:
            done["m", r, f] = mlp_points - 1
    for r, f in far_units:
        done["fold", r, f] = 0
        kids["fold", r, f] = [("m", r, f)]
    for r in range(s_.n_hid):
        for f in (0, 1):
            done["a", r, f] = chunk_points + 4 * (s_.n_hid - 1 - r) + 3
            kids["a", r, f] = [("a", child, f) for child, _ in tree.children(r, f)]
    plan = Schedule(done, kids, {"m": 11, "a": 4, "fold": 9}, last_point)

    def place(kind, r, f):
        return tree.pos[r, f] if kind == "a" else tree.m_pos[r, f]

    def own_grad(kind, r, f):
        if kind == "a":
            return ref["own_ga"].at[r, :, pl.ds(f * s_.half, s_.half)]
        return ref["own_gm"].at[tree.m_pos[r, f]]

    def sib_grad(kind, r, f):
        if kind == "a":
            return ref["sib_ga"].at[r, :, pl.ds(f * s_.half, s_.half)]
        return ref["sib_gm"].at[tree.m_pos[r, f]]

    def got_grad(kind, r, f):
        return ref["got_g" + kind].at[place(kind, r, f)]

    def part_of(whole, kind):
        return whole.at[:, pl.ds(0, s_.half if kind == "a" else s_.tb)]

    def spare(first, rows):
        return ref["ct_t"].at[:, first, rows, pl.ds(0, s_.wide)]

    def sum_buffer(unit):
        k = plan.turn[unit]
        if unit[0] != "a":
            return ref["acc"].at[k]
        rows = pl.ds(k % 2 * s_.half, s_.half)
        return ref["acc"].at[WHOLE_BUFFERS, :, rows] if k < 2 else spare(1, rows)

    def z_slot(kind, f, step):
        return ref["z_g" + kind].at[f, step]

    def scattered(kind, r, f):
        if r == 0:
            return "zg" + kind, f * s_.z, ref["z_g" + kind].at[f]
        return "zfar", tree.m_pos[r, f] * s_.z, ref["z_far"].at[tree.m_pos[r, f]]

    def scatters(kind, r):
        return r == 0 or (kind == "m" and r in tree.far)

    def free_buffer(holder):
        if holder is None:
            return
        kind, r, f = holder
        source = sum_buffer(holder)
        if kind == "fold":
            left("fold", tree.m_pos[r, f], source.at[0])
        elif scatters(kind, r):
            name, first, _ = scattered(kind, r, f)
            for step in range(1, s_.z):
                left(name, first + step, source.at[0])
        else:
            left("g" + kind, place(kind, r, f), source)

    def fetches(unit):
        kind, r, f = unit
        if kind == "fold":
            return [(30, ref["z_far"].at[tree.m_pos[r, f]], sum_buffer(unit))]
        out = [(30, own_grad(*unit), sum_buffer(unit))]
        out.append((31, sib_grad(*unit), part_of(ref["tmp"], kind)))
        if kids[unit]:
            out.append((32, got_grad(*kids[unit][0]), part_of(spare(0, pl.ds(0, s_.tb)), kind)))
        return out

    def fetch(unit):
        kind, r, f = unit
        free_buffer(plan.before[unit])
        if kind == "fold":
            for step in range(1, s_.z):
                name, first, slots = scattered("m", r, f)
                arrived(name, first + step, slots.at[step])
        elif kind == "m" or unit in plan.first:
            slot = tree.m_pos[r, f] if kind == "m" else r
            arrived("s" + kind, slot, ref["sib_g" + kind].at[slot])
        if kind != "fold":
            for kid in kids[unit][:1]:
                arrived("g" + kind, place(*kid), got_grad(*kid))
        for item in fetches(unit):
            local(*item).start()

    def finish(unit):
        kind, r, f = unit
        for item in fetches(unit):
            local(*item).wait()
        acc, tmp, more = sum_buffer(unit), part_of(ref["tmp"], kind), part_of(spare(0, pl.ds(0, s_.tb)), kind)
        if kind == "fold":
            total = acc[0].astype(F32)
            for zz in range(1, s_.z):
                total = total + acc[zz].astype(F32)
            acc[0] = total.astype(BF16)
            slot = ref["z_gm"].at[f, s_.z + tree.far.index(r)]
            send("fold", tree.m_pos[r, f], acc.at[0], slot, peer(r))
            return
        for zz in range(s_.z):
            total = acc[zz].astype(F32) + tmp[zz].astype(F32)
            if kids[unit]:
                total = total + more[zz].astype(F32)
            acc[zz] = total.astype(BF16)
        for kid in kids[unit][1:]:
            source = got_grad(*kid)
            arrived("g" + kind, place(*kid), source)
            copy = local(36, source, more)
            copy.start()
            copy.wait()
            for zz in range(s_.z):
                acc[zz] = (acc[zz].astype(F32) + more[zz].astype(F32)).astype(BF16)
        if scatters(kind, r):
            name, first, slots = scattered(kind, r, f)
            keep = local(40, acc.at[z], slots.at[0])
            keep.start()
            for step in range(1, s_.z):
                to = lax.rem(z + step, s_.z)
                send(name, first + step, acc.at[to], slots.at[step], z_peer(step))
            keep.wait()
        else:
            to = r if kind == "m" else 1 << tree.parent(r, f)
            send("g" + kind, place(kind, r, f), acc, got_grad(kind, r, f), peer(to))

    def act(point):
        for verb, unit in plan.at.get(point, ()):
            (fetch if verb == "fetch" else finish)(unit)

    def loop_point(step, first, stride, offset, count):
        for k in range(count):
            if first + stride * k + offset in plan.at:
                pl.when(step == k)(functools.partial(act, first + stride * k + offset))

    def stage_copies(kind, index, slot):
        own = ref["own_g" + kind].at[index]
        theirs = ref["sib_g" + kind].at[index]
        keep = pltpu.make_async_copy(ref["wa"].at[slot, :, c], own, ref["keep"].at[slot - 2])
        give = pltpu.make_async_remote_copy(
            src_ref=ref["wa"].at[slot, :, 1 - c],
            dst_ref=theirs,
            send_sem=ref["s" + kind + "_s"].at[index],
            recv_sem=ref["s" + kind + "_r"].at[index],
            device_id=sibling,
            device_id_type=MESH,
        )
        return keep, give

    def stage_out(kind, index, slot):
        for copy in stage_copies(kind, index, slot):
            copy.start()

    def stage_kept(kind, index, slot):
        stage_copies(kind, index, slot)[0].wait()

    def stage_free(kind, index, slot):
        stage_copies(kind, index, slot)[1].wait_send()

    for k in (0, 1):
        take_sibling("m", *tree.m_units[k])
    weight_load(0, ref["all_m"].at[0]).start()
    big = min(512, n)
    gelu_scale = (2.0 / jnp.pi) ** 0.5

    def feed(step, _):
        slot = lax.rem(step, 2)
        weight_load(slot, ref["all_m"].at[step]).wait()

        def rows_of(i, _):
            rows = pl.ds(pl.multiple_of(i * big, big), big)
            up, down = matrix(slot, 0, fs), matrix(slot, fs, fs)
            before = dot(ref["n2"][rows, :], up) + ref["hidden_bias"][step]
            square = before * before
            bent = jnp.tanh(before * (gelu_scale + (gelu_scale * 0.044715) * square))
            share = 0.5 + 0.5 * bent
            hidden = (before * share).astype(BF16)
            slope = share + 0.5 * before * (1.0 - bent * bent) * (
                gelu_scale + (3.0 * gelu_scale * 0.044715) * square
            )
            grad_before = (dot(ref["ct"][rows, :], down) * slope).astype(BF16)
            ref["hid"][rows, :] = hidden
            ref["gb"][rows, :] = grad_before
            ref["facc"][rows, :] = ref["facc"][rows, :] + dot_t(hidden, down)
            ref["gacc"][rows, :] = ref["gacc"][rows, :] + dot_t(grad_before, up)
            ref["hidden_sum"][step] = ref["hidden_sum"][step] + row_sum(grad_before.astype(F32))
            return 0

        lax.fori_loop(0, n // big, rows_of, 0)

        for k in range(1, n_units - 1, 2):

            @pl.when(step == k)
            def _(k=k):
                for unit in tree.m_units[k + 1 : k + 3]:
                    take_m(*unit)


        @pl.when(step >= 1)
        def _():
            stage_kept("m", step - 1, 3 - slot)

        loop_point(step, 0, 2, 0, n_units)
        stage = 2 + slot

        @pl.when(step >= 2)
        def _():
            stage_free("m", step - 2, stage)

        def grads(zz, _):
            rows = pl.ds(pl.multiple_of(zz * (4 * s_.tb), 4 * s_.tb), 4 * s_.tb)
            put_rows(stage, zz, 0, dot(ref["n2_t"][rows, :], ref["gb"][...]).astype(BF16))
            upstream = ref["ct_t"][pl.ds(zz * 2, 2)].reshape(4 * s_.tb, n)
            put_rows(stage, zz, fs, dot(upstream, ref["hid"][...]).astype(BF16))
            return 0

        lax.fori_loop(0, s_.z // 4, grads, 0)
        for k in range(n_units - 1):

            def load_next(k=k):
                if k:
                    take_sibling("m", *tree.m_units[k + 1])
                weight_load((k + 1) % 2, ref["all_m"].at[k + 1]).start()

            pl.when(step == k)(load_next)
        lax.fori_loop(s_.z // 4, s_.z // 2, grads, 0)
        stage_out("m", step, stage)
        loop_point(step, 0, 2, 1, n_units)
        return 0

    lax.fori_loop(0, n_units, feed, 0)

    stage_kept("m", n_units - 1, 2 + (n_units - 1) % 2)
    act(mlp_points)
    weight_load(0, ref["all_a"].at[s_.n_hid - 1]).start()

    def back_two(i, _):
        rows = pl.ds(pl.multiple_of(i * tile, tile), tile)
        ref["n2"][rows, :] = ref["facc"][rows, :].astype(BF16)
        scaled, inverse = ref["scaled_two"][rows, :].astype(F32), ref["inverse_two"][rows, :]
        grad = ref["gacc"][rows, :]
        add_sum(2, grad * scaled)
        add_sum(3, grad)
        grad = ref["ct"][rows, :].astype(F32) + norm_pull(grad, gain_row(2), scaled, inverse)
        mixed = grad.astype(BF16)
        add_sum(6, mixed.astype(F32))
        ref["facc"][rows, :] = grad
        ref["gacc"][rows, :] = jnp.zeros((tile, s_.d), F32)
        ref["nrm"][rows, :] = mixed
        return 0

    lax.fori_loop(0, s_.tiles, back_two, 0)

    def out_rows(name, j):
        return ref[name].at[columns(j, n)]

    for i in range(s_.tiles):
        rows = pl.ds(i * tile, tile)
        ref["n2_t"][:, rows] = ref["nrm"][rows, :].T
    act(mlp_points + 1)
    for r in range(1, s_.n_hid):
        send("lo", r, ref["n2"].at[:, columns(block_of(r), kh)], out_rows("layer_out", h), peer(r))
    own_lo = local(0, ref["n2"].at[:, columns(h, kh)], out_rows("layer_out", h))
    own_lo.start()
    for k in range(n_units - 2, n_units):
        stage_free("m", k, 2 + k % 2)

    def back_chunk(step, _):
        r = s_.n_hid - 1 - step
        slot = lax.rem(step, 2)
        stage = 2 + slot
        weight_load(slot, ref["all_a"].at[r]).wait()

        @pl.when(step + 1 < s_.n_hid)
        def _():
            weight_load(1 - slot, ref["all_a"].at[lax.rem(2 * s_.n_hid - 2 - step, s_.n_hid)]).start()

        def pull_out(i, _):
            rows = pl.ds(pl.multiple_of(i * tile, tile), tile)
            ref["hid"][rows, pl.ds(0, kh)] = dot(ref["nrm"][rows, :], matrix(slot, 3 * kh, kh)).astype(BF16)
            return 0

        lax.fori_loop(0, s_.tiles, pull_out, 0)

        @pl.when(step >= 1)
        def _():
            stage_kept("a", r + 1, 3 - slot)

        loop_point(step, chunk_points, 4, 0, s_.n_hid)

        def pull_attention(i, _):
            rows = pl.ds(pl.multiple_of(i * BLOCK, BLOCK), BLOCK)
            for p in range(s_.pairs):
                query, key, value = (ref["pj"][r, rows, pl.ds(k * kh + p * PAIR, PAIR)] for k in range(3))
                grad = ref["hid"][rows, pl.ds(p * PAIR, PAIR)]
                attention = ref["probs"][r, p, rows, :]
                weights = attention.astype(F32)
                grad_attention = dot_t(grad, two_heads(value))
                centre = spread(halves(weights * grad_attention, row_add))
                grad_scores = (weights * (grad_attention - centre) * HEAD ** (-0.5)).astype(BF16)
                grad_query = dot(grad_scores, two_heads(key))
                grad_key = pick_heads(dot_l(grad_scores, query))
                grad_value = pick_heads(dot_l(attention, grad))
                for k, values in enumerate((grad_query, grad_key, grad_value)):
                    ref["pj"][r, rows, pl.ds(k * kh + p * PAIR, PAIR)] = values.astype(BF16)
            return 0

        def pull_two(i, _):
            pull_attention(2 * i, 0)
            return pull_attention(2 * i + 1, 0)

        lax.fori_loop(0, s_.blocks // 2, pull_two, 0)
        loop_point(step, chunk_points, 4, 1, s_.n_hid)

        @pl.when(step >= 2)
        def _():
            stage_free("a", r + 2, stage)

        cols = columns(block_of(r), kh)

        def grads(zz, _):
            rows = pl.ds(pl.multiple_of(zz * (4 * s_.tb), 4 * s_.tb), 4 * s_.tb)
            put_rows(stage, zz, 0, dot(ref["nrm_t"][rows, :], ref["pj"][r]).astype(BF16))
            put_rows(stage, zz, 3 * kh, dot(ref["n2_t"][rows, :], ref["att"][r]).astype(BF16))
            return 0

        lax.fori_loop(0, s_.z // 2, grads, 0)
        stage_out("a", r, stage)
        loop_point(step, chunk_points, 4, 2, s_.n_hid)

        def pull_rows(i, _):
            rows = pl.ds(pl.multiple_of(i * tile, tile), tile)
            grad = ref["pj"][r, rows, :]
            ref["gacc"][rows, :] = ref["gacc"][rows, :] + dot_t(grad, matrix(slot, 0, 3 * kh))
            for k, first in ((4, 0), (5, 2 * kh)):
                part_sum = row_sum(ref["pj"][r, rows, pl.ds(first, kh)].astype(F32))
                ref["sums"][pl.ds(k, 1), cols] = ref["sums"][pl.ds(k, 1), cols] + part_sum
            return 0

        @pl.when(step + 2 < s_.n_hid)
        def _():
            lax.fori_loop(0, s_.tiles, pull_rows, 0)

        loop_point(step, chunk_points, 4, 3, s_.n_hid)
        return 0

    lax.fori_loop(0, s_.n_hid, back_chunk, 0)
    stage_kept("a", 0, 2 + (s_.n_hid - 1) % 2)
    last_two = [(r, (s_.n_hid - 1 - r) % 2) for r in (1, 0)]

    def back_one(i):
        rows = pl.ds(i * tile, tile)
        scaled, inverse = scaled_rows(ref["xs"][rows, :].astype(F32))
        grad = ref["gacc"][rows, :]
        for r, slot in last_two:
            grad = grad + dot_t(ref["pj"][r, rows, :], matrix(slot, 0, 3 * kh))
            for k, first in ((4, 0), (5, 2 * kh)):
                cols = columns(block_of(r), kh)
                part_sum = row_sum(ref["pj"][r, rows, pl.ds(first, kh)].astype(F32))
                ref["sums"][pl.ds(k, 1), cols] = ref["sums"][pl.ds(k, 1), cols] + part_sum
        add_sum(0, grad * scaled)
        add_sum(1, grad)
        total = ref["facc"][rows, :] + norm_pull(grad, gain_row(0), scaled, inverse)
        ref["ct"][rows, :] = total.astype(BF16)

    def row_copy(i, r):
        source = ref["ct"].at[pl.ds(i * tile, tile), columns(block_of(r), kh)]
        return source, ref["grad_rows"].at[pl.ds(pl.multiple_of(h * n + i * tile, tile), tile)]

    def send_rows(i):
        for r in range(1, s_.n_hid):
            send("gt", i * s_.n_hid + r, *row_copy(i, r), peer(r))
        local(41 + i, *row_copy(i, 0)).start()

    for i in range(s_.tiles):
        back_one(i)
    for k, (r, f) in enumerate(tree.m_units):
        for i in range(s_.fs // kh):
            ref["sums"][pl.ds(8 + 2 * f + i, 1), columns(block_of(r), kh)] = ref["hidden_sum"][
                k, :, pl.ds(i * kh, kh)
            ]
    for r in range(1, s_.n_hid):
        send("sum1", r, ref["sums"].at[:, columns(block_of(r), kh)], ref["sum1"].at[r], peer(r))
    for i in range(s_.tiles):
        send_rows(i)

    finals = [("m", 0), ("m", 1), ("a", 0), ("a", 1)]

    def final_loads(k, kind, f):
        slots = ref["z_g" + kind].at[f]
        room = ref["wa"].at[k % 2]
        if kind == "a":
            return [local(30, slots, room.at[:, 0, pl.ds(0, s_.half)])]
        out = [local(30, slots.at[pl.ds(0, s_.z)], room.at[:, 0])]
        if tree.far:
            out.append(local(31, slots.at[pl.ds(s_.z, len(tree.far))], room.at[pl.ds(0, len(tree.far)), 1]))
        return out

    def final_store(k, kind, f):
        if kind == "a":
            source = ref["facc"].at[pl.ds(k * s_.tb, s_.half), pl.ds(0, s_.wide)]
            return local(34 + k, source, ref["grad_a"].at[pl.ds(f * s_.half, s_.half)])
        return local(34 + k, ref["facc"].at[pl.ds(k * s_.tb, s_.tb), pl.ds(0, s_.wide)], ref["grad_m"].at[f])

    def final(k):
        kind, f = finals[k]
        for step in range(1, s_.z):
            arrived("zg" + kind, f * s_.z + step, z_slot(kind, f, step))
        if kind == "m":
            for i, r in enumerate(tree.far):
                arrived("fold", tree.m_pos[r, f], z_slot(kind, f, s_.z + i))
        for load in final_loads(k, kind, f):
            load.start()
        for load in final_loads(k, kind, f):
            load.wait()
        rows = pl.ds(0, s_.half if kind == "a" else s_.tb)
        total = ref["wa"][k % 2, 0, 0, rows].astype(F32)
        for step in range(1, s_.z):
            total = total + ref["wa"][k % 2, step, 0, rows].astype(F32)
        if kind == "m":
            for i in range(len(tree.far)):
                total = total + ref["wa"][k % 2, i, 1].astype(F32)
        ref["facc"][pl.ds(k * s_.tb, rows.size), pl.ds(0, s_.wide)] = total
        final_store(k, kind, f).start()

    def first_finals():
        final(0)
        final(1)

    def first_sums():
        total = ref["sums"][:, columns(h, kh)]
        for r in range(1, s_.n_hid):
            arrived("sum1", r, ref["sum1"].at[r])
            total = total + ref["sum1"][r]
        ref["sum2"][0] = total
        send("sum2", 0, ref["sum2"].at[0], ref["sum2"].at[1], sibling)
        arrived("sum2", 0, ref["sum2"].at[1])
        ref["sum3"][0] = ref["sum2"][0] + ref["sum2"][1]
        for step in range(1, s_.z):
            send("sum3", step, ref["sum3"].at[0], ref["sum3"].at[step], z_peer(step))

    feed_done = False
    for point in range(last_point, plan.end):
        units = [unit for verb, unit in plan.at.get(point, ()) if verb == "fetch"]
        if not feed_done and units and units[0][:2] == ("a", 0):
            first_finals()
            feed_done = True
        act(point)
        if ("a", 0, 1) in units:
            first_sums()
    if not feed_done:
        first_finals()

    final(2)
    final(3)
    total = ref["sum3"][0]
    for step in range(1, s_.z):
        arrived("sum3", step, ref["sum3"].at[step])
        total = total + ref["sum3"][step]
    ref["sum2"][2] = total
    small = local(2, ref["sum2"].at[2], ref["small"])
    small.start()

    small.wait()
    for k, (kind, f) in enumerate(finals):
        final_store(k, kind, f).wait()
    own_lo.wait()
    for holder in plan.holders:
        free_buffer(holder)
    for i in range(s_.tiles):
        local(41 + i, *row_copy(i, 0)).wait()
        for r in range(1, s_.n_hid):
            source, to = row_copy(i, r)
            arrived("gt", i * s_.n_hid + r, to)
            left("gt", i * s_.n_hid + r, source)
    for r in range(1, s_.n_hid):
        arrived("lo", r, out_rows("layer_out", h))
        left("params", r, ref["params"])
        left("ct", r, cot_rows(h))
        left("lo", r, cot_rows(h))
        left("sum1", r, ref["sum1"].at[r])
    left("sum2", 0, ref["sum2"].at[0])
    for step in range(1, s_.z):
        left("sum3", step, ref["sum3"].at[0])
    for r, f in tree.units:
        left("ac", tree.pos[r, f], a_part(r, f, c))
        if r:
            left("ax", tree.pos[r, f], a_part(r, f, c))
    for r, f in tree.m_units:
        left("mc", tree.m_pos[r, f], m_part(r, f, c))
    for r, f in tree.m_near:
        left("mx", tree.m_pos[r, f], m_part(r, f, c))
    for r, f in far_units:
        z_left("zf", tree.m_pos[r, f], m_block(r, f))
    for k in range(max(0, s_.n_hid - 2), s_.n_hid):
        stage_free("a", s_.n_hid - 1 - k, 2 + k % 2)


def scratch(size, tree):
    s_ = size
    units = len(tree.units)
    vmem = {
        "params_all": ((SMALL_ROWS, s_.d), F32),
        "xs": ((s_.n, s_.d), BF16),
        "ct": ((s_.n, s_.d), BF16),
        "nrm": ((s_.n, s_.d), BF16),
        "nrm_t": ((s_.d, s_.n), BF16),
        "n2": ((s_.n, s_.d), BF16),
        "n2_t": ((s_.d, s_.n), BF16),
        "ct_t": ((s_.z, 2, s_.tb, s_.n), BF16),
        "pj": ((s_.n_hid, s_.n, 3 * s_.kh), BF16),
        "probs": ((s_.n_hid, s_.pairs, s_.n, 2 * BLOCK), BF16),
        "att": ((s_.n_hid, s_.n, s_.kh), BF16),
        "scaled_two": ((s_.n, s_.d), BF16),
        "inverse_two": ((s_.n, 1), F32),
        "facc": ((s_.n, s_.d), F32),
        "gacc": ((s_.n, s_.d), F32),
        "wa": ((s_.n_hid, s_.z, 2, s_.tb, s_.wide), BF16),
        "out_in": ((s_.kh, s_.tb), BF16),
        "down_in": ((2 * s_.fs, s_.tb), BF16),
        "hid": ((s_.n, s_.fs), BF16),
        "gb": ((s_.n, s_.fs), BF16),
        "acc": ((WHOLE_BUFFERS + 1, s_.z, s_.tb, s_.wide), BF16),
        "tmp": ((s_.z, s_.tb, s_.wide), BF16),
        "hidden_bias": ((units, 1, s_.fs), F32),
        "hidden_sum": ((units, 1, s_.fs), F32),
        "sums": ((SMALL_ROWS, s_.d), F32),
        "sum1": ((s_.n_hid, SMALL_ROWS, s_.kh), F32),
        "sum2": ((3, SMALL_ROWS, s_.kh), F32),
        "sum3": ((s_.z, SMALL_ROWS, s_.kh), F32),
    }
    pairs = {
        "params": s_.n_hid,
        "za": s_.z,
        "zm": 2 * s_.z,
        "xs": s_.tiles * s_.n_hid,
        "ax": units,
        "ac": units,
        "mx": units,
        "mc": units,
        "ct": s_.n_hid,
        "sa": s_.n_hid,
        "sm": units,
        "ga": units,
        "gm": units,
        "fs": units,
        "zf": units * s_.z,
        "zfar": units * s_.z,
        "fold": units,
        "zga": 2 * s_.z,
        "zgm": 2 * s_.z,
        "lo": s_.n_hid,
        "gt": s_.tiles * s_.n_hid,
        "sum1": s_.n_hid,
        "sum2": 1,
        "sum3": s_.z,
    }
    out = {name: pltpu.VMEM(shape, kind) for name, (shape, kind) in vmem.items()}
    for name, count in pairs.items():
        out[name + "_s"] = pltpu.SemaphoreType.DMA((count,))
        out[name + "_r"] = pltpu.SemaphoreType.DMA((count,))
    out["local"] = pltpu.SemaphoreType.DMA((48,))
    out["wload"] = pltpu.SemaphoreType.DMA((s_.n_hid,))
    out["keep"] = pltpu.SemaphoreType.DMA((2,))
    return out


def finish_kernel(
    kh, fs, grad_ref, a_ref, m_ref, tokens_ref, middle_ref, coarse_ref, output_ref, up_ref, down_ref, attend_ref
):
    grad = grad_ref[...]
    rows = grad.shape[0]
    part = min(512, rows)
    by_4, by_16 = group_matrix(part, 4), group_matrix(part, 16)
    tokens_ref[...] = grad.astype(F32)
    for i in range(rows // part):
        piece = grad[i * part : i * part + part]
        middle_ref[pl.ds(i * part // 4, part // 4), :] = dot(by_4, piece)
        coarse_ref[pl.ds(i * part // 16, part // 16), :] = dot(by_16, piece)

    @pl.when(pl.program_id(0) == 0)
    def _():
        output_ref[...] = a_ref[:, pl.ds(3 * kh, kh)].T
        for k in range(3):
            attend_ref[k] = a_ref[:, pl.ds(k * kh, kh)]
        for f in (0, 1):
            up_ref[:, pl.ds(f * fs, fs)] = m_ref[f, :, pl.ds(0, fs)]
            down_ref[pl.ds(f * fs, fs), :] = m_ref[f, :, pl.ds(fs, fs)].T


def finish(size, grad, grad_a, grad_m):
    positions, features = grad.shape
    rows = min(1024, positions)
    tb, fs = size.tb, size.fs
    whole = [((features, tb), F32), ((tb, 2 * fs), F32), ((2 * fs, tb), F32), ((3, tb, features), F32)]
    return pl.pallas_call(
        functools.partial(finish_kernel, features, fs),
        grid=(positions // rows,),
        in_specs=[
            pl.BlockSpec((rows, features), lambda i: (i, 0)),
            pl.BlockSpec(grad_a.shape, lambda i: (0, 0)),
            pl.BlockSpec(grad_m.shape, lambda i: (0, 0, 0)),
        ],
        out_specs=[pl.BlockSpec((rows // t, features), lambda i: (i, 0)) for t in (1, 4, 16)]
        + [pl.BlockSpec(shape, lambda i, n=len(shape): (0,) * n) for shape, _ in whole],
        out_shape=[jax.ShapeDtypeStruct((positions // t, features), F32) for t in (1, 4, 16)]
        + [jax.ShapeDtypeStruct(*x) for x in whole],
        compiler_params=pltpu.CompilerParams(vmem_limit_bytes=60 * 2**20),
        name="token_gradients",
    )(grad, grad_a, grad_m)


def shards(
    tokens,
    middle_cond,
    coarse_cond,
    first_gain,
    first_shift,
    attend_weight,
    query_bias,
    value_bias,
    output_weight,
    mixer_bias,
    second_gain,
    second_shift,
    up_weight,
    hidden_bias,
    down_weight,
    down_bias,
    cotangent,
):
    positions, features = tokens.shape
    n_hid, n_tok = lax.axis_size("hid"), lax.axis_size("tok")
    d = features * n_hid
    ff = up_weight.shape[1] * n_hid
    size = Sizes(positions, features, d, ff, n_tok, n_hid)
    tree = Tree(n_hid)
    tb, fs, wide, z = size.tb, size.fs, size.wide, size.z
    vectors = (first_gain, first_shift, second_gain, second_shift, query_bias, value_bias, mixer_bias, down_bias)
    params = jnp.concatenate(
        [
            jnp.stack(vectors),
            hidden_bias.reshape(ff // d, features),
            jnp.zeros((SMALL_ROWS - 8 - ff // d, features), F32),
        ]
    )
    units = len(tree.units)
    outputs = {
        "layer_out": ((positions, features), BF16),
        "grad_rows": ((positions, features), BF16),
        "grad_a": ((tb, wide), F32),
        "grad_m": ((2, tb, wide), F32),
        "small": ((SMALL_ROWS, features), F32),
        "all_a": ((n_hid, z, 2, tb, wide), BF16),
        "all_m": ((units, z, 2, tb, wide), BF16),
        "own_ga": ((n_hid, z, tb, wide), BF16),
        "sib_ga": ((n_hid, z, tb, wide), BF16),
        "got_ga": ((units, z, size.half, wide), BF16),
        "own_gm": ((units, z, tb, wide), BF16),
        "sib_gm": ((units, z, tb, wide), BF16),
        "got_gm": ((units, z, tb, wide), BF16),
        "z_ga": ((2, z, size.half, wide), BF16),
        "z_gm": ((2, z + len(tree.far), tb, wide), BF16),
        "z_far": ((units, z, tb, wide), BF16),
    }
    hbm = pl.BlockSpec(memory_space=pltpu.HBM)
    results = pl.pallas_call(
        functools.partial(layer_kernel, size, tree),
        out_shape=[jax.ShapeDtypeStruct(*outputs[name]) for name in OUTPUTS],
        in_specs=[hbm] * len(INPUTS),
        out_specs=[hbm] * len(OUTPUTS),
        scratch_shapes=list(scratch(size, tree).values()),
        compiler_params=pltpu.CompilerParams(
            collective_id=0, has_side_effects=True, vmem_limit_bytes=63 * 2**20
        ),
        cost_estimate=pl.CostEstimate(flops=80 * 10**9, bytes_accessed=2 * 10**8, transcendentals=10**7),
        name="layer",
    )(
        tokens,
        middle_cond,
        coarse_cond,
        cotangent,
        attend_weight.transpose(1, 0, 2),
        output_weight,
        up_weight,
        down_weight,
        params,
    )
    layer_out, grad_rows, grad_a, grad_m, small = results[:5]
    grad_tokens, grad_middle, grad_coarse, grad_output, grad_up, grad_down, grad_attend = finish(
        size, grad_rows, grad_a, grad_m
    )
    tok = lax.axis_index("tok")
    share = features // n_tok
    mine = lax.dynamic_slice_in_dim(small[:8], tok * share, share, 1)
    hidden_share = fs * 2 // n_tok
    first = tok * hidden_share
    grad_hidden_bias = lax.dynamic_slice(
        small, (8 + first // features, lax.rem(first, features)), (1, hidden_share)
    ).reshape(hidden_share)
    return (
        layer_out,
        grad_tokens,
        grad_middle,
        grad_coarse,
        mine[0],
        mine[1],
        grad_attend.transpose(1, 0, 2),
        mine[4],
        mine[5],
        grad_output,
        mine[6],
        mine[2],
        mine[3],
        grad_up,
        grad_hidden_bias,
        grad_down,
        mine[7],
    )


def solution(mesh):
    return jax.shard_map(
        shards,
        mesh=mesh,
        in_specs=(
            P("tok", "hid"),
            P("tok", "hid"),
            P("tok", "hid"),
            P("hid"),
            P("hid"),
            P("tok", None, "hid"),
            P("hid"),
            P("hid"),
            P("hid", "tok"),
            P("hid"),
            P("hid"),
            P("hid"),
            P("tok", "hid"),
            P("hid"),
            P("hid", "tok"),
            P("hid"),
            P("tok", "hid"),
        ),
        out_specs=(
            P("tok", "hid"),
            P("tok", "hid"),
            P("tok", "hid"),
            P("tok", "hid"),
            P(("hid", "tok")),
            P(("hid", "tok")),
            P("tok", None, "hid"),
            P(("hid", "tok")),
            P(("hid", "tok")),
            P("hid", "tok"),
            P(("hid", "tok")),
            P(("hid", "tok")),
            P(("hid", "tok")),
            P("tok", "hid"),
            P(("hid", "tok")),
            P("hid", "tok"),
            P(("hid", "tok")),
        ),
        check_vma=False,
    )
```

```python
import functools

import jax
import jax.numpy as jnp
from jax import lax
from jax.experimental import pallas as pl
from jax.experimental.pallas import tpu as pltpu
from jax.sharding import PartitionSpec as P

HEAD = 64
BLOCK = 128
PAIR = 2 * HEAD
EPSILON = 1e-05
MESH = pl.DeviceIdType.MESH
BF16 = jnp.bfloat16
F32 = jnp.float32
SMALL_ROWS = 16
WHOLE_BUFFERS = 3
HALF_BUFFERS = 4


class Tree:
    def __init__(self, n_hid):
        self.n = n_hid
        self.bits = n_hid.bit_length() - 1
        units = [(r, f) for r in range(n_hid) for f in (0, 1)]
        self.units = sorted(units, key=lambda u: (u[0].bit_count(), len(self.children(*u)), u))
        self.pos = {u: k for k, u in enumerate(self.units)}
        self.near = [1 << b for b in range(self.bits)]
        self.far = [r for r in range(n_hid) if r.bit_count() > 1]
        first = [(1 << b, b % 2) for b in range(self.bits)]
        second = [(1 << b, 1 - b % 2) for b in range(self.bits)]
        self.m_near = first + second
        rest = [(r, f) for r in self.far for f in (0, 1)]
        self.m_units = [(0, 0), (0, 1)] + first + rest[:1] + second + rest[1:]
        self.m_pos = {u: k for k, u in enumerate(self.m_units)}

    def children(self, r, f):
        held = [b for b in range(self.bits) if r >> b & 1]
        free = [b for b in range(self.bits) if not r >> b & 1]
        if held:
            free = [b for b in free if (b < held[0] if f == 0 else b > held[-1])]
        return [(r | 1 << b, b) for b in free]

    def parent(self, r, f):
        held = [b for b in range(self.bits) if r >> b & 1]
        return held[0] if f == 0 else held[-1]


class Schedule:
    def __init__(self, done, kids, lag, last_point):
        self.at = {}
        self.turn = {}
        self.before = {}
        self.first = set()
        sent = {}
        seen = set()
        holders = {True: [None] * HALF_BUFFERS, False: [None] * (WHOLE_BUFFERS + 1)}
        turns = {True: -1, False: -1}
        waiting = sorted(done, key=lambda u: (u[0] != "a", done[u], len(kids[u])))
        held = None
        point = 0
        while waiting or held is not None:
            actions = []
            if held is not None:
                actions.append(("finish", held))
                sent[held] = point
                held = None
            for unit in waiting:
                if point <= done[unit] or any(k not in sent for k in kids[unit]):
                    continue
                if point < last_point and any(point < sent[k] + lag[unit[0]] for k in kids[unit]):
                    continue
                actions.append(("fetch", unit))
                held = unit
                pool = unit[0] == "a"
                size = HALF_BUFFERS if pool else WHOLE_BUFFERS + (turns[True] < 0)
                self.turn[unit] = k = turns[pool] = (turns[pool] + 1) % size
                self.before[unit] = holders[pool][k]
                holders[pool][k] = unit
                if pool and k == 2 and holders[False][-1]:
                    self.before[unit] = holders[False][-1]
                    holders[False][-1] = None
                if unit[:2] not in seen:
                    self.first.add(unit)
                seen.add(unit[:2])
                waiting.remove(unit)
                break
            if actions:
                self.at[point] = actions
            point += 1
        self.end = point
        self.holders = holders[True] + holders[False]


def dot(a, b):
    return jnp.dot(a, b, preferred_element_type=F32)


def dot_t(a, b):
    return lax.dot_general(a, b, (((1,), (1,)), ((), ())), preferred_element_type=F32)


def dot_l(a, b):
    return lax.dot_general(a, b, (((0,), (0,)), ((), ())), preferred_element_type=F32)


def repeat_matrix(rows, times):
    row = lax.broadcasted_iota(jnp.int32, (rows, rows // times), 0)
    column = lax.broadcasted_iota(jnp.int32, (rows, rows // times), 1) * times
    return ((row >= column) & (row < column + times)).astype(BF16)


def group_matrix(rows, times):
    row = lax.broadcasted_iota(jnp.int32, (rows // times, rows), 0) * times
    column = lax.broadcasted_iota(jnp.int32, (rows // times, rows), 1)
    return ((column >= row) & (column < row + times)).astype(BF16)


def scaled_rows(values):
    width = values.shape[1]
    average = jnp.sum(values, axis=1, keepdims=True) / width
    square = jnp.sum(values * values, axis=1, keepdims=True) / width
    inverse = lax.rsqrt(square - average * average + EPSILON)
    return (values - average) * inverse, inverse


def norm_pull(grad, gain, scaled, inverse):
    width = grad.shape[1]
    weighted = grad * gain
    mean = jnp.sum(weighted, axis=1, keepdims=True) / width
    along = jnp.sum(weighted * scaled, axis=1, keepdims=True) / width
    return inverse * (weighted - mean - scaled * along)


def row_sum(values):
    return jnp.sum(values, axis=0, keepdims=True)


def two_heads(values):
    low = lax.broadcasted_iota(jnp.int32, values.shape, 1) < HEAD
    zero = jnp.zeros_like(values)
    return jnp.concatenate([jnp.where(low, values, zero), jnp.where(low, zero, values)], axis=0)


def pick_heads(both):
    low = lax.broadcasted_iota(jnp.int32, (BLOCK, PAIR), 1) < HEAD
    return jnp.where(low, both[:BLOCK], both[BLOCK:])


INPUTS = ("tokens", "middle", "coarse", "cotangent", "attend_w", "output_w", "up_w", "down_w")
VECTORS = 8
OUTPUTS = (
    "layer_out",
    "grad_rows",
    "grad_a",
    "grad_m",
    "small",
    "all_a",
    "all_m",
    "own_ga",
    "sib_ga",
    "got_ga",
    "own_gm",
    "sib_gm",
    "got_gm",
    "z_ga",
    "z_gm",
    "z_far",
)


class Sizes:
    def __init__(self, positions, features, d, ff, n_tok, n_hid):
        self.d, self.n_hid, self.n_tok = d, n_hid, n_tok
        self.z = n_tok // 2
        self.n = positions // n_hid
        self.kh = features
        self.fs = ff // n_hid // 2
        self.tb = d // n_tok
        self.half = self.tb // 2
        self.wide = 4 * features
        self.vector_rows = ff // d
        self.pairs = features // PAIR
        self.tile = min(256, self.n)
        self.tiles = self.n // self.tile
        self.blocks = self.n // BLOCK
        self.positions = positions


def layer_kernel(size, tree, *refs):
    vectors = [f"vector_{k}" for k in range(VECTORS + 1)]
    names = list(INPUTS) + vectors + list(OUTPUTS) + list(scratch(size, tree))
    ref = dict(zip(names, refs, strict=True))
    s_ = size
    n_units = len(tree.units)
    tok, h = lax.axis_index("tok"), lax.axis_index("hid")
    z, c = tok // 2, lax.rem(tok, 2)

    def block_of(r):
        total = 0
        for b in range(tree.bits):
            total = total + lax.rem(h // (1 << b) + r // (1 << b), 2) * (1 << b)
        return total

    def peer(r):
        return (tok, block_of(r))

    sibling = (tok + 1 - 2 * c, h)

    def z_peer(step):
        return (lax.rem(z + step, s_.z) * 2 + c, h)

    def columns(j, width):
        return pl.ds(pl.multiple_of(j * width, width), width)

    def remote(name, index, src, dst, device):
        return pltpu.make_async_remote_copy(
            src_ref=src,
            dst_ref=dst,
            send_sem=ref[name + "_s"].at[index],
            recv_sem=ref[name + "_r"].at[index],
            device_id=device,
            device_id_type=MESH,
        )

    def send(name, index, src, dst, device):
        remote(name, index, src, dst, device).start()

    def arrived(name, index, dst):
        remote(name, index, dst, dst, sibling).wait_recv()

    def left(name, index, src):
        remote(name, index, src, src, sibling).wait_send()

    def local(index, src, dst):
        return pltpu.make_async_copy(src, dst, ref["local"].at[index])

    barrier = pltpu.get_barrier_semaphore()
    everyone = [peer(r) for r in range(1, s_.n_hid)] + [sibling]
    everyone += [z_peer(k) for k in range(1, s_.z)]
    for device in everyone:
        pl.semaphore_signal(barrier, inc=1, device_id=device, device_id_type=MESH)
    pl.semaphore_wait(barrier, len(everyone))

    def z_send(name, index, src, dst):
        for step in range(1, s_.z):
            send(name, index * s_.z + step, src, dst, z_peer(step))

    def z_arrived(name, index, dst):
        for step in range(1, s_.z):
            arrived(name, index * s_.z + step, dst)

    def z_left(name, index, src):
        for step in range(1, s_.z):
            left(name, index * s_.z + step, src)

    def a_part(r, f, core):
        return ref["all_a"].at[r, :, core, pl.ds(f * s_.half, s_.half)]

    def m_part(r, f, core):
        return ref["all_m"].at[tree.m_pos[r, f], :, core]

    part = {"a": a_part, "m": m_part}

    ref["sum2"][0] = jnp.zeros((SMALL_ROWS, s_.kh), F32)
    vector_loads = [
        local(44 + k, ref[name], ref["sum2"].at[0, pl.ds(k, s_.vector_rows if k == VECTORS else 1)])
        for k, name in enumerate(vectors)
    ]
    for copy in vector_loads:
        copy.start()
    kh, n, tile, fs = s_.kh, s_.n, s_.tile, s_.fs
    own_block = [ref["acc"].at[k, 0] for k in range(3)]
    own_loads = [local(1 + k, ref["attend_w"].at[k], own_block[0].at[:, pl.ds(k * kh, kh)]) for k in range(3)]
    own_loads.append(local(40, ref["output_w"], ref["out_in"]))
    for f in (0, 1):
        own_loads.append(local(41 + f, ref["up_w"].at[:, pl.ds(f * fs, fs)], own_block[1 + f].at[:, pl.ds(0, fs)]))
    own_loads.append(local(43, ref["down_w"], ref["down_in"]))
    for copy in own_loads:
        copy.start()
    for copy in vector_loads:
        copy.wait()
    own_params = local(0, ref["sum2"].at[0], ref["params_all"].at[:, columns(h, s_.kh)])
    own_params.start()
    for r in range(1, s_.n_hid):
        send("params", r, ref["sum2"].at[0], ref["params_all"].at[:, columns(h, s_.kh)], peer(r))

    def m_block(r, f):
        return ref["all_m"].at[tree.m_pos[r, f], z, c]

    far_units = [(r, f) for r in tree.far for f in (0, 1)]

    rows_m, rows_c = n // 4, n // 16
    loads = {}
    order = list(range(1, s_.n_hid)) + [0]
    for r in order:
        j = block_of(r)
        sources = (
            (ref["tokens"].at[columns(j, n)], ref["pj"].at[r, :, pl.ds(0, kh)]),
            (ref["middle"].at[columns(j, rows_m)], ref["pj"].at[r, pl.ds(0, rows_m), pl.ds(2 * kh, kh)]),
            (ref["coarse"].at[columns(j, rows_c)], ref["pj"].at[r, pl.ds(rows_m, rows_c), pl.ds(2 * kh, kh)]),
        )
        loads[r] = [local(4 + 3 * r + k, *pair) for k, pair in enumerate(sources)]
        for copy in loads[r]:
            copy.start()
    for copy in own_loads:
        copy.wait()
    ref["acc"][0, 0, :, pl.ds(3 * kh, kh)] = ref["out_in"][...].T
    z_send("za", 0, own_block[0], ref["all_a"].at[0, z, c])
    for f in (0, 1):
        ref["acc"][1 + f, 0, :, pl.ds(fs, fs)] = ref["down_in"][pl.ds(f * fs, fs), :].T
    for r, f in far_units:
        send("fs", tree.m_pos[r, f], own_block[1 + f], m_block(r, f), peer(r))
    own_places = [ref["all_a"].at[0, z, c], m_block(0, 0), m_block(0, 1)]
    own_out = [local(1 + k, own_block[k], place) for k, place in enumerate(own_places)]
    for store in own_out:
        store.start()
    repeat_4, repeat_16 = repeat_matrix(tile, 4), repeat_matrix(tile, 16)

    def xs_rows(i, j):
        return ref["xs"].at[pl.ds(i * tile, tile), columns(j, kh)]

    own_xs = []
    for i in range(s_.tiles):
        for r in order:
            if i == 0:
                for copy in loads[r]:
                    copy.wait()
            rows = pl.ds(i * tile, tile)
            middle = ref["pj"][r, pl.ds(i * (tile // 4), tile // 4), pl.ds(2 * kh, kh)]
            coarse = ref["pj"][r, pl.ds(rows_m + i * (tile // 16), tile // 16), pl.ds(2 * kh, kh)]
            total = ref["pj"][r, rows, pl.ds(0, kh)].astype(F32)
            total = total + dot(repeat_4, middle) + dot(repeat_16, coarse)
            ref["pj"][r, rows, pl.ds(kh, kh)] = total.astype(BF16)
            source = ref["pj"].at[r, rows, pl.ds(kh, kh)]
            if r:
                send("xs", i * s_.n_hid + r, source, xs_rows(i, h), peer(r))
            else:
                copy = local(4 + 3 * s_.n_hid + i, source, xs_rows(i, h))
                copy.start()
                own_xs.append(copy)


    def to_sibling(kind, r, f):
        k = tree.pos[r, f] if kind == "a" else tree.m_pos[r, f]
        send(kind + "c", k, part[kind](r, f, c), part[kind](r, f, c), sibling)

    def take_a(r, f):
        arrived("ax", tree.pos[r, f], a_part(r, f, c))
        for child, b in tree.children(r, f):
            send("ax", tree.pos[child, f], a_part(r, f, c), a_part(child, f, c), peer(1 << b))
        to_sibling("a", r, f)

    def take_m(r, f):
        if r in tree.far:
            z_arrived("zf", tree.m_pos[r, f], m_block(r, f))
        else:
            arrived("mx", tree.m_pos[r, f], m_part(r, f, c))
        to_sibling("m", r, f)

    def take_sibling(kind, r, f):
        k = tree.pos[r, f] if kind == "a" else tree.m_pos[r, f]
        arrived(kind + "c", k, part[kind](r, f, 1 - c))

    a_near = sorted([u for u in tree.units if u[0] in tree.near], key=lambda u: -len(tree.children(*u)))
    for store in own_out:
        store.wait()
    z_arrived("za", 0, ref["all_a"].at[0, z, c])
    for f in (0, 1):
        z_send("zm", f, own_block[1 + f], m_block(0, f))
    for r, f in far_units:
        arrived("fs", tree.m_pos[r, f], m_block(r, f))
        z_send("zf", tree.m_pos[r, f], m_block(r, f), m_block(r, f))
    for r, f in a_near:
        send("ax", tree.pos[r, f], a_part(0, f, c), a_part(r, f, c), peer(r))
    for f in (0, 1):
        to_sibling("a", 0, f)

    own_params.wait()
    for r in range(1, s_.n_hid):
        arrived("params", r, ref["params_all"].at[:, columns(h, kh)])
        left("params", r, ref["sum2"].at[0])

    def gain_row(k):
        return ref["params_all"][pl.ds(k, 1), :]

    for k, (r, f) in enumerate(tree.m_units):
        parts = [
            ref["params_all"][pl.ds(8 + 2 * f + i, 1), columns(block_of(r), kh)] for i in range(s_.fs // kh)
        ]
        ref["hidden_bias"][k] = jnp.concatenate(parts, axis=1)
        ref["hidden_sum"][k] = jnp.zeros((1, s_.fs), F32)
    ref["sums"][...] = jnp.zeros_like(ref["sums"])

    def add_sum(k, values):
        ref["sums"][pl.ds(k, 1), :] = ref["sums"][pl.ds(k, 1), :] + row_sum(values)

    for i in range(s_.tiles):
        own_xs[i].wait()
        for r in range(1, s_.n_hid):
            arrived("xs", i * s_.n_hid + r, xs_rows(i, h))
        rows = pl.ds(i * tile, tile)
        scaled, _ = scaled_rows(ref["xs"][rows, :].astype(F32))
        normed = (scaled * gain_row(0) + gain_row(1)).astype(BF16)
        ref["nrm"][rows, :] = normed
        ref["nrm_t"][:, rows] = normed.T

    for i in range(s_.tiles):
        for r in range(1, s_.n_hid):
            left("xs", i * s_.n_hid + r, xs_rows(i, h))

    def weight_load(slot, source):
        return pltpu.make_async_copy(source, ref["wa"].at[slot], ref["wload"].at[slot])

    def matrix(slot, first, width):
        return ref["wa"][slot, :, :, :, pl.ds(first, width)].reshape(s_.d, width)

    def put_rows(slot, zz, first, values):
        width = values.shape[1]
        ref["wa"][slot, pl.ds(zz * 2, 2), :, :, pl.ds(first, width)] = values.reshape(2, 2, s_.tb, width)

    def cot_rows(j):
        return ref["ct"].at[:, columns(j, kh)]

    own_ct = local(0, ref["cotangent"].at[columns(h, n)], cot_rows(h))

    def before_chunk(r):
        if r == 0:
            pass
        elif r.bit_count() == 1:
            if r == 1:
                for u, f in a_near:
                    take_a(u, f)
                own_ct.start()
                for k in range(1, s_.n_hid):
                    send("ct", k, ref["cotangent"].at[columns(block_of(k), n)], cot_rows(h), peer(k))
        else:
            for f in (0, 1):
                take_a(r, f)
        for f in (0, 1):
            take_sibling("a", r, f)
        load = weight_load(r, ref["all_a"].at[r])
        load.start()
        load.wait()

    causal_row = lax.broadcasted_iota(jnp.int32, (BLOCK, 2 * BLOCK), 0)
    causal_col = lax.rem(lax.broadcasted_iota(jnp.int32, (BLOCK, 2 * BLOCK), 1), BLOCK)
    allowed = causal_row >= causal_col

    def halves(values, f):
        return [f(values[:, :BLOCK]), f(values[:, BLOCK:])]

    def spread(pair):
        return jnp.concatenate([jnp.broadcast_to(v, (BLOCK, BLOCK)) for v in pair], axis=1)

    def row_max(v):
        return jnp.max(v, axis=1, keepdims=True)

    def row_add(v):
        return jnp.sum(v, axis=1, keepdims=True)

    def attend_chunk(r):
        for k in range(s_.n_hid):
            pl.when(r == k)(functools.partial(before_chunk, k))
        cols = columns(block_of(r), kh)
        bias = jnp.concatenate(
            [ref["params_all"][4:5, cols], jnp.zeros((1, kh), F32), ref["params_all"][5:6, cols]], axis=1
        )

        def project(i, _):
            rows = pl.ds(pl.multiple_of(i * tile, tile), tile)
            values = dot(ref["nrm"][rows, :], matrix(r, 0, 3 * kh)) + bias
            ref["pj"][r, rows, :] = values.astype(BF16)
            return 0

        lax.fori_loop(0, s_.tiles, project, 0)

        def attend(i, _):
            rows = pl.ds(pl.multiple_of(i * BLOCK, BLOCK), BLOCK)
            for p in range(s_.pairs):
                query, key, value = (ref["pj"][r, rows, pl.ds(k * kh + p * PAIR, PAIR)] for k in range(3))
                logits = jnp.where(allowed, dot_t(query, two_heads(key)) * HEAD ** (-0.5), -1e30)
                powers = jnp.exp(logits - spread(halves(logits, row_max)))
                shares = [1.0 / v for v in halves(powers, row_add)]
                attention = (powers * spread(shares)).astype(BF16)
                ref["probs"][r, p, rows, :] = attention
                out = dot(attention, two_heads(value))
                ref["att"][r, rows, pl.ds(p * PAIR, PAIR)] = out.astype(BF16)
            return 0

        def attend_two(i, _):
            attend(2 * i, 0)
            return attend(2 * i + 1, 0)

        lax.fori_loop(0, s_.blocks // 2, attend_two, 0)

    lax.fori_loop(0, s_.n_hid, lambda r, _: (attend_chunk(r), 0)[1], 0)

    for f in (0, 1):
        z_arrived("zm", f, m_block(0, f))
    for f in (0, 1):
        to_sibling("m", 0, f)
    z_left("za", 0, own_block[0])
    for f in (0, 1):
        z_left("zm", f, own_block[1 + f])
    for r, f in far_units:
        left("fs", tree.m_pos[r, f], own_block[1 + f])

    def mix(i, _):
        rows = pl.ds(pl.multiple_of(i * tile, tile), tile)
        total = ref["xs"][rows, :].astype(F32) + gain_row(6)
        for r in range(s_.n_hid):
            total = total + dot_t(ref["att"][r, rows, :], matrix(r, 3 * kh, kh))
        ref["facc"][rows, :] = total + gain_row(7)
        scaled, inverse = scaled_rows(total)
        ref["scaled_two"][rows, :] = scaled.astype(BF16)
        ref["inverse_two"][rows, :] = inverse
        normed = (scaled * gain_row(2) + gain_row(3)).astype(BF16)
        ref["n2"][rows, :] = normed
        return 0

    lax.fori_loop(0, s_.tiles, mix, 0)

    own_ct.wait()
    for k in range(1, s_.n_hid):
        arrived("ct", k, cot_rows(h))
    for r, f in tree.m_near:
        send("mx", tree.m_pos[r, f], m_part(0, f, c), m_part(r, f, c), peer(r))
    for i in range(s_.tiles):
        rows = pl.ds(i * tile, tile)
        ref["n2_t"][:, rows] = ref["n2"][rows, :].T
        upstream = ref["ct"][rows, :]
        ref["ct_t"][:, :, :, rows] = upstream.T.reshape(s_.z, 2, s_.tb, tile)
        add_sum(7, upstream.astype(F32))
        ref["gacc"][rows, :] = jnp.zeros((tile, s_.d), F32)

    mlp_points = 3 * n_units
    chunk_points = mlp_points + 2
    last_point = chunk_points + 5 * s_.n_hid
    done, kids = {}, {}
    for k, (r, f) in enumerate(tree.m_units):
        done["m", r, f] = 3 * k + 2
        kids["m", r, f] = [("m", u, f) for u in tree.near] if r == 0 else []
        if r == 0:
            done["m", r, f] = mlp_points - 1
    for r, f in far_units:
        done["fold", r, f] = 0
        kids["fold", r, f] = [("m", r, f)]
    for r in range(s_.n_hid):
        for f in (0, 1):
            done["a", r, f] = chunk_points + 5 * (s_.n_hid - 1 - r) + 4
            kids["a", r, f] = [("a", child, f) for child, _ in tree.children(r, f)]
    plan = Schedule(done, kids, {"m": 14, "a": 7, "fold": 10}, last_point)

    def place(kind, r, f):
        return tree.pos[r, f] if kind == "a" else tree.m_pos[r, f]

    def own_grad(kind, r, f):
        if kind == "a":
            return ref["own_ga"].at[r, :, pl.ds(f * s_.half, s_.half)]
        return ref["own_gm"].at[tree.m_pos[r, f]]

    def sib_grad(kind, r, f):
        if kind == "a":
            return ref["sib_ga"].at[r, :, pl.ds(f * s_.half, s_.half)]
        return ref["sib_gm"].at[tree.m_pos[r, f]]

    def got_grad(kind, r, f):
        return ref["got_g" + kind].at[place(kind, r, f)]

    def part_of(whole, kind):
        return whole.at[:, pl.ds(0, s_.half if kind == "a" else s_.tb)]

    def spare(first, rows):
        return ref["ct_t"].at[:, first, rows, pl.ds(0, s_.wide)]

    def sum_buffer(unit):
        k = plan.turn[unit]
        if unit[0] != "a":
            return ref["acc"].at[k]
        rows = pl.ds(k % 2 * s_.half, s_.half)
        return spare(1, rows) if k < 2 else ref["acc"].at[WHOLE_BUFFERS, :, rows]

    def z_slot(kind, f, step):
        return ref["z_g" + kind].at[f, step]

    def scattered(kind, r, f):
        if r == 0:
            return "zg" + kind, f * s_.z, ref["z_g" + kind].at[f]
        return "zfar", tree.m_pos[r, f] * s_.z, ref["z_far"].at[tree.m_pos[r, f]]

    def scatters(kind, r):
        return r == 0 or (kind == "m" and r in tree.far)

    def free_buffer(holder):
        if holder is None:
            return
        kind, r, f = holder
        source = sum_buffer(holder)
        if kind == "fold":
            left("fold", tree.m_pos[r, f], source.at[0])
        elif scatters(kind, r):
            name, first, _ = scattered(kind, r, f)
            for step in range(1, s_.z):
                left(name, first + step, source.at[0])
        else:
            left("g" + kind, place(kind, r, f), source)

    def fetches(unit):
        kind, r, f = unit
        if kind == "fold":
            return [(30, ref["z_far"].at[tree.m_pos[r, f]], sum_buffer(unit))]
        out = [(30, own_grad(*unit), sum_buffer(unit))]
        out.append((31, sib_grad(*unit), part_of(ref["tmp"], kind)))
        if kids[unit]:
            out.append((32, got_grad(*kids[unit][0]), part_of(spare(0, pl.ds(0, s_.tb)), kind)))
        return out

    def fetch(unit):
        kind, r, f = unit
        free_buffer(plan.before[unit])
        if kind == "fold":
            for step in range(1, s_.z):
                name, first, slots = scattered("m", r, f)
                arrived(name, first + step, slots.at[step])
        elif kind == "m" or unit in plan.first:
            slot = tree.m_pos[r, f] if kind == "m" else r
            arrived("s" + kind, slot, ref["sib_g" + kind].at[slot])
        if kind != "fold":
            for kid in kids[unit][:1]:
                arrived("g" + kind, place(*kid), got_grad(*kid))
        for item in fetches(unit):
            local(*item).start()

    def finish(unit):
        kind, r, f = unit
        for item in fetches(unit):
            local(*item).wait()
        acc, tmp, more = sum_buffer(unit), part_of(ref["tmp"], kind), part_of(spare(0, pl.ds(0, s_.tb)), kind)
        if kind == "fold":
            total = acc[0].astype(F32)
            for zz in range(1, s_.z):
                total = total + acc[zz].astype(F32)
            acc[0] = total.astype(BF16)
            slot = ref["z_gm"].at[f, s_.z + tree.far.index(r)]
            send("fold", tree.m_pos[r, f], acc.at[0], slot, peer(r))
            return
        for zz in range(s_.z):
            total = acc[zz].astype(F32) + tmp[zz].astype(F32)
            if kids[unit]:
                total = total + more[zz].astype(F32)
            acc[zz] = total.astype(BF16)
        for kid in kids[unit][1:]:
            source = got_grad(*kid)
            arrived("g" + kind, place(*kid), source)
            copy = local(36, source, more)
            copy.start()
            copy.wait()
            for zz in range(s_.z):
                acc[zz] = (acc[zz].astype(F32) + more[zz].astype(F32)).astype(BF16)
        if scatters(kind, r):
            name, first, slots = scattered(kind, r, f)
            keep = local(40, acc.at[z], slots.at[0])
            keep.start()
            for step in range(1, s_.z):
                to = lax.rem(z + step, s_.z)
                send(name, first + step, acc.at[to], slots.at[step], z_peer(step))
            keep.wait()
        else:
            to = r if kind == "m" else 1 << tree.parent(r, f)
            send("g" + kind, place(kind, r, f), acc, got_grad(kind, r, f), peer(to))

    def act(point):
        for verb, unit in plan.at.get(point, ()):
            (fetch if verb == "fetch" else finish)(unit)

    def loop_point(step, first, stride, offset, count):
        for k in range(count):
            if first + stride * k + offset in plan.at:
                pl.when(step == k)(functools.partial(act, first + stride * k + offset))

    def stage_copies(kind, index, slot):
        own = ref["own_g" + kind].at[index]
        theirs = ref["sib_g" + kind].at[index]
        keep = pltpu.make_async_copy(ref["wa"].at[slot, :, c], own, ref["keep"].at[slot - 2])
        give = pltpu.make_async_remote_copy(
            src_ref=ref["wa"].at[slot, :, 1 - c],
            dst_ref=theirs,
            send_sem=ref["s" + kind + "_s"].at[index],
            recv_sem=ref["s" + kind + "_r"].at[index],
            device_id=sibling,
            device_id_type=MESH,
        )
        return keep, give

    def stage_out(kind, index, slot):
        for copy in stage_copies(kind, index, slot):
            copy.start()

    def stage_kept(kind, index, slot):
        stage_copies(kind, index, slot)[0].wait()

    def stage_free(kind, index, slot):
        stage_copies(kind, index, slot)[1].wait_send()

    for k in (0, 1):
        take_sibling("m", *tree.m_units[k])
    weight_load(0, ref["all_m"].at[0]).start()
    big = min(512, n)
    gelu_scale = (2.0 / jnp.pi) ** 0.5

    def feed(step, _):
        slot = lax.rem(step, 2)
        weight_load(slot, ref["all_m"].at[step]).wait()

        def rows_of(i, _):
            rows = pl.ds(pl.multiple_of(i * big, big), big)
            up, down = matrix(slot, 0, fs), matrix(slot, fs, fs)
            before = dot(ref["n2"][rows, :], up) + ref["hidden_bias"][step]
            square = before * before
            bent = jnp.tanh(before * (gelu_scale + (gelu_scale * 0.044715) * square))
            share = 0.5 + 0.5 * bent
            hidden = (before * share).astype(BF16)
            slope = share + 0.5 * before * (1.0 - bent * bent) * (
                gelu_scale + (3.0 * gelu_scale * 0.044715) * square
            )
            grad_before = (dot(ref["ct"][rows, :], down) * slope).astype(BF16)
            ref["hid"][rows, :] = hidden
            ref["gb"][rows, :] = grad_before
            ref["facc"][rows, :] = ref["facc"][rows, :] + dot_t(hidden, down)
            ref["gacc"][rows, :] = ref["gacc"][rows, :] + dot_t(grad_before, up)
            ref["hidden_sum"][step] = ref["hidden_sum"][step] + row_sum(grad_before.astype(F32))
            return 0

        lax.fori_loop(0, n // big // 2, rows_of, 0)

        @pl.when(step >= 1)
        def _():
            stage_kept("m", step - 1, 3 - slot)

        loop_point(step, 0, 3, 0, n_units)
        lax.fori_loop(n // big // 2, n // big, rows_of, 0)

        for k in range(1, n_units - 1, 2):

            @pl.when(step == k)
            def _(k=k):
                for unit in tree.m_units[k + 1 : k + 3]:
                    take_m(*unit)


        loop_point(step, 0, 3, 1, n_units)
        stage = 2 + slot

        @pl.when(step >= 2)
        def _():
            stage_free("m", step - 2, stage)

        def grads(zz, _):
            rows = pl.ds(pl.multiple_of(zz * (4 * s_.tb), 4 * s_.tb), 4 * s_.tb)
            put_rows(stage, zz, 0, dot(ref["n2_t"][rows, :], ref["gb"][...]).astype(BF16))
            upstream = ref["ct_t"][pl.ds(zz * 2, 2)].reshape(4 * s_.tb, n)
            put_rows(stage, zz, fs, dot(upstream, ref["hid"][...]).astype(BF16))
            return 0

        lax.fori_loop(0, s_.z // 4, grads, 0)
        for k in range(n_units - 1):

            def load_next(k=k):
                if k:
                    take_sibling("m", *tree.m_units[k + 1])
                weight_load((k + 1) % 2, ref["all_m"].at[k + 1]).start()

            pl.when(step == k)(load_next)
        lax.fori_loop(s_.z // 4, s_.z // 2, grads, 0)
        stage_out("m", step, stage)
        loop_point(step, 0, 3, 2, n_units)
        return 0

    lax.fori_loop(0, n_units, feed, 0)

    stage_kept("m", n_units - 1, 2 + (n_units - 1) % 2)
    act(mlp_points)
    weight_load(0, ref["all_a"].at[s_.n_hid - 1]).start()

    def back_two(i, _):
        rows = pl.ds(pl.multiple_of(i * tile, tile), tile)
        ref["n2"][rows, :] = ref["facc"][rows, :].astype(BF16)
        scaled, inverse = ref["scaled_two"][rows, :].astype(F32), ref["inverse_two"][rows, :]
        grad = ref["gacc"][rows, :]
        add_sum(2, grad * scaled)
        add_sum(3, grad)
        grad = ref["ct"][rows, :].astype(F32) + norm_pull(grad, gain_row(2), scaled, inverse)
        mixed = grad.astype(BF16)
        add_sum(6, mixed.astype(F32))
        ref["facc"][rows, :] = grad
        ref["gacc"][rows, :] = jnp.zeros((tile, s_.d), F32)
        ref["nrm"][rows, :] = mixed
        return 0

    lax.fori_loop(0, s_.tiles, back_two, 0)

    def out_rows(name, j):
        return ref[name].at[columns(j, n)]

    for i in range(s_.tiles):
        rows = pl.ds(i * tile, tile)
        ref["n2_t"][:, rows] = ref["nrm"][rows, :].T
    act(mlp_points + 1)
    for r in range(1, s_.n_hid):
        send("lo", r, ref["n2"].at[:, columns(block_of(r), kh)], out_rows("layer_out", h), peer(r))
    own_lo = local(0, ref["n2"].at[:, columns(h, kh)], out_rows("layer_out", h))
    own_lo.start()
    for k in range(n_units - 2, n_units):
        stage_free("m", k, 2 + k % 2)

    def back_chunk(step, _):
        r = s_.n_hid - 1 - step
        slot = lax.rem(step, 2)
        stage = 2 + slot
        weight_load(slot, ref["all_a"].at[r]).wait()

        @pl.when(step + 1 < s_.n_hid)
        def _():
            weight_load(1 - slot, ref["all_a"].at[lax.rem(2 * s_.n_hid - 2 - step, s_.n_hid)]).start()

        def pull_out(i, _):
            rows = pl.ds(pl.multiple_of(i * tile, tile), tile)
            ref["hid"][rows, pl.ds(0, kh)] = dot(ref["nrm"][rows, :], matrix(slot, 3 * kh, kh)).astype(BF16)
            return 0

        lax.fori_loop(0, s_.tiles, pull_out, 0)

        @pl.when(step >= 1)
        def _():
            stage_kept("a", r + 1, 3 - slot)

        loop_point(step, chunk_points, 5, 0, s_.n_hid)

        def pull_attention(i, _):
            rows = pl.ds(pl.multiple_of(i * BLOCK, BLOCK), BLOCK)
            for p in range(s_.pairs):
                query, key, value = (ref["pj"][r, rows, pl.ds(k * kh + p * PAIR, PAIR)] for k in range(3))
                grad = ref["hid"][rows, pl.ds(p * PAIR, PAIR)]
                attention = ref["probs"][r, p, rows, :]
                weights = attention.astype(F32)
                grad_attention = dot_t(grad, two_heads(value))
                centre = spread(halves(weights * grad_attention, row_add))
                grad_scores = (weights * (grad_attention - centre) * HEAD ** (-0.5)).astype(BF16)
                grad_query = dot(grad_scores, two_heads(key))
                grad_key = pick_heads(dot_l(grad_scores, query))
                grad_value = pick_heads(dot_l(attention, grad))
                for k, values in enumerate((grad_query, grad_key, grad_value)):
                    ref["pj"][r, rows, pl.ds(k * kh + p * PAIR, PAIR)] = values.astype(BF16)
            return 0

        def pull_two(i, _):
            pull_attention(2 * i, 0)
            return pull_attention(2 * i + 1, 0)

        lax.fori_loop(0, s_.blocks // 4, pull_two, 0)
        loop_point(step, chunk_points, 5, 1, s_.n_hid)
        lax.fori_loop(s_.blocks // 4, s_.blocks // 2, pull_two, 0)
        loop_point(step, chunk_points, 5, 2, s_.n_hid)

        @pl.when(step >= 2)
        def _():
            stage_free("a", r + 2, stage)

        cols = columns(block_of(r), kh)

        def grads(zz, _):
            rows = pl.ds(pl.multiple_of(zz * (4 * s_.tb), 4 * s_.tb), 4 * s_.tb)
            put_rows(stage, zz, 0, dot(ref["nrm_t"][rows, :], ref["pj"][r]).astype(BF16))
            put_rows(stage, zz, 3 * kh, dot(ref["n2_t"][rows, :], ref["att"][r]).astype(BF16))
            return 0

        lax.fori_loop(0, s_.z // 2, grads, 0)
        stage_out("a", r, stage)
        loop_point(step, chunk_points, 5, 3, s_.n_hid)

        def pull_rows(i, _):
            rows = pl.ds(pl.multiple_of(i * tile, tile), tile)
            grad = ref["pj"][r, rows, :]
            ref["gacc"][rows, :] = ref["gacc"][rows, :] + dot_t(grad, matrix(slot, 0, 3 * kh))
            for k, first in ((4, 0), (5, 2 * kh)):
                part_sum = row_sum(ref["pj"][r, rows, pl.ds(first, kh)].astype(F32))
                ref["sums"][pl.ds(k, 1), cols] = ref["sums"][pl.ds(k, 1), cols] + part_sum
            return 0

        @pl.when(step + 2 < s_.n_hid)
        def _():
            lax.fori_loop(0, s_.tiles, pull_rows, 0)

        loop_point(step, chunk_points, 5, 4, s_.n_hid)
        return 0

    lax.fori_loop(0, s_.n_hid, back_chunk, 0)
    stage_kept("a", 0, 2 + (s_.n_hid - 1) % 2)
    last_two = [(r, (s_.n_hid - 1 - r) % 2) for r in (1, 0)]

    def back_one(i):
        rows = pl.ds(i * tile, tile)
        scaled, inverse = scaled_rows(ref["xs"][rows, :].astype(F32))
        grad = ref["gacc"][rows, :]
        for r, slot in last_two:
            grad = grad + dot_t(ref["pj"][r, rows, :], matrix(slot, 0, 3 * kh))
            for k, first in ((4, 0), (5, 2 * kh)):
                cols = columns(block_of(r), kh)
                part_sum = row_sum(ref["pj"][r, rows, pl.ds(first, kh)].astype(F32))
                ref["sums"][pl.ds(k, 1), cols] = ref["sums"][pl.ds(k, 1), cols] + part_sum
        add_sum(0, grad * scaled)
        add_sum(1, grad)
        total = ref["facc"][rows, :] + norm_pull(grad, gain_row(0), scaled, inverse)
        ref["ct"][rows, :] = total.astype(BF16)

    def row_copy(i, r):
        source = ref["ct"].at[pl.ds(i * tile, tile), columns(block_of(r), kh)]
        return source, ref["grad_rows"].at[pl.ds(pl.multiple_of(h * n + i * tile, tile), tile)]

    def send_rows(blocks):
        for i in range(s_.tiles):
            for r in blocks:
                send("gt", i * s_.n_hid + r, *row_copy(i, r), peer(r))

    for i in range(s_.tiles):
        back_one(i)
    for k, (r, f) in enumerate(tree.m_units):
        for i in range(s_.fs // kh):
            ref["sums"][pl.ds(8 + 2 * f + i, 1), columns(block_of(r), kh)] = ref["hidden_sum"][
                k, :, pl.ds(i * kh, kh)
            ]
    for r in range(1, s_.n_hid):
        send("sum1", r, ref["sums"].at[:, columns(block_of(r), kh)], ref["sum1"].at[r], peer(r))
    send_rows(tree.near)
    for i in range(s_.tiles):
        local(41 + i, *row_copy(i, 0)).start()

    finals = [("m", 0), ("m", 1), ("a", 0), ("a", 1)]

    def final_loads(k, kind, f):
        slots = ref["z_g" + kind].at[f]
        room = ref["wa"].at[k % 2]
        if kind == "a":
            return [local(30, slots, room.at[:, 0, pl.ds(0, s_.half)])]
        out = [local(30, slots.at[pl.ds(0, s_.z)], room.at[:, 0])]
        if tree.far:
            out.append(local(31, slots.at[pl.ds(s_.z, len(tree.far))], room.at[pl.ds(0, len(tree.far)), 1]))
        return out

    def final_store(k, kind, f):
        if kind == "a":
            source = ref["facc"].at[pl.ds(k * s_.tb, s_.half), pl.ds(0, s_.wide)]
            return local(34 + k, source, ref["grad_a"].at[pl.ds(f * s_.half, s_.half)])
        return local(34 + k, ref["facc"].at[pl.ds(k * s_.tb, s_.tb), pl.ds(0, s_.wide)], ref["grad_m"].at[f])

    def final(k):
        kind, f = finals[k]
        for step in range(1, s_.z):
            arrived("zg" + kind, f * s_.z + step, z_slot(kind, f, step))
        if kind == "m":
            for i, r in enumerate(tree.far):
                arrived("fold", tree.m_pos[r, f], z_slot(kind, f, s_.z + i))
        for load in final_loads(k, kind, f):
            load.start()
        for load in final_loads(k, kind, f):
            load.wait()
        rows = pl.ds(0, s_.half if kind == "a" else s_.tb)
        total = ref["wa"][k % 2, 0, 0, rows].astype(F32)
        for step in range(1, s_.z):
            total = total + ref["wa"][k % 2, step, 0, rows].astype(F32)
        if kind == "m":
            for i in range(len(tree.far)):
                total = total + ref["wa"][k % 2, i, 1].astype(F32)
        ref["facc"][pl.ds(k * s_.tb, rows.size), pl.ds(0, s_.wide)] = total
        final_store(k, kind, f).start()

    def first_finals():
        final(0)
        final(1)

    def first_sums():
        total = ref["sums"][:, columns(h, kh)]
        for r in range(1, s_.n_hid):
            arrived("sum1", r, ref["sum1"].at[r])
            total = total + ref["sum1"][r]
        ref["sum2"][0] = total
        send("sum2", 0, ref["sum2"].at[0], ref["sum2"].at[1], sibling)

    def second_sums():
        arrived("sum2", 0, ref["sum2"].at[1])
        ref["sum3"][0] = ref["sum2"][0] + ref["sum2"][1]
        for step in range(1, s_.z):
            send("sum3", step, ref["sum3"].at[0], ref["sum3"].at[step], z_peer(step))

    feed_done = False
    for point in range(last_point, plan.end):
        units = [unit for verb, unit in plan.at.get(point, ()) if verb == "fetch"]
        if not feed_done and units and units[0][:2] == ("a", 0):
            first_finals()
            feed_done = True
        for verb, unit in plan.at.get(point, ()):
            if verb == "fetch" and unit == ("a", 0, 1):
                first_sums()
            (fetch if verb == "fetch" else finish)(unit)
        if ("a", 0, 1) in units:
            send_rows(tree.far)
            second_sums()
    if not feed_done:
        first_finals()

    final(2)
    final(3)
    total = ref["sum3"][0]
    for step in range(1, s_.z):
        arrived("sum3", step, ref["sum3"].at[step])
        total = total + ref["sum3"][step]
    ref["sum2"][2] = total
    small = local(2, ref["sum2"].at[2], ref["small"])
    small.start()

    small.wait()
    for k, (kind, f) in enumerate(finals):
        final_store(k, kind, f).wait()
    own_lo.wait()
    for holder in plan.holders:
        free_buffer(holder)
    for i in range(s_.tiles):
        local(41 + i, *row_copy(i, 0)).wait()
        for r in range(1, s_.n_hid):
            source, to = row_copy(i, r)
            arrived("gt", i * s_.n_hid + r, to)
            left("gt", i * s_.n_hid + r, source)
    for r in range(1, s_.n_hid):
        arrived("lo", r, out_rows("layer_out", h))
        left("ct", r, cot_rows(h))
        left("lo", r, cot_rows(h))
        left("sum1", r, ref["sum1"].at[r])
    left("sum2", 0, ref["sum2"].at[0])
    for step in range(1, s_.z):
        left("sum3", step, ref["sum3"].at[0])
    for r, f in tree.units:
        left("ac", tree.pos[r, f], a_part(r, f, c))
        if r:
            left("ax", tree.pos[r, f], a_part(r, f, c))
    for r, f in tree.m_units:
        left("mc", tree.m_pos[r, f], m_part(r, f, c))
    for r, f in tree.m_near:
        left("mx", tree.m_pos[r, f], m_part(r, f, c))
    for r, f in far_units:
        z_left("zf", tree.m_pos[r, f], m_block(r, f))
    for k in range(max(0, s_.n_hid - 2), s_.n_hid):
        stage_free("a", s_.n_hid - 1 - k, 2 + k % 2)


def scratch(size, tree):
    s_ = size
    units = len(tree.units)
    vmem = {
        "params_all": ((SMALL_ROWS, s_.d), F32),
        "xs": ((s_.n, s_.d), BF16),
        "ct": ((s_.n, s_.d), BF16),
        "nrm": ((s_.n, s_.d), BF16),
        "nrm_t": ((s_.d, s_.n), BF16),
        "n2": ((s_.n, s_.d), BF16),
        "n2_t": ((s_.d, s_.n), BF16),
        "ct_t": ((s_.z, 2, s_.tb, s_.n), BF16),
        "pj": ((s_.n_hid, s_.n, 3 * s_.kh), BF16),
        "probs": ((s_.n_hid, s_.pairs, s_.n, 2 * BLOCK), BF16),
        "att": ((s_.n_hid, s_.n, s_.kh), BF16),
        "scaled_two": ((s_.n, s_.d), BF16),
        "inverse_two": ((s_.n, 1), F32),
        "facc": ((s_.n, s_.d), F32),
        "gacc": ((s_.n, s_.d), F32),
        "wa": ((s_.n_hid, s_.z, 2, s_.tb, s_.wide), BF16),
        "out_in": ((s_.kh, s_.tb), BF16),
        "down_in": ((2 * s_.fs, s_.tb), BF16),
        "hid": ((s_.n, s_.fs), BF16),
        "gb": ((s_.n, s_.fs), BF16),
        "acc": ((WHOLE_BUFFERS + 1, s_.z, s_.tb, s_.wide), BF16),
        "tmp": ((s_.z, s_.tb, s_.wide), BF16),
        "hidden_bias": ((units, 1, s_.fs), F32),
        "hidden_sum": ((units, 1, s_.fs), F32),
        "sums": ((SMALL_ROWS, s_.d), F32),
        "sum1": ((s_.n_hid, SMALL_ROWS, s_.kh), F32),
        "sum2": ((3, SMALL_ROWS, s_.kh), F32),
        "sum3": ((s_.z, SMALL_ROWS, s_.kh), F32),
    }
    pairs = {
        "params": s_.n_hid,
        "za": s_.z,
        "zm": 2 * s_.z,
        "xs": s_.tiles * s_.n_hid,
        "ax": units,
        "ac": units,
        "mx": units,
        "mc": units,
        "ct": s_.n_hid,
        "sa": s_.n_hid,
        "sm": units,
        "ga": units,
        "gm": units,
        "fs": units,
        "zf": units * s_.z,
        "zfar": units * s_.z,
        "fold": units,
        "zga": 2 * s_.z,
        "zgm": 2 * s_.z,
        "lo": s_.n_hid,
        "gt": s_.tiles * s_.n_hid,
        "sum1": s_.n_hid,
        "sum2": 1,
        "sum3": s_.z,
    }
    out = {name: pltpu.VMEM(shape, kind) for name, (shape, kind) in vmem.items()}
    for name, count in pairs.items():
        out[name + "_s"] = pltpu.SemaphoreType.DMA((count,))
        out[name + "_r"] = pltpu.SemaphoreType.DMA((count,))
    out["local"] = pltpu.SemaphoreType.DMA((64,))
    out["wload"] = pltpu.SemaphoreType.DMA((s_.n_hid,))
    out["keep"] = pltpu.SemaphoreType.DMA((2,))
    return out


def finish_kernel(
    kh, fs, grad_ref, a_ref, m_ref, tokens_ref, middle_ref, coarse_ref, output_ref, up_ref, down_ref, attend_ref
):
    grad = grad_ref[...]
    rows = grad.shape[0]
    part = min(512, rows)
    by_4, by_16 = group_matrix(part, 4), group_matrix(part, 16)
    tokens_ref[...] = grad.astype(F32)
    for i in range(rows // part):
        piece = grad[i * part : i * part + part]
        middle_ref[pl.ds(i * part // 4, part // 4), :] = dot(by_4, piece)
        coarse_ref[pl.ds(i * part // 16, part // 16), :] = dot(by_16, piece)

    @pl.when(pl.program_id(0) == 0)
    def _():
        output_ref[...] = a_ref[:, pl.ds(3 * kh, kh)].T
        for k in range(3):
            attend_ref[k] = a_ref[:, pl.ds(k * kh, kh)]
        for f in (0, 1):
            up_ref[:, pl.ds(f * fs, fs)] = m_ref[f, :, pl.ds(0, fs)]
            down_ref[pl.ds(f * fs, fs), :] = m_ref[f, :, pl.ds(fs, fs)].T


def finish(size, grad, grad_a, grad_m):
    positions, features = grad.shape
    rows = min(2048, positions)
    tb, fs = size.tb, size.fs
    whole = [((features, tb), F32), ((tb, 2 * fs), F32), ((2 * fs, tb), F32), ((3, tb, features), F32)]
    return pl.pallas_call(
        functools.partial(finish_kernel, features, fs),
        grid=(positions // rows,),
        in_specs=[
            pl.BlockSpec((rows, features), lambda i: (i, 0)),
            pl.BlockSpec(grad_a.shape, lambda i: (0, 0)),
            pl.BlockSpec(grad_m.shape, lambda i: (0, 0, 0)),
        ],
        out_specs=[pl.BlockSpec((rows // t, features), lambda i: (i, 0)) for t in (1, 4, 16)]
        + [pl.BlockSpec(shape, lambda i, n=len(shape): (0,) * n) for shape, _ in whole],
        out_shape=[jax.ShapeDtypeStruct((positions // t, features), F32) for t in (1, 4, 16)]
        + [jax.ShapeDtypeStruct(*x) for x in whole],
        compiler_params=pltpu.CompilerParams(vmem_limit_bytes=60 * 2**20),
        name="token_gradients",
    )(grad, grad_a, grad_m)


def shards(
    tokens,
    middle_cond,
    coarse_cond,
    first_gain,
    first_shift,
    attend_weight,
    query_bias,
    value_bias,
    output_weight,
    mixer_bias,
    second_gain,
    second_shift,
    up_weight,
    hidden_bias,
    down_weight,
    down_bias,
    cotangent,
):
    positions, features = tokens.shape
    n_hid, n_tok = lax.axis_size("hid"), lax.axis_size("tok")
    d = features * n_hid
    ff = up_weight.shape[1] * n_hid
    size = Sizes(positions, features, d, ff, n_tok, n_hid)
    tree = Tree(n_hid)
    tb, fs, wide, z = size.tb, size.fs, size.wide, size.z
    vectors = (first_gain, first_shift, second_gain, second_shift, query_bias, value_bias, mixer_bias, down_bias)
    rows = [v.reshape(1, features) for v in vectors] + [hidden_bias.reshape(ff // d, features)]
    units = len(tree.units)
    outputs = {
        "layer_out": ((positions, features), BF16),
        "grad_rows": ((positions, features), BF16),
        "grad_a": ((tb, wide), F32),
        "grad_m": ((2, tb, wide), F32),
        "small": ((SMALL_ROWS, features), F32),
        "all_a": ((n_hid, z, 2, tb, wide), BF16),
        "all_m": ((units, z, 2, tb, wide), BF16),
        "own_ga": ((n_hid, z, tb, wide), BF16),
        "sib_ga": ((n_hid, z, tb, wide), BF16),
        "got_ga": ((units, z, size.half, wide), BF16),
        "own_gm": ((units, z, tb, wide), BF16),
        "sib_gm": ((units, z, tb, wide), BF16),
        "got_gm": ((units, z, tb, wide), BF16),
        "z_ga": ((2, z, size.half, wide), BF16),
        "z_gm": ((2, z + len(tree.far), tb, wide), BF16),
        "z_far": ((units, z, tb, wide), BF16),
    }
    hbm = pl.BlockSpec(memory_space=pltpu.HBM)
    results = pl.pallas_call(
        functools.partial(layer_kernel, size, tree),
        out_shape=[jax.ShapeDtypeStruct(*outputs[name]) for name in OUTPUTS],
        in_specs=[hbm] * (len(INPUTS) + len(rows)),
        out_specs=[hbm] * len(OUTPUTS),
        scratch_shapes=list(scratch(size, tree).values()),
        compiler_params=pltpu.CompilerParams(
            collective_id=0, has_side_effects=True, vmem_limit_bytes=63 * 2**20
        ),
        cost_estimate=pl.CostEstimate(flops=80 * 10**9, bytes_accessed=2 * 10**8, transcendentals=10**7),
        name="layer",
    )(
        tokens,
        middle_cond,
        coarse_cond,
        cotangent,
        attend_weight.transpose(1, 0, 2),
        output_weight,
        up_weight,
        down_weight,
        *rows,
    )
    layer_out, grad_rows, grad_a, grad_m, small = results[:5]
    grad_tokens, grad_middle, grad_coarse, grad_output, grad_up, grad_down, grad_attend = finish(
        size, grad_rows, grad_a, grad_m
    )
    tok = lax.axis_index("tok")
    share = features // n_tok
    mine = lax.dynamic_slice_in_dim(small[:8], tok * share, share, 1)
    hidden_share = fs * 2 // n_tok
    first = tok * hidden_share
    grad_hidden_bias = lax.dynamic_slice(
        small, (8 + first // features, lax.rem(first, features)), (1, hidden_share)
    ).reshape(hidden_share)
    return (
        layer_out,
        grad_tokens,
        grad_middle,
        grad_coarse,
        mine[0],
        mine[1],
        grad_attend.transpose(1, 0, 2),
        mine[4],
        mine[5],
        grad_output,
        mine[6],
        mine[2],
        mine[3],
        grad_up,
        grad_hidden_bias,
        grad_down,
        mine[7],
    )


def solution(mesh):
    return jax.shard_map(
        shards,
        mesh=mesh,
        in_specs=(
            P("tok", "hid"),
            P("tok", "hid"),
            P("tok", "hid"),
            P("hid"),
            P("hid"),
            P("tok", None, "hid"),
            P("hid"),
            P("hid"),
            P("hid", "tok"),
            P("hid"),
            P("hid"),
            P("hid"),
            P("tok", "hid"),
            P("hid"),
            P("hid", "tok"),
            P("hid"),
            P("tok", "hid"),
        ),
        out_specs=(
            P("tok", "hid"),
            P("tok", "hid"),
            P("tok", "hid"),
            P("tok", "hid"),
            P(("hid", "tok")),
            P(("hid", "tok")),
            P("tok", None, "hid"),
            P(("hid", "tok")),
            P(("hid", "tok")),
            P("hid", "tok"),
            P(("hid", "tok")),
            P(("hid", "tok")),
            P(("hid", "tok")),
            P("tok", "hid"),
            P(("hid", "tok")),
            P("hid", "tok"),
            P(("hid", "tok")),
        ),
        check_vma=False,
    )
```

```python
import functools

import jax
import jax.numpy as jnp
from jax import lax
from jax.experimental import pallas as pl
from jax.experimental.pallas import tpu as pltpu
from jax.sharding import PartitionSpec as P

HEAD = 64
BLOCK = 128
PAIR = 2 * HEAD
EPSILON = 1e-05
MESH = pl.DeviceIdType.MESH
BF16 = jnp.bfloat16
F32 = jnp.float32
SMALL_ROWS = 16
WHOLE_BUFFERS = 3
HALF_BUFFERS = 4


class Tree:
    def __init__(self, n_hid):
        self.n = n_hid
        self.bits = n_hid.bit_length() - 1
        units = [(r, f) for r in range(n_hid) for f in (0, 1)]
        self.units = sorted(units, key=lambda u: (u[0].bit_count(), len(self.children(*u)), u))
        self.pos = {u: k for k, u in enumerate(self.units)}
        self.near = [1 << b for b in range(self.bits)]
        self.far = [r for r in range(n_hid) if r.bit_count() > 1]
        first = [(1 << b, b % 2) for b in range(self.bits)]
        second = [(1 << b, 1 - b % 2) for b in range(self.bits)]
        self.m_near = first + second
        rest = [(r, f) for r in self.far for f in (0, 1)]
        self.m_units = [(0, 0), (0, 1)] + first + rest[:1] + second + rest[1:]
        self.m_pos = {u: k for k, u in enumerate(self.m_units)}

    def children(self, r, f):
        held = [b for b in range(self.bits) if r >> b & 1]
        free = [b for b in range(self.bits) if not r >> b & 1]
        if held:
            free = [b for b in free if (b < held[0] if f == 0 else b > held[-1])]
        return [(r | 1 << b, b) for b in free]

    def parent(self, r, f):
        held = [b for b in range(self.bits) if r >> b & 1]
        return held[0] if f == 0 else held[-1]


class Schedule:
    def __init__(self, done, kids, lag, last_point):
        self.at = {}
        self.turn = {}
        self.before = {}
        self.first = set()
        sent = {}
        seen = set()
        holders = {True: [None] * HALF_BUFFERS, False: [None] * (WHOLE_BUFFERS + 1)}
        turns = {True: -1, False: -1}
        waiting = sorted(done, key=lambda u: (u[0] != "a", done[u], len(kids[u])))
        held = None
        point = 0
        while waiting or held is not None:
            actions = []
            if held is not None:
                actions.append(("finish", held))
                sent[held] = point
                held = None
            for unit in waiting:
                if point <= done[unit] or any(k not in sent for k in kids[unit]):
                    continue
                if point < last_point and any(point < sent[k] + lag[unit[0]] for k in kids[unit]):
                    continue
                actions.append(("fetch", unit))
                held = unit
                pool = unit[0] == "a"
                size = HALF_BUFFERS if pool else WHOLE_BUFFERS + (turns[True] < 0)
                self.turn[unit] = k = turns[pool] = (turns[pool] + 1) % size
                self.before[unit] = holders[pool][k]
                holders[pool][k] = unit
                if pool and k == 2 and holders[False][-1]:
                    self.before[unit] = holders[False][-1]
                    holders[False][-1] = None
                if unit[:2] not in seen:
                    self.first.add(unit)
                seen.add(unit[:2])
                waiting.remove(unit)
                break
            if actions:
                self.at[point] = actions
            point += 1
        self.end = point
        self.holders = holders[True] + holders[False]


def dot(a, b):
    return jnp.dot(a, b, preferred_element_type=F32)


def dot_t(a, b):
    return lax.dot_general(a, b, (((1,), (1,)), ((), ())), preferred_element_type=F32)


def dot_l(a, b):
    return lax.dot_general(a, b, (((0,), (0,)), ((), ())), preferred_element_type=F32)


def repeat_matrix(rows, times):
    row = lax.broadcasted_iota(jnp.int32, (rows, rows // times), 0)
    column = lax.broadcasted_iota(jnp.int32, (rows, rows // times), 1) * times
    return ((row >= column) & (row < column + times)).astype(BF16)


def group_matrix(rows, times):
    row = lax.broadcasted_iota(jnp.int32, (rows // times, rows), 0) * times
    column = lax.broadcasted_iota(jnp.int32, (rows // times, rows), 1)
    return ((column >= row) & (column < row + times)).astype(BF16)


def scaled_rows(values):
    width = values.shape[1]
    average = jnp.sum(values, axis=1, keepdims=True) / width
    square = jnp.sum(values * values, axis=1, keepdims=True) / width
    inverse = lax.rsqrt(square - average * average + EPSILON)
    return (values - average) * inverse, inverse


def norm_pull(grad, gain, scaled, inverse):
    width = grad.shape[1]
    weighted = grad * gain
    mean = jnp.sum(weighted, axis=1, keepdims=True) / width
    along = jnp.sum(weighted * scaled, axis=1, keepdims=True) / width
    return inverse * (weighted - mean - scaled * along)


def row_sum(values):
    return jnp.sum(values, axis=0, keepdims=True)


def two_heads(values):
    low = lax.broadcasted_iota(jnp.int32, values.shape, 1) < HEAD
    zero = jnp.zeros_like(values)
    return jnp.concatenate([jnp.where(low, values, zero), jnp.where(low, zero, values)], axis=0)


def pick_heads(both):
    low = lax.broadcasted_iota(jnp.int32, (BLOCK, PAIR), 1) < HEAD
    return jnp.where(low, both[:BLOCK], both[BLOCK:])


INPUTS = ("tokens", "middle", "coarse", "cotangent", "attend_w", "output_w", "up_w", "down_w")
VECTORS = 8
OUTPUTS = (
    "layer_out",
    "grad_rows",
    "grad_a",
    "grad_m",
    "small",
    "all_a",
    "all_m",
    "own_ga",
    "sib_ga",
    "got_ga",
    "own_gm",
    "sib_gm",
    "got_gm",
    "z_ga",
    "z_gm",
    "z_far",
)


class Sizes:
    def __init__(self, positions, features, d, ff, n_tok, n_hid):
        self.d, self.n_hid, self.n_tok = d, n_hid, n_tok
        self.z = n_tok // 2
        self.n = positions // n_hid
        self.kh = features
        self.fs = ff // n_hid // 2
        self.tb = d // n_tok
        self.half = self.tb // 2
        self.wide = 4 * features
        self.vector_rows = ff // d
        self.pairs = features // PAIR
        self.tile = min(256, self.n)
        self.tiles = self.n // self.tile
        self.blocks = self.n // BLOCK
        self.positions = positions


def layer_kernel(size, tree, *refs):
    vectors = [f"vector_{k}" for k in range(VECTORS + 1)]
    names = list(INPUTS) + vectors + list(OUTPUTS) + list(scratch(size, tree))
    ref = dict(zip(names, refs, strict=True))
    s_ = size
    n_units = len(tree.units)
    tok, h = lax.axis_index("tok"), lax.axis_index("hid")
    z, c = tok // 2, lax.rem(tok, 2)

    def block_of(r):
        total = 0
        for b in range(tree.bits):
            total = total + lax.rem(h // (1 << b) + r // (1 << b), 2) * (1 << b)
        return total

    def peer(r):
        return (tok, block_of(r))

    sibling = (tok + 1 - 2 * c, h)

    def z_peer(step):
        return (lax.rem(z + step, s_.z) * 2 + c, h)

    def columns(j, width):
        return pl.ds(pl.multiple_of(j * width, width), width)

    def remote(name, index, src, dst, device):
        return pltpu.make_async_remote_copy(
            src_ref=src,
            dst_ref=dst,
            send_sem=ref[name + "_s"].at[index],
            recv_sem=ref[name + "_r"].at[index],
            device_id=device,
            device_id_type=MESH,
        )

    def send(name, index, src, dst, device):
        remote(name, index, src, dst, device).start()

    def arrived(name, index, dst):
        remote(name, index, dst, dst, sibling).wait_recv()

    def left(name, index, src):
        remote(name, index, src, src, sibling).wait_send()

    def local(index, src, dst):
        return pltpu.make_async_copy(src, dst, ref["local"].at[index])

    barrier = pltpu.get_barrier_semaphore()
    everyone = [peer(r) for r in range(1, s_.n_hid)] + [sibling]
    everyone += [z_peer(k) for k in range(1, s_.z)]
    for device in everyone:
        pl.semaphore_signal(barrier, inc=1, device_id=device, device_id_type=MESH)
    pl.semaphore_wait(barrier, len(everyone))

    def z_send(name, index, src, dst):
        for step in range(1, s_.z):
            send(name, index * s_.z + step, src, dst, z_peer(step))

    def z_arrived(name, index, dst):
        for step in range(1, s_.z):
            arrived(name, index * s_.z + step, dst)

    def z_left(name, index, src):
        for step in range(1, s_.z):
            left(name, index * s_.z + step, src)

    def a_part(r, f, core):
        return ref["all_a"].at[r, :, core, pl.ds(f * s_.half, s_.half)]

    def m_part(r, f, core):
        return ref["all_m"].at[tree.m_pos[r, f], :, core]

    part = {"a": a_part, "m": m_part}

    ref["sum2"][0] = jnp.zeros((SMALL_ROWS, s_.kh), F32)
    vector_loads = [
        local(44 + k, ref[name], ref["sum2"].at[0, pl.ds(k, s_.vector_rows if k == VECTORS else 1)])
        for k, name in enumerate(vectors)
    ]
    for copy in vector_loads:
        copy.start()
    kh, n, tile, fs = s_.kh, s_.n, s_.tile, s_.fs
    own_block = [ref["acc"].at[k, 0] for k in range(3)]
    own_loads = [local(1 + k, ref["attend_w"].at[k], own_block[0].at[:, pl.ds(k * kh, kh)]) for k in range(3)]
    own_loads.append(local(40, ref["output_w"], ref["out_in"]))
    for f in (0, 1):
        own_loads.append(local(41 + f, ref["up_w"].at[:, pl.ds(f * fs, fs)], own_block[1 + f].at[:, pl.ds(0, fs)]))
    own_loads.append(local(43, ref["down_w"], ref["down_in"]))
    for copy in own_loads:
        copy.start()
    for copy in vector_loads:
        copy.wait()
    own_params = local(0, ref["sum2"].at[0], ref["params_all"].at[:, columns(h, s_.kh)])
    own_params.start()
    for r in range(1, s_.n_hid):
        send("params", r, ref["sum2"].at[0], ref["params_all"].at[:, columns(h, s_.kh)], peer(r))

    def m_block(r, f):
        return ref["all_m"].at[tree.m_pos[r, f], z, c]

    far_units = [(r, f) for r in tree.far for f in (0, 1)]

    rows_m, rows_c = n // 4, n // 16
    loads = {}
    order = list(range(1, s_.n_hid)) + [0]
    for r in order:
        j = block_of(r)
        sources = (
            (ref["tokens"].at[columns(j, n)], ref["pj"].at[r, :, pl.ds(0, kh)]),
            (ref["middle"].at[columns(j, rows_m)], ref["pj"].at[r, pl.ds(0, rows_m), pl.ds(2 * kh, kh)]),
            (ref["coarse"].at[columns(j, rows_c)], ref["pj"].at[r, pl.ds(rows_m, rows_c), pl.ds(2 * kh, kh)]),
        )
        loads[r] = [local(4 + 3 * r + k, *pair) for k, pair in enumerate(sources)]
        for copy in loads[r]:
            copy.start()
    for copy in own_loads:
        copy.wait()
    ref["acc"][0, 0, :, pl.ds(3 * kh, kh)] = ref["out_in"][...].T
    z_send("za", 0, own_block[0], ref["all_a"].at[0, z, c])
    for f in (0, 1):
        ref["acc"][1 + f, 0, :, pl.ds(fs, fs)] = ref["down_in"][pl.ds(f * fs, fs), :].T
    for r, f in far_units:
        send("fs", tree.m_pos[r, f], own_block[1 + f], m_block(r, f), peer(r))
    own_places = [ref["all_a"].at[0, z, c], m_block(0, 0), m_block(0, 1)]
    own_out = [local(1 + k, own_block[k], place) for k, place in enumerate(own_places)]
    for store in own_out:
        store.start()
    repeat_4, repeat_16 = repeat_matrix(tile, 4), repeat_matrix(tile, 16)

    def xs_rows(i, j):
        return ref["xs"].at[pl.ds(i * tile, tile), columns(j, kh)]

    own_xs = []
    for i in range(s_.tiles):
        for r in order:
            if i == 0:
                for copy in loads[r]:
                    copy.wait()
            rows = pl.ds(i * tile, tile)
            middle = ref["pj"][r, pl.ds(i * (tile // 4), tile // 4), pl.ds(2 * kh, kh)]
            coarse = ref["pj"][r, pl.ds(rows_m + i * (tile // 16), tile // 16), pl.ds(2 * kh, kh)]
            total = ref["pj"][r, rows, pl.ds(0, kh)].astype(F32)
            total = total + dot(repeat_4, middle) + dot(repeat_16, coarse)
            ref["pj"][r, rows, pl.ds(kh, kh)] = total.astype(BF16)
            source = ref["pj"].at[r, rows, pl.ds(kh, kh)]
            if r:
                send("xs", i * s_.n_hid + r, source, xs_rows(i, h), peer(r))
            else:
                copy = local(4 + 3 * s_.n_hid + i, source, xs_rows(i, h))
                copy.start()
                own_xs.append(copy)


    def to_sibling(kind, r, f):
        k = tree.pos[r, f] if kind == "a" else tree.m_pos[r, f]
        send(kind + "c", k, part[kind](r, f, c), part[kind](r, f, c), sibling)

    def take_a(r, f):
        arrived("ax", tree.pos[r, f], a_part(r, f, c))
        for child, b in tree.children(r, f):
            send("ax", tree.pos[child, f], a_part(r, f, c), a_part(child, f, c), peer(1 << b))
        to_sibling("a", r, f)

    def take_m(r, f):
        if r in tree.far:
            z_arrived("zf", tree.m_pos[r, f], m_block(r, f))
        else:
            arrived("mx", tree.m_pos[r, f], m_part(r, f, c))
        to_sibling("m", r, f)

    def take_sibling(kind, r, f):
        k = tree.pos[r, f] if kind == "a" else tree.m_pos[r, f]
        arrived(kind + "c", k, part[kind](r, f, 1 - c))

    a_near = sorted([u for u in tree.units if u[0] in tree.near], key=lambda u: -len(tree.children(*u)))
    for store in own_out:
        store.wait()
    z_arrived("za", 0, ref["all_a"].at[0, z, c])
    for f in (0, 1):
        z_send("zm", f, own_block[1 + f], m_block(0, f))
    for r, f in far_units:
        arrived("fs", tree.m_pos[r, f], m_block(r, f))
        z_send("zf", tree.m_pos[r, f], m_block(r, f), m_block(r, f))
    for r, f in a_near:
        send("ax", tree.pos[r, f], a_part(0, f, c), a_part(r, f, c), peer(r))
    for f in (0, 1):
        to_sibling("a", 0, f)

    own_params.wait()
    for r in range(1, s_.n_hid):
        arrived("params", r, ref["params_all"].at[:, columns(h, kh)])
        left("params", r, ref["sum2"].at[0])

    def gain_row(k):
        return ref["params_all"][pl.ds(k, 1), :]

    for k, (r, f) in enumerate(tree.m_units):
        parts = [
            ref["params_all"][pl.ds(8 + 2 * f + i, 1), columns(block_of(r), kh)] for i in range(s_.fs // kh)
        ]
        ref["hidden_bias"][k] = jnp.concatenate(parts, axis=1)
        ref["hidden_sum"][k] = jnp.zeros((1, s_.fs), F32)
    ref["sums"][...] = jnp.zeros_like(ref["sums"])

    def add_sum(k, values):
        ref["sums"][pl.ds(k, 1), :] = ref["sums"][pl.ds(k, 1), :] + row_sum(values)

    for i in range(s_.tiles):
        own_xs[i].wait()
        for r in range(1, s_.n_hid):
            arrived("xs", i * s_.n_hid + r, xs_rows(i, h))
        rows = pl.ds(i * tile, tile)
        scaled, _ = scaled_rows(ref["xs"][rows, :].astype(F32))
        normed = (scaled * gain_row(0) + gain_row(1)).astype(BF16)
        ref["nrm"][rows, :] = normed
        ref["nrm_t"][:, rows] = normed.T

    for i in range(s_.tiles):
        for r in range(1, s_.n_hid):
            left("xs", i * s_.n_hid + r, xs_rows(i, h))

    def weight_load(slot, source):
        return pltpu.make_async_copy(source, ref["wa"].at[slot], ref["wload"].at[slot])

    def matrix(slot, first, width):
        return ref["wa"][slot, :, :, :, pl.ds(first, width)].reshape(s_.d, width)

    def put_rows(slot, zz, first, values):
        width = values.shape[1]
        ref["wa"][slot, pl.ds(zz * 2, 2), :, :, pl.ds(first, width)] = values.reshape(2, 2, s_.tb, width)

    def cot_rows(j):
        return ref["ct"].at[:, columns(j, kh)]

    own_ct = local(0, ref["cotangent"].at[columns(h, n)], cot_rows(h))

    def before_chunk(r):
        if r == 0:
            pass
        elif r.bit_count() == 1:
            if r == 1:
                for u, f in a_near:
                    take_a(u, f)
                own_ct.start()
                for k in range(1, s_.n_hid):
                    send("ct", k, ref["cotangent"].at[columns(block_of(k), n)], cot_rows(h), peer(k))
        else:
            for f in (0, 1):
                take_a(r, f)
        for f in (0, 1):
            take_sibling("a", r, f)
        load = weight_load(r, ref["all_a"].at[r])
        load.start()
        load.wait()

    causal_row = lax.broadcasted_iota(jnp.int32, (BLOCK, 2 * BLOCK), 0)
    causal_col = lax.rem(lax.broadcasted_iota(jnp.int32, (BLOCK, 2 * BLOCK), 1), BLOCK)
    allowed = causal_row >= causal_col

    def halves(values, f):
        return [f(values[:, :BLOCK]), f(values[:, BLOCK:])]

    def spread(pair):
        return jnp.concatenate([jnp.broadcast_to(v, (BLOCK, BLOCK)) for v in pair], axis=1)

    def row_max(v):
        return jnp.max(v, axis=1, keepdims=True)

    def row_add(v):
        return jnp.sum(v, axis=1, keepdims=True)

    def attend_chunk(r):
        for k in range(s_.n_hid):
            pl.when(r == k)(functools.partial(before_chunk, k))
        cols = columns(block_of(r), kh)
        bias = jnp.concatenate(
            [ref["params_all"][4:5, cols], jnp.zeros((1, kh), F32), ref["params_all"][5:6, cols]], axis=1
        )

        def project(i, _):
            rows = pl.ds(pl.multiple_of(i * tile, tile), tile)
            values = dot(ref["nrm"][rows, :], matrix(r, 0, 3 * kh)) + bias
            ref["pj"][r, rows, :] = values.astype(BF16)
            return 0

        lax.fori_loop(0, s_.tiles, project, 0)

        def attend(i, _):
            rows = pl.ds(pl.multiple_of(i * BLOCK, BLOCK), BLOCK)
            for p in range(s_.pairs):
                query, key, value = (ref["pj"][r, rows, pl.ds(k * kh + p * PAIR, PAIR)] for k in range(3))
                logits = jnp.where(allowed, dot_t(query, two_heads(key)) * HEAD ** (-0.5), -1e30)
                powers = jnp.exp(logits - spread(halves(logits, row_max)))
                shares = [1.0 / v for v in halves(powers, row_add)]
                attention = (powers * spread(shares)).astype(BF16)
                ref["probs"][r, p, rows, :] = attention
                out = dot(attention, two_heads(value))
                ref["att"][r, rows, pl.ds(p * PAIR, PAIR)] = out.astype(BF16)
            return 0

        def attend_two(i, _):
            attend(2 * i, 0)
            return attend(2 * i + 1, 0)

        lax.fori_loop(0, s_.blocks // 2, attend_two, 0)

    lax.fori_loop(0, s_.n_hid, lambda r, _: (attend_chunk(r), 0)[1], 0)

    for f in (0, 1):
        z_arrived("zm", f, m_block(0, f))
    for f in (0, 1):
        to_sibling("m", 0, f)
    z_left("za", 0, own_block[0])
    for f in (0, 1):
        z_left("zm", f, own_block[1 + f])
    for r, f in far_units:
        left("fs", tree.m_pos[r, f], own_block[1 + f])

    def mix(i, _):
        rows = pl.ds(pl.multiple_of(i * tile, tile), tile)
        total = ref["xs"][rows, :].astype(F32) + gain_row(6)
        for r in range(s_.n_hid):
            total = total + dot_t(ref["att"][r, rows, :], matrix(r, 3 * kh, kh))
        ref["facc"][rows, :] = total + gain_row(7)
        scaled, inverse = scaled_rows(total)
        ref["scaled_two"][rows, :] = scaled.astype(BF16)
        ref["inverse_two"][rows, :] = inverse
        normed = (scaled * gain_row(2) + gain_row(3)).astype(BF16)
        ref["n2"][rows, :] = normed
        return 0

    lax.fori_loop(0, s_.tiles, mix, 0)

    own_ct.wait()
    for k in range(1, s_.n_hid):
        arrived("ct", k, cot_rows(h))
    for r, f in tree.m_near:
        send("mx", tree.m_pos[r, f], m_part(0, f, c), m_part(r, f, c), peer(r))
    for i in range(s_.tiles):
        rows = pl.ds(i * tile, tile)
        ref["n2_t"][:, rows] = ref["n2"][rows, :].T
        upstream = ref["ct"][rows, :]
        ref["ct_t"][:, :, :, rows] = upstream.T.reshape(s_.z, 2, s_.tb, tile)
        add_sum(7, upstream.astype(F32))
        ref["gacc"][rows, :] = jnp.zeros((tile, s_.d), F32)

    mlp_points = 3 * n_units
    chunk_points = mlp_points + 2
    last_point = chunk_points + 5 * s_.n_hid
    done, kids = {}, {}
    for k, (r, f) in enumerate(tree.m_units):
        done["m", r, f] = 3 * k + 2
        kids["m", r, f] = [("m", u, f) for u in tree.near] if r == 0 else []
        if r == 0:
            done["m", r, f] = mlp_points - 1
    for r, f in far_units:
        done["fold", r, f] = 0
        kids["fold", r, f] = [("m", r, f)]
    for r in range(s_.n_hid):
        for f in (0, 1):
            done["a", r, f] = chunk_points + 5 * (s_.n_hid - 1 - r) + 4
            kids["a", r, f] = [("a", child, f) for child, _ in tree.children(r, f)]
    plan = Schedule(done, kids, {"m": 14, "a": 7, "fold": 10}, last_point)

    def place(kind, r, f):
        return tree.pos[r, f] if kind == "a" else tree.m_pos[r, f]

    def own_grad(kind, r, f):
        if kind == "a":
            return ref["own_ga"].at[r, :, pl.ds(f * s_.half, s_.half)]
        return ref["own_gm"].at[tree.m_pos[r, f]]

    def sib_grad(kind, r, f):
        if kind == "a":
            return ref["sib_ga"].at[r, :, pl.ds(f * s_.half, s_.half)]
        return ref["sib_gm"].at[tree.m_pos[r, f]]

    def got_grad(kind, r, f):
        return ref["got_g" + kind].at[place(kind, r, f)]

    def part_of(whole, kind):
        return whole.at[:, pl.ds(0, s_.half if kind == "a" else s_.tb)]

    def spare(first, rows):
        return ref["ct_t"].at[:, first, rows, pl.ds(0, s_.wide)]

    def sum_buffer(unit):
        k = plan.turn[unit]
        if unit[0] != "a":
            return ref["acc"].at[k]
        rows = pl.ds(k % 2 * s_.half, s_.half)
        return spare(1, rows) if k < 2 else ref["acc"].at[WHOLE_BUFFERS, :, rows]

    def z_slot(kind, f, step):
        return ref["z_g" + kind].at[f, step]

    def scattered(kind, r, f):
        if r == 0:
            return "zg" + kind, f * s_.z, ref["z_g" + kind].at[f]
        return "zfar", tree.m_pos[r, f] * s_.z, ref["z_far"].at[tree.m_pos[r, f]]

    def scatters(kind, r):
        return r == 0 or (kind == "m" and r in tree.far)

    def free_buffer(holder):
        if holder is None:
            return
        kind, r, f = holder
        source = sum_buffer(holder)
        if kind == "fold":
            left("fold", tree.m_pos[r, f], source.at[0])
        elif scatters(kind, r):
            name, first, _ = scattered(kind, r, f)
            for step in range(1, s_.z):
                left(name, first + step, source.at[0])
        else:
            left("g" + kind, place(kind, r, f), source)

    def fetches(unit):
        kind, r, f = unit
        if kind == "fold":
            return [(30, ref["z_far"].at[tree.m_pos[r, f]], sum_buffer(unit))]
        out = [(30, own_grad(*unit), sum_buffer(unit))]
        out.append((31, sib_grad(*unit), part_of(ref["tmp"], kind)))
        if kids[unit]:
            out.append((32, got_grad(*kids[unit][0]), part_of(spare(0, pl.ds(0, s_.tb)), kind)))
        return out

    def fetch(unit):
        kind, r, f = unit
        free_buffer(plan.before[unit])
        if kind == "fold":
            for step in range(1, s_.z):
                name, first, slots = scattered("m", r, f)
                arrived(name, first + step, slots.at[step])
        elif kind == "m" or unit in plan.first:
            slot = tree.m_pos[r, f] if kind == "m" else r
            arrived("s" + kind, slot, ref["sib_g" + kind].at[slot])
        if kind != "fold":
            for kid in kids[unit][:1]:
                arrived("g" + kind, place(*kid), got_grad(*kid))
        for item in fetches(unit):
            local(*item).start()

    def finish(unit):
        kind, r, f = unit
        for item in fetches(unit):
            local(*item).wait()
        acc, tmp, more = sum_buffer(unit), part_of(ref["tmp"], kind), part_of(spare(0, pl.ds(0, s_.tb)), kind)
        if kind == "fold":
            total = acc[0].astype(F32)
            for zz in range(1, s_.z):
                total = total + acc[zz].astype(F32)
            acc[0] = total.astype(BF16)
            slot = ref["z_gm"].at[f, s_.z + tree.far.index(r)]
            send("fold", tree.m_pos[r, f], acc.at[0], slot, peer(r))
            return
        for zz in range(s_.z):
            total = acc[zz].astype(F32) + tmp[zz].astype(F32)
            if kids[unit]:
                total = total + more[zz].astype(F32)
            acc[zz] = total.astype(BF16)
        for kid in kids[unit][1:]:
            source = got_grad(*kid)
            arrived("g" + kind, place(*kid), source)
            copy = local(36, source, more)
            copy.start()
            copy.wait()
            for zz in range(s_.z):
                acc[zz] = (acc[zz].astype(F32) + more[zz].astype(F32)).astype(BF16)
        if scatters(kind, r):
            name, first, slots = scattered(kind, r, f)
            keep = local(40, acc.at[z], slots.at[0])
            keep.start()
            for step in range(1, s_.z):
                to = lax.rem(z + step, s_.z)
                send(name, first + step, acc.at[to], slots.at[step], z_peer(step))
            keep.wait()
        else:
            to = r if kind == "m" else 1 << tree.parent(r, f)
            send("g" + kind, place(kind, r, f), acc, got_grad(kind, r, f), peer(to))

    def act(point):
        for verb, unit in plan.at.get(point, ()):
            (fetch if verb == "fetch" else finish)(unit)

    def loop_point(step, first, stride, offset, count):
        for k in range(count):
            if first + stride * k + offset in plan.at:
                pl.when(step == k)(functools.partial(act, first + stride * k + offset))

    def stage_copies(kind, index, slot):
        own = ref["own_g" + kind].at[index]
        theirs = ref["sib_g" + kind].at[index]
        keep = pltpu.make_async_copy(ref["wa"].at[slot, :, c], own, ref["keep"].at[slot - 2])
        give = pltpu.make_async_remote_copy(
            src_ref=ref["wa"].at[slot, :, 1 - c],
            dst_ref=theirs,
            send_sem=ref["s" + kind + "_s"].at[index],
            recv_sem=ref["s" + kind + "_r"].at[index],
            device_id=sibling,
            device_id_type=MESH,
        )
        return keep, give

    def stage_out(kind, index, slot):
        for copy in stage_copies(kind, index, slot):
            copy.start()

    def stage_kept(kind, index, slot):
        stage_copies(kind, index, slot)[0].wait()

    def stage_free(kind, index, slot):
        stage_copies(kind, index, slot)[1].wait_send()

    for k in (0, 1):
        take_sibling("m", *tree.m_units[k])
    weight_load(0, ref["all_m"].at[0]).start()
    big = min(512, n)
    gelu_scale = (2.0 / jnp.pi) ** 0.5

    def feed(step, _):
        slot = lax.rem(step, 2)
        weight_load(slot, ref["all_m"].at[step]).wait()

        def rows_of(i, _):
            rows = pl.ds(pl.multiple_of(i * big, big), big)
            up, down = matrix(slot, 0, fs), matrix(slot, fs, fs)
            before = dot(ref["n2"][rows, :], up) + ref["hidden_bias"][step]
            square = before * before
            bent = jnp.tanh(before * (gelu_scale + (gelu_scale * 0.044715) * square))
            share = 0.5 + 0.5 * bent
            hidden = (before * share).astype(BF16)
            slope = share + 0.5 * before * (1.0 - bent * bent) * (
                gelu_scale + (3.0 * gelu_scale * 0.044715) * square
            )
            grad_before = (dot(ref["ct"][rows, :], down) * slope).astype(BF16)
            ref["hid"][rows, :] = hidden
            ref["gb"][rows, :] = grad_before
            ref["facc"][rows, :] = ref["facc"][rows, :] + dot_t(hidden, down)
            ref["gacc"][rows, :] = ref["gacc"][rows, :] + dot_t(grad_before, up)
            ref["hidden_sum"][step] = ref["hidden_sum"][step] + row_sum(grad_before.astype(F32))
            return 0

        lax.fori_loop(0, n // big // 2, rows_of, 0)

        @pl.when(step >= 1)
        def _():
            stage_kept("m", step - 1, 3 - slot)

        loop_point(step, 0, 3, 0, n_units)
        lax.fori_loop(n // big // 2, n // big, rows_of, 0)

        for k in range(1, n_units - 1, 2):

            @pl.when(step == k)
            def _(k=k):
                for unit in tree.m_units[k + 1 : k + 3]:
                    take_m(*unit)


        loop_point(step, 0, 3, 1, n_units)
        stage = 2 + slot

        @pl.when(step >= 2)
        def _():
            stage_free("m", step - 2, stage)

        def grads(zz, _):
            rows = pl.ds(pl.multiple_of(zz * (4 * s_.tb), 4 * s_.tb), 4 * s_.tb)
            put_rows(stage, zz, 0, dot(ref["n2_t"][rows, :], ref["gb"][...]).astype(BF16))
            upstream = ref["ct_t"][pl.ds(zz * 2, 2)].reshape(4 * s_.tb, n)
            put_rows(stage, zz, fs, dot(upstream, ref["hid"][...]).astype(BF16))
            return 0

        lax.fori_loop(0, s_.z // 4, grads, 0)
        for k in range(n_units - 1):

            def load_next(k=k):
                if k:
                    take_sibling("m", *tree.m_units[k + 1])
                weight_load((k + 1) % 2, ref["all_m"].at[k + 1]).start()

            pl.when(step == k)(load_next)
        lax.fori_loop(s_.z // 4, s_.z // 2, grads, 0)
        stage_out("m", step, stage)
        loop_point(step, 0, 3, 2, n_units)
        return 0

    lax.fori_loop(0, n_units, feed, 0)

    stage_kept("m", n_units - 1, 2 + (n_units - 1) % 2)
    act(mlp_points)
    weight_load(0, ref["all_a"].at[s_.n_hid - 1]).start()

    def back_two(i, _):
        rows = pl.ds(pl.multiple_of(i * tile, tile), tile)
        ref["n2"][rows, :] = ref["facc"][rows, :].astype(BF16)
        scaled, inverse = ref["scaled_two"][rows, :].astype(F32), ref["inverse_two"][rows, :]
        grad = ref["gacc"][rows, :]
        add_sum(2, grad * scaled)
        add_sum(3, grad)
        grad = ref["ct"][rows, :].astype(F32) + norm_pull(grad, gain_row(2), scaled, inverse)
        mixed = grad.astype(BF16)
        add_sum(6, mixed.astype(F32))
        ref["facc"][rows, :] = grad
        ref["gacc"][rows, :] = jnp.zeros((tile, s_.d), F32)
        ref["nrm"][rows, :] = mixed
        return 0

    lax.fori_loop(0, s_.tiles, back_two, 0)

    def out_rows(name, j):
        return ref[name].at[columns(j, n)]

    for i in range(s_.tiles):
        rows = pl.ds(i * tile, tile)
        ref["n2_t"][:, rows] = ref["nrm"][rows, :].T
    act(mlp_points + 1)
    for r in range(1, s_.n_hid):
        send("lo", r, ref["n2"].at[:, columns(block_of(r), kh)], out_rows("layer_out", h), peer(r))
    own_lo = local(0, ref["n2"].at[:, columns(h, kh)], out_rows("layer_out", h))
    own_lo.start()
    for k in range(n_units - 2, n_units):
        stage_free("m", k, 2 + k % 2)

    def back_chunk(step, _):
        r = s_.n_hid - 1 - step
        slot = lax.rem(step, 2)
        stage = 2 + slot
        weight_load(slot, ref["all_a"].at[r]).wait()

        @pl.when(step + 1 < s_.n_hid)
        def _():
            weight_load(1 - slot, ref["all_a"].at[lax.rem(2 * s_.n_hid - 2 - step, s_.n_hid)]).start()

        def pull_out(i, _):
            rows = pl.ds(pl.multiple_of(i * tile, tile), tile)
            ref["hid"][rows, pl.ds(0, kh)] = dot(ref["nrm"][rows, :], matrix(slot, 3 * kh, kh)).astype(BF16)
            return 0

        lax.fori_loop(0, s_.tiles, pull_out, 0)

        @pl.when(step >= 1)
        def _():
            stage_kept("a", r + 1, 3 - slot)

        loop_point(step, chunk_points, 5, 0, s_.n_hid)

        def pull_attention(i, _):
            rows = pl.ds(pl.multiple_of(i * BLOCK, BLOCK), BLOCK)
            for p in range(s_.pairs):
                query, key, value = (ref["pj"][r, rows, pl.ds(k * kh + p * PAIR, PAIR)] for k in range(3))
                grad = ref["hid"][rows, pl.ds(p * PAIR, PAIR)]
                attention = ref["probs"][r, p, rows, :]
                weights = attention.astype(F32)
                grad_attention = dot_t(grad, two_heads(value))
                shares = zip(halves(weights * grad_attention, row_add), halves(weights, row_add), strict=True)
                centre = spread([part / whole for part, whole in shares])
                grad_scores = (weights * (grad_attention - centre) * HEAD ** (-0.5)).astype(BF16)
                grad_query = dot(grad_scores, two_heads(key))
                grad_key = pick_heads(dot_l(grad_scores, query))
                grad_value = pick_heads(dot_l(attention, grad))
                for k, values in enumerate((grad_query, grad_key, grad_value)):
                    ref["pj"][r, rows, pl.ds(k * kh + p * PAIR, PAIR)] = values.astype(BF16)
            return 0

        def pull_two(i, _):
            pull_attention(2 * i, 0)
            return pull_attention(2 * i + 1, 0)

        lax.fori_loop(0, s_.blocks // 4, pull_two, 0)
        loop_point(step, chunk_points, 5, 1, s_.n_hid)
        lax.fori_loop(s_.blocks // 4, s_.blocks // 2, pull_two, 0)
        loop_point(step, chunk_points, 5, 2, s_.n_hid)

        @pl.when(step >= 2)
        def _():
            stage_free("a", r + 2, stage)

        cols = columns(block_of(r), kh)

        def grads(zz, _):
            rows = pl.ds(pl.multiple_of(zz * (4 * s_.tb), 4 * s_.tb), 4 * s_.tb)
            put_rows(stage, zz, 0, dot(ref["nrm_t"][rows, :], ref["pj"][r]).astype(BF16))
            put_rows(stage, zz, 3 * kh, dot(ref["n2_t"][rows, :], ref["att"][r]).astype(BF16))
            return 0

        lax.fori_loop(0, s_.z // 2, grads, 0)
        stage_out("a", r, stage)
        loop_point(step, chunk_points, 5, 3, s_.n_hid)

        def pull_rows(i, _):
            rows = pl.ds(pl.multiple_of(i * tile, tile), tile)
            grad = ref["pj"][r, rows, :]
            ref["gacc"][rows, :] = ref["gacc"][rows, :] + dot_t(grad, matrix(slot, 0, 3 * kh))
            for k, first in ((4, 0), (5, 2 * kh)):
                part_sum = row_sum(ref["pj"][r, rows, pl.ds(first, kh)].astype(F32))
                ref["sums"][pl.ds(k, 1), cols] = ref["sums"][pl.ds(k, 1), cols] + part_sum
            return 0

        @pl.when(step + 2 < s_.n_hid)
        def _():
            lax.fori_loop(0, s_.tiles, pull_rows, 0)

        loop_point(step, chunk_points, 5, 4, s_.n_hid)
        return 0

    lax.fori_loop(0, s_.n_hid, back_chunk, 0)
    stage_kept("a", 0, 2 + (s_.n_hid - 1) % 2)
    last_two = [(r, (s_.n_hid - 1 - r) % 2) for r in (1, 0)]

    def back_one(i):
        rows = pl.ds(i * tile, tile)
        scaled, inverse = scaled_rows(ref["xs"][rows, :].astype(F32))
        grad = ref["gacc"][rows, :]
        for r, slot in last_two:
            grad = grad + dot_t(ref["pj"][r, rows, :], matrix(slot, 0, 3 * kh))
            for k, first in ((4, 0), (5, 2 * kh)):
                cols = columns(block_of(r), kh)
                part_sum = row_sum(ref["pj"][r, rows, pl.ds(first, kh)].astype(F32))
                ref["sums"][pl.ds(k, 1), cols] = ref["sums"][pl.ds(k, 1), cols] + part_sum
        add_sum(0, grad * scaled)
        add_sum(1, grad)
        total = ref["facc"][rows, :] + norm_pull(grad, gain_row(0), scaled, inverse)
        ref["ct"][rows, :] = total.astype(BF16)

    def row_copy(i, r):
        source = ref["ct"].at[pl.ds(i * tile, tile), columns(block_of(r), kh)]
        return source, ref["grad_rows"].at[pl.ds(pl.multiple_of(h * n + i * tile, tile), tile)]

    def send_rows(blocks):
        for i in range(s_.tiles):
            for r in blocks:
                send("gt", i * s_.n_hid + r, *row_copy(i, r), peer(r))

    for i in range(s_.tiles):
        back_one(i)
    for k, (r, f) in enumerate(tree.m_units):
        for i in range(s_.fs // kh):
            ref["sums"][pl.ds(8 + 2 * f + i, 1), columns(block_of(r), kh)] = ref["hidden_sum"][
                k, :, pl.ds(i * kh, kh)
            ]
    for r in range(1, s_.n_hid):
        send("sum1", r, ref["sums"].at[:, columns(block_of(r), kh)], ref["sum1"].at[r], peer(r))
    send_rows(tree.near)
    for i in range(s_.tiles):
        local(41 + i, *row_copy(i, 0)).start()

    finals = [("m", 0), ("m", 1), ("a", 0), ("a", 1)]

    def final_loads(k, kind, f):
        slots = ref["z_g" + kind].at[f]
        room = ref["wa"].at[k % 2]
        if kind == "a":
            return [local(30, slots, room.at[:, 0, pl.ds(0, s_.half)])]
        out = [local(30, slots.at[pl.ds(0, s_.z)], room.at[:, 0])]
        if tree.far:
            out.append(local(31, slots.at[pl.ds(s_.z, len(tree.far))], room.at[pl.ds(0, len(tree.far)), 1]))
        return out

    def final_store(k, kind, f):
        if kind == "a":
            source = ref["facc"].at[pl.ds(k * s_.tb, s_.half), pl.ds(0, s_.wide)]
            return local(34 + k, source, ref["grad_a"].at[pl.ds(f * s_.half, s_.half)])
        return local(34 + k, ref["facc"].at[pl.ds(k * s_.tb, s_.tb), pl.ds(0, s_.wide)], ref["grad_m"].at[f])

    def final(k):
        kind, f = finals[k]
        for step in range(1, s_.z):
            arrived("zg" + kind, f * s_.z + step, z_slot(kind, f, step))
        if kind == "m":
            for i, r in enumerate(tree.far):
                arrived("fold", tree.m_pos[r, f], z_slot(kind, f, s_.z + i))
        for load in final_loads(k, kind, f):
            load.start()
        for load in final_loads(k, kind, f):
            load.wait()
        rows = pl.ds(0, s_.half if kind == "a" else s_.tb)
        total = ref["wa"][k % 2, 0, 0, rows].astype(F32)
        for step in range(1, s_.z):
            total = total + ref["wa"][k % 2, step, 0, rows].astype(F32)
        if kind == "m":
            for i in range(len(tree.far)):
                total = total + ref["wa"][k % 2, i, 1].astype(F32)
        ref["facc"][pl.ds(k * s_.tb, rows.size), pl.ds(0, s_.wide)] = total
        final_store(k, kind, f).start()

    def first_finals():
        final(0)
        final(1)

    def first_sums():
        total = ref["sums"][:, columns(h, kh)]
        for r in range(1, s_.n_hid):
            arrived("sum1", r, ref["sum1"].at[r])
            total = total + ref["sum1"][r]
        ref["sum2"][0] = total
        send("sum2", 0, ref["sum2"].at[0], ref["sum2"].at[1], sibling)

    def second_sums():
        arrived("sum2", 0, ref["sum2"].at[1])
        ref["sum3"][0] = ref["sum2"][0] + ref["sum2"][1]
        for step in range(1, s_.z):
            send("sum3", step, ref["sum3"].at[0], ref["sum3"].at[step], z_peer(step))

    feed_done = False
    for point in range(last_point, plan.end):
        units = [unit for verb, unit in plan.at.get(point, ()) if verb == "fetch"]
        if not feed_done and units and units[0][:2] == ("a", 0):
            first_finals()
            feed_done = True
        for verb, unit in plan.at.get(point, ()):
            if verb == "fetch" and unit == ("a", 0, 1):
                first_sums()
            (fetch if verb == "fetch" else finish)(unit)
        if ("a", 0, 1) in units:
            send_rows(tree.far)
            second_sums()
    if not feed_done:
        first_finals()

    final(2)
    final(3)
    total = ref["sum3"][0]
    for step in range(1, s_.z):
        arrived("sum3", step, ref["sum3"].at[step])
        total = total + ref["sum3"][step]
    ref["sum2"][2] = total
    small = local(2, ref["sum2"].at[2], ref["small"])
    small.start()

    small.wait()
    for k, (kind, f) in enumerate(finals):
        final_store(k, kind, f).wait()
    own_lo.wait()
    for holder in plan.holders:
        free_buffer(holder)
    for i in range(s_.tiles):
        local(41 + i, *row_copy(i, 0)).wait()
        for r in range(1, s_.n_hid):
            source, to = row_copy(i, r)
            arrived("gt", i * s_.n_hid + r, to)
            left("gt", i * s_.n_hid + r, source)
    for r in range(1, s_.n_hid):
        arrived("lo", r, out_rows("layer_out", h))
        left("ct", r, cot_rows(h))
        left("lo", r, cot_rows(h))
        left("sum1", r, ref["sum1"].at[r])
    left("sum2", 0, ref["sum2"].at[0])
    for step in range(1, s_.z):
        left("sum3", step, ref["sum3"].at[0])
    for r, f in tree.units:
        left("ac", tree.pos[r, f], a_part(r, f, c))
        if r:
            left("ax", tree.pos[r, f], a_part(r, f, c))
    for r, f in tree.m_units:
        left("mc", tree.m_pos[r, f], m_part(r, f, c))
    for r, f in tree.m_near:
        left("mx", tree.m_pos[r, f], m_part(r, f, c))
    for r, f in far_units:
        z_left("zf", tree.m_pos[r, f], m_block(r, f))
    for k in range(max(0, s_.n_hid - 2), s_.n_hid):
        stage_free("a", s_.n_hid - 1 - k, 2 + k % 2)


def scratch(size, tree):
    s_ = size
    units = len(tree.units)
    vmem = {
        "params_all": ((SMALL_ROWS, s_.d), F32),
        "xs": ((s_.n, s_.d), BF16),
        "ct": ((s_.n, s_.d), BF16),
        "nrm": ((s_.n, s_.d), BF16),
        "nrm_t": ((s_.d, s_.n), BF16),
        "n2": ((s_.n, s_.d), BF16),
        "n2_t": ((s_.d, s_.n), BF16),
        "ct_t": ((s_.z, 2, s_.tb, s_.n), BF16),
        "pj": ((s_.n_hid, s_.n, 3 * s_.kh), BF16),
        "probs": ((s_.n_hid, s_.pairs, s_.n, 2 * BLOCK), BF16),
        "att": ((s_.n_hid, s_.n, s_.kh), BF16),
        "scaled_two": ((s_.n, s_.d), BF16),
        "inverse_two": ((s_.n, 1), F32),
        "facc": ((s_.n, s_.d), F32),
        "gacc": ((s_.n, s_.d), F32),
        "wa": ((s_.n_hid, s_.z, 2, s_.tb, s_.wide), BF16),
        "out_in": ((s_.kh, s_.tb), BF16),
        "down_in": ((2 * s_.fs, s_.tb), BF16),
        "hid": ((s_.n, s_.fs), BF16),
        "gb": ((s_.n, s_.fs), BF16),
        "acc": ((WHOLE_BUFFERS + 1, s_.z, s_.tb, s_.wide), BF16),
        "tmp": ((s_.z, s_.tb, s_.wide), BF16),
        "hidden_bias": ((units, 1, s_.fs), F32),
        "hidden_sum": ((units, 1, s_.fs), F32),
        "sums": ((SMALL_ROWS, s_.d), F32),
        "sum1": ((s_.n_hid, SMALL_ROWS, s_.kh), F32),
        "sum2": ((3, SMALL_ROWS, s_.kh), F32),
        "sum3": ((s_.z, SMALL_ROWS, s_.kh), F32),
    }
    pairs = {
        "params": s_.n_hid,
        "za": s_.z,
        "zm": 2 * s_.z,
        "xs": s_.tiles * s_.n_hid,
        "ax": units,
        "ac": units,
        "mx": units,
        "mc": units,
        "ct": s_.n_hid,
        "sa": s_.n_hid,
        "sm": units,
        "ga": units,
        "gm": units,
        "fs": units,
        "zf": units * s_.z,
        "zfar": units * s_.z,
        "fold": units,
        "zga": 2 * s_.z,
        "zgm": 2 * s_.z,
        "lo": s_.n_hid,
        "gt": s_.tiles * s_.n_hid,
        "sum1": s_.n_hid,
        "sum2": 1,
        "sum3": s_.z,
    }
    out = {name: pltpu.VMEM(shape, kind) for name, (shape, kind) in vmem.items()}
    for name, count in pairs.items():
        out[name + "_s"] = pltpu.SemaphoreType.DMA((count,))
        out[name + "_r"] = pltpu.SemaphoreType.DMA((count,))
    out["local"] = pltpu.SemaphoreType.DMA((64,))
    out["wload"] = pltpu.SemaphoreType.DMA((s_.n_hid,))
    out["keep"] = pltpu.SemaphoreType.DMA((2,))
    return out


def finish_kernel(
    kh, fs, grad_ref, a_ref, m_ref, tokens_ref, middle_ref, coarse_ref, output_ref, up_ref, down_ref, attend_ref
):
    grad = grad_ref[...]
    rows = grad.shape[0]
    part = min(512, rows)
    by_4, by_16 = group_matrix(part, 4), group_matrix(part, 16)
    tokens_ref[...] = grad.astype(F32)
    for i in range(rows // part):
        piece = grad[i * part : i * part + part]
        middle_ref[pl.ds(i * part // 4, part // 4), :] = dot(by_4, piece)
        coarse_ref[pl.ds(i * part // 16, part // 16), :] = dot(by_16, piece)

    @pl.when(pl.program_id(0) == 0)
    def _():
        output_ref[...] = a_ref[:, pl.ds(3 * kh, kh)].T
        for k in range(3):
            attend_ref[k] = a_ref[:, pl.ds(k * kh, kh)]
        for f in (0, 1):
            up_ref[:, pl.ds(f * fs, fs)] = m_ref[f, :, pl.ds(0, fs)]
            down_ref[pl.ds(f * fs, fs), :] = m_ref[f, :, pl.ds(fs, fs)].T


def finish(size, grad, grad_a, grad_m):
    positions, features = grad.shape
    rows = min(2048, positions)
    tb, fs = size.tb, size.fs
    whole = [((features, tb), F32), ((tb, 2 * fs), F32), ((2 * fs, tb), F32), ((3, tb, features), F32)]
    return pl.pallas_call(
        functools.partial(finish_kernel, features, fs),
        grid=(positions // rows,),
        in_specs=[
            pl.BlockSpec((rows, features), lambda i: (i, 0)),
            pl.BlockSpec(grad_a.shape, lambda i: (0, 0)),
            pl.BlockSpec(grad_m.shape, lambda i: (0, 0, 0)),
        ],
        out_specs=[pl.BlockSpec((rows // t, features), lambda i: (i, 0)) for t in (1, 4, 16)]
        + [pl.BlockSpec(shape, lambda i, n=len(shape): (0,) * n) for shape, _ in whole],
        out_shape=[jax.ShapeDtypeStruct((positions // t, features), F32) for t in (1, 4, 16)]
        + [jax.ShapeDtypeStruct(*x) for x in whole],
        compiler_params=pltpu.CompilerParams(vmem_limit_bytes=60 * 2**20),
        name="token_gradients",
    )(grad, grad_a, grad_m)


def shards(
    tokens,
    middle_cond,
    coarse_cond,
    first_gain,
    first_shift,
    attend_weight,
    query_bias,
    value_bias,
    output_weight,
    mixer_bias,
    second_gain,
    second_shift,
    up_weight,
    hidden_bias,
    down_weight,
    down_bias,
    cotangent,
):
    positions, features = tokens.shape
    n_hid, n_tok = lax.axis_size("hid"), lax.axis_size("tok")
    d = features * n_hid
    ff = up_weight.shape[1] * n_hid
    size = Sizes(positions, features, d, ff, n_tok, n_hid)
    tree = Tree(n_hid)
    tb, fs, wide, z = size.tb, size.fs, size.wide, size.z
    vectors = (first_gain, first_shift, second_gain, second_shift, query_bias, value_bias, mixer_bias, down_bias)
    rows = [v.reshape(1, features) for v in vectors] + [hidden_bias.reshape(ff // d, features)]
    units = len(tree.units)
    outputs = {
        "layer_out": ((positions, features), BF16),
        "grad_rows": ((positions, features), BF16),
        "grad_a": ((tb, wide), F32),
        "grad_m": ((2, tb, wide), F32),
        "small": ((SMALL_ROWS, features), F32),
        "all_a": ((n_hid, z, 2, tb, wide), BF16),
        "all_m": ((units, z, 2, tb, wide), BF16),
        "own_ga": ((n_hid, z, tb, wide), BF16),
        "sib_ga": ((n_hid, z, tb, wide), BF16),
        "got_ga": ((units, z, size.half, wide), BF16),
        "own_gm": ((units, z, tb, wide), BF16),
        "sib_gm": ((units, z, tb, wide), BF16),
        "got_gm": ((units, z, tb, wide), BF16),
        "z_ga": ((2, z, size.half, wide), BF16),
        "z_gm": ((2, z + len(tree.far), tb, wide), BF16),
        "z_far": ((units, z, tb, wide), BF16),
    }
    hbm = pl.BlockSpec(memory_space=pltpu.HBM)
    results = pl.pallas_call(
        functools.partial(layer_kernel, size, tree),
        out_shape=[jax.ShapeDtypeStruct(*outputs[name]) for name in OUTPUTS],
        in_specs=[hbm] * (len(INPUTS) + len(rows)),
        out_specs=[hbm] * len(OUTPUTS),
        scratch_shapes=list(scratch(size, tree).values()),
        compiler_params=pltpu.CompilerParams(
            collective_id=0, has_side_effects=True, vmem_limit_bytes=63 * 2**20
        ),
        cost_estimate=pl.CostEstimate(flops=80 * 10**9, bytes_accessed=2 * 10**8, transcendentals=10**7),
        name="layer",
    )(
        tokens,
        middle_cond,
        coarse_cond,
        cotangent,
        attend_weight.transpose(1, 0, 2),
        output_weight,
        up_weight,
        down_weight,
        *rows,
    )
    layer_out, grad_rows, grad_a, grad_m, small = results[:5]
    grad_tokens, grad_middle, grad_coarse, grad_output, grad_up, grad_down, grad_attend = finish(
        size, grad_rows, grad_a, grad_m
    )
    tok = lax.axis_index("tok")
    share = features // n_tok
    mine = lax.dynamic_slice_in_dim(small[:8], tok * share, share, 1)
    hidden_share = fs * 2 // n_tok
    first = tok * hidden_share
    grad_hidden_bias = lax.dynamic_slice(
        small, (8 + first // features, lax.rem(first, features)), (1, hidden_share)
    ).reshape(hidden_share)
    return (
        layer_out,
        grad_tokens,
        grad_middle,
        grad_coarse,
        mine[0],
        mine[1],
        grad_attend.transpose(1, 0, 2),
        mine[4],
        mine[5],
        grad_output,
        mine[6],
        mine[2],
        mine[3],
        grad_up,
        grad_hidden_bias,
        grad_down,
        mine[7],
    )


def solution(mesh):
    return jax.shard_map(
        shards,
        mesh=mesh,
        in_specs=(
            P("tok", "hid"),
            P("tok", "hid"),
            P("tok", "hid"),
            P("hid"),
            P("hid"),
            P("tok", None, "hid"),
            P("hid"),
            P("hid"),
            P("hid", "tok"),
            P("hid"),
            P("hid"),
            P("hid"),
            P("tok", "hid"),
            P("hid"),
            P("hid", "tok"),
            P("hid"),
            P("tok", "hid"),
        ),
        out_specs=(
            P("tok", "hid"),
            P("tok", "hid"),
            P("tok", "hid"),
            P("tok", "hid"),
            P(("hid", "tok")),
            P(("hid", "tok")),
            P("tok", None, "hid"),
            P(("hid", "tok")),
            P(("hid", "tok")),
            P("hid", "tok"),
            P(("hid", "tok")),
            P(("hid", "tok")),
            P(("hid", "tok")),
            P("tok", "hid"),
            P(("hid", "tok")),
            P("hid", "tok"),
            P(("hid", "tok")),
        ),
        check_vma=False,
    )
```
